32 devices in a mesh: parts: 2 (over x), dp: 16 (over z, y, core).
Axes of the slice: x: 2, y: 2, z: 4, core: 2. Of those that a mesh axis runs over, the one named last changes fastest.
Arguments:
- acts: bfloat16 [16384, 4096], P(('parts', 'dp')), parts along dimension 0, may hold values from -24 to 24
- grads: bfloat16 [16384, 4096], P(('parts', 'dp')), parts along dimension 0, may hold values from -24 to 24
- proj_act: bfloat16 [4096, 64], replicated, may hold values from -0.09375 to 0.09375
- proj_grad: bfloat16 [4096, 64], replicated, may hold values from -0.09375 to 0.09375
- queries: bfloat16 [128, 4096], P('dp'), may hold values from -6 to 6
Outputs:
- token_scores: float32 [16384, 128], P(('parts', 'dp')), parts along dimension 0
The draws below stay inside these ranges and needn't reach their ends.
There are 2 independent parts, one for each index of `parts`. The reference program is written for one: setup_inputs(seed, part) draws one part's arguments, and reference() takes and returns one part's arrays. A program takes and returns all parts, laid end to end along the dimension named above; an argument that names none is the same for every part. Nothing has to cross between parts.
All inputs are finite; a program needn't handle non-finite values.
Results may differ from the reference program's by a relative error of at most 0.0003.
Values may be sent and summed in bfloat16 or wider, within the bound.
No kernel may reach another device: no remote copies, remote signals or barrier semaphores. Data moves between devices by JAX's collectives and lax.ppermute only.
A program may use at most 128 MiB of HBM per device.

```python
import math
import jax
import jax.numpy as jnp
from jax import lax

D = 4096
RANK = 64
TOK_DEV = 512
TOKENS = 8192
QUERIES = 128
N_DP = 16


def scaled_rows(base, key, low, high):
    rise = 1.0 + 2.0 * jnp.arange(TOKENS, dtype=jnp.float32)[:, None] / TOKENS
    factor = jnp.exp(jax.random.uniform(key, (TOKENS, 1), jnp.float32, math.log(low), math.log(high)))
    return jnp.clip(base * rise * factor, -24.0, 24.0).astype(jnp.bfloat16)


def draw_acts(key, part):
    key = jax.random.fold_in(key, 11)
    first, second = jax.random.split(key, 2)
    base = jax.random.normal(first, (TOKENS, D), jnp.float32)
    return scaled_rows(base, second, 0.5, 2.0)


def draw_grads(key, part):
    key = jax.random.fold_in(key, 23)
    first, second = jax.random.split(key, 2)
    base = jax.random.normal(first, (TOKENS, D), jnp.float32)
    return scaled_rows(base, second, 0.5, 2.0)


def block_scale(rng, shape, shards, smallest, top_value):
    level, own = 1.0, jax.random.fold_in(rng, 6)
    for axis_at, parts in shards:
        draws = jnp.exp(jax.random.uniform(jax.random.fold_in(own, axis_at), (parts,), jnp.float32, smallest / len(shards), top_value / len(shards)))
        level = level * jnp.repeat(draws, shape[axis_at] // parts).reshape([-1 if axis == axis_at else 1 for axis in range(len(shape))])
    return level


def bell_draw(own_key, shape, scale, bound, cuts=(), held_as=jnp.bfloat16):
    result = scale * jax.random.normal(own_key, shape, jnp.float32)
    if cuts:
        result = result * block_scale(own_key, shape, cuts, -0.22, 0.18)
    return jnp.clip(result, -bound, bound).astype(held_as)


def setup_inputs(seed: int = 0, part: int = 0) -> dict:
    key_list = jax.random.split(jax.random.key(seed), 6)
    part_keys = jax.random.split(jax.random.fold_in(key_list[5], part), 6)
    acts = draw_acts(jax.random.fold_in(jax.random.fold_in(key_list[5], part), 71), part)
    grads = draw_grads(jax.random.fold_in(jax.random.fold_in(key_list[5], part), 71), part)
    proj_act = bell_draw(key_list[2], (D, RANK), D ** -0.5, 0.09375)
    proj_grad = bell_draw(key_list[3], (D, RANK), D ** -0.5, 0.09375)
    queries = bell_draw(key_list[4], (QUERIES, RANK * RANK), 1.0, 6.0, ((0, 16),))
    return dict(acts=acts, grads=grads, proj_act=proj_act, proj_grad=proj_grad, queries=queries)


DAMP = 0.1

def inverse_of(cov):
    identity = jnp.eye(cov.shape[0], dtype=jnp.float32)
    lower = jnp.linalg.cholesky(cov)
    solved = lax.linalg.triangular_solve(lower, identity, left_side=True, lower=True)
    return jnp.dot(solved.T, solved, precision=lax.Precision.HIGHEST)

def reference(acts, grads, proj_act, proj_grad, queries):
    act_proj = jnp.dot(acts.astype(jnp.float32), proj_act.astype(jnp.float32), preferred_element_type=jnp.float32)
    grad_proj = jnp.dot(grads.astype(jnp.float32), proj_grad.astype(jnp.float32), preferred_element_type=jnp.float32)
    identity = jnp.eye(RANK, dtype=jnp.float32)
    cov_act = jnp.dot(act_proj.T, act_proj, precision=lax.Precision.HIGHEST) / TOKENS + DAMP * identity
    cov_grad = jnp.dot(grad_proj.T, grad_proj, precision=lax.Precision.HIGHEST) / TOKENS + DAMP * identity
    inverse_act = inverse_of(cov_act)
    inverse_grad = inverse_of(cov_grad)
    blocks = queries.astype(jnp.float32).reshape(QUERIES, RANK, RANK)
    precond = jnp.einsum('ik,qkl,lj->qij', inverse_grad, blocks, inverse_act, precision=lax.Precision.HIGHEST)
    precond = precond.reshape(QUERIES, RANK * RANK)
    outer = (grad_proj[:, :, None] * act_proj[:, None, :]).reshape(TOKENS, RANK * RANK)
    tok_blocks = outer.reshape(N_DP, TOK_DEV, RANK * RANK)

    def score_block(block):
        return jnp.dot(block, precond.T, precision=lax.Precision.HIGHEST)
    token_scores = lax.map(score_block, tok_blocks)
    return token_scores.reshape(TOKENS, QUERIES)
```

```python
import functools

import jax
import jax.numpy as jnp
from jax import lax
from jax.experimental import pallas as pl
from jax.experimental.pallas import tpu as pltpu
from jax.sharding import PartitionSpec as P

DAMP = 0.1
HIGHEST = lax.Precision.HIGHEST
CHUNKS = 4


def dot_nt(left, right, precision=None):
    return lax.dot_general(
        left, right, (((1,), (1,)), ((), ())), precision=precision, preferred_element_type=jnp.float32
    )


def project_kernel(acts, grads, proj_act, proj_grad, proj_t, cov, tok_buf, weight_buf, tok_sems, weight_sems):
    factor, width = proj_act.shape
    step = width // CHUNKS
    weight_copies = [
        pltpu.make_async_copy(src, weight_buf.at[at, pl.ds(at * factor, factor), :], weight_sems.at[at])
        for at, src in enumerate((proj_act, proj_grad))
    ]
    tok_copies = [
        [
            pltpu.make_async_copy(
                src.at[:, pl.ds(part * step, step)], tok_buf.at[at, part], tok_sems.at[at, part]
            )
            for at, src in enumerate((acts, grads))
        ]
        for part in range(CHUNKS)
    ]
    for copy in weight_copies:
        copy.start()
    for pair in tok_copies:
        for copy in pair:
            copy.start()
    blank = jnp.zeros((factor, width), weight_buf.dtype)
    weight_buf[0, factor:, :] = blank
    weight_buf[1, :factor, :] = blank
    for copy in weight_copies:
        copy.wait()
    both = None
    for part in range(CHUNKS):
        for at in range(2):
            tok_copies[part][at].wait()
            term = dot_nt(tok_buf[at, part], weight_buf[at, :, part * step : (part + 1) * step])
            both = term if both is None else both + term
    flipped = both.T
    proj_t[...] = flipped
    gram = jnp.dot(flipped, both, precision=HIGHEST, preferred_element_type=jnp.float32)
    lane = lax.broadcasted_iota(jnp.int32, (factor, 2 * factor), 1)
    cov[...] = jnp.where(lane < factor, gram[:factor, :], gram[factor:, :])


def project(acts, grads, proj_act, proj_grad):
    tok_rows, width = acts.shape
    factor = proj_act.shape[1]
    return pl.pallas_call(
        project_kernel,
        out_shape=(
            jax.ShapeDtypeStruct((2 * factor, tok_rows), jnp.float32),
            jax.ShapeDtypeStruct((factor, 2 * factor), jnp.float32),
        ),
        in_specs=[pl.BlockSpec(memory_space=pl.ANY)] * 4,
        out_specs=[pl.BlockSpec(memory_space=pltpu.VMEM)] * 2,
        scratch_shapes=[
            pltpu.VMEM((2, CHUNKS, tok_rows, width // CHUNKS), acts.dtype),
            pltpu.VMEM((2, 2 * factor, width), proj_act.dtype),
            pltpu.SemaphoreType.DMA((2, CHUNKS)),
            pltpu.SemaphoreType.DMA((2,)),
        ],
        compiler_params=pltpu.CompilerParams(vmem_limit_bytes=40 * 2**20),
        name="project",
    )(acts, grads, proj_act.T, proj_grad.T)


def inverse_pair(both):
    factor = both.shape[0]
    lane = lax.broadcasted_iota(jnp.int32, both.shape, 1)
    row_at = lax.broadcasted_iota(jnp.int32, both.shape, 0)
    left_half = lane < factor
    inner = jnp.where(left_half, lane, lane - factor)
    for k in range(factor):
        column = jnp.where(left_half, both[:, k : k + 1], both[:, factor + k : factor + k + 1])
        on_lane = inner == k
        scale = 1.0 / column[k : k + 1, :]
        pivot_row = jnp.where(on_lane[:1], 1.0, both[k : k + 1, :]) * scale
        rest = jnp.where(on_lane, 0.0, both) - column * pivot_row
        both = jnp.where(row_at == k, pivot_row, rest)
    return both


def score_kernel(tok_total, terms, proj_t, queries, scores, queries_buf, moved, total, sem):
    factor = proj_t.shape[0] // 2
    copy = pltpu.make_async_copy(queries, queries_buf, sem)
    copy.start()
    both = terms[0][...]
    for term in terms[1:]:
        both = both + term[...]
    lane = lax.broadcasted_iota(jnp.int32, both.shape, 1)
    row_at = lax.broadcasted_iota(jnp.int32, both.shape, 0)
    left_half = lane < factor
    inner = jnp.where(left_half, lane, lane - factor)
    both = both / tok_total + jnp.where(inner == row_at, DAMP, 0.0)
    both = inverse_pair(both)
    blocks = jnp.concatenate(
        [jnp.where(left_half, both, 0.0), jnp.where(left_half, 0.0, both)], axis=0
    )
    moved[...] = jnp.dot(blocks, proj_t[...], precision=HIGHEST, preferred_element_type=jnp.float32)
    copy.wait()
    group = 4
    act_side = moved[:factor, :]
    for first in range(0, factor, group):
        outer = jnp.concatenate(
            [act_side * moved[factor + i : factor + i + 1, :] for i in range(first, first + group)], axis=0
        )
        high = outer.astype(jnp.bfloat16)
        low = (outer - high.astype(jnp.float32)).astype(jnp.bfloat16)
        piece = queries_buf[:, first * factor : (first + group) * factor]
        term = jnp.dot(piece, high, preferred_element_type=jnp.float32)
        term = term + jnp.dot(piece, low, preferred_element_type=jnp.float32)
        if first == 0:
            total[...] = term
        else:
            total[...] += term
    scores[...] = total[...].T


def score(tok_total, terms, proj_t, queries):
    tok_rows = proj_t.shape[1]
    n_queries, flat = queries.shape

    def kernel(*refs):
        n = len(terms)
        score_kernel(tok_total, refs[:n], *refs[n:])

    return pl.pallas_call(
        kernel,
        out_shape=jax.ShapeDtypeStruct((tok_rows, n_queries), jnp.float32),
        in_specs=[pl.BlockSpec(memory_space=pltpu.VMEM)] * (len(terms) + 1)
        + [pl.BlockSpec(memory_space=pl.ANY)],
        out_specs=pl.BlockSpec(memory_space=pltpu.VMEM),
        scratch_shapes=[
            pltpu.VMEM((n_queries, flat), queries.dtype),
            pltpu.VMEM(proj_t.shape, jnp.float32),
            pltpu.VMEM((n_queries, tok_rows), jnp.float32),
            pltpu.SemaphoreType.DMA,
        ],
        compiler_params=pltpu.CompilerParams(vmem_limit_bytes=40 * 2**20),
        name="score",
    )(*terms, proj_t, queries)


def stages_of(size):
    low = 1
    while low * low < size:
        low *= 2
    if size % low:
        return [(1, size)]
    return [(1, low), (low, size // low)]


def shifted(value, size, stride, radix, shift):
    perm = []
    for at in range(size):
        digit = at // stride % radix
        perm.append((at, at + ((digit + shift) % radix - digit) * stride))
    return lax.ppermute(value, "dp", perm)


def on_device(acts, grads, proj_act, proj_grad, queries):
    size = lax.axis_size("dp")
    tok_total = acts.shape[0] * size
    all_queries = lax.all_gather(queries, "dp", axis=0, tiled=True)
    proj_t, cov = project(acts, grads, proj_act, proj_grad)
    terms = [cov]
    for stride, radix in stages_of(size):
        own = functools.reduce(jnp.add, terms)
        terms = [own] + [shifted(own, size, stride, radix, shift) for shift in range(1, radix)]
    return score(tok_total, terms, proj_t, all_queries)


def solution(mesh):
    in_specs = (P(("parts", "dp"), None), P(("parts", "dp"), None), P(), P(), P("dp", None))
    out_specs = P(("parts", "dp"), None)
    return jax.shard_map(
        on_device, mesh=mesh, in_specs=in_specs, out_specs=out_specs, check_vma=False
    )
```

```python
import functools

import jax
import jax.numpy as jnp
from jax import lax
from jax.experimental import pallas as pl
from jax.experimental.pallas import tpu as pltpu
from jax.sharding import PartitionSpec as P

DAMP = 0.1
HIGHEST = lax.Precision.HIGHEST
CHUNKS = 8


def dot_nt(left, right, precision=None):
    return lax.dot_general(
        left, right, (((1,), (1,)), ((), ())), precision=precision, preferred_element_type=jnp.float32
    )


def project_kernel(acts, grads, proj_act, proj_grad, proj_t, cov, tok_buf, weight_buf, tok_sems, weight_sems):
    factor, width = proj_act.shape
    step = width // CHUNKS
    weight_copies = [
        pltpu.make_async_copy(src, weight_buf.at[at, pl.ds(at * factor, factor), :], weight_sems.at[at])
        for at, src in enumerate((proj_act, proj_grad))
    ]
    tok_copies = [
        [
            pltpu.make_async_copy(
                src.at[:, pl.ds(part * step, step)], tok_buf.at[at, part], tok_sems.at[at, part]
            )
            for at, src in enumerate((acts, grads))
        ]
        for part in range(CHUNKS)
    ]
    for copy in weight_copies:
        copy.start()
    for pair in tok_copies:
        for copy in pair:
            copy.start()
    blank = jnp.zeros((factor, width), weight_buf.dtype)
    weight_buf[0, factor:, :] = blank
    weight_buf[1, :factor, :] = blank
    for copy in weight_copies:
        copy.wait()
    both = None
    for part in range(CHUNKS):
        for at in range(2):
            tok_copies[part][at].wait()
            term = dot_nt(tok_buf[at, part], weight_buf[at, :, part * step : (part + 1) * step])
            both = term if both is None else both + term
    flipped = both.T
    proj_t[...] = flipped
    gram = jnp.dot(flipped, both, precision=HIGHEST, preferred_element_type=jnp.float32)
    lane = lax.broadcasted_iota(jnp.int32, (factor, 2 * factor), 1)
    cov[...] = jnp.where(lane < factor, gram[:factor, :], gram[factor:, :])


def project(acts, grads, proj_act, proj_grad):
    tok_rows, width = acts.shape
    factor = proj_act.shape[1]
    return pl.pallas_call(
        project_kernel,
        out_shape=(
            jax.ShapeDtypeStruct((2 * factor, tok_rows), jnp.float32),
            jax.ShapeDtypeStruct((factor, 2 * factor), jnp.float32),
        ),
        in_specs=[pl.BlockSpec(memory_space=pltpu.HBM)] * 4,
        out_specs=[pl.BlockSpec(memory_space=pltpu.VMEM)] * 2,
        scratch_shapes=[
            pltpu.VMEM((2, CHUNKS, tok_rows, width // CHUNKS), acts.dtype),
            pltpu.VMEM((2, 2 * factor, width), proj_act.dtype),
            pltpu.SemaphoreType.DMA((2, CHUNKS)),
            pltpu.SemaphoreType.DMA((2,)),
        ],
        compiler_params=pltpu.CompilerParams(vmem_limit_bytes=60 * 2**20),
        cost_estimate=pl.CostEstimate(
            flops=4 * tok_rows * width * factor, bytes_accessed=4 * tok_rows * width, transcendentals=0
        ),
        name="project",
    )(acts, grads, proj_act.T, proj_grad.T)


def inverse_pair(both):
    factor = both.shape[0]
    lane = lax.broadcasted_iota(jnp.int32, both.shape, 1)
    row_at = lax.broadcasted_iota(jnp.int32, both.shape, 0)
    left_half = lane < factor
    inner = jnp.where(left_half, lane, lane - factor)
    for k in range(factor):
        column = jnp.where(left_half, both[:, k : k + 1], both[:, factor + k : factor + k + 1])
        on_lane = inner == k
        scale = 1.0 / column[k : k + 1, :]
        pivot_row = jnp.where(on_lane[:1], 1.0, both[k : k + 1, :]) * scale
        rest = jnp.where(on_lane, 0.0, both) - column * pivot_row
        both = jnp.where(row_at == k, pivot_row, rest)
    return both


def precondition_kernel(tok_total, n_terms, *refs):
    terms, (proj_t, moved) = refs[:n_terms], refs[n_terms:]
    both = terms[0][...]
    for term in terms[1:]:
        both = both + term[...]
    factor = both.shape[0]
    lane = lax.broadcasted_iota(jnp.int32, both.shape, 1)
    row_at = lax.broadcasted_iota(jnp.int32, both.shape, 0)
    left_half = lane < factor
    inner = jnp.where(left_half, lane, lane - factor)
    both = both / tok_total + jnp.where(inner == row_at, DAMP, 0.0)
    both = inverse_pair(both)
    blocks = jnp.concatenate(
        [jnp.where(left_half, both, 0.0), jnp.where(left_half, 0.0, both)], axis=0
    )
    moved[...] = jnp.dot(blocks, proj_t[...], precision=HIGHEST, preferred_element_type=jnp.float32)


def precondition(tok_total, terms, proj_t):
    n_terms = len(terms)
    rows, tok_rows = proj_t.shape
    return pl.pallas_call(
        functools.partial(precondition_kernel, tok_total, n_terms),
        out_shape=jax.ShapeDtypeStruct(proj_t.shape, jnp.float32),
        in_specs=[pl.BlockSpec(memory_space=pltpu.VMEM)] * (n_terms + 1),
        out_specs=pl.BlockSpec(memory_space=pltpu.VMEM),
        compiler_params=pltpu.CompilerParams(vmem_limit_bytes=24 * 2**20),
        cost_estimate=pl.CostEstimate(
            flops=400 * rows * rows * tok_rows, bytes_accessed=8 * rows * tok_rows, transcendentals=0
        ),
        name="precondition",
    )(*terms, proj_t)


def score_kernel(size, n_pieces, moved, *refs):
    queries, (scores, total, ordered) = refs[:n_pieces], refs[n_pieces:]
    factor = moved.shape[0] // 2
    group = 4
    act_side = moved[:factor, :]
    for first in range(0, factor, group):
        outer = jnp.concatenate(
            [act_side * moved[factor + i : factor + i + 1, :] for i in range(first, first + group)], axis=0
        )
        high = outer.astype(jnp.bfloat16)
        low = (outer - high.astype(jnp.float32)).astype(jnp.bfloat16)
        done = 0
        for piece in queries:
            rows = piece.shape[0]
            values = piece[:, first * factor : (first + group) * factor]
            term = jnp.dot(values, high, preferred_element_type=jnp.float32)
            term = term + jnp.dot(values, low, preferred_element_type=jnp.float32)
            if first == 0:
                total[done : done + rows, :] = term
            else:
                total[done : done + rows, :] += term
            done += rows
    rows = total.shape[0] // size
    for at, owner in enumerate(owners_of(lax.axis_index("dp"), size)):
        ordered[pl.ds(pl.multiple_of(owner * rows, rows), rows), :] = total[at * rows : (at + 1) * rows, :]
    scores[...] = ordered[...].T


def score(size, moved, queries):
    tok_rows = moved.shape[1]
    n_queries = sum(piece.shape[0] for piece in queries)
    n_pieces = len(queries)
    return pl.pallas_call(
        functools.partial(score_kernel, size, n_pieces),
        out_shape=jax.ShapeDtypeStruct((tok_rows, n_queries), jnp.float32),
        in_specs=[pl.BlockSpec(memory_space=pltpu.VMEM)] * (1 + n_pieces),
        out_specs=pl.BlockSpec(memory_space=pltpu.VMEM),
        scratch_shapes=[
            pltpu.VMEM((n_queries, tok_rows), jnp.float32),
            pltpu.VMEM((n_queries, tok_rows), jnp.float32),
        ],
        compiler_params=pltpu.CompilerParams(vmem_limit_bytes=32 * 2**20),
        name="score",
    )(moved, *queries)


def gather_stages(size):
    core = 2 if size % 2 == 0 else 1
    rest = size // core
    near = max(d for d in range(1, rest + 1) if rest % d == 0 and d * d <= rest)
    return [(core * near, rest // near), (core, near), (1, core)]


def stages_of(size):
    low = 1
    while low * low < size:
        low *= 2
    if size % low:
        return [(1, 1), (1, size)]
    return [(1, low), (low, size // low)]


def shifted(value, size, stride, radix, shift):
    perm = []
    for at in range(size):
        digit = at // stride % radix
        perm.append((at, at + ((digit + shift) % radix - digit) * stride))
    return lax.ppermute(value, "dp", perm)


def after(value, other):
    return lax.optimization_barrier((value, other))[0]


def owners_of(me, size):
    owners = [me]
    for stride, radix in gather_stages(size):
        digit = lax.rem(lax.div(me, stride), radix)
        steps = [(lax.rem(digit + (radix - shift), radix) - digit) * stride for shift in range(radix)]
        owners = [owner + step for step in steps for owner in owners]
    return owners


def exchanged(held, size, stride, radix):
    mine = held[0] if len(held) == 1 else jnp.concatenate(held, axis=0)
    return [mine] + [shifted(mine, size, stride, radix, shift) for shift in range(1, radix)]


def on_device(acts, grads, proj_act, proj_grad, queries):
    size = lax.axis_size("dp")
    tok_total = acts.shape[0] * size
    far, near, core = gather_stages(size)
    first, second = stages_of(size)
    pieces = exchanged([queries], size, *far)
    proj_t, cov = project(acts, grads, proj_act, proj_grad)
    *pieces, cov = lax.optimization_barrier((*pieces, cov))
    terms = exchanged([cov], size, *first)
    pieces = exchanged(pieces, size, *near)
    terms = exchanged([functools.reduce(jnp.add, terms)], size, *second)
    pieces = exchanged([after(piece, terms) for piece in pieces], size, *core)
    moved = precondition(tok_total, terms, proj_t)
    return score(size, moved, pieces)


def solution(mesh):
    in_specs = (P(("parts", "dp"), None), P(("parts", "dp"), None), P(), P(), P("dp", None))
    out_specs = P(("parts", "dp"), None)
    return jax.shard_map(
        on_device, mesh=mesh, in_specs=in_specs, out_specs=out_specs, check_vma=False
    )
```

```python
import functools

import jax
import jax.numpy as jnp
from jax import lax
from jax.experimental import pallas as pl
from jax.experimental.pallas import tpu as pltpu
from jax.sharding import PartitionSpec as P

DAMP = 0.1
HIGHEST = lax.Precision.HIGHEST
COPY_ROWS = 128
DOT_ROWS = 256


def dot_nt(left, right, precision=None):
    return lax.dot_general(
        left, right, (((1,), (1,)), ((), ())), precision=precision, preferred_element_type=jnp.float32
    )


def project_kernel(acts, grads, proj_act, proj_grad, proj_t, cov, tok_buf, weight_buf, tok_sems, weight_sems):
    factor = proj_act.shape[0]
    tok_rows = acts.shape[0]
    weight_copies = [
        pltpu.make_async_copy(src, weight_buf.at[at], weight_sems.at[at]) for at, src in enumerate((proj_act, proj_grad))
    ]
    tok_copies = [
        [
            pltpu.make_async_copy(
                src.at[pl.ds(part * COPY_ROWS, COPY_ROWS), :],
                tok_buf.at[at, pl.ds(part * COPY_ROWS, COPY_ROWS), :],
                tok_sems.at[at, part],
            )
            for part in range(tok_rows // COPY_ROWS)
        ]
        for at, src in enumerate((acts, grads))
    ]
    for at in range(2):
        weight_copies[at].start()
        for copy in tok_copies[at]:
            copy.start()
    for at in range(2):
        weight_copies[at].wait()
        for first in range(0, tok_rows, DOT_ROWS):
            for part in range(first // COPY_ROWS, (first + DOT_ROWS) // COPY_ROWS):
                tok_copies[at][part].wait()
            proj_t[at * factor : (at + 1) * factor, first : first + DOT_ROWS] = dot_nt(
                weight_buf[at], tok_buf[at, first : first + DOT_ROWS, :]
            )
    both = proj_t[...]
    gram = dot_nt(both, both, HIGHEST)
    lane = lax.broadcasted_iota(jnp.int32, (factor, 2 * factor), 1)
    paired = jnp.where(lane < factor, gram[:factor, :], gram[factor:, :])
    step = cov.shape[1]
    for at in range(cov.shape[0]):
        cov[at] = paired[at * step : (at + 1) * step, :]


def project(n_slices, acts, grads, proj_act, proj_grad):
    tok_rows, width = acts.shape
    factor = proj_act.shape[1]
    operands = [
        pltpu.with_memory_space_constraint(value, pltpu.HBM) for value in (acts, grads, proj_act.T, proj_grad.T)
    ]
    return pl.pallas_call(
        project_kernel,
        out_shape=(
            jax.ShapeDtypeStruct((2 * factor, tok_rows), jnp.float32),
            jax.ShapeDtypeStruct((n_slices, factor // n_slices, 2 * factor), jnp.float32),
        ),
        in_specs=[pl.BlockSpec(memory_space=pltpu.HBM)] * 4,
        out_specs=[pl.BlockSpec(memory_space=pltpu.VMEM)] * 2,
        scratch_shapes=[
            pltpu.VMEM((2, tok_rows, width), acts.dtype),
            pltpu.VMEM((2, factor, width), proj_act.dtype),
            pltpu.SemaphoreType.DMA((2, tok_rows // COPY_ROWS)),
            pltpu.SemaphoreType.DMA((2,)),
        ],
        compiler_params=pltpu.CompilerParams(vmem_limit_bytes=24 * 2**20),
        cost_estimate=pl.CostEstimate(
            flops=4 * tok_rows * width * factor, bytes_accessed=4 * tok_rows * width, transcendentals=0
        ),
        name="project",
    )(*operands)


def inverse_pair(both):
    factor = both.shape[0]
    lane = lax.broadcasted_iota(jnp.int32, both.shape, 1)
    row_at = lax.broadcasted_iota(jnp.int32, both.shape, 0)
    left_half = lane < factor
    inner = jnp.where(left_half, lane, lane - factor)
    for k in range(factor):
        column = jnp.where(left_half, both[:, k : k + 1], both[:, factor + k : factor + k + 1])
        on_lane = inner == k
        scale = 1.0 / column[k : k + 1, :]
        pivot_row = jnp.where(on_lane[:1], 1.0, both[k : k + 1, :]) * scale
        rest = jnp.where(on_lane, 0.0, both) - column * pivot_row
        both = jnp.where(row_at == k, pivot_row, rest)
    return both


def precondition_kernel(tok_total, sums, proj_t, moved, proj_buf, sem):
    copy = pltpu.make_async_copy(proj_t, proj_buf, sem)
    copy.start()
    both = jnp.concatenate([sums[at] for at in range(sums.shape[0])], axis=0)
    factor = both.shape[0]
    lane = lax.broadcasted_iota(jnp.int32, both.shape, 1)
    row_at = lax.broadcasted_iota(jnp.int32, both.shape, 0)
    left_half = lane < factor
    inner = jnp.where(left_half, lane, lane - factor)
    both = both / tok_total + jnp.where(inner == row_at, DAMP, 0.0)
    both = inverse_pair(both)
    blocks = jnp.concatenate(
        [jnp.where(left_half, both, 0.0), jnp.where(left_half, 0.0, both)], axis=0
    )
    copy.wait()
    moved[...] = jnp.dot(blocks, proj_buf[...], precision=HIGHEST, preferred_element_type=jnp.float32)


def precondition(tok_total, sums, proj_t):
    rows, tok_rows = proj_t.shape
    return pl.pallas_call(
        functools.partial(precondition_kernel, tok_total),
        out_shape=jax.ShapeDtypeStruct(proj_t.shape, jnp.float32),
        in_specs=[pl.BlockSpec(memory_space=pltpu.VMEM), pl.BlockSpec(memory_space=pl.ANY)],
        out_specs=pl.BlockSpec(memory_space=pltpu.VMEM),
        scratch_shapes=[pltpu.VMEM(proj_t.shape, jnp.float32), pltpu.SemaphoreType.DMA],
        compiler_params=pltpu.CompilerParams(vmem_limit_bytes=24 * 2**20),
        cost_estimate=pl.CostEstimate(
            flops=400 * rows * rows * tok_rows, bytes_accessed=8 * rows * tok_rows, transcendentals=0
        ),
        name="precondition",
    )(sums, proj_t)


def score_kernel(size, n_pieces, moved, *refs):
    queries, (scores, total, ordered) = refs[:n_pieces], refs[n_pieces:]
    factor = moved.shape[0] // 2
    group = 4
    act_side = moved[:factor, :]
    for first in range(0, factor, group):
        outer = jnp.concatenate(
            [act_side * moved[factor + i : factor + i + 1, :] for i in range(first, first + group)], axis=0
        )
        high = outer.astype(jnp.bfloat16)
        low = (outer - high.astype(jnp.float32)).astype(jnp.bfloat16)
        done = 0
        for piece in queries:
            rows = piece.shape[0]
            values = piece[:, first * factor : (first + group) * factor]
            term = jnp.dot(values, high, preferred_element_type=jnp.float32)
            term = term + jnp.dot(values, low, preferred_element_type=jnp.float32)
            if first == 0:
                total[done : done + rows, :] = term
            else:
                total[done : done + rows, :] += term
            done += rows
    rows = total.shape[0] // size
    for at, owner in enumerate(owners_of(lax.axis_index("dp"), size)):
        ordered[pl.ds(pl.multiple_of(owner * rows, rows), rows), :] = total[at * rows : (at + 1) * rows, :]
    scores[...] = ordered[...].T


def score(size, moved, queries):
    tok_rows = moved.shape[1]
    n_queries = sum(piece.shape[0] for piece in queries)
    n_pieces = len(queries)
    return pl.pallas_call(
        functools.partial(score_kernel, size, n_pieces),
        out_shape=jax.ShapeDtypeStruct((tok_rows, n_queries), jnp.float32),
        in_specs=[pl.BlockSpec(memory_space=pltpu.VMEM)] * (1 + n_pieces),
        out_specs=pl.BlockSpec(memory_space=pltpu.VMEM),
        scratch_shapes=[
            pltpu.VMEM((n_queries, tok_rows), jnp.float32),
            pltpu.VMEM((n_queries, tok_rows), jnp.float32),
        ],
        compiler_params=pltpu.CompilerParams(vmem_limit_bytes=32 * 2**20),
        name="score",
    )(moved, *queries)


def gather_stages(size):
    core = 2 if size % 2 == 0 else 1
    rest = size // core
    near = max(d for d in range(1, rest + 1) if rest % d == 0 and d * d <= rest)
    return [(core * near, rest // near), (core, near), (1, core)]


def partner(digit, radix, shift):
    return digit ^ shift if radix & (radix - 1) == 0 else (digit + shift) % radix


def swapped(value, size, stride, radix, shift):
    perm = []
    for at in range(size):
        digit = at // stride % radix
        perm.append((at, at + (partner(digit, radix, shift) - digit) * stride))
    return lax.ppermute(value, "dp", perm)


def owners_of(me, size):
    owners = [me]
    for stride, radix in gather_stages(size):
        digit = lax.rem(lax.div(me, stride), radix)
        back = [shift if radix & (radix - 1) == 0 else radix - shift for shift in range(radix)]
        steps = [(partner(digit, radix, shift) - digit) * stride for shift in back]
        owners = [owner + step for step in steps for owner in owners]
    return owners


def exchanged(held, size, stride, radix):
    mine = held[0] if len(held) == 1 else jnp.concatenate(held, axis=0)
    return [mine] + [swapped(mine, size, stride, radix, shift) for shift in range(1, radix)]


def on_device(acts, grads, proj_act, proj_grad, queries):
    size = lax.axis_size("dp")
    factor = proj_act.shape[1]
    tok_total = acts.shape[0] * size
    far, near, core = gather_stages(size)
    pieces = exchanged([queries], size, *far)
    sliced = factor % size == 0
    proj_t, cov = project(size if sliced else 1, acts, grads, proj_act, proj_grad)
    *pieces, cov = lax.optimization_barrier((*pieces, cov))
    pieces = exchanged(pieces, size, *near)
    if sliced:
        mine = jnp.sum(lax.all_to_all(cov, "dp", 0, 0, tiled=True), axis=0)
        *pieces, mine = lax.optimization_barrier((*pieces, mine))
        sums = lax.all_to_all(jnp.broadcast_to(mine, cov.shape), "dp", 0, 0, tiled=True)
    else:
        sums = lax.psum(cov, "dp")
    pieces = exchanged(pieces, size, *core)
    moved = precondition(tok_total, sums, proj_t)
    return score(size, moved, pieces)


def solution(mesh):
    in_specs = (P(("parts", "dp"), None), P(("parts", "dp"), None), P(), P(), P("dp", None))
    out_specs = P(("parts", "dp"), None)
    return jax.shard_map(
        on_device, mesh=mesh, in_specs=in_specs, out_specs=out_specs, check_vma=False
    )
```

```python
import functools

import jax
import jax.numpy as jnp
from jax import lax
from jax.experimental import pallas as pl
from jax.experimental.pallas import tpu as pltpu
from jax.sharding import PartitionSpec as P

DAMP = 0.1
HIGHEST = lax.Precision.HIGHEST
COPY_ROWS = 128
DOT_ROWS = 256
IN_FLIGHT = 2


def dot_nt(left, right, precision=None):
    return lax.dot_general(
        left, right, (((1,), (1,)), ((), ())), precision=precision, preferred_element_type=jnp.float32
    )


def project_kernel(tokens, weight, *refs):
    *before, proj_t, gram, tok_buf, weight_buf, tok_sems, weight_sem = refs
    tok_rows = tokens.shape[0]
    weight_copy = pltpu.make_async_copy(weight, weight_buf, weight_sem)
    copies = [
        pltpu.make_async_copy(
            tokens.at[pl.ds(part * COPY_ROWS, COPY_ROWS), :],
            tok_buf.at[pl.ds(part * COPY_ROWS, COPY_ROWS), :],
            tok_sems.at[part],
        )
        for part in range(tok_rows // COPY_ROWS)
    ]
    weight_copy.start()
    for copy in copies[:IN_FLIGHT]:
        copy.start()
    weight_copy.wait()
    for first in range(0, tok_rows, DOT_ROWS):
        for part in range(first // COPY_ROWS, (first + DOT_ROWS) // COPY_ROWS):
            copies[part].wait()
            if part + IN_FLIGHT < len(copies):
                copies[part + IN_FLIGHT].start()
        proj_t[:, first : first + DOT_ROWS] = dot_nt(weight_buf[...], tok_buf[first : first + DOT_ROWS, :])
    result = dot_nt(proj_t[...], proj_t[...], HIGHEST)
    gram[...] = jnp.concatenate([ref[...] for ref in before] + [result], axis=1)


def project(tokens, weight, *before):
    tok_rows, width = tokens.shape
    factor = weight.shape[1]
    operands = [pltpu.with_memory_space_constraint(value, pltpu.HBM) for value in (tokens, weight.T)]
    return pl.pallas_call(
        project_kernel,
        out_shape=(
            jax.ShapeDtypeStruct((factor, tok_rows), jnp.float32),
            jax.ShapeDtypeStruct((factor, (1 + len(before)) * factor), jnp.float32),
        ),
        in_specs=[pl.BlockSpec(memory_space=pltpu.HBM)] * 2
        + [pl.BlockSpec(memory_space=pltpu.VMEM)] * len(before),
        out_specs=[pl.BlockSpec(memory_space=pltpu.VMEM)] * 2,
        scratch_shapes=[
            pltpu.VMEM((tok_rows, width), tokens.dtype),
            pltpu.VMEM((factor, width), weight.dtype),
            pltpu.SemaphoreType.DMA((tok_rows // COPY_ROWS,)),
            pltpu.SemaphoreType.DMA,
        ],
        compiler_params=pltpu.CompilerParams(vmem_limit_bytes=24 * 2**20),
        cost_estimate=pl.CostEstimate(
            flops=2 * tok_rows * width * factor, bytes_accessed=2 * tok_rows * width, transcendentals=0
        ),
        name="project",
    )(*operands, *before)


def inverse_pair(both):
    factor = both.shape[0]
    tile = (8, both.shape[1])
    lane = lax.broadcasted_iota(jnp.int32, tile, 1)
    row_at = lax.broadcasted_iota(jnp.int32, tile, 0)
    left_half = lane < factor
    inner = jnp.where(left_half, lane, lane - factor)
    parts = [both[at : at + 8, :] for at in range(0, factor, 8)]

    def column(part, at):
        left = jnp.broadcast_to(part[:, at : at + 1], tile)
        right = jnp.broadcast_to(part[:, factor + at : factor + at + 1], tile)
        return jnp.where(left_half, left, right)

    def row(part, at):
        return jnp.broadcast_to(part[at : at + 1, :], tile)

    for k in range(0, factor, 4):
        home, off = divmod(k, 8)
        columns = [[column(part, k + a) for part in parts] for a in range(4)]
        pivot = [[row(columns[b][home], off + a) if a <= b else None for b in range(4)] for a in range(4)]
        p00, p01, p02, p03 = pivot[0]
        _, p11, p12, p13 = pivot[1]
        _, _, p22, p23 = pivot[2]
        p33 = pivot[3][3]
        on_block = (inner >= k) & (inner < k + 4)
        r0, r1, r2, r3 = [
            jnp.where(on_block, jnp.where(inner == k + a, 1.0, 0.0), row(parts[home], off + a)) for a in range(4)
        ]
        scale = 1.0 / (p00 * p11 - p01 * p01)
        e02 = scale * (p11 * p02 - p01 * p12)
        e03 = scale * (p11 * p03 - p01 * p13)
        e12 = scale * (p00 * p12 - p01 * p02)
        e13 = scale * (p00 * p13 - p01 * p03)
        s22 = p22 - (p02 * e02 + p12 * e12)
        s23 = p23 - (p02 * e03 + p12 * e13)
        s33 = p33 - (p03 * e03 + p13 * e13)
        scale_s = 1.0 / (s22 * s33 - s23 * s23)
        y0 = scale * (p11 * r0 - p01 * r1)
        y1 = scale * (p00 * r1 - p01 * r0)
        t2 = r2 - (p02 * y0 + p12 * y1)
        t3 = r3 - (p03 * y0 + p13 * y1)
        w2 = scale_s * (s33 * t2 - s23 * t3)
        w3 = scale_s * (s22 * t3 - s23 * t2)
        w0 = y0 - (e02 * w2 + e03 * w3)
        w1 = y1 - (e12 * w2 + e13 * w3)
        solved = (w0, w1, w2, w3)
        for m, part in enumerate(parts):
            change = (columns[0][m] * w0 + columns[1][m] * w1) + (columns[2][m] * w2 + columns[3][m] * w3)
            part = jnp.where(on_block, 0.0, part) - change
            if m == home:
                for a in range(4):
                    part = jnp.where(row_at == off + a, solved[a], part)
            parts[m] = part
    return jnp.concatenate(parts, axis=0)


def precondition_kernel(tok_total, n_terms, *refs):
    terms, (act_t, grad_t, moved) = refs[:n_terms], refs[n_terms:]
    both = terms[0][...]
    for term in terms[1:]:
        both = both + term[...]
    factor = both.shape[0]
    lane = lax.broadcasted_iota(jnp.int32, both.shape, 1)
    row_at = lax.broadcasted_iota(jnp.int32, both.shape, 0)
    left_half = lane < factor
    inner = jnp.where(left_half, lane, lane - factor)
    both = both / tok_total + jnp.where(inner == row_at, DAMP, 0.0)
    both = inverse_pair(both)
    blocks = jnp.concatenate(
        [jnp.where(left_half, both, 0.0), jnp.where(left_half, 0.0, both)], axis=0
    )
    proj_t = jnp.concatenate([act_t[...], grad_t[...]], axis=0)
    moved[...] = jnp.dot(blocks, proj_t, precision=HIGHEST, preferred_element_type=jnp.float32)


def precondition(tok_total, terms, act_t, grad_t):
    factor, tok_rows = act_t.shape
    n_terms = len(terms)
    return pl.pallas_call(
        functools.partial(precondition_kernel, tok_total, n_terms),
        out_shape=jax.ShapeDtypeStruct((2 * factor, tok_rows), jnp.float32),
        in_specs=[pl.BlockSpec(memory_space=pltpu.VMEM)] * (n_terms + 2),
        out_specs=pl.BlockSpec(memory_space=pltpu.VMEM),
        compiler_params=pltpu.CompilerParams(vmem_limit_bytes=24 * 2**20),
        cost_estimate=pl.CostEstimate(
            flops=1600 * factor * factor * tok_rows, bytes_accessed=16 * factor * tok_rows, transcendentals=0
        ),
        name="precondition",
    )(*terms, act_t, grad_t)


def score_kernel(size, n_pieces, moved, *refs):
    queries, (scores, total, ordered) = refs[:n_pieces], refs[n_pieces:]
    factor = moved.shape[0] // 2
    group = 4
    act_side = moved[:factor, :]
    for first in range(0, factor, group):
        outer = jnp.concatenate(
            [act_side * moved[factor + i : factor + i + 1, :] for i in range(first, first + group)], axis=0
        )
        high = outer.astype(jnp.bfloat16)
        low = (outer - high.astype(jnp.float32)).astype(jnp.bfloat16)
        columns = slice(first * factor, (first + group) * factor)
        values = jnp.concatenate([piece[:, columns] for piece in queries], axis=0)
        term = jnp.dot(
            jnp.concatenate([values, values], axis=1),
            jnp.concatenate([high, low], axis=0),
            preferred_element_type=jnp.float32,
        )
        if first == 0:
            total[...] = term
        else:
            total[...] += term
    rows = total.shape[0] // size
    for at, owner in enumerate(owners_of(lax.axis_index("dp"), size)):
        ordered[pl.ds(pl.multiple_of(owner * rows, rows), rows), :] = total[at * rows : (at + 1) * rows, :]
    scores[...] = ordered[...].T


def score(size, moved, queries):
    tok_rows = moved.shape[1]
    n_queries = sum(piece.shape[0] for piece in queries)
    n_pieces = len(queries)
    return pl.pallas_call(
        functools.partial(score_kernel, size, n_pieces),
        out_shape=jax.ShapeDtypeStruct((tok_rows, n_queries), jnp.float32),
        in_specs=[pl.BlockSpec(memory_space=pltpu.VMEM)] * (1 + n_pieces),
        out_specs=pl.BlockSpec(memory_space=pltpu.VMEM),
        scratch_shapes=[
            pltpu.VMEM((n_queries, tok_rows), jnp.float32),
            pltpu.VMEM((n_queries, tok_rows), jnp.float32),
        ],
        compiler_params=pltpu.CompilerParams(vmem_limit_bytes=32 * 2**20),
        name="score",
    )(moved, *queries)


def stages_of(size):
    if size & (size - 1):
        return [(1, size)]
    return [(size >> level, 2) for level in range(1, size.bit_length())]


def after(value, other):
    return lax.optimization_barrier((value, other))[0]


def partner(digit, radix, shift):
    return digit ^ shift if radix & (radix - 1) == 0 else (digit + shift) % radix


def swapped(value, size, stride, radix, shift):
    perm = []
    for at in range(size):
        digit = at // stride % radix
        perm.append((at, at + (partner(digit, radix, shift) - digit) * stride))
    return lax.ppermute(value, "dp", perm)


def owners_of(me, size):
    owners = [me]
    for stride, radix in stages_of(size):
        digit = lax.rem(lax.div(me, stride), radix)
        back = [shift if radix & (radix - 1) == 0 else radix - shift for shift in range(radix)]
        steps = [(partner(digit, radix, shift) - digit) * stride for shift in back]
        owners = [owner + step for step in steps for owner in owners]
    return owners


def exchanged(held, size, stride, radix):
    mine = held[0] if len(held) == 1 else jnp.concatenate(held, axis=0)
    return [mine] + [swapped(mine, size, stride, radix, shift) for shift in range(1, radix)]


def on_device(acts, grads, proj_act, proj_grad, queries):
    size = lax.axis_size("dp")
    tok_total = acts.shape[0] * size
    stages = stages_of(size)
    last = len(stages) - 1
    waiting = list(stages)
    pieces = exchanged([queries], size, *waiting.pop(0))
    act_t, gram = project(acts, proj_act)
    pieces = [after(piece, gram) for piece in pieces]
    if waiting:
        pieces = exchanged(pieces, size, *waiting.pop(0))
    grad_t, own = project(grads, proj_grad, gram)
    begins = [at * last // max(1, len(waiting) - 1) for at in range(len(waiting))]
    for level, stage in enumerate(stages):
        if level in begins:
            *pieces, own = lax.optimization_barrier((*pieces, own))
            pieces = exchanged(pieces, size, *waiting.pop(0))
        terms = exchanged([own], size, *stage)
        own = functools.reduce(jnp.add, terms)
    moved = precondition(tok_total, terms, act_t, grad_t)
    return score(size, moved, pieces)


def solution(mesh):
    in_specs = (P(("parts", "dp"), None), P(("parts", "dp"), None), P(), P(), P("dp", None))
    out_specs = P(("parts", "dp"), None)
    return jax.shard_map(
        on_device, mesh=mesh, in_specs=in_specs, out_specs=out_specs, check_vma=False
    )
```

```python
import functools

import jax
import jax.numpy as jnp
from jax import lax
from jax.experimental import pallas as pl
from jax.experimental.pallas import tpu as pltpu
from jax.sharding import PartitionSpec as P

DAMP = 0.1
HIGHEST = lax.Precision.HIGHEST
COPY_ROWS = 128
IN_FLIGHT = 2


def project_kernel(
    acts, grads, weight_act, weight_grad, act_t, grad_t, cov, tok_buf, weight_buf, weight_t, tok_sems, weight_sems
):
    factor, width = weight_act.shape
    n_parts = acts.shape[0] // COPY_ROWS
    weight_copies = [
        pltpu.make_async_copy(src, weight_buf.at[at], weight_sems.at[at])
        for at, src in enumerate((weight_act, weight_grad))
    ]
    copies = [
        pltpu.make_async_copy(
            src.at[pl.ds(part * COPY_ROWS, COPY_ROWS), :],
            tok_buf.at[at, pl.ds(part * COPY_ROWS, COPY_ROWS), :],
            tok_sems.at[at, part],
        )
        for at, src in enumerate((acts, grads))
        for part in range(n_parts)
    ]
    for copy in weight_copies + copies[:IN_FLIGHT]:
        copy.start()
    grams = []
    for at, out in enumerate((act_t, grad_t)):
        weight_copies[at].wait()
        for first in range(0, width, 512):
            block = weight_buf[at, :, first : first + 512].astype(jnp.float32)
            weight_t[at, first : first + 512, :] = block.T.astype(weight_t.dtype)
        gram = None
        part = 0
        while part < n_parts:
            many = 1 if at == 1 and part >= n_parts - 2 else min(2, n_parts - part)
            for done in range(at * n_parts + part, at * n_parts + part + many):
                copies[done].wait()
                if done + IN_FLIGHT < len(copies):
                    copies[done + IN_FLIGHT].start()
            rows = slice(part * COPY_ROWS, (part + many) * COPY_ROWS)
            block = jnp.dot(tok_buf[at, rows, :], weight_t[at], preferred_element_type=jnp.float32)
            flipped = block.T
            out[:, rows] = flipped
            term = jnp.dot(flipped, block, precision=HIGHEST, preferred_element_type=jnp.float32)
            gram = term if gram is None else gram + term
            part += many
        grams.append(gram)
    cov[...] = jnp.concatenate(grams, axis=1)


def project(acts, grads, proj_act, proj_grad):
    tok_rows, width = acts.shape
    factor = proj_act.shape[1]
    operands = [
        pltpu.with_memory_space_constraint(value, pltpu.HBM) for value in (acts, grads, proj_act.T, proj_grad.T)
    ]
    return pl.pallas_call(
        project_kernel,
        out_shape=(
            jax.ShapeDtypeStruct((factor, tok_rows), jnp.float32),
            jax.ShapeDtypeStruct((factor, tok_rows), jnp.float32),
            jax.ShapeDtypeStruct((factor, 2 * factor), jnp.float32),
        ),
        in_specs=[pl.BlockSpec(memory_space=pltpu.HBM)] * 4,
        out_specs=[pl.BlockSpec(memory_space=pltpu.VMEM)] * 3,
        scratch_shapes=[
            pltpu.VMEM((2, tok_rows, width), acts.dtype),
            pltpu.VMEM((2, factor, width), proj_act.dtype),
            pltpu.VMEM((2, width, factor), proj_act.dtype),
            pltpu.SemaphoreType.DMA((2, tok_rows // COPY_ROWS)),
            pltpu.SemaphoreType.DMA((2,)),
        ],
        compiler_params=pltpu.CompilerParams(vmem_limit_bytes=24 * 2**20),
        cost_estimate=pl.CostEstimate(
            flops=4 * tok_rows * width * factor, bytes_accessed=4 * tok_rows * width, transcendentals=0
        ),
        name="project",
    )(*operands)


def inverse_pair(both):
    factor = both.shape[0]
    tile = (8, both.shape[1])
    lane = lax.broadcasted_iota(jnp.int32, tile, 1)
    row_at = lax.broadcasted_iota(jnp.int32, tile, 0)
    left_half = lane < factor
    inner = jnp.where(left_half, lane, lane - factor)
    parts = [both[at : at + 8, :] for at in range(0, factor, 8)]

    def column(part, at):
        left = jnp.broadcast_to(part[:, at : at + 1], tile)
        right = jnp.broadcast_to(part[:, factor + at : factor + at + 1], tile)
        return jnp.where(left_half, left, right)

    def row(part, at):
        return jnp.broadcast_to(part[at : at + 1, :], tile)

    for k in range(0, factor, 4):
        home, off = divmod(k, 8)
        columns = [[column(part, k + a) for part in parts] for a in range(4)]
        pivot = [[row(columns[b][home], off + a) if a <= b else None for b in range(4)] for a in range(4)]
        p00, p01, p02, p03 = pivot[0]
        _, p11, p12, p13 = pivot[1]
        _, _, p22, p23 = pivot[2]
        p33 = pivot[3][3]
        on_block = (inner >= k) & (inner < k + 4)
        r0, r1, r2, r3 = [
            jnp.where(on_block, jnp.where(inner == k + a, 1.0, 0.0), row(parts[home], off + a)) for a in range(4)
        ]
        scale = 1.0 / (p00 * p11 - p01 * p01)
        e02 = scale * (p11 * p02 - p01 * p12)
        e03 = scale * (p11 * p03 - p01 * p13)
        e12 = scale * (p00 * p12 - p01 * p02)
        e13 = scale * (p00 * p13 - p01 * p03)
        s22 = p22 - (p02 * e02 + p12 * e12)
        s23 = p23 - (p02 * e03 + p12 * e13)
        s33 = p33 - (p03 * e03 + p13 * e13)
        scale_s = 1.0 / (s22 * s33 - s23 * s23)
        y0 = scale * (p11 * r0 - p01 * r1)
        y1 = scale * (p00 * r1 - p01 * r0)
        t2 = r2 - (p02 * y0 + p12 * y1)
        t3 = r3 - (p03 * y0 + p13 * y1)
        w2 = scale_s * (s33 * t2 - s23 * t3)
        w3 = scale_s * (s22 * t3 - s23 * t2)
        w0 = y0 - (e02 * w2 + e03 * w3)
        w1 = y1 - (e12 * w2 + e13 * w3)
        solved = (w0, w1, w2, w3)
        for m, part in enumerate(parts):
            change = (columns[0][m] * w0 + columns[1][m] * w1) + (columns[2][m] * w2 + columns[3][m] * w3)
            part = jnp.where(on_block, 0.0, part) - change
            if m == home:
                for a in range(4):
                    part = jnp.where(row_at == off + a, solved[a], part)
            parts[m] = part
    return jnp.concatenate(parts, axis=0)


def precondition_kernel(tok_total, n_terms, *refs):
    terms, (act_t, grad_t, moved) = refs[:n_terms], refs[n_terms:]
    both = terms[0][...]
    for term in terms[1:]:
        both = both + term[...]
    factor = both.shape[0]
    lane = lax.broadcasted_iota(jnp.int32, both.shape, 1)
    row_at = lax.broadcasted_iota(jnp.int32, both.shape, 0)
    left_half = lane < factor
    inner = jnp.where(left_half, lane, lane - factor)
    both = both / tok_total + jnp.where(inner == row_at, DAMP, 0.0)
    both = inverse_pair(both)
    blocks = jnp.concatenate(
        [jnp.where(left_half, both, 0.0), jnp.where(left_half, 0.0, both)], axis=0
    )
    proj_t = jnp.concatenate([act_t[...], grad_t[...]], axis=0)
    moved[...] = jnp.dot(blocks, proj_t, precision=HIGHEST, preferred_element_type=jnp.float32)


def precondition(tok_total, terms, act_t, grad_t):
    factor, tok_rows = act_t.shape
    n_terms = len(terms)
    return pl.pallas_call(
        functools.partial(precondition_kernel, tok_total, n_terms),
        out_shape=jax.ShapeDtypeStruct((2 * factor, tok_rows), jnp.float32),
        in_specs=[pl.BlockSpec(memory_space=pltpu.VMEM)] * (n_terms + 2),
        out_specs=pl.BlockSpec(memory_space=pltpu.VMEM),
        compiler_params=pltpu.CompilerParams(vmem_limit_bytes=24 * 2**20),
        cost_estimate=pl.CostEstimate(
            flops=1600 * factor * factor * tok_rows, bytes_accessed=16 * factor * tok_rows, transcendentals=0
        ),
        name="precondition",
    )(*terms, act_t, grad_t)


def score_kernel(size, n_pieces, moved, *refs):
    queries, (scores, total, ordered) = refs[:n_pieces], refs[n_pieces:]
    factor = moved.shape[0] // 2
    group = 4
    act_side = moved[:factor, :]
    for first in range(0, factor, group):
        outer = jnp.concatenate(
            [act_side * moved[factor + i : factor + i + 1, :] for i in range(first, first + group)], axis=0
        )
        high = outer.astype(jnp.bfloat16)
        low = (outer - high.astype(jnp.float32)).astype(jnp.bfloat16)
        columns = slice(first * factor, (first + group) * factor)
        values = jnp.concatenate([piece[:, columns] for piece in queries], axis=0)
        term = jnp.dot(
            jnp.concatenate([values, values], axis=1),
            jnp.concatenate([high, low], axis=0),
            preferred_element_type=jnp.float32,
        )
        if first == 0:
            total[...] = term
        else:
            total[...] += term
    rows = total.shape[0] // size
    for at, owner in enumerate(owners_of(lax.axis_index("dp"), size)):
        ordered[pl.ds(pl.multiple_of(owner * rows, rows), rows), :] = total[at * rows : (at + 1) * rows, :]
    scores[...] = ordered[...].T


def score(size, moved, queries):
    tok_rows = moved.shape[1]
    n_queries = sum(piece.shape[0] for piece in queries)
    n_pieces = len(queries)
    return pl.pallas_call(
        functools.partial(score_kernel, size, n_pieces),
        out_shape=jax.ShapeDtypeStruct((tok_rows, n_queries), jnp.float32),
        in_specs=[pl.BlockSpec(memory_space=pltpu.VMEM)] * (1 + n_pieces),
        out_specs=pl.BlockSpec(memory_space=pltpu.VMEM),
        scratch_shapes=[
            pltpu.VMEM((n_queries, tok_rows), jnp.float32),
            pltpu.VMEM((n_queries, tok_rows), jnp.float32),
        ],
        compiler_params=pltpu.CompilerParams(vmem_limit_bytes=32 * 2**20),
        name="score",
    )(moved, *queries)


def gather_stages(size):
    if size & (size - 1):
        return [(1, size)]
    return [(size >> level, 2) for level in range(1, size.bit_length())]


def sum_rounds(size):
    core = 2 if size % 2 == 0 else 1
    rest = size // core
    near = max(d for d in range(1, rest + 1) if rest % d == 0 and d * d <= rest)
    return [(1, core * near), (core * near, rest // near)]


def after(value, other):
    return lax.optimization_barrier((value, other))[0]


def partner(digit, radix, shift):
    return digit ^ shift if radix & (radix - 1) == 0 else (digit + shift) % radix


def swapped(value, size, stride, radix, shift):
    perm = []
    for at in range(size):
        digit = at // stride % radix
        perm.append((at, at + (partner(digit, radix, shift) - digit) * stride))
    return lax.ppermute(value, "dp", perm)


def owners_of(me, size):
    owners = [me]
    for stride, radix in gather_stages(size):
        digit = lax.rem(lax.div(me, stride), radix)
        back = [shift if radix & (radix - 1) == 0 else radix - shift for shift in range(radix)]
        steps = [(partner(digit, radix, shift) - digit) * stride for shift in back]
        owners = [owner + step for step in steps for owner in owners]
    return owners


def exchanged(held, size, stride, radix):
    mine = held[0] if len(held) == 1 else jnp.concatenate(held, axis=0)
    return [mine] + [swapped(mine, size, stride, radix, shift) for shift in range(1, radix)]


def on_device(acts, grads, proj_act, proj_grad, queries):
    size = lax.axis_size("dp")
    tok_total = acts.shape[0] * size
    stages = gather_stages(size)
    first, second = sum_rounds(size)

    def gathered(pieces, some):
        for stage in some:
            pieces = exchanged(pieces, size, *stage)
        return pieces

    pieces = gathered([queries], stages[:1])
    act_t, grad_t, own = project(acts, grads, proj_act, proj_grad)
    *pieces, own = lax.optimization_barrier((*pieces, own))
    pieces = gathered(pieces, stages[1:2])
    own = functools.reduce(jnp.add, exchanged([own], size, *first))
    pieces = gathered([after(piece, own) for piece in pieces], stages[2:-1])
    terms = exchanged([own], size, *second)
    pieces = gathered([after(piece, terms) for piece in pieces], stages[max(2, len(stages) - 1) :])
    moved = precondition(tok_total, terms, act_t, grad_t)
    return score(size, moved, pieces)


def solution(mesh):
    in_specs = (P(("parts", "dp"), None), P(("parts", "dp"), None), P(), P(), P("dp", None))
    out_specs = P(("parts", "dp"), None)
    return jax.shard_map(
        on_device, mesh=mesh, in_specs=in_specs, out_specs=out_specs, check_vma=False
    )
```

```python
import functools

import jax
import jax.numpy as jnp
from jax import lax
from jax.experimental import pallas as pl
from jax.experimental.pallas import tpu as pltpu
from jax.sharding import PartitionSpec as P

DAMP = 0.1
HIGHEST = lax.Precision.HIGHEST
COPY_ROWS = 128
IN_FLIGHT = 4


def project_kernel(
    acts, grads, weight_act, weight_grad, act_t, grad_t, cov, tok_buf, weight_buf, weight_t, tok_sems, weight_sems
):
    width = weight_act.shape[1]
    n_parts = acts.shape[0] // COPY_ROWS
    weight_copies = [
        pltpu.make_async_copy(src, weight_buf.at[at], weight_sems.at[at])
        for at, src in enumerate((weight_act, weight_grad))
    ]
    tok_copies = [
        [
            pltpu.make_async_copy(
                src.at[pl.ds(part * COPY_ROWS, COPY_ROWS), :],
                tok_buf.at[at, pl.ds(part * COPY_ROWS, COPY_ROWS), :],
                tok_sems.at[at, part],
            )
            for part in range(n_parts)
        ]
        for at, src in enumerate((acts, grads))
    ]
    queue = [weight_copies[0], *tok_copies[0], *tok_copies[1]]
    queue.insert(3, weight_copies[1])

    def start_next(many):
        for copy in queue[:many]:
            copy.start()
        del queue[:many]

    def turned(at):
        for first in range(0, width, 512):
            block = weight_buf[at, :, first : first + 512].astype(jnp.float32)
            weight_t[at, first : first + 512, :] = block.T.astype(weight_t.dtype)

    steps = [(at, part, min(2, n_parts - part)) for at in range(2) for part in range(0, n_parts, 2)]
    at, part, many = steps.pop()
    steps += [(at, part + one, 1) for one in range(many)]
    grams = [None, None]

    def add_gram(at, flipped, block):
        term = jnp.dot(flipped, block, precision=HIGHEST, preferred_element_type=jnp.float32)
        grams[at] = term if grams[at] is None else grams[at] + term

    start_next(1 + IN_FLIGHT)
    weight_copies[0].wait()
    turned(0)
    before = None
    for step, (at, part, many) in enumerate(steps):
        for copy in tok_copies[at][part : part + many]:
            copy.wait()
            start_next(1)
        if step == 1:
            weight_copies[1].wait()
            start_next(1)
        rows = slice(part * COPY_ROWS, (part + many) * COPY_ROWS)
        block = jnp.dot(tok_buf[at, rows, :], weight_t[at], preferred_element_type=jnp.float32)
        if step == 1:
            turned(1)
        if before is not None:
            add_gram(*before)
        flipped = block.T
        (act_t, grad_t)[at][:, rows] = flipped
        before = (at, flipped, block)
    add_gram(*before)
    cov[...] = jnp.concatenate(grams, axis=1)


def project(acts, grads, proj_act, proj_grad):
    tok_rows, width = acts.shape
    factor = proj_act.shape[1]
    operands = [
        pltpu.with_memory_space_constraint(value, pltpu.HBM) for value in (acts, grads, proj_act.T, proj_grad.T)
    ]
    return pl.pallas_call(
        project_kernel,
        out_shape=(
            jax.ShapeDtypeStruct((factor, tok_rows), jnp.float32),
            jax.ShapeDtypeStruct((factor, tok_rows), jnp.float32),
            jax.ShapeDtypeStruct((factor, 2 * factor), jnp.float32),
        ),
        in_specs=[pl.BlockSpec(memory_space=pltpu.HBM)] * 4,
        out_specs=[pl.BlockSpec(memory_space=pltpu.VMEM)] * 3,
        scratch_shapes=[
            pltpu.VMEM((2, tok_rows, width), acts.dtype),
            pltpu.VMEM((2, factor, width), proj_act.dtype),
            pltpu.VMEM((2, width, factor), proj_act.dtype),
            pltpu.SemaphoreType.DMA((2, tok_rows // COPY_ROWS)),
            pltpu.SemaphoreType.DMA((2,)),
        ],
        compiler_params=pltpu.CompilerParams(vmem_limit_bytes=24 * 2**20),
        cost_estimate=pl.CostEstimate(
            flops=4 * tok_rows * width * factor, bytes_accessed=4 * tok_rows * width, transcendentals=0
        ),
        name="project",
    )(*operands)


def inverse_pair(both):
    factor = both.shape[0]
    tile = (8, both.shape[1])
    lane = lax.broadcasted_iota(jnp.int32, tile, 1)
    row_at = lax.broadcasted_iota(jnp.int32, tile, 0)
    left_half = lane < factor
    inner = jnp.where(left_half, lane, lane - factor)
    parts = [both[at : at + 8, :] for at in range(0, factor, 8)]

    def column(part, at):
        left = jnp.broadcast_to(part[:, at : at + 1], tile)
        right = jnp.broadcast_to(part[:, factor + at : factor + at + 1], tile)
        return jnp.where(left_half, left, right)

    def row(part, at):
        return jnp.broadcast_to(part[at : at + 1, :], tile)

    for k in range(0, factor, 4):
        home, off = divmod(k, 8)
        columns = [[column(part, k + a) for part in parts] for a in range(4)]
        pivot = [[row(columns[b][home], off + a) if a <= b else None for b in range(4)] for a in range(4)]
        p00, p01, p02, p03 = pivot[0]
        _, p11, p12, p13 = pivot[1]
        _, _, p22, p23 = pivot[2]
        p33 = pivot[3][3]
        on_block = (inner >= k) & (inner < k + 4)
        r0, r1, r2, r3 = [
            jnp.where(on_block, jnp.where(inner == k + a, 1.0, 0.0), row(parts[home], off + a)) for a in range(4)
        ]
        scale = 1.0 / (p00 * p11 - p01 * p01)
        e02 = scale * (p11 * p02 - p01 * p12)
        e03 = scale * (p11 * p03 - p01 * p13)
        e12 = scale * (p00 * p12 - p01 * p02)
        e13 = scale * (p00 * p13 - p01 * p03)
        s22 = p22 - (p02 * e02 + p12 * e12)
        s23 = p23 - (p02 * e03 + p12 * e13)
        s33 = p33 - (p03 * e03 + p13 * e13)
        scale_s = 1.0 / (s22 * s33 - s23 * s23)
        y0 = scale * (p11 * r0 - p01 * r1)
        y1 = scale * (p00 * r1 - p01 * r0)
        t2 = r2 - (p02 * y0 + p12 * y1)
        t3 = r3 - (p03 * y0 + p13 * y1)
        w2 = scale_s * (s33 * t2 - s23 * t3)
        w3 = scale_s * (s22 * t3 - s23 * t2)
        w0 = y0 - (e02 * w2 + e03 * w3)
        w1 = y1 - (e12 * w2 + e13 * w3)
        solved = (w0, w1, w2, w3)
        for m, part in enumerate(parts):
            change = (columns[0][m] * w0 + columns[1][m] * w1) + (columns[2][m] * w2 + columns[3][m] * w3)
            part = jnp.where(on_block, 0.0, part) - change
            if m == home:
                for a in range(4):
                    part = jnp.where(row_at == off + a, solved[a], part)
            parts[m] = part
    return jnp.concatenate(parts, axis=0)


def precondition_kernel(tok_total, n_terms, *refs):
    terms, (act_t, grad_t, moved) = refs[:n_terms], refs[n_terms:]
    both = terms[0][...]
    for term in terms[1:]:
        both = both + term[...]
    factor = both.shape[0]
    lane = lax.broadcasted_iota(jnp.int32, both.shape, 1)
    row_at = lax.broadcasted_iota(jnp.int32, both.shape, 0)
    left_half = lane < factor
    inner = jnp.where(left_half, lane, lane - factor)
    both = both / tok_total + jnp.where(inner == row_at, DAMP, 0.0)
    both = inverse_pair(both)
    blocks = jnp.concatenate(
        [jnp.where(left_half, both, 0.0), jnp.where(left_half, 0.0, both)], axis=0
    )
    proj_t = jnp.concatenate([act_t[...], grad_t[...]], axis=0)
    moved[...] = jnp.dot(blocks, proj_t, precision=HIGHEST, preferred_element_type=jnp.float32)


def precondition(tok_total, terms, act_t, grad_t):
    factor, tok_rows = act_t.shape
    n_terms = len(terms)
    return pl.pallas_call(
        functools.partial(precondition_kernel, tok_total, n_terms),
        out_shape=jax.ShapeDtypeStruct((2 * factor, tok_rows), jnp.float32),
        in_specs=[pl.BlockSpec(memory_space=pltpu.VMEM)] * (n_terms + 2),
        out_specs=pl.BlockSpec(memory_space=pltpu.VMEM),
        compiler_params=pltpu.CompilerParams(vmem_limit_bytes=24 * 2**20),
        cost_estimate=pl.CostEstimate(
            flops=1600 * factor * factor * tok_rows, bytes_accessed=16 * factor * tok_rows, transcendentals=0
        ),
        name="precondition",
    )(*terms, act_t, grad_t)


def score_kernel(size, n_pieces, moved, *refs):
    queries, (scores, total, ordered) = refs[:n_pieces], refs[n_pieces:]
    factor = moved.shape[0] // 2
    group = 4
    act_side = moved[:factor, :]
    for first in range(0, factor, group):
        outer = jnp.concatenate(
            [act_side * moved[factor + i : factor + i + 1, :] for i in range(first, first + group)], axis=0
        )
        high = outer.astype(jnp.bfloat16)
        low = (outer - high.astype(jnp.float32)).astype(jnp.bfloat16)
        columns = slice(first * factor, (first + group) * factor)
        values = jnp.concatenate([piece[:, columns] for piece in queries], axis=0)
        term = jnp.dot(
            jnp.concatenate([values, values], axis=1),
            jnp.concatenate([high, low], axis=0),
            preferred_element_type=jnp.float32,
        )
        if first == 0:
            total[...] = term
        else:
            total[...] += term
    rows = total.shape[0] // size
    for at, owner in enumerate(owners_of(lax.axis_index("dp"), size)):
        ordered[pl.ds(pl.multiple_of(owner * rows, rows), rows), :] = total[at * rows : (at + 1) * rows, :]
    scores[...] = ordered[...].T


def score(size, moved, queries):
    tok_rows = moved.shape[1]
    n_queries = sum(piece.shape[0] for piece in queries)
    n_pieces = len(queries)
    return pl.pallas_call(
        functools.partial(score_kernel, size, n_pieces),
        out_shape=jax.ShapeDtypeStruct((tok_rows, n_queries), jnp.float32),
        in_specs=[pl.BlockSpec(memory_space=pltpu.VMEM)] * (1 + n_pieces),
        out_specs=pl.BlockSpec(memory_space=pltpu.VMEM),
        scratch_shapes=[
            pltpu.VMEM((n_queries, tok_rows), jnp.float32),
            pltpu.VMEM((n_queries, tok_rows), jnp.float32),
        ],
        compiler_params=pltpu.CompilerParams(vmem_limit_bytes=32 * 2**20),
        name="score",
    )(moved, *queries)


def gather_stages(size):
    if size & (size - 1):
        return [(1, size)]
    return [(size >> level, 2) for level in range(1, size.bit_length())]


def sum_rounds(size):
    core = 2 if size % 2 == 0 else 1
    rest = size // core
    near = max(d for d in range(1, rest + 1) if rest % d == 0 and d * d <= rest)
    return [(1, core * near), (core * near, rest // near)]


def after(value, other):
    return lax.optimization_barrier((value, other))[0]


def partner(digit, radix, shift):
    return digit ^ shift if radix & (radix - 1) == 0 else (digit + shift) % radix


def swapped(value, size, stride, radix, shift):
    perm = []
    for at in range(size):
        digit = at // stride % radix
        perm.append((at, at + (partner(digit, radix, shift) - digit) * stride))
    return lax.ppermute(value, "dp", perm)


def owners_of(me, size):
    owners = [me]
    for stride, radix in gather_stages(size):
        digit = lax.rem(lax.div(me, stride), radix)
        back = [shift if radix & (radix - 1) == 0 else radix - shift for shift in range(radix)]
        steps = [(partner(digit, radix, shift) - digit) * stride for shift in back]
        owners = [owner + step for step in steps for owner in owners]
    return owners


def exchanged(held, size, stride, radix):
    mine = held[0] if len(held) == 1 else jnp.concatenate(held, axis=0)
    return [mine] + [swapped(mine, size, stride, radix, shift) for shift in range(1, radix)]


def on_device(acts, grads, proj_act, proj_grad, queries):
    size = lax.axis_size("dp")
    tok_total = acts.shape[0] * size
    stages = gather_stages(size)
    first, second = sum_rounds(size)

    def gathered(pieces, some):
        for stage in some:
            pieces = exchanged(pieces, size, *stage)
        return pieces

    pieces = gathered([queries], stages[:1])
    act_t, grad_t, own = project(acts, grads, proj_act, proj_grad)
    *pieces, own = lax.optimization_barrier((*pieces, own))
    pieces = gathered(pieces, stages[1:2])
    own = functools.reduce(jnp.add, exchanged([own], size, *first))
    *pieces, own = lax.optimization_barrier((*pieces, own))
    pieces = gathered(pieces, stages[2:-1])
    terms = exchanged([own], size, *second)
    *both, = lax.optimization_barrier((*pieces, *terms))
    pieces, terms = both[: len(pieces)], both[len(pieces) :]
    pieces = gathered(pieces, stages[max(2, len(stages) - 1) :])
    moved = precondition(tok_total, terms, act_t, grad_t)
    return score(size, moved, pieces)


def solution(mesh):
    in_specs = (P(("parts", "dp"), None), P(("parts", "dp"), None), P(), P(), P("dp", None))
    out_specs = P(("parts", "dp"), None)
    return jax.shard_map(
        on_device, mesh=mesh, in_specs=in_specs, out_specs=out_specs, check_vma=False
    )
```

```python
import functools

import jax
import jax.numpy as jnp
from jax import lax
from jax.experimental import pallas as pl
from jax.experimental.pallas import tpu as pltpu
from jax.sharding import PartitionSpec as P

DAMP = 0.1
HIGHEST = lax.Precision.HIGHEST
COPY_ROWS = 128


def dot_nt(left, right, precision=None):
    return lax.dot_general(
        left, right, (((1,), (1,)), ((), ())), precision=precision, preferred_element_type=jnp.float32
    )


def project_kernel(tokens, weight, *refs):
    *refs, tok_buf, weight_buf, weight_t, tok_sems, weight_sem = refs
    before, proj_t, cov = refs if len(refs) == 3 else (None, *refs, None)
    width = weight.shape[1]
    n_parts = tokens.shape[0] // COPY_ROWS
    copies = [
        pltpu.make_async_copy(
            tokens.at[pl.ds(part * COPY_ROWS, COPY_ROWS), :],
            tok_buf.at[pl.ds(part * COPY_ROWS, COPY_ROWS), :],
            tok_sems.at[part],
        )
        for part in range(n_parts)
    ]
    weight_copy = pltpu.make_async_copy(weight, weight_buf, weight_sem)
    weight_copy.start()
    for copy in copies:
        copy.start()
    if before is not None:
        early = dot_nt(before[...], before[...], HIGHEST)
    weight_copy.wait()
    for first in range(0, width, 512):
        block = weight_buf[:, first : first + 512].astype(jnp.float32)
        weight_t[first : first + 512, :] = block.T.astype(weight_t.dtype)
    steps = [(part, min(2, n_parts - part)) for part in range(0, n_parts, 2)]
    part, many = steps.pop()
    steps += [(part + one, 1) for one in range(many)]
    gram = late = None
    for part, many in steps:
        for copy in copies[part : part + many]:
            copy.wait()
        rows = slice(part * COPY_ROWS, (part + many) * COPY_ROWS)
        block = jnp.dot(tok_buf[rows, :], weight_t[...], preferred_element_type=jnp.float32)
        if late is not None:
            term = jnp.dot(*late, precision=HIGHEST, preferred_element_type=jnp.float32)
            gram = term if gram is None else gram + term
        flipped = block.T
        proj_t[:, rows] = flipped
        late = (flipped, block) if cov is not None else None
    if cov is not None:
        term = jnp.dot(*late, precision=HIGHEST, preferred_element_type=jnp.float32)
        cov[...] = jnp.concatenate([early, term if gram is None else gram + term], axis=1)


def project(tokens, weight, *before):
    tok_rows, width = tokens.shape
    factor = weight.shape[1]
    operands = [pltpu.with_memory_space_constraint(value, pltpu.HBM) for value in (tokens, weight.T)]
    out_shape = [jax.ShapeDtypeStruct((factor, tok_rows), jnp.float32)]
    out_shape += [jax.ShapeDtypeStruct((factor, 2 * factor), jnp.float32)] * len(before)
    return pl.pallas_call(
        project_kernel,
        out_shape=out_shape,
        in_specs=[pl.BlockSpec(memory_space=pltpu.HBM)] * 2
        + [pl.BlockSpec(memory_space=pltpu.VMEM)] * len(before),
        out_specs=[pl.BlockSpec(memory_space=pltpu.VMEM)] * len(out_shape),
        scratch_shapes=[
            pltpu.VMEM((tok_rows, width), tokens.dtype),
            pltpu.VMEM((factor, width), weight.dtype),
            pltpu.VMEM((width, factor), weight.dtype),
            pltpu.SemaphoreType.DMA((tok_rows // COPY_ROWS,)),
            pltpu.SemaphoreType.DMA,
        ],
        compiler_params=pltpu.CompilerParams(vmem_limit_bytes=24 * 2**20),
        cost_estimate=pl.CostEstimate(
            flops=2 * tok_rows * width * factor, bytes_accessed=2 * tok_rows * width, transcendentals=0
        ),
        name="project",
    )(*operands, *before)


def inverse_pair(both):
    factor = both.shape[0]
    tile = (8, both.shape[1])
    lane = lax.broadcasted_iota(jnp.int32, tile, 1)
    row_at = lax.broadcasted_iota(jnp.int32, tile, 0)
    left_half = lane < factor
    inner = jnp.where(left_half, lane, lane - factor)
    parts = [both[at : at + 8, :] for at in range(0, factor, 8)]

    def column(part, at):
        left = jnp.broadcast_to(part[:, at : at + 1], tile)
        right = jnp.broadcast_to(part[:, factor + at : factor + at + 1], tile)
        return jnp.where(left_half, left, right)

    def row(part, at):
        return jnp.broadcast_to(part[at : at + 1, :], tile)

    for k in range(0, factor, 4):
        home, off = divmod(k, 8)
        columns = [[column(part, k + a) for part in parts] for a in range(4)]
        pivot = [[row(columns[b][home], off + a) if a <= b else None for b in range(4)] for a in range(4)]
        p00, p01, p02, p03 = pivot[0]
        _, p11, p12, p13 = pivot[1]
        _, _, p22, p23 = pivot[2]
        p33 = pivot[3][3]
        on_block = (inner >= k) & (inner < k + 4)
        r0, r1, r2, r3 = [
            jnp.where(on_block, jnp.where(inner == k + a, 1.0, 0.0), row(parts[home], off + a)) for a in range(4)
        ]
        scale = 1.0 / (p00 * p11 - p01 * p01)
        e02 = scale * (p11 * p02 - p01 * p12)
        e03 = scale * (p11 * p03 - p01 * p13)
        e12 = scale * (p00 * p12 - p01 * p02)
        e13 = scale * (p00 * p13 - p01 * p03)
        s22 = p22 - (p02 * e02 + p12 * e12)
        s23 = p23 - (p02 * e03 + p12 * e13)
        s33 = p33 - (p03 * e03 + p13 * e13)
        scale_s = 1.0 / (s22 * s33 - s23 * s23)
        y0 = scale * (p11 * r0 - p01 * r1)
        y1 = scale * (p00 * r1 - p01 * r0)
        t2 = r2 - (p02 * y0 + p12 * y1)
        t3 = r3 - (p03 * y0 + p13 * y1)
        w2 = scale_s * (s33 * t2 - s23 * t3)
        w3 = scale_s * (s22 * t3 - s23 * t2)
        w0 = y0 - (e02 * w2 + e03 * w3)
        w1 = y1 - (e12 * w2 + e13 * w3)
        solved = (w0, w1, w2, w3)
        for m, part in enumerate(parts):
            change = (columns[0][m] * w0 + columns[1][m] * w1) + (columns[2][m] * w2 + columns[3][m] * w3)
            part = jnp.where(on_block, 0.0, part) - change
            if m == home:
                for a in range(4):
                    part = jnp.where(row_at == off + a, solved[a], part)
            parts[m] = part
    return jnp.concatenate(parts, axis=0)


def precondition_kernel(tok_total, terms, act_t, grad_t, moved):
    both = terms[0]
    for at in range(1, terms.shape[0]):
        both = both + terms[at]
    factor = both.shape[0]
    lane = lax.broadcasted_iota(jnp.int32, both.shape, 1)
    row_at = lax.broadcasted_iota(jnp.int32, both.shape, 0)
    left_half = lane < factor
    inner = jnp.where(left_half, lane, lane - factor)
    both = both / tok_total + jnp.where(inner == row_at, DAMP, 0.0)
    both = inverse_pair(both)
    blocks = jnp.concatenate(
        [jnp.where(left_half, both, 0.0), jnp.where(left_half, 0.0, both)], axis=0
    )
    proj_t = jnp.concatenate([act_t[...], grad_t[...]], axis=0)
    moved[...] = jnp.dot(blocks, proj_t, precision=HIGHEST, preferred_element_type=jnp.float32)


def precondition(tok_total, terms, act_t, grad_t):
    factor, tok_rows = act_t.shape
    return pl.pallas_call(
        functools.partial(precondition_kernel, tok_total),
        out_shape=jax.ShapeDtypeStruct((2 * factor, tok_rows), jnp.float32),
        in_specs=[pl.BlockSpec(memory_space=pltpu.VMEM)] * 3,
        out_specs=pl.BlockSpec(memory_space=pltpu.VMEM),
        compiler_params=pltpu.CompilerParams(vmem_limit_bytes=24 * 2**20),
        cost_estimate=pl.CostEstimate(
            flops=1600 * factor * factor * tok_rows, bytes_accessed=16 * factor * tok_rows, transcendentals=0
        ),
        name="precondition",
    )(terms, act_t, grad_t)


def score_kernel(size, n_pieces, moved, *refs):
    queries, (scores, total, ordered) = refs[:n_pieces], refs[n_pieces:]
    factor = moved.shape[0] // 2
    group = 4
    act_side = moved[:factor, :]
    for first in range(0, factor, group):
        outer = jnp.concatenate(
            [act_side * moved[factor + i : factor + i + 1, :] for i in range(first, first + group)], axis=0
        )
        high = outer.astype(jnp.bfloat16)
        low = (outer - high.astype(jnp.float32)).astype(jnp.bfloat16)
        columns = slice(first * factor, (first + group) * factor)
        values = jnp.concatenate([piece[:, columns] for piece in queries], axis=0)
        term = jnp.dot(
            jnp.concatenate([values, values], axis=1),
            jnp.concatenate([high, low], axis=0),
            preferred_element_type=jnp.float32,
        )
        if first == 0:
            total[...] = term
        else:
            total[...] += term
    rows = total.shape[0] // size
    for at, owner in enumerate(owners_of(lax.axis_index("dp"), size)):
        ordered[pl.ds(pl.multiple_of(owner * rows, rows), rows), :] = total[at * rows : (at + 1) * rows, :]
    scores[...] = ordered[...].T


def score(size, moved, queries):
    tok_rows = moved.shape[1]
    n_queries = sum(piece.shape[0] for piece in queries)
    n_pieces = len(queries)
    return pl.pallas_call(
        functools.partial(score_kernel, size, n_pieces),
        out_shape=jax.ShapeDtypeStruct((tok_rows, n_queries), jnp.float32),
        in_specs=[pl.BlockSpec(memory_space=pltpu.VMEM)] * (1 + n_pieces),
        out_specs=pl.BlockSpec(memory_space=pltpu.VMEM),
        scratch_shapes=[
            pltpu.VMEM((n_queries, tok_rows), jnp.float32),
            pltpu.VMEM((n_queries, tok_rows), jnp.float32),
        ],
        compiler_params=pltpu.CompilerParams(vmem_limit_bytes=32 * 2**20),
        name="score",
    )(moved, *queries)


def gather_stages(size):
    if size & (size - 1):
        return [(1, size)]
    return [(size >> level, 2) for level in range(1, size.bit_length())]


def sum_rounds(size):
    core = 2 if size % 2 == 0 else 1
    rest = size // core
    near = max(d for d in range(1, rest + 1) if rest % d == 0 and d * d <= rest)
    return [(1, core * near), (core * near, rest // near)]


def after(value, other):
    return lax.optimization_barrier((value, other))[0]


def partner(digit, radix, shift):
    return digit ^ shift if radix & (radix - 1) == 0 else (digit + shift) % radix


def swapped(value, size, stride, radix, shift):
    perm = []
    for at in range(size):
        digit = at // stride % radix
        perm.append((at, at + (partner(digit, radix, shift) - digit) * stride))
    return lax.ppermute(value, "dp", perm)


def owners_of(me, size):
    owners = [me]
    for stride, radix in gather_stages(size):
        digit = lax.rem(lax.div(me, stride), radix)
        back = [shift if radix & (radix - 1) == 0 else radix - shift for shift in range(radix)]
        steps = [(partner(digit, radix, shift) - digit) * stride for shift in back]
        owners = [owner + step for step in steps for owner in owners]
    return owners


def exchanged(held, size, stride, radix):
    mine = held[0] if len(held) == 1 else jnp.concatenate(held, axis=0)
    return [mine] + [swapped(mine, size, stride, radix, shift) for shift in range(1, radix)]


def replicated(own, size, stride, radix):
    groups = [
        [at + step * stride for step in range(radix)] for at in range(size) if at // stride % radix == 0
    ]
    copies = jnp.broadcast_to(own, (radix, *own.shape))
    return lax.all_to_all(copies, "dp", 0, 0, axis_index_groups=groups, tiled=True)


def on_device(acts, grads, proj_act, proj_grad, queries):
    size = lax.axis_size("dp")
    tok_total = acts.shape[0] * size
    stages = gather_stages(size)
    first, second = sum_rounds(size)

    def gathered(pieces, some):
        for stage in some:
            pieces = exchanged(pieces, size, *stage)
        return pieces

    pieces = gathered([queries], stages[:1])
    (act_t,) = project(acts, proj_act)
    *pieces, act_t = lax.optimization_barrier((*pieces, act_t))
    pieces = gathered(pieces, stages[1:2])
    grad_t, own = project(grads, proj_grad, act_t)
    *pieces, own = lax.optimization_barrier((*pieces, own))
    pieces = gathered(pieces, stages[2:-1])
    own = functools.reduce(jnp.add, exchanged([own], size, *first))
    terms = replicated(own, size, *second)
    *pieces, terms = lax.optimization_barrier((*pieces, terms))
    pieces = gathered(pieces, stages[max(2, len(stages) - 1) :])
    moved = precondition(tok_total, terms, act_t, grad_t)
    return score(size, moved, pieces)


def solution(mesh):
    in_specs = (P(("parts", "dp"), None), P(("parts", "dp"), None), P(), P(), P("dp", None))
    out_specs = P(("parts", "dp"), None)
    return jax.shard_map(
        on_device, mesh=mesh, in_specs=in_specs, out_specs=out_specs, check_vma=False
    )
```

```python
import functools

import jax
import jax.numpy as jnp
from jax import lax
from jax.experimental import pallas as pl
from jax.experimental.pallas import tpu as pltpu
from jax.sharding import PartitionSpec as P

DAMP = 0.1
HIGHEST = lax.Precision.HIGHEST
COPY_ROWS = 128
IN_FLIGHT = 4


def project_kernel(
    acts, grads, weight_act, weight_grad, act_t, grad_t, cov, tok_buf, weight_buf, weight_t, tok_sems, weight_sems
):
    width = weight_act.shape[1]
    n_parts = acts.shape[0] // COPY_ROWS
    weight_copies = [
        pltpu.make_async_copy(src, weight_buf.at[at], weight_sems.at[at])
        for at, src in enumerate((weight_act, weight_grad))
    ]
    tok_copies = [
        [
            pltpu.make_async_copy(
                src.at[pl.ds(part * COPY_ROWS, COPY_ROWS), :],
                tok_buf.at[at, pl.ds(part * COPY_ROWS, COPY_ROWS), :],
                tok_sems.at[at, part],
            )
            for part in range(n_parts)
        ]
        for at, src in enumerate((acts, grads))
    ]
    queue = [weight_copies[0], *tok_copies[0], *tok_copies[1]]
    queue.insert(3, weight_copies[1])

    def start_next(many):
        for copy in queue[:many]:
            copy.start()
        del queue[:many]

    def turned(at):
        for first in range(0, width, 512):
            block = weight_buf[at, :, first : first + 512].astype(jnp.float32)
            weight_t[at, first : first + 512, :] = block.T.astype(weight_t.dtype)

    steps = [(at, part, min(2, n_parts - part)) for at in range(2) for part in range(0, n_parts, 2)]
    last_act = len(steps) // 2 - 1
    at, part, many = steps.pop()
    steps += [(at, part + one, 1) for one in range(many)]
    grams = [None, None]

    def add_gram(at, flipped, block):
        term = jnp.dot(flipped, block, precision=HIGHEST, preferred_element_type=jnp.float32)
        grams[at] = term if grams[at] is None else grams[at] + term

    start_next(1 + IN_FLIGHT)
    weight_copies[0].wait()
    turned(0)
    before = None
    for step, (at, part, many) in enumerate(steps):
        for copy in tok_copies[at][part : part + many]:
            copy.wait()
            start_next(1)
        if step == last_act:
            weight_copies[1].wait()
            start_next(1)
        rows = slice(part * COPY_ROWS, (part + many) * COPY_ROWS)
        block = jnp.dot(tok_buf[at, rows, :], weight_t[at], preferred_element_type=jnp.float32)
        if step == last_act:
            turned(1)
        if before is not None:
            add_gram(*before)
        flipped = block.T
        (act_t, grad_t)[at][:, rows] = flipped
        before = (at, flipped, block)
    add_gram(*before)
    cov[...] = jnp.concatenate(grams, axis=1)


def project(acts, grads, proj_act, proj_grad):
    tok_rows, width = acts.shape
    factor = proj_act.shape[1]
    operands = [
        pltpu.with_memory_space_constraint(value, pltpu.HBM) for value in (acts, grads, proj_act.T, proj_grad.T)
    ]
    return pl.pallas_call(
        project_kernel,
        out_shape=(
            jax.ShapeDtypeStruct((factor, tok_rows), jnp.float32),
            jax.ShapeDtypeStruct((factor, tok_rows), jnp.float32),
            jax.ShapeDtypeStruct((factor, 2 * factor), jnp.float32),
        ),
        in_specs=[pl.BlockSpec(memory_space=pltpu.HBM)] * 4,
        out_specs=[pl.BlockSpec(memory_space=pltpu.VMEM)] * 3,
        scratch_shapes=[
            pltpu.VMEM((2, tok_rows, width), acts.dtype),
            pltpu.VMEM((2, factor, width), proj_act.dtype),
            pltpu.VMEM((2, width, factor), proj_act.dtype),
            pltpu.SemaphoreType.DMA((2, tok_rows // COPY_ROWS)),
            pltpu.SemaphoreType.DMA((2,)),
        ],
        compiler_params=pltpu.CompilerParams(vmem_limit_bytes=24 * 2**20),
        cost_estimate=pl.CostEstimate(
            flops=4 * tok_rows * width * factor, bytes_accessed=4 * tok_rows * width, transcendentals=0
        ),
        name="project",
    )(*operands)


def inverse_pair(both):
    factor = both.shape[0]
    tile = (8, both.shape[1])
    lane = lax.broadcasted_iota(jnp.int32, tile, 1)
    row_at = lax.broadcasted_iota(jnp.int32, tile, 0)
    left_half = lane < factor
    inner = jnp.where(left_half, lane, lane - factor)
    parts = [both[at : at + 8, :] for at in range(0, factor, 8)]

    def column(part, at):
        left = jnp.broadcast_to(part[:, at : at + 1], tile)
        right = jnp.broadcast_to(part[:, factor + at : factor + at + 1], tile)
        return jnp.where(left_half, left, right)

    def row(part, at):
        return jnp.broadcast_to(part[at : at + 1, :], tile)

    for k in range(0, factor, 4):
        home, off = divmod(k, 8)
        columns = [[column(part, k + a) for part in parts] for a in range(4)]
        pivot = [[row(columns[b][home], off + a) if a <= b else None for b in range(4)] for a in range(4)]
        p00, p01, p02, p03 = pivot[0]
        _, p11, p12, p13 = pivot[1]
        _, _, p22, p23 = pivot[2]
        p33 = pivot[3][3]
        on_block = (inner >= k) & (inner < k + 4)
        r0, r1, r2, r3 = [
            jnp.where(on_block, jnp.where(inner == k + a, 1.0, 0.0), row(parts[home], off + a)) for a in range(4)
        ]
        scale = 1.0 / (p00 * p11 - p01 * p01)
        e02 = scale * (p11 * p02 - p01 * p12)
        e03 = scale * (p11 * p03 - p01 * p13)
        e12 = scale * (p00 * p12 - p01 * p02)
        e13 = scale * (p00 * p13 - p01 * p03)
        s22 = p22 - (p02 * e02 + p12 * e12)
        s23 = p23 - (p02 * e03 + p12 * e13)
        s33 = p33 - (p03 * e03 + p13 * e13)
        scale_s = 1.0 / (s22 * s33 - s23 * s23)
        y0 = scale * (p11 * r0 - p01 * r1)
        y1 = scale * (p00 * r1 - p01 * r0)
        t2 = r2 - (p02 * y0 + p12 * y1)
        t3 = r3 - (p03 * y0 + p13 * y1)
        w2 = scale_s * (s33 * t2 - s23 * t3)
        w3 = scale_s * (s22 * t3 - s23 * t2)
        w0 = y0 - (e02 * w2 + e03 * w3)
        w1 = y1 - (e12 * w2 + e13 * w3)
        solved = (w0, w1, w2, w3)
        for m, part in enumerate(parts):
            change = (columns[0][m] * w0 + columns[1][m] * w1) + (columns[2][m] * w2 + columns[3][m] * w3)
            part = jnp.where(on_block, 0.0, part) - change
            if m == home:
                for a in range(4):
                    part = jnp.where(row_at == off + a, solved[a], part)
            parts[m] = part
    return jnp.concatenate(parts, axis=0)


def is_even():
    return lax.rem(lax.axis_index("dp"), 2) == 0


def precondition_kernel(tok_total, own, other, act_t, grad_t, moved):
    both = jnp.where(is_even(), other[...], own[...])
    factor = both.shape[0]
    lane = lax.broadcasted_iota(jnp.int32, both.shape, 1)
    row_at = lax.broadcasted_iota(jnp.int32, both.shape, 0)
    left_half = lane < factor
    inner = jnp.where(left_half, lane, lane - factor)
    both = both / tok_total + jnp.where(inner == row_at, DAMP, 0.0)
    both = inverse_pair(both)
    blocks = jnp.concatenate(
        [jnp.where(left_half, both, 0.0), jnp.where(left_half, 0.0, both)], axis=0
    )
    proj_t = jnp.concatenate([act_t[...], grad_t[...]], axis=0)
    moved[...] = jnp.dot(blocks, proj_t, precision=HIGHEST, preferred_element_type=jnp.float32)


def precondition(tok_total, own, other, act_t, grad_t):
    factor, tok_rows = act_t.shape
    return pl.pallas_call(
        functools.partial(precondition_kernel, tok_total),
        out_shape=jax.ShapeDtypeStruct((2 * factor, tok_rows), jnp.float32),
        in_specs=[pl.BlockSpec(memory_space=pltpu.VMEM)] * 4,
        out_specs=pl.BlockSpec(memory_space=pltpu.VMEM),
        compiler_params=pltpu.CompilerParams(vmem_limit_bytes=24 * 2**20),
        cost_estimate=pl.CostEstimate(
            flops=1600 * factor * factor * tok_rows, bytes_accessed=16 * factor * tok_rows, transcendentals=0
        ),
        name="precondition",
    )(own, other, act_t, grad_t)


def score_kernel(owners, moved, own, other, scores, total, ordered):
    even = is_even()
    factor = moved.shape[0] // 2
    group = 4
    act_side = moved[:factor, :]
    for first in range(0, factor, group):
        outer = jnp.concatenate(
            [act_side * moved[factor + i : factor + i + 1, :] for i in range(first, first + group)], axis=0
        )
        high = outer.astype(jnp.bfloat16)
        low = (outer - high.astype(jnp.float32)).astype(jnp.bfloat16)
        columns = slice(first * factor, (first + group) * factor)
        values = jnp.where(even, own[:, columns], other[:, columns])
        term = jnp.dot(
            jnp.concatenate([values, values], axis=1),
            jnp.concatenate([high, low], axis=0),
            preferred_element_type=jnp.float32,
        )
        if first == 0:
            total[...] = term
        else:
            total[...] += term
    places = owners(lax.axis_index("dp"))
    rows = total.shape[0] // len(places)
    for at, place in enumerate(places):
        ordered[pl.ds(pl.multiple_of(place * rows, rows), rows), :] = total[at * rows : (at + 1) * rows, :]
    scores[...] = ordered[...].T


def score(owners, moved, own, other):
    tok_rows = moved.shape[1]
    n_queries = own.shape[0]
    return pl.pallas_call(
        functools.partial(score_kernel, owners),
        out_shape=jax.ShapeDtypeStruct((tok_rows, n_queries), jnp.float32),
        in_specs=[pl.BlockSpec(memory_space=pltpu.VMEM)] * 3,
        out_specs=pl.BlockSpec(memory_space=pltpu.VMEM),
        scratch_shapes=[
            pltpu.VMEM((n_queries, tok_rows), jnp.float32),
            pltpu.VMEM((n_queries, tok_rows), jnp.float32),
        ],
        compiler_params=pltpu.CompilerParams(vmem_limit_bytes=48 * 2**20),
        name="score",
    )(moved, own, other)


def within(chips, core, flip):
    return [(2 * chip + core, 2 * (chip ^ flip) + core) for chip in range(chips)]


def across(chips, core):
    return [(2 * chip + core, 2 * chip + 1 - core) for chip in range(chips)]


def moved_by(pairs, value):
    return lax.ppermute(value, "dp", pairs)


def owners_among(chips, me):
    chip = lax.div(me, 2)
    top, under = chips // 2, chips // 4
    owners = [(chip ^ flip) * 2 + core for core in range(2) for flip in (0, top, under)]
    owners += [(chip ^ top ^ under) * 2 + core for core in range(2)]
    flip = under // 2
    while flip:
        owners += [owner ^ (2 * flip) for owner in owners]
        flip //= 2
    return owners


def on_chips(chips, tok_total, acts, grads, proj_act, proj_grad, queries):
    rows = queries.shape[0]
    top, under = chips // 2, chips // 4
    both_cores = [within(chips, 0, flip) + within(chips, 1, flip) for flip in (top, under)]
    pieces = [queries] + [moved_by(pairs, queries) for pairs in both_cores]
    act_t, grad_t, own = project(acts, grads, proj_act, proj_grad)
    *pieces, own = lax.optimization_barrier((*pieces, own))

    mine = jnp.concatenate(pieces, axis=0)
    held = [mine, moved_by(across(chips, 1), mine)]
    own = own + moved_by(across(chips, 0), own)
    *held, own = lax.optimization_barrier((*held, own))
    far = jnp.concatenate([part[rows : 2 * rows] for part in held], axis=0)
    held.append(moved_by(within(chips, 0, under), far))
    held = jnp.concatenate(held, axis=0)
    come = [held]
    flip = under // 2
    while flip:
        held = come[0] if len(come) == 1 else jnp.concatenate(come, axis=0)
        come = [held, moved_by(within(chips, 0, flip), held)]
        own = own + moved_by(within(chips, 1, flip), own)
        flip //= 2
    own = own + sum(moved_by(within(chips, 1, flip), own) for flip in (under, top, top | under))
    other_own = moved_by(across(chips, 1), own)
    *come, own, other_own = lax.optimization_barrier((*come, own, other_own))
    held = jnp.concatenate(come, axis=0)
    other_held = moved_by(across(chips, 0), held)
    moved = precondition(tok_total, own, other_own, act_t, grad_t)
    return score(functools.partial(owners_among, chips), moved, held, other_held)


def on_device(acts, grads, proj_act, proj_grad, queries):
    size = lax.axis_size("dp")
    tok_total = acts.shape[0] * size
    chips = size // 2
    if size % 2 == 0 and chips >= 4 and chips & (chips - 1) == 0:
        return on_chips(chips, tok_total, acts, grads, proj_act, proj_grad, queries)
    held = lax.all_gather(queries, "dp", axis=0, tiled=True)
    act_t, grad_t, own = project(acts, grads, proj_act, proj_grad)
    own = lax.psum(own, "dp")
    moved = precondition(tok_total, own, own, act_t, grad_t)
    return score(lambda me: list(range(size)), moved, held, held)


def solution(mesh):
    in_specs = (P(("parts", "dp"), None), P(("parts", "dp"), None), P(), P(), P("dp", None))
    out_specs = P(("parts", "dp"), None)
    return jax.shard_map(
        on_device, mesh=mesh, in_specs=in_specs, out_specs=out_specs, check_vma=False
    )
```

```python
import functools

import jax
import jax.numpy as jnp
from jax import lax
from jax.experimental import pallas as pl
from jax.experimental.pallas import tpu as pltpu
from jax.sharding import PartitionSpec as P

DAMP = 0.1
HIGHEST = lax.Precision.HIGHEST
COPY_ROWS = 128
IN_FLIGHT = 8
TOKENS_AT_ONCE = 256


def project_kernel(
    acts, grads, weight_act, weight_grad, act_t, grad_t, cov, tok_buf, weight_buf, weight_t, tok_sems, weight_sems
):
    width = weight_act.shape[1]
    n_parts = acts.shape[0] // COPY_ROWS
    weight_copies = [
        pltpu.make_async_copy(src, weight_buf.at[at], weight_sems.at[at])
        for at, src in enumerate((weight_act, weight_grad))
    ]
    tok_copies = [
        [
            pltpu.make_async_copy(
                src.at[pl.ds(part * COPY_ROWS, COPY_ROWS), :],
                tok_buf.at[at, pl.ds(part * COPY_ROWS, COPY_ROWS), :],
                tok_sems.at[at, part],
            )
            for part in range(n_parts)
        ]
        for at, src in enumerate((acts, grads))
    ]
    queue = [weight_copies[0], *tok_copies[0], *tok_copies[1]]
    queue.insert(3, weight_copies[1])

    def start_next(many):
        for copy in queue[:many]:
            copy.start()
        del queue[:many]

    def turned(at):
        for first in range(0, width, 512):
            block = weight_buf[at, :, first : first + 512].astype(jnp.float32)
            weight_t[at, first : first + 512, :] = block.T.astype(weight_t.dtype)

    steps = [(at, part, min(2, n_parts - part)) for at in range(2) for part in range(0, n_parts, 2)]
    last_act = len(steps) // 2 - 1
    at, part, many = steps.pop()
    steps += [(at, part + one, 1) for one in range(many)]
    grams = [None, None]

    def add_gram(at, flipped, block):
        term = jnp.dot(flipped, block, precision=HIGHEST, preferred_element_type=jnp.float32)
        grams[at] = term if grams[at] is None else grams[at] + term

    start_next(1 + IN_FLIGHT)
    weight_copies[0].wait()
    turned(0)
    before = None
    for step, (at, part, many) in enumerate(steps):
        for copy in tok_copies[at][part : part + many]:
            copy.wait()
            start_next(1)
        if step == last_act:
            weight_copies[1].wait()
            start_next(1)
        rows = slice(part * COPY_ROWS, (part + many) * COPY_ROWS)
        block = jnp.dot(tok_buf[at, rows, :], weight_t[at], preferred_element_type=jnp.float32)
        if step == last_act:
            turned(1)
        if before is not None:
            add_gram(*before)
        flipped = block.T
        (act_t, grad_t)[at][:, rows] = flipped
        before = (at, flipped, block)
    add_gram(*before)
    cov[...] = jnp.concatenate(grams, axis=1)


def project(acts, grads, proj_act, proj_grad):
    tok_rows, width = acts.shape
    factor = proj_act.shape[1]
    operands = [
        pltpu.with_memory_space_constraint(value, pltpu.HBM) for value in (acts, grads, proj_act.T, proj_grad.T)
    ]
    return pl.pallas_call(
        project_kernel,
        out_shape=(
            jax.ShapeDtypeStruct((factor, tok_rows), jnp.float32),
            jax.ShapeDtypeStruct((factor, tok_rows), jnp.float32),
            jax.ShapeDtypeStruct((factor, 2 * factor), jnp.float32),
        ),
        in_specs=[pl.BlockSpec(memory_space=pltpu.HBM)] * 4,
        out_specs=[pl.BlockSpec(memory_space=pltpu.VMEM)] * 3,
        scratch_shapes=[
            pltpu.VMEM((2, tok_rows, width), acts.dtype),
            pltpu.VMEM((2, factor, width), proj_act.dtype),
            pltpu.VMEM((2, width, factor), proj_act.dtype),
            pltpu.SemaphoreType.DMA((2, tok_rows // COPY_ROWS)),
            pltpu.SemaphoreType.DMA((2,)),
        ],
        compiler_params=pltpu.CompilerParams(vmem_limit_bytes=24 * 2**20),
        cost_estimate=pl.CostEstimate(
            flops=4 * tok_rows * width * factor, bytes_accessed=4 * tok_rows * width, transcendentals=0
        ),
        name="project",
    )(*operands)


def inverse_pair(both):
    factor = both.shape[0]
    tile = (8, both.shape[1])
    lane = lax.broadcasted_iota(jnp.int32, tile, 1)
    row_at = lax.broadcasted_iota(jnp.int32, tile, 0)
    left_half = lane < factor
    inner = jnp.where(left_half, lane, lane - factor)
    parts = [both[at : at + 8, :] for at in range(0, factor, 8)]

    def column(part, at):
        left = jnp.broadcast_to(part[:, at : at + 1], tile)
        right = jnp.broadcast_to(part[:, factor + at : factor + at + 1], tile)
        return jnp.where(left_half, left, right)

    def row(part, at):
        return jnp.broadcast_to(part[at : at + 1, :], tile)

    for k in range(0, factor, 4):
        home, off = divmod(k, 8)
        columns = [[column(part, k + a) for part in parts] for a in range(4)]
        pivot = [[row(columns[b][home], off + a) if a <= b else None for b in range(4)] for a in range(4)]
        p00, p01, p02, p03 = pivot[0]
        _, p11, p12, p13 = pivot[1]
        _, _, p22, p23 = pivot[2]
        p33 = pivot[3][3]
        on_block = (inner >= k) & (inner < k + 4)
        r0, r1, r2, r3 = [
            jnp.where(on_block, jnp.where(inner == k + a, 1.0, 0.0), row(parts[home], off + a)) for a in range(4)
        ]
        scale = 1.0 / (p00 * p11 - p01 * p01)
        e02 = scale * (p11 * p02 - p01 * p12)
        e03 = scale * (p11 * p03 - p01 * p13)
        e12 = scale * (p00 * p12 - p01 * p02)
        e13 = scale * (p00 * p13 - p01 * p03)
        s22 = p22 - (p02 * e02 + p12 * e12)
        s23 = p23 - (p02 * e03 + p12 * e13)
        s33 = p33 - (p03 * e03 + p13 * e13)
        scale_s = 1.0 / (s22 * s33 - s23 * s23)
        y0 = scale * (p11 * r0 - p01 * r1)
        y1 = scale * (p00 * r1 - p01 * r0)
        t2 = r2 - (p02 * y0 + p12 * y1)
        t3 = r3 - (p03 * y0 + p13 * y1)
        w2 = scale_s * (s33 * t2 - s23 * t3)
        w3 = scale_s * (s22 * t3 - s23 * t2)
        w0 = y0 - (e02 * w2 + e03 * w3)
        w1 = y1 - (e12 * w2 + e13 * w3)
        solved = (w0, w1, w2, w3)
        for m, part in enumerate(parts):
            change = (columns[0][m] * w0 + columns[1][m] * w1) + (columns[2][m] * w2 + columns[3][m] * w3)
            part = jnp.where(on_block, 0.0, part) - change
            if m == home:
                for a in range(4):
                    part = jnp.where(row_at == off + a, solved[a], part)
            parts[m] = part
    return jnp.concatenate(parts, axis=0)


def precondition_kernel(tok_total, n_terms, *refs):
    terms, (act_t, grad_t, moved) = refs[:n_terms], refs[n_terms:]
    both = terms[0][...]
    for term in terms[1:]:
        both = both + term[...]
    factor = both.shape[0]
    lane = lax.broadcasted_iota(jnp.int32, both.shape, 1)
    row_at = lax.broadcasted_iota(jnp.int32, both.shape, 0)
    left_half = lane < factor
    inner = jnp.where(left_half, lane, lane - factor)
    both = both / tok_total + jnp.where(inner == row_at, DAMP, 0.0)
    both = inverse_pair(both)
    blocks = jnp.concatenate(
        [jnp.where(left_half, both, 0.0), jnp.where(left_half, 0.0, both)], axis=0
    )
    proj_t = jnp.concatenate([act_t[...], grad_t[...]], axis=0)
    moved[...] = jnp.dot(blocks, proj_t, precision=HIGHEST, preferred_element_type=jnp.float32)


def precondition(tok_total, terms, act_t, grad_t):
    factor, tok_rows = act_t.shape
    n_terms = len(terms)
    return pl.pallas_call(
        functools.partial(precondition_kernel, tok_total, n_terms),
        out_shape=jax.ShapeDtypeStruct((2 * factor, tok_rows), jnp.float32),
        in_specs=[pl.BlockSpec(memory_space=pltpu.VMEM)] * (n_terms + 2),
        out_specs=pl.BlockSpec(memory_space=pltpu.VMEM),
        compiler_params=pltpu.CompilerParams(vmem_limit_bytes=24 * 2**20),
        cost_estimate=pl.CostEstimate(
            flops=1600 * factor * factor * tok_rows, bytes_accessed=16 * factor * tok_rows, transcendentals=0
        ),
        name="precondition",
    )(*terms, act_t, grad_t)


def score_kernel(size, n_pieces, moved, *refs):
    queries, (scores, ordered, result, sems) = refs[:n_pieces], refs[n_pieces:]
    factor = moved.shape[0] // 2
    owners = owners_of(lax.axis_index("dp"), size)
    group = 4
    copies = []
    for part, begin in enumerate(range(0, moved.shape[1], TOKENS_AT_ONCE)):
        tokens = slice(begin, begin + TOKENS_AT_ONCE)
        act_side = moved[:factor, tokens]
        total = None
        for first in range(0, factor, group):
            outer = jnp.concatenate(
                [act_side * moved[factor + i : factor + i + 1, tokens] for i in range(first, first + group)], axis=0
            )
            high = outer.astype(jnp.bfloat16)
            low = (outer - high.astype(jnp.float32)).astype(jnp.bfloat16)
            columns = slice(first * factor, (first + group) * factor)
            values = jnp.concatenate([piece[:, columns] for piece in queries], axis=0)
            term = jnp.dot(
                jnp.concatenate([values, values], axis=1),
                jnp.concatenate([high, low], axis=0),
                preferred_element_type=jnp.float32,
            )
            total = term if total is None else total + term
        rows = total.shape[0] // size
        for at, owner in enumerate(owners):
            place = pl.ds(pl.multiple_of(owner * rows, rows), rows)
            ordered[part, place, :] = total[at * rows : (at + 1) * rows, :]
        result[tokens, :] = ordered[part].T
        copies.append(
            pltpu.make_async_copy(
                result.at[pl.ds(begin, TOKENS_AT_ONCE), :], scores.at[pl.ds(begin, TOKENS_AT_ONCE), :], sems.at[part]
            )
        )
        copies[-1].start()
    for copy in copies:
        copy.wait()


def score(size, moved, queries):
    tok_rows = moved.shape[1]
    n_queries = sum(piece.shape[0] for piece in queries)
    n_pieces = len(queries)
    n_parts = tok_rows // TOKENS_AT_ONCE
    return pl.pallas_call(
        functools.partial(score_kernel, size, n_pieces),
        out_shape=jax.ShapeDtypeStruct((tok_rows, n_queries), jnp.float32),
        in_specs=[pl.BlockSpec(memory_space=pltpu.VMEM)] * (1 + n_pieces),
        out_specs=pl.BlockSpec(memory_space=pl.ANY),
        scratch_shapes=[
            pltpu.VMEM((n_parts, n_queries, TOKENS_AT_ONCE), jnp.float32),
            pltpu.VMEM((tok_rows, n_queries), jnp.float32),
            pltpu.SemaphoreType.DMA((n_parts,)),
        ],
        compiler_params=pltpu.CompilerParams(vmem_limit_bytes=32 * 2**20),
        name="score",
    )(moved, *queries)


def gather_stages(size):
    if size & (size - 1):
        return [(1, size)]
    return [(size >> level, 2) for level in range(1, size.bit_length())]


def sum_rounds(size):
    core = 2 if size % 2 == 0 else 1
    rest = size // core
    near = max(d for d in range(1, rest + 1) if rest % d == 0 and d * d <= rest)
    return [(1, core * near), (core * near, rest // near)]


def after(value, other):
    return lax.optimization_barrier((value, other))[0]


def partner(digit, radix, shift):
    return digit ^ shift if radix & (radix - 1) == 0 else (digit + shift) % radix


def swapped(value, size, stride, radix, shift):
    perm = []
    for at in range(size):
        digit = at // stride % radix
        perm.append((at, at + (partner(digit, radix, shift) - digit) * stride))
    return lax.ppermute(value, "dp", perm)


def owners_of(me, size):
    owners = [me]
    for stride, radix in gather_stages(size):
        digit = lax.rem(lax.div(me, stride), radix)
        back = [shift if radix & (radix - 1) == 0 else radix - shift for shift in range(radix)]
        steps = [(partner(digit, radix, shift) - digit) * stride for shift in back]
        owners = [owner + step for step in steps for owner in owners]
    return owners


def exchanged(held, size, stride, radix):
    mine = held[0] if len(held) == 1 else jnp.concatenate(held, axis=0)
    return [mine] + [swapped(mine, size, stride, radix, shift) for shift in range(1, radix)]


def on_device(acts, grads, proj_act, proj_grad, queries):
    size = lax.axis_size("dp")
    tok_total = acts.shape[0] * size
    stages = gather_stages(size)
    first, second = sum_rounds(size)

    def gathered(pieces, some):
        for stage in some:
            pieces = exchanged(pieces, size, *stage)
        return pieces

    if len(stages) > 1:
        pieces = [queries] + [swapped(queries, size, *stage, 1) for stage in stages[:2]]
    else:
        pieces = exchanged([queries], size, *stages[0])
    act_t, grad_t, own = project(acts, grads, proj_act, proj_grad)
    *pieces, own = lax.optimization_barrier((*pieces, own))
    if len(stages) > 1:
        pieces.append(swapped(pieces[1], size, *stages[1], 1))
    own = functools.reduce(jnp.add, exchanged([own], size, *first))
    *pieces, own = lax.optimization_barrier((*pieces, own))
    pieces = gathered(pieces, stages[2:-1])
    terms = exchanged([own], size, *second)
    *both, = lax.optimization_barrier((*pieces, *terms))
    pieces, terms = both[: len(pieces)], both[len(pieces) :]
    pieces = gathered(pieces, stages[max(2, len(stages) - 1) :])
    moved = precondition(tok_total, terms, act_t, grad_t)
    return score(size, moved, pieces)


def solution(mesh):
    in_specs = (P(("parts", "dp"), None), P(("parts", "dp"), None), P(), P(), P("dp", None))
    out_specs = P(("parts", "dp"), None)
    return jax.shard_map(
        on_device, mesh=mesh, in_specs=in_specs, out_specs=out_specs, check_vma=False
    )
```

```python
import functools

import jax
import jax.numpy as jnp
from jax import lax
from jax.experimental import pallas as pl
from jax.experimental.pallas import tpu as pltpu
from jax.sharding import PartitionSpec as P

DAMP = 0.1
HIGHEST = lax.Precision.HIGHEST
COPY_ROWS = 128
IN_FLIGHT = 4
TOKENS_AT_ONCE = 256


def project_kernel(
    acts, grads, weight_act, weight_grad, act_t, grad_t, cov, tok_buf, weight_buf, weight_t, tok_sems, weight_sems
):
    width = weight_act.shape[1]
    n_parts = acts.shape[0] // COPY_ROWS
    weight_copies = [
        pltpu.make_async_copy(src, weight_buf.at[at], weight_sems.at[at])
        for at, src in enumerate((weight_act, weight_grad))
    ]
    tok_copies = [
        [
            pltpu.make_async_copy(
                src.at[pl.ds(part * COPY_ROWS, COPY_ROWS), :],
                tok_buf.at[at, pl.ds(part * COPY_ROWS, COPY_ROWS), :],
                tok_sems.at[at, part],
            )
            for part in range(n_parts)
        ]
        for at, src in enumerate((acts, grads))
    ]
    queue = [weight_copies[0], *tok_copies[0], *tok_copies[1]]
    queue.insert(3, weight_copies[1])

    def start_next(many):
        for copy in queue[:many]:
            copy.start()
        del queue[:many]

    def turned(at):
        for first in range(0, width, 512):
            block = weight_buf[at, :, first : first + 512].astype(jnp.float32)
            weight_t[at, first : first + 512, :] = block.T.astype(weight_t.dtype)

    steps = [(at, part, min(2, n_parts - part)) for at in range(2) for part in range(0, n_parts, 2)]
    last_act = len(steps) // 2 - 1
    at, part, many = steps.pop()
    steps += [(at, part + one, 1) for one in range(many)]
    grams = [None, None]

    def add_gram(at, flipped, block):
        term = jnp.dot(flipped, block, precision=HIGHEST, preferred_element_type=jnp.float32)
        grams[at] = term if grams[at] is None else grams[at] + term

    start_next(1 + IN_FLIGHT)
    weight_copies[0].wait()
    turned(0)
    before = None
    for step, (at, part, many) in enumerate(steps):
        for copy in tok_copies[at][part : part + many]:
            copy.wait()
            start_next(1)
        if step == last_act:
            weight_copies[1].wait()
            start_next(1)
        rows = slice(part * COPY_ROWS, (part + many) * COPY_ROWS)
        block = jnp.dot(tok_buf[at, rows, :], weight_t[at], preferred_element_type=jnp.float32)
        if step == last_act:
            turned(1)
        if before is not None:
            add_gram(*before)
        flipped = block.T
        (act_t, grad_t)[at][:, rows] = flipped
        before = (at, flipped, block)
    add_gram(*before)
    cov[...] = jnp.concatenate(grams, axis=1)


def project(acts, grads, proj_act, proj_grad):
    tok_rows, width = acts.shape
    factor = proj_act.shape[1]
    operands = [
        pltpu.with_memory_space_constraint(value, pltpu.HBM) for value in (acts, grads, proj_act.T, proj_grad.T)
    ]
    return pl.pallas_call(
        project_kernel,
        out_shape=(
            jax.ShapeDtypeStruct((factor, tok_rows), jnp.float32),
            jax.ShapeDtypeStruct((factor, tok_rows), jnp.float32),
            jax.ShapeDtypeStruct((factor, 2 * factor), jnp.float32),
        ),
        in_specs=[pl.BlockSpec(memory_space=pltpu.HBM)] * 4,
        out_specs=[pl.BlockSpec(memory_space=pltpu.VMEM)] * 3,
        scratch_shapes=[
            pltpu.VMEM((2, tok_rows, width), acts.dtype),
            pltpu.VMEM((2, factor, width), proj_act.dtype),
            pltpu.VMEM((2, width, factor), proj_act.dtype),
            pltpu.SemaphoreType.DMA((2, tok_rows // COPY_ROWS)),
            pltpu.SemaphoreType.DMA((2,)),
        ],
        compiler_params=pltpu.CompilerParams(vmem_limit_bytes=24 * 2**20),
        cost_estimate=pl.CostEstimate(
            flops=4 * tok_rows * width * factor, bytes_accessed=4 * tok_rows * width, transcendentals=0
        ),
        name="project",
    )(*operands)


def inverse_pair(both):
    factor = both.shape[0]
    tile = (8, both.shape[1])
    lane = lax.broadcasted_iota(jnp.int32, tile, 1)
    row_at = lax.broadcasted_iota(jnp.int32, tile, 0)
    left_half = lane < factor
    inner = jnp.where(left_half, lane, lane - factor)
    parts = [both[at : at + 8, :] for at in range(0, factor, 8)]

    def column(part, at):
        left = jnp.broadcast_to(part[:, at : at + 1], tile)
        right = jnp.broadcast_to(part[:, factor + at : factor + at + 1], tile)
        return jnp.where(left_half, left, right)

    def row(part, at):
        return jnp.broadcast_to(part[at : at + 1, :], tile)

    for k in range(0, factor, 4):
        home, off = divmod(k, 8)
        columns = [[column(part, k + a) for part in parts] for a in range(4)]
        pivot = [[row(columns[b][home], off + a) if a <= b else None for b in range(4)] for a in range(4)]
        p00, p01, p02, p03 = pivot[0]
        _, p11, p12, p13 = pivot[1]
        _, _, p22, p23 = pivot[2]
        p33 = pivot[3][3]
        on_block = (inner >= k) & (inner < k + 4)
        r0, r1, r2, r3 = [
            jnp.where(on_block, jnp.where(inner == k + a, 1.0, 0.0), row(parts[home], off + a)) for a in range(4)
        ]
        scale = 1.0 / (p00 * p11 - p01 * p01)
        e02 = scale * (p11 * p02 - p01 * p12)
        e03 = scale * (p11 * p03 - p01 * p13)
        e12 = scale * (p00 * p12 - p01 * p02)
        e13 = scale * (p00 * p13 - p01 * p03)
        s22 = p22 - (p02 * e02 + p12 * e12)
        s23 = p23 - (p02 * e03 + p12 * e13)
        s33 = p33 - (p03 * e03 + p13 * e13)
        scale_s = 1.0 / (s22 * s33 - s23 * s23)
        y0 = scale * (p11 * r0 - p01 * r1)
        y1 = scale * (p00 * r1 - p01 * r0)
        t2 = r2 - (p02 * y0 + p12 * y1)
        t3 = r3 - (p03 * y0 + p13 * y1)
        w2 = scale_s * (s33 * t2 - s23 * t3)
        w3 = scale_s * (s22 * t3 - s23 * t2)
        w0 = y0 - (e02 * w2 + e03 * w3)
        w1 = y1 - (e12 * w2 + e13 * w3)
        solved = (w0, w1, w2, w3)
        for m, part in enumerate(parts):
            change = (columns[0][m] * w0 + columns[1][m] * w1) + (columns[2][m] * w2 + columns[3][m] * w3)
            part = jnp.where(on_block, 0.0, part) - change
            if m == home:
                for a in range(4):
                    part = jnp.where(row_at == off + a, solved[a], part)
            parts[m] = part
    return jnp.concatenate(parts, axis=0)


def precondition_kernel(tok_total, n_terms, *refs):
    terms, (act_t, grad_t, moved) = refs[:n_terms], refs[n_terms:]
    both = terms[0][...]
    for term in terms[1:]:
        both = both + term[...]
    factor = both.shape[0]
    lane = lax.broadcasted_iota(jnp.int32, both.shape, 1)
    row_at = lax.broadcasted_iota(jnp.int32, both.shape, 0)
    left_half = lane < factor
    inner = jnp.where(left_half, lane, lane - factor)
    both = both / tok_total + jnp.where(inner == row_at, DAMP, 0.0)
    both = inverse_pair(both)
    blocks = jnp.concatenate(
        [jnp.where(left_half, both, 0.0), jnp.where(left_half, 0.0, both)], axis=0
    )
    proj_t = jnp.concatenate([act_t[...], grad_t[...]], axis=0)
    moved[...] = jnp.dot(blocks, proj_t, precision=HIGHEST, preferred_element_type=jnp.float32)


def precondition(tok_total, terms, act_t, grad_t):
    factor, tok_rows = act_t.shape
    n_terms = len(terms)
    return pl.pallas_call(
        functools.partial(precondition_kernel, tok_total, n_terms),
        out_shape=jax.ShapeDtypeStruct((2 * factor, tok_rows), jnp.float32),
        in_specs=[pl.BlockSpec(memory_space=pltpu.VMEM)] * (n_terms + 2),
        out_specs=pl.BlockSpec(memory_space=pltpu.VMEM),
        compiler_params=pltpu.CompilerParams(vmem_limit_bytes=24 * 2**20),
        cost_estimate=pl.CostEstimate(
            flops=1600 * factor * factor * tok_rows, bytes_accessed=16 * factor * tok_rows, transcendentals=0
        ),
        name="precondition",
    )(*terms, act_t, grad_t)


def score_kernel(size, n_pieces, moved, *refs):
    queries, (scores, ordered, result, sems) = refs[:n_pieces], refs[n_pieces:]
    factor = moved.shape[0] // 2
    owners = owners_of(lax.axis_index("dp"), size)
    group = 4
    copies = []
    for part, begin in enumerate(range(0, moved.shape[1], TOKENS_AT_ONCE)):
        tokens = slice(begin, begin + TOKENS_AT_ONCE)
        act_side = moved[:factor, tokens]
        total = None
        for first in range(0, factor, group):
            outer = jnp.concatenate(
                [act_side * moved[factor + i : factor + i + 1, tokens] for i in range(first, first + group)], axis=0
            )
            high = outer.astype(jnp.bfloat16)
            low = (outer - high.astype(jnp.float32)).astype(jnp.bfloat16)
            columns = slice(first * factor, (first + group) * factor)
            values = jnp.concatenate([piece[:, columns] for piece in queries], axis=0)
            term = jnp.dot(
                jnp.concatenate([values, values], axis=1),
                jnp.concatenate([high, low], axis=0),
                preferred_element_type=jnp.float32,
            )
            total = term if total is None else total + term
        rows = total.shape[0] // size
        for at, owner in enumerate(owners):
            place = pl.ds(pl.multiple_of(owner * rows, rows), rows)
            ordered[part, place, :] = total[at * rows : (at + 1) * rows, :]
        result[tokens, :] = ordered[part].T
        copies.append(
            pltpu.make_async_copy(
                result.at[pl.ds(begin, TOKENS_AT_ONCE), :], scores.at[pl.ds(begin, TOKENS_AT_ONCE), :], sems.at[part]
            )
        )
        copies[-1].start()
    for copy in copies:
        copy.wait()


def score(size, moved, queries):
    tok_rows = moved.shape[1]
    n_queries = sum(piece.shape[0] for piece in queries)
    n_pieces = len(queries)
    n_parts = tok_rows // TOKENS_AT_ONCE
    return pl.pallas_call(
        functools.partial(score_kernel, size, n_pieces),
        out_shape=jax.ShapeDtypeStruct((tok_rows, n_queries), jnp.float32),
        in_specs=[pl.BlockSpec(memory_space=pltpu.VMEM)] * (1 + n_pieces),
        out_specs=pl.BlockSpec(memory_space=pl.ANY),
        scratch_shapes=[
            pltpu.VMEM((n_parts, n_queries, TOKENS_AT_ONCE), jnp.float32),
            pltpu.VMEM((tok_rows, n_queries), jnp.float32),
            pltpu.SemaphoreType.DMA((n_parts,)),
        ],
        compiler_params=pltpu.CompilerParams(vmem_limit_bytes=32 * 2**20),
        name="score",
    )(moved, *queries)


def gather_stages(size):
    core = 2 if size % 2 == 0 else 1
    rest = size // core
    near = max(d for d in range(1, rest + 1) if rest % d == 0 and d * d <= rest)
    return [(core * near, rest // near), (core, near), (1, core)]


def sum_rounds(size):
    (stride, radix), *_ = gather_stages(size)
    return [(1, stride), (stride, radix)]


def after(value, other):
    return lax.optimization_barrier((value, other))[0]


def partner(digit, radix, shift):
    return digit ^ shift if radix & (radix - 1) == 0 else (digit + shift) % radix


def swapped(value, size, stride, radix, shift):
    perm = []
    for at in range(size):
        digit = at // stride % radix
        perm.append((at, at + (partner(digit, radix, shift) - digit) * stride))
    return lax.ppermute(value, "dp", perm)


def owners_of(me, size):
    owners = [me]
    for stride, radix in gather_stages(size):
        digit = lax.rem(lax.div(me, stride), radix)
        back = [shift if radix & (radix - 1) == 0 else radix - shift for shift in range(radix)]
        steps = [(partner(digit, radix, shift) - digit) * stride for shift in back]
        owners = [owner + step for step in steps for owner in owners]
    return owners


def exchanged(held, size, stride, radix):
    mine = held[0] if len(held) == 1 else jnp.concatenate(held, axis=0)
    return [mine] + [swapped(mine, size, stride, radix, shift) for shift in range(1, radix)]


def on_device(acts, grads, proj_act, proj_grad, queries):
    size = lax.axis_size("dp")
    tok_total = acts.shape[0] * size
    far, near, core = gather_stages(size)
    first, second = sum_rounds(size)

    pieces = exchanged([queries], size, *far)
    act_t, grad_t, own = project(acts, grads, proj_act, proj_grad)
    *pieces, own = lax.optimization_barrier((*pieces, own))
    pieces = exchanged(pieces, size, *near)
    own = functools.reduce(jnp.add, exchanged([own], size, *first))
    terms = exchanged([own], size, *second)
    *both, = lax.optimization_barrier((*pieces, *terms))
    pieces, terms = both[: len(pieces)], both[len(pieces) :]
    pieces = exchanged(pieces, size, *core)
    moved = precondition(tok_total, terms, act_t, grad_t)
    return score(size, moved, pieces)


def solution(mesh):
    in_specs = (P(("parts", "dp"), None), P(("parts", "dp"), None), P(), P(), P("dp", None))
    out_specs = P(("parts", "dp"), None)
    return jax.shard_map(
        on_device, mesh=mesh, in_specs=in_specs, out_specs=out_specs, check_vma=False
    )
```

```python
import functools

import jax
import jax.numpy as jnp
from jax import lax
from jax.experimental import pallas as pl
from jax.experimental.pallas import tpu as pltpu
from jax.sharding import PartitionSpec as P

DAMP = 0.1
HIGHEST = lax.Precision.HIGHEST
COPY_ROWS = 128
IN_FLIGHT = 3
TOKENS_AT_ONCE = 256
ORDER = (3, 2, 1)


def project_kernel(
    acts, grads, weight_act, weight_grad, act_t, grad_t, cov, tok_buf, weight_buf, weight_t, tok_sems, weight_sems
):
    width = weight_act.shape[1]
    n_parts = acts.shape[0] // COPY_ROWS
    weight_copies = [
        pltpu.make_async_copy(src, weight_buf.at[at], weight_sems.at[at])
        for at, src in enumerate((weight_act, weight_grad))
    ]
    tok_copies = [
        [
            pltpu.make_async_copy(
                src.at[pl.ds(part * COPY_ROWS, COPY_ROWS), :],
                tok_buf.at[at, pl.ds(part * COPY_ROWS, COPY_ROWS), :],
                tok_sems.at[at, part],
            )
            for part in range(n_parts)
        ]
        for at, src in enumerate((acts, grads))
    ]
    queue = [weight_copies[0], *tok_copies[0], *tok_copies[1]]
    queue.insert(4, weight_copies[1])

    def start_next(many):
        for copy in queue[:many]:
            copy.start()
        del queue[:many]

    def turned(at):
        for first in range(0, width, 512):
            block = weight_buf[at, :, first : first + 512].astype(jnp.float32)
            weight_t[at, first : first + 512, :] = block.T.astype(weight_t.dtype)

    steps = [(at, part, min(2, n_parts - part)) for at in range(2) for part in range(0, n_parts, 2)]
    last_act = len(steps) // 2 - 1
    at, part, many = steps.pop()
    steps += [(at, part + one, 1) for one in range(many)]
    grams = [None, None]

    def add_gram(at, flipped, block):
        term = jnp.dot(flipped, block, precision=HIGHEST, preferred_element_type=jnp.float32)
        grams[at] = term if grams[at] is None else grams[at] + term

    start_next(1 + IN_FLIGHT)
    weight_copies[0].wait()
    turned(0)
    before = None
    for step, (at, part, many) in enumerate(steps):
        for copy in tok_copies[at][part : part + many]:
            copy.wait()
            start_next(1)
        if step == last_act:
            weight_copies[1].wait()
            start_next(1)
        rows = slice(part * COPY_ROWS, (part + many) * COPY_ROWS)
        block = jnp.dot(tok_buf[at, rows, :], weight_t[at], preferred_element_type=jnp.float32)
        if step == last_act:
            turned(1)
        if before is not None:
            add_gram(*before)
        flipped = block.T
        (act_t, grad_t)[at][:, rows] = flipped
        before = (at, flipped, block)
    add_gram(*before)
    cov[...] = jnp.concatenate(grams, axis=1)


def project(acts, grads, proj_act, proj_grad):
    tok_rows, width = acts.shape
    factor = proj_act.shape[1]
    operands = [
        pltpu.with_memory_space_constraint(value, pltpu.HBM) for value in (acts, grads, proj_act.T, proj_grad.T)
    ]
    return pl.pallas_call(
        project_kernel,
        out_shape=(
            jax.ShapeDtypeStruct((factor, tok_rows), jnp.float32),
            jax.ShapeDtypeStruct((factor, tok_rows), jnp.float32),
            jax.ShapeDtypeStruct((factor, 2 * factor), jnp.float32),
        ),
        in_specs=[pl.BlockSpec(memory_space=pltpu.HBM)] * 4,
        out_specs=[pl.BlockSpec(memory_space=pltpu.VMEM)] * 3,
        scratch_shapes=[
            pltpu.VMEM((2, tok_rows, width), acts.dtype),
            pltpu.VMEM((2, factor, width), proj_act.dtype),
            pltpu.VMEM((2, width, factor), proj_act.dtype),
            pltpu.SemaphoreType.DMA((2, tok_rows // COPY_ROWS)),
            pltpu.SemaphoreType.DMA((2,)),
        ],
        compiler_params=pltpu.CompilerParams(vmem_limit_bytes=24 * 2**20),
        cost_estimate=pl.CostEstimate(
            flops=4 * tok_rows * width * factor, bytes_accessed=4 * tok_rows * width, transcendentals=0
        ),
        name="project",
    )(*operands)


def inverse_pair(both):
    factor = both.shape[0]
    tile = (8, both.shape[1])
    lane = lax.broadcasted_iota(jnp.int32, tile, 1)
    row_at = lax.broadcasted_iota(jnp.int32, tile, 0)
    left_half = lane < factor
    inner = jnp.where(left_half, lane, lane - factor)
    parts = [both[at : at + 8, :] for at in range(0, factor, 8)]

    def column(part, at):
        left = jnp.broadcast_to(part[:, at : at + 1], tile)
        right = jnp.broadcast_to(part[:, factor + at : factor + at + 1], tile)
        return jnp.where(left_half, left, right)

    def row(part, at):
        return jnp.broadcast_to(part[at : at + 1, :], tile)

    for k in range(0, factor, 4):
        home, off = divmod(k, 8)
        columns = [[column(part, k + a) for part in parts] for a in range(4)]
        pivot = [[row(columns[b][home], off + a) if a <= b else None for b in range(4)] for a in range(4)]
        p00, p01, p02, p03 = pivot[0]
        _, p11, p12, p13 = pivot[1]
        _, _, p22, p23 = pivot[2]
        p33 = pivot[3][3]
        on_block = (inner >= k) & (inner < k + 4)
        r0, r1, r2, r3 = [
            jnp.where(on_block, jnp.where(inner == k + a, 1.0, 0.0), row(parts[home], off + a)) for a in range(4)
        ]
        scale = 1.0 / (p00 * p11 - p01 * p01)
        e02 = scale * (p11 * p02 - p01 * p12)
        e03 = scale * (p11 * p03 - p01 * p13)
        e12 = scale * (p00 * p12 - p01 * p02)
        e13 = scale * (p00 * p13 - p01 * p03)
        s22 = p22 - (p02 * e02 + p12 * e12)
        s23 = p23 - (p02 * e03 + p12 * e13)
        s33 = p33 - (p03 * e03 + p13 * e13)
        scale_s = 1.0 / (s22 * s33 - s23 * s23)
        y0 = scale * (p11 * r0 - p01 * r1)
        y1 = scale * (p00 * r1 - p01 * r0)
        t2 = r2 - (p02 * y0 + p12 * y1)
        t3 = r3 - (p03 * y0 + p13 * y1)
        w2 = scale_s * (s33 * t2 - s23 * t3)
        w3 = scale_s * (s22 * t3 - s23 * t2)
        w0 = y0 - (e02 * w2 + e03 * w3)
        w1 = y1 - (e12 * w2 + e13 * w3)
        solved = (w0, w1, w2, w3)
        for m, part in enumerate(parts):
            change = (columns[0][m] * w0 + columns[1][m] * w1) + (columns[2][m] * w2 + columns[3][m] * w3)
            part = jnp.where(on_block, 0.0, part) - change
            if m == home:
                for a in range(4):
                    part = jnp.where(row_at == off + a, solved[a], part)
            parts[m] = part
    return jnp.concatenate(parts, axis=0)


def precondition_kernel(tok_total, n_terms, *refs):
    terms, (act_t, grad_t, moved) = refs[:n_terms], refs[n_terms:]
    both = terms[0][...]
    for term in terms[1:]:
        both = both + term[...]
    factor = both.shape[0]
    lane = lax.broadcasted_iota(jnp.int32, both.shape, 1)
    row_at = lax.broadcasted_iota(jnp.int32, both.shape, 0)
    left_half = lane < factor
    inner = jnp.where(left_half, lane, lane - factor)
    both = both / tok_total + jnp.where(inner == row_at, DAMP, 0.0)
    both = inverse_pair(both)
    blocks = jnp.concatenate(
        [jnp.where(left_half, both, 0.0), jnp.where(left_half, 0.0, both)], axis=0
    )
    proj_t = jnp.concatenate([act_t[...], grad_t[...]], axis=0)
    moved[...] = jnp.dot(blocks, proj_t, precision=HIGHEST, preferred_element_type=jnp.float32)


def precondition(tok_total, terms, act_t, grad_t):
    factor, tok_rows = act_t.shape
    n_terms = len(terms)
    return pl.pallas_call(
        functools.partial(precondition_kernel, tok_total, n_terms),
        out_shape=jax.ShapeDtypeStruct((2 * factor, tok_rows), jnp.float32),
        in_specs=[pl.BlockSpec(memory_space=pltpu.VMEM)] * (n_terms + 2),
        out_specs=pl.BlockSpec(memory_space=pltpu.VMEM),
        compiler_params=pltpu.CompilerParams(vmem_limit_bytes=24 * 2**20),
        cost_estimate=pl.CostEstimate(
            flops=1600 * factor * factor * tok_rows, bytes_accessed=16 * factor * tok_rows, transcendentals=0
        ),
        name="precondition",
    )(*terms, act_t, grad_t)


def score_kernel(size, n_pieces, moved, *refs):
    queries, (scores, ordered, result, sems) = refs[:n_pieces], refs[n_pieces:]
    factor = moved.shape[0] // 2
    owners = owners_of(lax.axis_index("dp"), size)
    group = 4
    copies = []
    for part, begin in enumerate(range(0, moved.shape[1], TOKENS_AT_ONCE)):
        tokens = slice(begin, begin + TOKENS_AT_ONCE)
        act_side = moved[:factor, tokens]
        total = None
        for first in range(0, factor, group):
            outer = jnp.concatenate(
                [act_side * moved[factor + i : factor + i + 1, tokens] for i in range(first, first + group)], axis=0
            )
            high = outer.astype(jnp.bfloat16)
            low = (outer - high.astype(jnp.float32)).astype(jnp.bfloat16)
            columns = slice(first * factor, (first + group) * factor)
            values = jnp.concatenate([piece[:, columns] for piece in queries], axis=0)
            term = jnp.dot(
                jnp.concatenate([values, values], axis=1),
                jnp.concatenate([high, low], axis=0),
                preferred_element_type=jnp.float32,
            )
            total = term if total is None else total + term
        rows = total.shape[0] // size
        for at, owner in enumerate(owners):
            place = pl.ds(pl.multiple_of(owner * rows, rows), rows)
            ordered[part, place, :] = total[at * rows : (at + 1) * rows, :]
        result[tokens, :] = ordered[part].T
        copies.append(
            pltpu.make_async_copy(
                result.at[pl.ds(begin, TOKENS_AT_ONCE), :], scores.at[pl.ds(begin, TOKENS_AT_ONCE), :], sems.at[part]
            )
        )
        copies[-1].start()
    for copy in copies:
        copy.wait()


def score(size, moved, queries):
    tok_rows = moved.shape[1]
    n_queries = sum(piece.shape[0] for piece in queries)
    n_pieces = len(queries)
    n_parts = tok_rows // TOKENS_AT_ONCE
    return pl.pallas_call(
        functools.partial(score_kernel, size, n_pieces),
        out_shape=jax.ShapeDtypeStruct((tok_rows, n_queries), jnp.float32),
        in_specs=[pl.BlockSpec(memory_space=pltpu.VMEM)] * (1 + n_pieces),
        out_specs=pl.BlockSpec(memory_space=pl.ANY),
        scratch_shapes=[
            pltpu.VMEM((n_parts, n_queries, TOKENS_AT_ONCE), jnp.float32),
            pltpu.VMEM((tok_rows, n_queries), jnp.float32),
            pltpu.SemaphoreType.DMA((n_parts,)),
        ],
        compiler_params=pltpu.CompilerParams(vmem_limit_bytes=32 * 2**20),
        name="score",
    )(moved, *queries)


def gather_stages(size):
    core = 2 if size % 2 == 0 else 1
    rest = size // core
    near = max(d for d in range(1, rest + 1) if rest % d == 0 and d * d <= rest)
    return [(core * near, rest // near), (core, near), (1, core)]


def sum_rounds(size):
    (stride, radix), *_ = gather_stages(size)
    return [(1, stride), (stride, radix)]


def after(value, other):
    return lax.optimization_barrier((value, other))[0]


def partner(digit, radix, shift):
    return digit ^ shift if radix & (radix - 1) == 0 else (digit + shift) % radix


def shifts_of(radix):
    return ORDER if radix == 4 else range(1, radix)


def swapped(value, size, stride, radix, shift):
    perm = []
    for at in range(size):
        digit = at // stride % radix
        perm.append((at, at + (partner(digit, radix, shift) - digit) * stride))
    return lax.ppermute(value, "dp", perm)


def owners_of(me, size):
    owners = [me]
    for stride, radix in gather_stages(size):
        digit = lax.rem(lax.div(me, stride), radix)
        back = [shift if radix & (radix - 1) == 0 else radix - shift for shift in (0, *shifts_of(radix))]
        steps = [(partner(digit, radix, shift) - digit) * stride for shift in back]
        owners = [owner + step for step in steps for owner in owners]
    return owners


def exchanged(held, size, stride, radix):
    mine = held[0] if len(held) == 1 else jnp.concatenate(held, axis=0)
    return [mine] + [swapped(mine, size, stride, radix, shift) for shift in shifts_of(radix)]


def on_device(acts, grads, proj_act, proj_grad, queries):
    size = lax.axis_size("dp")
    tok_total = acts.shape[0] * size
    far, near, core = gather_stages(size)
    first, second = sum_rounds(size)

    pieces = exchanged([queries], size, *far)
    act_t, grad_t, own = project(acts, grads, proj_act, proj_grad)
    *pieces, own = lax.optimization_barrier((*pieces, own))
    pieces = exchanged(pieces, size, *near)
    own = functools.reduce(jnp.add, exchanged([own], size, *first))
    terms = exchanged([own], size, *second)
    *both, = lax.optimization_barrier((*pieces, *terms))
    pieces, terms = both[: len(pieces)], both[len(pieces) :]
    pieces = exchanged(pieces, size, *core)
    moved = precondition(tok_total, terms, act_t, grad_t)
    return score(size, moved, pieces)


def solution(mesh):
    in_specs = (P(("parts", "dp"), None), P(("parts", "dp"), None), P(), P(), P("dp", None))
    out_specs = P(("parts", "dp"), None)
    return jax.shard_map(
        on_device, mesh=mesh, in_specs=in_specs, out_specs=out_specs, check_vma=False
    )
```

```python
import functools

import jax
import jax.numpy as jnp
from jax import lax
from jax.experimental import pallas as pl
from jax.experimental.pallas import tpu as pltpu
from jax.sharding import PartitionSpec as P

DAMP = 0.1
HIGHEST = lax.Precision.HIGHEST
COPY_ROWS = 128
IN_FLIGHT = 4
TOKENS_AT_ONCE = 256


def project_kernel(
    acts, grads, weight_act, weight_grad, act_t, grad_t, cov, tok_buf, weight_buf, weight_t, tok_sems, weight_sems
):
    width = weight_act.shape[1]
    n_parts = acts.shape[0] // COPY_ROWS
    weight_copies = [
        pltpu.make_async_copy(src, weight_buf.at[at], weight_sems.at[at])
        for at, src in enumerate((weight_act, weight_grad))
    ]
    tok_copies = [
        [
            pltpu.make_async_copy(
                src.at[pl.ds(part * COPY_ROWS, COPY_ROWS), :],
                tok_buf.at[at, pl.ds(part * COPY_ROWS, COPY_ROWS), :],
                tok_sems.at[at, part],
            )
            for part in range(n_parts)
        ]
        for at, src in enumerate((acts, grads))
    ]
    queue = [weight_copies[0], *tok_copies[0], *tok_copies[1]]
    queue.insert(3, weight_copies[1])

    def start_next(many):
        for copy in queue[:many]:
            copy.start()
        del queue[:many]

    def turned(at):
        for first in range(0, width, 512):
            block = weight_buf[at, :, first : first + 512].astype(jnp.float32)
            weight_t[at, first : first + 512, :] = block.T.astype(weight_t.dtype)

    steps = [(at, part, min(2, n_parts - part)) for at in range(2) for part in range(0, n_parts, 2)]
    last_act = len(steps) // 2 - 1
    at, part, many = steps.pop()
    steps += [(at, part + one, 1) for one in range(many)]
    blocks = [[], []]
    grams = [[], []]

    def add_gram(at):
        flipped, plain = [jnp.concatenate(parts, axis=axis) for parts, axis in zip(zip(*blocks[at]), (1, 0))]
        grams[at].append(jnp.dot(flipped, plain, precision=HIGHEST, preferred_element_type=jnp.float32))
        blocks[at].clear()

    start_next(1 + IN_FLIGHT)
    weight_copies[0].wait()
    turned(0)
    for step, (at, part, many) in enumerate(steps):
        for copy in tok_copies[at][part : part + many]:
            copy.wait()
            start_next(1)
        if step == last_act:
            weight_copies[1].wait()
            start_next(1)
        rows = slice(part * COPY_ROWS, (part + many) * COPY_ROWS)
        block = jnp.dot(tok_buf[at, rows, :], weight_t[at], preferred_element_type=jnp.float32)
        if step == last_act:
            turned(1)
        if step == last_act + 1:
            add_gram(0)
        if step == len(steps) - 1:
            add_gram(1)
        flipped = block.T
        (act_t, grad_t)[at][:, rows] = flipped
        blocks[at].append((flipped, block))
    add_gram(1)
    cov[...] = jnp.concatenate([functools.reduce(jnp.add, terms) for terms in grams], axis=1)


def project(acts, grads, proj_act, proj_grad):
    tok_rows, width = acts.shape
    factor = proj_act.shape[1]
    operands = [
        pltpu.with_memory_space_constraint(value, pltpu.HBM) for value in (acts, grads, proj_act.T, proj_grad.T)
    ]
    return pl.pallas_call(
        project_kernel,
        out_shape=(
            jax.ShapeDtypeStruct((factor, tok_rows), jnp.float32),
            jax.ShapeDtypeStruct((factor, tok_rows), jnp.float32),
            jax.ShapeDtypeStruct((factor, 2 * factor), jnp.float32),
        ),
        in_specs=[pl.BlockSpec(memory_space=pltpu.HBM)] * 4,
        out_specs=[pl.BlockSpec(memory_space=pltpu.VMEM)] * 3,
        scratch_shapes=[
            pltpu.VMEM((2, tok_rows, width), acts.dtype),
            pltpu.VMEM((2, factor, width), proj_act.dtype),
            pltpu.VMEM((2, width, factor), proj_act.dtype),
            pltpu.SemaphoreType.DMA((2, tok_rows // COPY_ROWS)),
            pltpu.SemaphoreType.DMA((2,)),
        ],
        compiler_params=pltpu.CompilerParams(vmem_limit_bytes=24 * 2**20),
        cost_estimate=pl.CostEstimate(
            flops=4 * tok_rows * width * factor, bytes_accessed=4 * tok_rows * width, transcendentals=0
        ),
        name="project",
    )(*operands)


def inverse_pair(both):
    factor = both.shape[0]
    tile = (8, both.shape[1])
    lane = lax.broadcasted_iota(jnp.int32, tile, 1)
    row_at = lax.broadcasted_iota(jnp.int32, tile, 0)
    left_half = lane < factor
    inner = jnp.where(left_half, lane, lane - factor)
    parts = [both[at : at + 8, :] for at in range(0, factor, 8)]

    def column(part, at):
        left = jnp.broadcast_to(part[:, at : at + 1], tile)
        right = jnp.broadcast_to(part[:, factor + at : factor + at + 1], tile)
        return jnp.where(left_half, left, right)

    def row(part, at):
        return jnp.broadcast_to(part[at : at + 1, :], tile)

    for k in range(0, factor, 4):
        home, off = divmod(k, 8)
        columns = [[column(part, k + a) for part in parts] for a in range(4)]
        pivot = [[row(columns[b][home], off + a) if a <= b else None for b in range(4)] for a in range(4)]
        p00, p01, p02, p03 = pivot[0]
        _, p11, p12, p13 = pivot[1]
        _, _, p22, p23 = pivot[2]
        p33 = pivot[3][3]
        on_block = (inner >= k) & (inner < k + 4)
        r0, r1, r2, r3 = [
            jnp.where(on_block, jnp.where(inner == k + a, 1.0, 0.0), row(parts[home], off + a)) for a in range(4)
        ]
        scale = 1.0 / (p00 * p11 - p01 * p01)
        e02 = scale * (p11 * p02 - p01 * p12)
        e03 = scale * (p11 * p03 - p01 * p13)
        e12 = scale * (p00 * p12 - p01 * p02)
        e13 = scale * (p00 * p13 - p01 * p03)
        s22 = p22 - (p02 * e02 + p12 * e12)
        s23 = p23 - (p02 * e03 + p12 * e13)
        s33 = p33 - (p03 * e03 + p13 * e13)
        scale_s = 1.0 / (s22 * s33 - s23 * s23)
        y0 = scale * (p11 * r0 - p01 * r1)
        y1 = scale * (p00 * r1 - p01 * r0)
        t2 = r2 - (p02 * y0 + p12 * y1)
        t3 = r3 - (p03 * y0 + p13 * y1)
        w2 = scale_s * (s33 * t2 - s23 * t3)
        w3 = scale_s * (s22 * t3 - s23 * t2)
        w0 = y0 - (e02 * w2 + e03 * w3)
        w1 = y1 - (e12 * w2 + e13 * w3)
        solved = (w0, w1, w2, w3)
        for m, part in enumerate(parts):
            change = (columns[0][m] * w0 + columns[1][m] * w1) + (columns[2][m] * w2 + columns[3][m] * w3)
            part = jnp.where(on_block, 0.0, part) - change
            if m == home:
                for a in range(4):
                    part = jnp.where(row_at == off + a, solved[a], part)
            parts[m] = part
    return jnp.concatenate(parts, axis=0)


def precondition_kernel(tok_total, n_terms, *refs):
    terms, (act_t, grad_t, moved) = refs[:n_terms], refs[n_terms:]
    both = terms[0][...]
    for term in terms[1:]:
        both = both + term[...]
    factor = both.shape[0]
    lane = lax.broadcasted_iota(jnp.int32, both.shape, 1)
    row_at = lax.broadcasted_iota(jnp.int32, both.shape, 0)
    left_half = lane < factor
    inner = jnp.where(left_half, lane, lane - factor)
    both = both / tok_total + jnp.where(inner == row_at, DAMP, 0.0)
    both = inverse_pair(both)
    blocks = jnp.concatenate(
        [jnp.where(left_half, both, 0.0), jnp.where(left_half, 0.0, both)], axis=0
    )
    proj_t = jnp.concatenate([act_t[...], grad_t[...]], axis=0)
    moved[...] = jnp.dot(blocks, proj_t, precision=HIGHEST, preferred_element_type=jnp.float32)


def precondition(tok_total, terms, act_t, grad_t):
    factor, tok_rows = act_t.shape
    n_terms = len(terms)
    return pl.pallas_call(
        functools.partial(precondition_kernel, tok_total, n_terms),
        out_shape=jax.ShapeDtypeStruct((2 * factor, tok_rows), jnp.float32),
        in_specs=[pl.BlockSpec(memory_space=pltpu.VMEM)] * (n_terms + 2),
        out_specs=pl.BlockSpec(memory_space=pltpu.VMEM),
        compiler_params=pltpu.CompilerParams(vmem_limit_bytes=24 * 2**20),
        cost_estimate=pl.CostEstimate(
            flops=1600 * factor * factor * tok_rows, bytes_accessed=16 * factor * tok_rows, transcendentals=0
        ),
        name="precondition",
    )(*terms, act_t, grad_t)


def score_kernel(size, n_pieces, moved, *refs):
    queries, (scores, ordered, result, sems) = refs[:n_pieces], refs[n_pieces:]
    factor = moved.shape[0] // 2
    owners = owners_of(lax.axis_index("dp"), size)
    group = 4
    copies = []
    for part, begin in enumerate(range(0, moved.shape[1], TOKENS_AT_ONCE)):
        tokens = slice(begin, begin + TOKENS_AT_ONCE)
        act_side = moved[:factor, tokens]
        total = None
        for first in range(0, factor, group):
            outer = jnp.concatenate(
                [act_side * moved[factor + i : factor + i + 1, tokens] for i in range(first, first + group)], axis=0
            )
            high = outer.astype(jnp.bfloat16)
            low = (outer - high.astype(jnp.float32)).astype(jnp.bfloat16)
            columns = slice(first * factor, (first + group) * factor)
            values = jnp.concatenate([piece[:, columns] for piece in queries], axis=0)
            term = jnp.dot(
                jnp.concatenate([values, values], axis=1),
                jnp.concatenate([high, low], axis=0),
                preferred_element_type=jnp.float32,
            )
            total = term if total is None else total + term
        rows = total.shape[0] // size
        for at, owner in enumerate(owners):
            place = pl.ds(pl.multiple_of(owner * rows, rows), rows)
            ordered[part, place, :] = total[at * rows : (at + 1) * rows, :]
        result[tokens, :] = ordered[part].T
        copies.append(
            pltpu.make_async_copy(
                result.at[pl.ds(begin, TOKENS_AT_ONCE), :], scores.at[pl.ds(begin, TOKENS_AT_ONCE), :], sems.at[part]
            )
        )
        copies[-1].start()
    for copy in copies:
        copy.wait()


def score(size, moved, queries):
    tok_rows = moved.shape[1]
    n_queries = sum(piece.shape[0] for piece in queries)
    n_pieces = len(queries)
    n_parts = tok_rows // TOKENS_AT_ONCE
    return pl.pallas_call(
        functools.partial(score_kernel, size, n_pieces),
        out_shape=jax.ShapeDtypeStruct((tok_rows, n_queries), jnp.float32),
        in_specs=[pl.BlockSpec(memory_space=pltpu.VMEM)] * (1 + n_pieces),
        out_specs=pl.BlockSpec(memory_space=pl.ANY),
        scratch_shapes=[
            pltpu.VMEM((n_parts, n_queries, TOKENS_AT_ONCE), jnp.float32),
            pltpu.VMEM((tok_rows, n_queries), jnp.float32),
            pltpu.SemaphoreType.DMA((n_parts,)),
        ],
        compiler_params=pltpu.CompilerParams(vmem_limit_bytes=32 * 2**20),
        name="score",
    )(moved, *queries)


def gather_stages(size):
    core = 2 if size % 2 == 0 else 1
    rest = size // core
    near = max(d for d in range(1, rest + 1) if rest % d == 0 and d * d <= rest)
    return [(core * near, rest // near), (core, near), (1, core)]


def sum_rounds(size):
    (stride, radix), *_ = gather_stages(size)
    return [(1, stride), (stride, radix)]


def after(value, other):
    return lax.optimization_barrier((value, other))[0]


def partner(digit, radix, shift):
    return digit ^ shift if radix & (radix - 1) == 0 else (digit + shift) % radix


def swapped(value, size, stride, radix, shift):
    perm = []
    for at in range(size):
        digit = at // stride % radix
        perm.append((at, at + (partner(digit, radix, shift) - digit) * stride))
    return lax.ppermute(value, "dp", perm)


def owners_of(me, size):
    owners = [me]
    for at, (stride, radix) in enumerate(gather_stages(size)):
        digit = lax.rem(lax.div(me, stride), radix)
        shifts = [0, *(range(radix - 1, 0, -1) if at == 0 else range(1, radix))]
        back = [shift if radix & (radix - 1) == 0 else (radix - shift) % radix for shift in shifts]
        steps = [(partner(digit, radix, shift) - digit) * stride for shift in back]
        owners = [owner + step for step in steps for owner in owners]
    return owners


def exchanged(held, size, stride, radix, backwards=False):
    mine = held[0] if len(held) == 1 else jnp.concatenate(held, axis=0)
    shifts = range(radix - 1, 0, -1) if backwards else range(1, radix)
    return [mine] + [swapped(mine, size, stride, radix, shift) for shift in shifts]


def on_device(acts, grads, proj_act, proj_grad, queries):
    size = lax.axis_size("dp")
    tok_total = acts.shape[0] * size
    far, near, core = gather_stages(size)
    first, second = sum_rounds(size)

    pieces = exchanged([queries], size, *far, backwards=True)
    act_t, grad_t, own = project(acts, grads, proj_act, proj_grad)
    *pieces, own = lax.optimization_barrier((*pieces, own))
    pieces = exchanged(pieces, size, *near)
    own = functools.reduce(jnp.add, exchanged([own], size, *first))
    terms = exchanged([own], size, *second)
    *both, = lax.optimization_barrier((*pieces, *terms))
    pieces, terms = both[: len(pieces)], both[len(pieces) :]
    pieces = exchanged(pieces, size, *core)
    moved = precondition(tok_total, terms, act_t, grad_t)
    return score(size, moved, pieces)


def solution(mesh):
    in_specs = (P(("parts", "dp"), None), P(("parts", "dp"), None), P(), P(), P("dp", None))
    out_specs = P(("parts", "dp"), None)
    return jax.shard_map(
        on_device, mesh=mesh, in_specs=in_specs, out_specs=out_specs, check_vma=False
    )
```

```python
import functools

import jax
import jax.numpy as jnp
from jax import lax
from jax.experimental import pallas as pl
from jax.experimental.pallas import tpu as pltpu
from jax.sharding import PartitionSpec as P

DAMP = 0.1
HIGHEST = lax.Precision.HIGHEST
COPY_ROWS = 128
IN_FLIGHT = 4
TOKENS_AT_ONCE = 256


def project_kernel(
    acts, grads, weight_act, weight_grad, act_t, grad_t, cov, tok_buf, weight_buf, weight_t, tok_sems, weight_sems
):
    width = weight_act.shape[1]
    n_parts = acts.shape[0] // COPY_ROWS
    weight_copies = [
        pltpu.make_async_copy(src, weight_buf.at[at], weight_sems.at[at])
        for at, src in enumerate((weight_act, weight_grad))
    ]
    tok_copies = [
        [
            pltpu.make_async_copy(
                src.at[pl.ds(part * COPY_ROWS, COPY_ROWS), :],
                tok_buf.at[at, pl.ds(part * COPY_ROWS, COPY_ROWS), :],
                tok_sems.at[at, part],
            )
            for part in range(n_parts)
        ]
        for at, src in enumerate((acts, grads))
    ]
    queue = [weight_copies[0], *tok_copies[0], *tok_copies[1]]
    queue.insert(3, weight_copies[1])

    def start_next(many):
        for copy in queue[:many]:
            copy.start()
        del queue[:many]

    def turned(at):
        for first in range(0, width, 512):
            block = weight_buf[at, :, first : first + 512].astype(jnp.float32)
            weight_t[at, first : first + 512, :] = block.T.astype(weight_t.dtype)

    steps = [(at, part, min(2, n_parts - part)) for at in range(2) for part in range(0, n_parts, 2)]
    last_act = len(steps) // 2 - 1
    at, part, many = steps.pop()
    steps += [(at, part + one, 1) for one in range(many)]
    blocks = [[], []]
    grams = [[], []]

    def add_gram(at):
        flipped, plain = [jnp.concatenate(parts, axis=axis) for parts, axis in zip(zip(*blocks[at]), (1, 0))]
        grams[at].append(jnp.dot(flipped, plain, precision=HIGHEST, preferred_element_type=jnp.float32))
        blocks[at].clear()

    start_next(1 + IN_FLIGHT)
    weight_copies[0].wait()
    turned(0)
    for step, (at, part, many) in enumerate(steps):
        for copy in tok_copies[at][part : part + many]:
            copy.wait()
            start_next(1)
        if step == last_act:
            weight_copies[1].wait()
            start_next(1)
        rows = slice(part * COPY_ROWS, (part + many) * COPY_ROWS)
        quarters = [slice(begin, begin + width // 4) for begin in range(0, width, width // 4)]
        terms = [
            jnp.dot(tok_buf[at, rows, some], weight_t[at, some, :], preferred_element_type=jnp.float32)
            for some in quarters
        ]
        block = (terms[0] + terms[1]) + (terms[2] + terms[3])
        if step == last_act:
            turned(1)
        if step == last_act + 1:
            add_gram(0)
        if step == len(steps) - 1:
            add_gram(1)
        flipped = block.T
        (act_t, grad_t)[at][:, rows] = flipped
        blocks[at].append((flipped, block))
    add_gram(1)
    cov[...] = jnp.concatenate([functools.reduce(jnp.add, terms) for terms in grams], axis=1)


def project(acts, grads, proj_act, proj_grad):
    tok_rows, width = acts.shape
    factor = proj_act.shape[1]
    operands = [
        pltpu.with_memory_space_constraint(value, pltpu.HBM) for value in (acts, grads, proj_act.T, proj_grad.T)
    ]
    return pl.pallas_call(
        project_kernel,
        out_shape=(
            jax.ShapeDtypeStruct((factor, tok_rows), jnp.float32),
            jax.ShapeDtypeStruct((factor, tok_rows), jnp.float32),
            jax.ShapeDtypeStruct((factor, 2 * factor), jnp.float32),
        ),
        in_specs=[pl.BlockSpec(memory_space=pltpu.HBM)] * 4,
        out_specs=[pl.BlockSpec(memory_space=pltpu.VMEM)] * 3,
        scratch_shapes=[
            pltpu.VMEM((2, tok_rows, width), acts.dtype),
            pltpu.VMEM((2, factor, width), proj_act.dtype),
            pltpu.VMEM((2, width, factor), proj_act.dtype),
            pltpu.SemaphoreType.DMA((2, tok_rows // COPY_ROWS)),
            pltpu.SemaphoreType.DMA((2,)),
        ],
        compiler_params=pltpu.CompilerParams(vmem_limit_bytes=24 * 2**20),
        cost_estimate=pl.CostEstimate(
            flops=4 * tok_rows * width * factor, bytes_accessed=4 * tok_rows * width, transcendentals=0
        ),
        name="project",
    )(*operands)


def inverse_of(value):
    guess = pl.reciprocal(value, approx=True)
    guess = guess * (2.0 - value * guess)
    return guess * (2.0 - value * guess)


def inverse_pair(both):
    factor = both.shape[0]
    tile = (8, both.shape[1])
    lane = lax.broadcasted_iota(jnp.int32, tile, 1)
    row_at = lax.broadcasted_iota(jnp.int32, tile, 0)
    left_half = lane < factor
    inner = jnp.where(left_half, lane, lane - factor)
    parts = [both[at : at + 8, :] for at in range(0, factor, 8)]

    def column(part, at):
        left = jnp.broadcast_to(part[:, at : at + 1], tile)
        right = jnp.broadcast_to(part[:, factor + at : factor + at + 1], tile)
        return jnp.where(left_half, left, right)

    def row(part, at):
        return jnp.broadcast_to(part[at : at + 1, :], tile)

    for k in range(0, factor, 4):
        home, off = divmod(k, 8)
        columns = [[column(part, k + a) for part in parts] for a in range(4)]
        pivot = [[row(columns[b][home], off + a) if a <= b else None for b in range(4)] for a in range(4)]
        p00, p01, p02, p03 = pivot[0]
        _, p11, p12, p13 = pivot[1]
        _, _, p22, p23 = pivot[2]
        p33 = pivot[3][3]
        on_block = (inner >= k) & (inner < k + 4)
        r0, r1, r2, r3 = [
            jnp.where(on_block, jnp.where(inner == k + a, 1.0, 0.0), row(parts[home], off + a)) for a in range(4)
        ]
        scale = inverse_of(p00 * p11 - p01 * p01)
        m02 = p11 * p02 - p01 * p12
        m03 = p11 * p03 - p01 * p13
        m12 = p00 * p12 - p01 * p02
        m13 = p00 * p13 - p01 * p03
        z0 = p11 * r0 - p01 * r1
        z1 = p00 * r1 - p01 * r0
        s22 = p22 - scale * (p02 * m02 + p12 * m12)
        s23 = p23 - scale * (p02 * m03 + p12 * m13)
        s33 = p33 - scale * (p03 * m03 + p13 * m13)
        t2 = r2 - scale * (p02 * z0 + p12 * z1)
        t3 = r3 - scale * (p03 * z0 + p13 * z1)
        scale_s = inverse_of(s22 * s33 - s23 * s23)
        u2 = s33 * t2 - s23 * t3
        u3 = s22 * t3 - s23 * t2
        w2 = scale_s * u2
        w3 = scale_s * u3
        w0 = scale * z0 - scale_s * (scale * m02 * u2 + scale * m03 * u3)
        w1 = scale * z1 - scale_s * (scale * m12 * u2 + scale * m13 * u3)
        solved = (w0, w1, w2, w3)
        for m, part in enumerate(parts):
            change = (columns[0][m] * w0 + columns[1][m] * w1) + (columns[2][m] * w2 + columns[3][m] * w3)
            part = jnp.where(on_block, 0.0, part) - change
            if m == home:
                for a in range(4):
                    part = jnp.where(row_at == off + a, solved[a], part)
            parts[m] = part
    return jnp.concatenate(parts, axis=0)


def precondition_kernel(tok_total, n_terms, *refs):
    terms, (act_t, grad_t, moved) = refs[:n_terms], refs[n_terms:]
    both = terms[0][...]
    for term in terms[1:]:
        both = both + term[...]
    factor = both.shape[0]
    lane = lax.broadcasted_iota(jnp.int32, both.shape, 1)
    row_at = lax.broadcasted_iota(jnp.int32, both.shape, 0)
    left_half = lane < factor
    inner = jnp.where(left_half, lane, lane - factor)
    both = both / tok_total + jnp.where(inner == row_at, DAMP, 0.0)
    both = inverse_pair(both)
    blocks = jnp.concatenate(
        [jnp.where(left_half, both, 0.0), jnp.where(left_half, 0.0, both)], axis=0
    )
    proj_t = jnp.concatenate([act_t[...], grad_t[...]], axis=0)
    moved[...] = jnp.dot(blocks, proj_t, precision=HIGHEST, preferred_element_type=jnp.float32)


def precondition(tok_total, terms, act_t, grad_t):
    factor, tok_rows = act_t.shape
    n_terms = len(terms)
    return pl.pallas_call(
        functools.partial(precondition_kernel, tok_total, n_terms),
        out_shape=jax.ShapeDtypeStruct((2 * factor, tok_rows), jnp.float32),
        in_specs=[pl.BlockSpec(memory_space=pltpu.VMEM)] * (n_terms + 2),
        out_specs=pl.BlockSpec(memory_space=pltpu.VMEM),
        compiler_params=pltpu.CompilerParams(vmem_limit_bytes=24 * 2**20),
        cost_estimate=pl.CostEstimate(
            flops=1600 * factor * factor * tok_rows, bytes_accessed=16 * factor * tok_rows, transcendentals=0
        ),
        name="precondition",
    )(*terms, act_t, grad_t)


def score_kernel(size, n_pieces, moved, *refs):
    queries, (scores, ordered, result, sems) = refs[:n_pieces], refs[n_pieces:]
    factor = moved.shape[0] // 2
    owners = owners_of(lax.axis_index("dp"), size)
    group = 4
    copies = []
    for part, begin in enumerate(range(0, moved.shape[1], TOKENS_AT_ONCE)):
        tokens = slice(begin, begin + TOKENS_AT_ONCE)
        act_side = moved[:factor, tokens]
        total = None
        for first in range(0, factor, group):
            outer = jnp.concatenate(
                [act_side * moved[factor + i : factor + i + 1, tokens] for i in range(first, first + group)], axis=0
            )
            high = outer.astype(jnp.bfloat16)
            low = (outer - high.astype(jnp.float32)).astype(jnp.bfloat16)
            columns = slice(first * factor, (first + group) * factor)
            values = jnp.concatenate([piece[:, columns] for piece in queries], axis=0)
            term = jnp.dot(
                jnp.concatenate([values, values], axis=1),
                jnp.concatenate([high, low], axis=0),
                preferred_element_type=jnp.float32,
            )
            total = term if total is None else total + term
        rows = total.shape[0] // size
        for at, owner in enumerate(owners):
            place = pl.ds(pl.multiple_of(owner * rows, rows), rows)
            ordered[part, place, :] = total[at * rows : (at + 1) * rows, :]
        result[tokens, :] = ordered[part].T
        copies.append(
            pltpu.make_async_copy(
                result.at[pl.ds(begin, TOKENS_AT_ONCE), :], scores.at[pl.ds(begin, TOKENS_AT_ONCE), :], sems.at[part]
            )
        )
        copies[-1].start()
    for copy in copies:
        copy.wait()


def score(size, moved, queries):
    tok_rows = moved.shape[1]
    n_queries = sum(piece.shape[0] for piece in queries)
    n_pieces = len(queries)
    n_parts = tok_rows // TOKENS_AT_ONCE
    return pl.pallas_call(
        functools.partial(score_kernel, size, n_pieces),
        out_shape=jax.ShapeDtypeStruct((tok_rows, n_queries), jnp.float32),
        in_specs=[pl.BlockSpec(memory_space=pltpu.VMEM)] * (1 + n_pieces),
        out_specs=pl.BlockSpec(memory_space=pl.ANY),
        scratch_shapes=[
            pltpu.VMEM((n_parts, n_queries, TOKENS_AT_ONCE), jnp.float32),
            pltpu.VMEM((tok_rows, n_queries), jnp.float32),
            pltpu.SemaphoreType.DMA((n_parts,)),
        ],
        compiler_params=pltpu.CompilerParams(vmem_limit_bytes=32 * 2**20),
        name="score",
    )(moved, *queries)


def gather_stages(size):
    core = 2 if size % 2 == 0 else 1
    rest = size // core
    near = max(d for d in range(1, rest + 1) if rest % d == 0 and d * d <= rest)
    return [(core * near, rest // near), (core, near), (1, core)]


def sum_rounds(size):
    (stride, radix), *_ = gather_stages(size)
    return [(1, stride), (stride, radix)]


def after(value, other):
    return lax.optimization_barrier((value, other))[0]


def partner(digit, radix, shift):
    return digit ^ shift if radix & (radix - 1) == 0 else (digit + shift) % radix


def swapped(value, size, stride, radix, shift):
    perm = []
    for at in range(size):
        digit = at // stride % radix
        perm.append((at, at + (partner(digit, radix, shift) - digit) * stride))
    return lax.ppermute(value, "dp", perm)


def owners_of(me, size):
    owners = [me]
    for at, (stride, radix) in enumerate(gather_stages(size)):
        digit = lax.rem(lax.div(me, stride), radix)
        shifts = [0, *(range(radix - 1, 0, -1) if at == 0 else range(1, radix))]
        back = [shift if radix & (radix - 1) == 0 else (radix - shift) % radix for shift in shifts]
        steps = [(partner(digit, radix, shift) - digit) * stride for shift in back]
        owners = [owner + step for step in steps for owner in owners]
    return owners


def exchanged(held, size, stride, radix, backwards=False):
    mine = held[0] if len(held) == 1 else jnp.concatenate(held, axis=0)
    shifts = range(radix - 1, 0, -1) if backwards else range(1, radix)
    return [mine] + [swapped(mine, size, stride, radix, shift) for shift in shifts]


def on_device(acts, grads, proj_act, proj_grad, queries):
    size = lax.axis_size("dp")
    tok_total = acts.shape[0] * size
    far, near, core = gather_stages(size)
    first, second = sum_rounds(size)

    pieces = exchanged([queries], size, *far, backwards=True)
    act_t, grad_t, own = project(acts, grads, proj_act, proj_grad)
    *pieces, own = lax.optimization_barrier((*pieces, own))
    pieces = exchanged(pieces, size, *near)
    own = functools.reduce(jnp.add, exchanged([own], size, *first))
    terms = exchanged([own], size, *second)
    *both, = lax.optimization_barrier((*pieces, *terms))
    pieces, terms = both[: len(pieces)], both[len(pieces) :]
    pieces = exchanged(pieces, size, *core)
    moved = precondition(tok_total, terms, act_t, grad_t)
    return score(size, moved, pieces)


def solution(mesh):
    in_specs = (P(("parts", "dp"), None), P(("parts", "dp"), None), P(), P(), P("dp", None))
    out_specs = P(("parts", "dp"), None)
    return jax.shard_map(
        on_device, mesh=mesh, in_specs=in_specs, out_specs=out_specs, check_vma=False
    )
```

```python
import functools

import jax
import jax.numpy as jnp
from jax import lax
from jax.experimental import pallas as pl
from jax.experimental.pallas import tpu as pltpu
from jax.sharding import PartitionSpec as P

DAMP = 0.1
HIGHEST = lax.Precision.HIGHEST
COPY_ROWS = 128
IN_FLIGHT = 5
TOKENS_AT_ONCE = 256


def project_kernel(
    acts, grads, weight_act, weight_grad, act_t, grad_t, cov, tok_buf, weight_buf, weight_t, tok_sems, weight_sems
):
    width = weight_act.shape[1]
    n_parts = acts.shape[0] // COPY_ROWS
    weight_copies = [
        pltpu.make_async_copy(src, weight_buf.at[at], weight_sems.at[at])
        for at, src in enumerate((weight_act, weight_grad))
    ]
    tok_copies = [
        [
            pltpu.make_async_copy(
                src.at[pl.ds(part * COPY_ROWS, COPY_ROWS), :],
                tok_buf.at[at, pl.ds(part * COPY_ROWS, COPY_ROWS), :],
                tok_sems.at[at, part],
            )
            for part in range(n_parts)
        ]
        for at, src in enumerate((acts, grads))
    ]
    queue = [weight_copies[0], *tok_copies[0], *tok_copies[1]]
    queue.insert(3, weight_copies[1])

    def start_next(many):
        for copy in queue[:many]:
            copy.start()
        del queue[:many]

    def turned(at):
        for first in range(0, width, 512):
            block = weight_buf[at, :, first : first + 512].astype(jnp.float32)
            weight_t[at, first : first + 512, :] = block.T.astype(weight_t.dtype)

    steps = [(at, part, min(2, n_parts - part)) for at in range(2) for part in range(0, n_parts, 2)]
    last_act = len(steps) // 2 - 1
    at, part, many = steps.pop()
    steps += [(at, part + one, 1) for one in range(many)]
    blocks = [[], []]
    grams = [[], []]

    def add_gram(at):
        flipped, plain = [jnp.concatenate(parts, axis=axis) for parts, axis in zip(zip(*blocks[at]), (1, 0))]
        grams[at].append(jnp.dot(flipped, plain, precision=HIGHEST, preferred_element_type=jnp.float32))
        blocks[at].clear()

    start_next(1 + IN_FLIGHT)
    weight_copies[0].wait()
    turned(0)
    for step, (at, part, many) in enumerate(steps):
        for copy in tok_copies[at][part : part + many]:
            copy.wait()
            start_next(1)
        if step == last_act:
            weight_copies[1].wait()
            start_next(1)
        rows = slice(part * COPY_ROWS, (part + many) * COPY_ROWS)
        block = jnp.dot(tok_buf[at, rows, :], weight_t[at], preferred_element_type=jnp.float32)
        if step == last_act:
            turned(1)
        if step == last_act + 1:
            add_gram(0)
        if step == len(steps) - 1:
            add_gram(1)
        flipped = block.T
        (act_t, grad_t)[at][:, rows] = flipped
        blocks[at].append((flipped, block))
    add_gram(1)
    cov[...] = jnp.concatenate([functools.reduce(jnp.add, terms) for terms in grams], axis=1)


def project(acts, grads, proj_act, proj_grad):
    tok_rows, width = acts.shape
    factor = proj_act.shape[1]
    operands = [
        pltpu.with_memory_space_constraint(value, pltpu.HBM) for value in (acts, grads, proj_act.T, proj_grad.T)
    ]
    return pl.pallas_call(
        project_kernel,
        out_shape=(
            jax.ShapeDtypeStruct((factor, tok_rows), jnp.float32),
            jax.ShapeDtypeStruct((factor, tok_rows), jnp.float32),
            jax.ShapeDtypeStruct((factor, 2 * factor), jnp.float32),
        ),
        in_specs=[pl.BlockSpec(memory_space=pltpu.HBM)] * 4,
        out_specs=[pl.BlockSpec(memory_space=pltpu.VMEM)] * 3,
        scratch_shapes=[
            pltpu.VMEM((2, tok_rows, width), acts.dtype),
            pltpu.VMEM((2, factor, width), proj_act.dtype),
            pltpu.VMEM((2, width, factor), proj_act.dtype),
            pltpu.SemaphoreType.DMA((2, tok_rows // COPY_ROWS)),
            pltpu.SemaphoreType.DMA((2,)),
        ],
        compiler_params=pltpu.CompilerParams(vmem_limit_bytes=24 * 2**20),
        cost_estimate=pl.CostEstimate(
            flops=4 * tok_rows * width * factor, bytes_accessed=4 * tok_rows * width, transcendentals=0
        ),
        name="project",
    )(*operands)


def inverse_pair(both):
    factor = both.shape[0]
    tile = (8, both.shape[1])
    lane = lax.broadcasted_iota(jnp.int32, tile, 1)
    row_at = lax.broadcasted_iota(jnp.int32, tile, 0)
    left_half = lane < factor
    inner = jnp.where(left_half, lane, lane - factor)
    parts = [both[at : at + 8, :] for at in range(0, factor, 8)]

    def column(part, at):
        index = jnp.where(left_half, at, factor + at)
        return jnp.take_along_axis(part, index, axis=1, mode="promise_in_bounds")

    def row(part, at):
        return jnp.broadcast_to(part[at : at + 1, :], tile)

    for k in range(0, factor, 4):
        home, off = divmod(k, 8)
        columns = [[column(part, k + a) for part in parts] for a in range(4)]
        pivot = [[row(columns[b][home], off + a) if a <= b else None for b in range(4)] for a in range(4)]
        p00, p01, p02, p03 = pivot[0]
        _, p11, p12, p13 = pivot[1]
        _, _, p22, p23 = pivot[2]
        p33 = pivot[3][3]
        on_block = (inner >= k) & (inner < k + 4)
        r0, r1, r2, r3 = [
            jnp.where(on_block, jnp.where(inner == k + a, 1.0, 0.0), row(parts[home], off + a)) for a in range(4)
        ]
        scale = 1.0 / (p00 * p11 - p01 * p01)
        e02 = scale * (p11 * p02 - p01 * p12)
        e03 = scale * (p11 * p03 - p01 * p13)
        e12 = scale * (p00 * p12 - p01 * p02)
        e13 = scale * (p00 * p13 - p01 * p03)
        s22 = p22 - (p02 * e02 + p12 * e12)
        s23 = p23 - (p02 * e03 + p12 * e13)
        s33 = p33 - (p03 * e03 + p13 * e13)
        scale_s = 1.0 / (s22 * s33 - s23 * s23)
        y0 = scale * (p11 * r0 - p01 * r1)
        y1 = scale * (p00 * r1 - p01 * r0)
        t2 = r2 - (p02 * y0 + p12 * y1)
        t3 = r3 - (p03 * y0 + p13 * y1)
        w2 = scale_s * (s33 * t2 - s23 * t3)
        w3 = scale_s * (s22 * t3 - s23 * t2)
        w0 = y0 - (e02 * w2 + e03 * w3)
        w1 = y1 - (e12 * w2 + e13 * w3)
        solved = (w0, w1, w2, w3)
        for m, part in enumerate(parts):
            change = (columns[0][m] * w0 + columns[1][m] * w1) + (columns[2][m] * w2 + columns[3][m] * w3)
            part = jnp.where(on_block, 0.0, part) - change
            if m == home:
                for a in range(4):
                    part = jnp.where(row_at == off + a, solved[a], part)
            parts[m] = part
    return jnp.concatenate(parts, axis=0)


def precondition_kernel(tok_total, n_terms, *refs):
    terms, (act_t, grad_t, moved) = refs[:n_terms], refs[n_terms:]
    both = terms[0][...]
    for term in terms[1:]:
        both = both + term[...]
    factor = both.shape[0]
    lane = lax.broadcasted_iota(jnp.int32, both.shape, 1)
    row_at = lax.broadcasted_iota(jnp.int32, both.shape, 0)
    left_half = lane < factor
    inner = jnp.where(left_half, lane, lane - factor)
    both = both / tok_total + jnp.where(inner == row_at, DAMP, 0.0)
    both = inverse_pair(both)
    blocks = jnp.concatenate(
        [jnp.where(left_half, both, 0.0), jnp.where(left_half, 0.0, both)], axis=0
    )
    proj_t = jnp.concatenate([act_t[...], grad_t[...]], axis=0)
    moved[...] = jnp.dot(blocks, proj_t, precision=HIGHEST, preferred_element_type=jnp.float32)


def precondition(tok_total, terms, act_t, grad_t):
    factor, tok_rows = act_t.shape
    n_terms = len(terms)
    return pl.pallas_call(
        functools.partial(precondition_kernel, tok_total, n_terms),
        out_shape=jax.ShapeDtypeStruct((2 * factor, tok_rows), jnp.float32),
        in_specs=[pl.BlockSpec(memory_space=pltpu.VMEM)] * (n_terms + 2),
        out_specs=pl.BlockSpec(memory_space=pltpu.VMEM),
        compiler_params=pltpu.CompilerParams(vmem_limit_bytes=24 * 2**20),
        cost_estimate=pl.CostEstimate(
            flops=1600 * factor * factor * tok_rows, bytes_accessed=16 * factor * tok_rows, transcendentals=0
        ),
        name="precondition",
    )(*terms, act_t, grad_t)


def score_kernel(size, n_pieces, moved, *refs):
    queries, (scores, ordered, result, sems) = refs[:n_pieces], refs[n_pieces:]
    factor = moved.shape[0] // 2
    owners = owners_of(lax.axis_index("dp"), size)
    group = 4
    copies = []
    for part, begin in enumerate(range(0, moved.shape[1], TOKENS_AT_ONCE)):
        tokens = slice(begin, begin + TOKENS_AT_ONCE)
        act_side = moved[:factor, tokens]
        total = None
        for first in range(0, factor, group):
            outer = jnp.concatenate(
                [act_side * moved[factor + i : factor + i + 1, tokens] for i in range(first, first + group)], axis=0
            )
            high = outer.astype(jnp.bfloat16)
            low = (outer - high.astype(jnp.float32)).astype(jnp.bfloat16)
            columns = slice(first * factor, (first + group) * factor)
            values = jnp.concatenate([piece[:, columns] for piece in queries], axis=0)
            term = jnp.dot(
                jnp.concatenate([values, values], axis=1),
                jnp.concatenate([high, low], axis=0),
                preferred_element_type=jnp.float32,
            )
            total = term if total is None else total + term
        rows = total.shape[0] // size
        for at, owner in enumerate(owners):
            place = pl.ds(pl.multiple_of(owner * rows, rows), rows)
            ordered[part, place, :] = total[at * rows : (at + 1) * rows, :]
        result[tokens, :] = ordered[part].T
        copies.append(
            pltpu.make_async_copy(
                result.at[pl.ds(begin, TOKENS_AT_ONCE), :], scores.at[pl.ds(begin, TOKENS_AT_ONCE), :], sems.at[part]
            )
        )
        copies[-1].start()
    for copy in copies:
        copy.wait()


def score(size, moved, queries):
    tok_rows = moved.shape[1]
    n_queries = sum(piece.shape[0] for piece in queries)
    n_pieces = len(queries)
    n_parts = tok_rows // TOKENS_AT_ONCE
    return pl.pallas_call(
        functools.partial(score_kernel, size, n_pieces),
        out_shape=jax.ShapeDtypeStruct((tok_rows, n_queries), jnp.float32),
        in_specs=[pl.BlockSpec(memory_space=pltpu.VMEM)] * (1 + n_pieces),
        out_specs=pl.BlockSpec(memory_space=pl.ANY),
        scratch_shapes=[
            pltpu.VMEM((n_parts, n_queries, TOKENS_AT_ONCE), jnp.float32),
            pltpu.VMEM((tok_rows, n_queries), jnp.float32),
            pltpu.SemaphoreType.DMA((n_parts,)),
        ],
        compiler_params=pltpu.CompilerParams(vmem_limit_bytes=32 * 2**20),
        name="score",
    )(moved, *queries)


def gather_stages(size):
    core = 2 if size % 2 == 0 else 1
    rest = size // core
    near = max(d for d in range(1, rest + 1) if rest % d == 0 and d * d <= rest)
    return [(core * near, rest // near), (core, near), (1, core)]


def sum_rounds(size):
    (stride, radix), *_ = gather_stages(size)
    return [(1, stride), (stride, radix)]


def after(value, other):
    return lax.optimization_barrier((value, other))[0]


def partner(digit, radix, shift):
    return digit ^ shift if radix & (radix - 1) == 0 else (digit + shift) % radix


def swapped(value, size, stride, radix, shift):
    perm = []
    for at in range(size):
        digit = at // stride % radix
        perm.append((at, at + (partner(digit, radix, shift) - digit) * stride))
    return lax.ppermute(value, "dp", perm)


def owners_of(me, size):
    owners = [me]
    for at, (stride, radix) in enumerate(gather_stages(size)):
        digit = lax.rem(lax.div(me, stride), radix)
        shifts = [0, *(range(radix - 1, 0, -1) if at == 0 else range(1, radix))]
        back = [shift if radix & (radix - 1) == 0 else (radix - shift) % radix for shift in shifts]
        steps = [(partner(digit, radix, shift) - digit) * stride for shift in back]
        owners = [owner + step for step in steps for owner in owners]
    return owners


def exchanged(held, size, stride, radix, backwards=False):
    mine = held[0] if len(held) == 1 else jnp.concatenate(held, axis=0)
    shifts = range(radix - 1, 0, -1) if backwards else range(1, radix)
    return [mine] + [swapped(mine, size, stride, radix, shift) for shift in shifts]


def on_device(acts, grads, proj_act, proj_grad, queries):
    size = lax.axis_size("dp")
    tok_total = acts.shape[0] * size
    far, near, core = gather_stages(size)
    first, second = sum_rounds(size)

    pieces = exchanged([queries], size, *far, backwards=True)
    act_t, grad_t, own = project(acts, grads, proj_act, proj_grad)
    *pieces, own = lax.optimization_barrier((*pieces, own))
    pieces = exchanged(pieces, size, *near)
    own = functools.reduce(jnp.add, exchanged([own], size, *first))
    terms = exchanged([own], size, *second)
    *both, = lax.optimization_barrier((*pieces, *terms))
    pieces, terms = both[: len(pieces)], both[len(pieces) :]
    pieces = exchanged(pieces, size, *core)
    moved = precondition(tok_total, terms, act_t, grad_t)
    return score(size, moved, pieces)


def solution(mesh):
    in_specs = (P(("parts", "dp"), None), P(("parts", "dp"), None), P(), P(), P("dp", None))
    out_specs = P(("parts", "dp"), None)
    return jax.shard_map(
        on_device, mesh=mesh, in_specs=in_specs, out_specs=out_specs, check_vma=False
    )
```

```python
import functools

import jax
import jax.numpy as jnp
from jax import lax
from jax.experimental import pallas as pl
from jax.experimental.pallas import tpu as pltpu
from jax.sharding import PartitionSpec as P

DAMP = 0.1
HIGHEST = lax.Precision.HIGHEST
COPY_ROWS = 128
IN_FLIGHT = 5
TOKENS_AT_ONCE = 256


def places(factor):
    return [lax.broadcasted_iota(jnp.int32, (factor, factor), axis) for axis in (0, 1)]


def packed(act, grad):
    factor = act.shape[0]
    row_at, lane = places(factor)
    mixed = jnp.where(row_at <= lane, act, grad)
    diagonal = jnp.sum(jnp.where(row_at == lane, grad, 0.0), axis=0, keepdims=True)
    last = jnp.broadcast_to(jnp.concatenate([diagonal, diagonal], axis=1), (8, 2 * factor))
    half = factor // 2
    return jnp.concatenate([jnp.concatenate([mixed[:half], mixed[half:]], axis=1), last], axis=0)


def unpacked(value):
    factor = value.shape[1] // 2
    half = factor // 2
    row_at, lane = places(factor)
    mixed = jnp.concatenate([value[:half, :factor], value[:half, factor:]], axis=0)
    flipped = mixed.T
    diagonal = jnp.broadcast_to(value[half : half + 1, :factor], (factor, factor))
    act = jnp.where(row_at <= lane, mixed, flipped)
    grad = jnp.where(row_at > lane, mixed, jnp.where(row_at < lane, flipped, diagonal))
    return jnp.concatenate([act, grad], axis=1)


def project_kernel(
    acts, grads, weight_act, weight_grad, act_t, grad_t, cov, tok_buf, weight_buf, weight_t, tok_sems, weight_sems
):
    width = weight_act.shape[1]
    n_parts = acts.shape[0] // COPY_ROWS
    weight_copies = [
        pltpu.make_async_copy(src, weight_buf.at[at], weight_sems.at[at])
        for at, src in enumerate((weight_act, weight_grad))
    ]
    tok_copies = [
        [
            pltpu.make_async_copy(
                src.at[pl.ds(part * COPY_ROWS, COPY_ROWS), :],
                tok_buf.at[at, pl.ds(part * COPY_ROWS, COPY_ROWS), :],
                tok_sems.at[at, part],
            )
            for part in range(n_parts)
        ]
        for at, src in enumerate((acts, grads))
    ]
    queue = [weight_copies[0], *tok_copies[0], *tok_copies[1]]
    queue.insert(3, weight_copies[1])

    def start_next(many):
        for copy in queue[:many]:
            copy.start()
        del queue[:many]

    def turned(at):
        for first in range(0, width, 512):
            block = weight_buf[at, :, first : first + 512].astype(jnp.float32)
            weight_t[at, first : first + 512, :] = block.T.astype(weight_t.dtype)

    steps = [(at, part, min(2, n_parts - part)) for at in range(2) for part in range(0, n_parts, 2)]
    last_act = len(steps) // 2 - 1
    at, part, many = steps.pop()
    steps += [(at, part + one, 1) for one in range(many)]
    blocks = [[], []]
    grams = [[], []]

    def add_gram(at):
        flipped, plain = [jnp.concatenate(parts, axis=axis) for parts, axis in zip(zip(*blocks[at]), (1, 0))]
        grams[at].append(jnp.dot(flipped, plain, precision=HIGHEST, preferred_element_type=jnp.float32))
        blocks[at].clear()

    start_next(1 + IN_FLIGHT)
    weight_copies[0].wait()
    turned(0)
    for step, (at, part, many) in enumerate(steps):
        for copy in tok_copies[at][part : part + many]:
            copy.wait()
            start_next(1)
        if step == last_act:
            weight_copies[1].wait()
            start_next(1)
        rows = slice(part * COPY_ROWS, (part + many) * COPY_ROWS)
        block = jnp.dot(tok_buf[at, rows, :], weight_t[at], preferred_element_type=jnp.float32)
        if step == last_act:
            turned(1)
        if step == last_act + 1:
            add_gram(0)
        if step == len(steps) - 1:
            add_gram(1)
        flipped = block.T
        (act_t, grad_t)[at][:, rows] = flipped
        blocks[at].append((flipped, block))
    add_gram(1)
    cov[...] = packed(*[functools.reduce(jnp.add, terms) for terms in grams])


def project(acts, grads, proj_act, proj_grad):
    tok_rows, width = acts.shape
    factor = proj_act.shape[1]
    operands = [
        pltpu.with_memory_space_constraint(value, pltpu.HBM) for value in (acts, grads, proj_act.T, proj_grad.T)
    ]
    return pl.pallas_call(
        project_kernel,
        out_shape=(
            jax.ShapeDtypeStruct((factor, tok_rows), jnp.float32),
            jax.ShapeDtypeStruct((factor, tok_rows), jnp.float32),
            jax.ShapeDtypeStruct((factor // 2 + 8, 2 * factor), jnp.float32),
        ),
        in_specs=[pl.BlockSpec(memory_space=pltpu.HBM)] * 4,
        out_specs=[pl.BlockSpec(memory_space=pltpu.VMEM)] * 3,
        scratch_shapes=[
            pltpu.VMEM((2, tok_rows, width), acts.dtype),
            pltpu.VMEM((2, factor, width), proj_act.dtype),
            pltpu.VMEM((2, width, factor), proj_act.dtype),
            pltpu.SemaphoreType.DMA((2, tok_rows // COPY_ROWS)),
            pltpu.SemaphoreType.DMA((2,)),
        ],
        compiler_params=pltpu.CompilerParams(vmem_limit_bytes=24 * 2**20),
        cost_estimate=pl.CostEstimate(
            flops=4 * tok_rows * width * factor, bytes_accessed=4 * tok_rows * width, transcendentals=0
        ),
        name="project",
    )(*operands)


def inverse_pair(both):
    factor = both.shape[0]
    tile = (8, both.shape[1])
    lane = lax.broadcasted_iota(jnp.int32, tile, 1)
    row_at = lax.broadcasted_iota(jnp.int32, tile, 0)
    left_half = lane < factor
    inner = jnp.where(left_half, lane, lane - factor)
    parts = [both[at : at + 8, :] for at in range(0, factor, 8)]

    def column(part, at):
        index = jnp.where(left_half, at, factor + at)
        return jnp.take_along_axis(part, index, axis=1, mode="promise_in_bounds")

    def row(part, at):
        return jnp.broadcast_to(part[at : at + 1, :], tile)

    for k in range(0, factor, 4):
        home, off = divmod(k, 8)
        columns = [[column(part, k + a) for part in parts] for a in range(4)]
        pivot = [[row(columns[b][home], off + a) if a <= b else None for b in range(4)] for a in range(4)]
        p00, p01, p02, p03 = pivot[0]
        _, p11, p12, p13 = pivot[1]
        _, _, p22, p23 = pivot[2]
        p33 = pivot[3][3]
        on_block = (inner >= k) & (inner < k + 4)
        r0, r1, r2, r3 = [
            jnp.where(on_block, jnp.where(inner == k + a, 1.0, 0.0), row(parts[home], off + a)) for a in range(4)
        ]
        scale = 1.0 / (p00 * p11 - p01 * p01)
        e02 = scale * (p11 * p02 - p01 * p12)
        e03 = scale * (p11 * p03 - p01 * p13)
        e12 = scale * (p00 * p12 - p01 * p02)
        e13 = scale * (p00 * p13 - p01 * p03)
        s22 = p22 - (p02 * e02 + p12 * e12)
        s23 = p23 - (p02 * e03 + p12 * e13)
        s33 = p33 - (p03 * e03 + p13 * e13)
        scale_s = 1.0 / (s22 * s33 - s23 * s23)
        y0 = scale * (p11 * r0 - p01 * r1)
        y1 = scale * (p00 * r1 - p01 * r0)
        t2 = r2 - (p02 * y0 + p12 * y1)
        t3 = r3 - (p03 * y0 + p13 * y1)
        w2 = scale_s * (s33 * t2 - s23 * t3)
        w3 = scale_s * (s22 * t3 - s23 * t2)
        w0 = y0 - (e02 * w2 + e03 * w3)
        w1 = y1 - (e12 * w2 + e13 * w3)
        solved = (w0, w1, w2, w3)
        for m, part in enumerate(parts):
            change = (columns[0][m] * w0 + columns[1][m] * w1) + (columns[2][m] * w2 + columns[3][m] * w3)
            part = jnp.where(on_block, 0.0, part) - change
            if m == home:
                for a in range(4):
                    part = jnp.where(row_at == off + a, solved[a], part)
            parts[m] = part
    return jnp.concatenate(parts, axis=0)


def precondition_kernel(tok_total, n_terms, *refs):
    terms, (act_t, grad_t, moved) = refs[:n_terms], refs[n_terms:]
    both = terms[0][...]
    for term in terms[1:]:
        both = both + term[...]
    both = unpacked(both)
    factor = both.shape[0]
    lane = lax.broadcasted_iota(jnp.int32, both.shape, 1)
    row_at = lax.broadcasted_iota(jnp.int32, both.shape, 0)
    left_half = lane < factor
    inner = jnp.where(left_half, lane, lane - factor)
    both = both / tok_total + jnp.where(inner == row_at, DAMP, 0.0)
    both = inverse_pair(both)
    blocks = jnp.concatenate(
        [jnp.where(left_half, both, 0.0), jnp.where(left_half, 0.0, both)], axis=0
    )
    proj_t = jnp.concatenate([act_t[...], grad_t[...]], axis=0)
    moved[...] = jnp.dot(blocks, proj_t, precision=HIGHEST, preferred_element_type=jnp.float32)


def precondition(tok_total, terms, act_t, grad_t):
    factor, tok_rows = act_t.shape
    n_terms = len(terms)
    return pl.pallas_call(
        functools.partial(precondition_kernel, tok_total, n_terms),
        out_shape=jax.ShapeDtypeStruct((2 * factor, tok_rows), jnp.float32),
        in_specs=[pl.BlockSpec(memory_space=pltpu.VMEM)] * (n_terms + 2),
        out_specs=pl.BlockSpec(memory_space=pltpu.VMEM),
        compiler_params=pltpu.CompilerParams(vmem_limit_bytes=24 * 2**20),
        cost_estimate=pl.CostEstimate(
            flops=1600 * factor * factor * tok_rows, bytes_accessed=16 * factor * tok_rows, transcendentals=0
        ),
        name="precondition",
    )(*terms, act_t, grad_t)


def score_kernel(size, n_pieces, moved, *refs):
    queries, (scores, ordered, result, sems) = refs[:n_pieces], refs[n_pieces:]
    factor = moved.shape[0] // 2
    owners = owners_of(lax.axis_index("dp"), size)
    group = 4
    copies = []
    for part, begin in enumerate(range(0, moved.shape[1], TOKENS_AT_ONCE)):
        tokens = slice(begin, begin + TOKENS_AT_ONCE)
        act_side = moved[:factor, tokens]
        total = None
        for first in range(0, factor, group):
            outer = jnp.concatenate(
                [act_side * moved[factor + i : factor + i + 1, tokens] for i in range(first, first + group)], axis=0
            )
            high = outer.astype(jnp.bfloat16)
            low = (outer - high.astype(jnp.float32)).astype(jnp.bfloat16)
            columns = slice(first * factor, (first + group) * factor)
            values = jnp.concatenate([piece[:, columns] for piece in queries], axis=0)
            term = jnp.dot(
                jnp.concatenate([values, values], axis=1),
                jnp.concatenate([high, low], axis=0),
                preferred_element_type=jnp.float32,
            )
            total = term if total is None else total + term
        rows = total.shape[0] // size
        for at, owner in enumerate(owners):
            place = pl.ds(pl.multiple_of(owner * rows, rows), rows)
            ordered[part, place, :] = total[at * rows : (at + 1) * rows, :]
        result[tokens, :] = ordered[part].T
        copies.append(
            pltpu.make_async_copy(
                result.at[pl.ds(begin, TOKENS_AT_ONCE), :], scores.at[pl.ds(begin, TOKENS_AT_ONCE), :], sems.at[part]
            )
        )
        copies[-1].start()
    for copy in copies:
        copy.wait()


def score(size, moved, queries):
    tok_rows = moved.shape[1]
    n_queries = sum(piece.shape[0] for piece in queries)
    n_pieces = len(queries)
    n_parts = tok_rows // TOKENS_AT_ONCE
    return pl.pallas_call(
        functools.partial(score_kernel, size, n_pieces),
        out_shape=jax.ShapeDtypeStruct((tok_rows, n_queries), jnp.float32),
        in_specs=[pl.BlockSpec(memory_space=pltpu.VMEM)] * (1 + n_pieces),
        out_specs=pl.BlockSpec(memory_space=pl.ANY),
        scratch_shapes=[
            pltpu.VMEM((n_parts, n_queries, TOKENS_AT_ONCE), jnp.float32),
            pltpu.VMEM((tok_rows, n_queries), jnp.float32),
            pltpu.SemaphoreType.DMA((n_parts,)),
        ],
        compiler_params=pltpu.CompilerParams(vmem_limit_bytes=32 * 2**20),
        name="score",
    )(moved, *queries)


def gather_stages(size):
    core = 2 if size % 2 == 0 else 1
    rest = size // core
    near = max(d for d in range(1, rest + 1) if rest % d == 0 and d * d <= rest)
    return [(core * near, rest // near), (core, near), (1, core)]


def sum_rounds(size):
    (stride, radix), *_ = gather_stages(size)
    return [(1, stride), (stride, radix)]


def after(value, other):
    return lax.optimization_barrier((value, other))[0]


def partner(digit, radix, shift):
    return digit ^ shift if radix & (radix - 1) == 0 else (digit + shift) % radix


def swapped(value, size, stride, radix, shift):
    perm = []
    for at in range(size):
        digit = at // stride % radix
        perm.append((at, at + (partner(digit, radix, shift) - digit) * stride))
    return lax.ppermute(value, "dp", perm)


def owners_of(me, size):
    owners = [me]
    for at, (stride, radix) in enumerate(gather_stages(size)):
        digit = lax.rem(lax.div(me, stride), radix)
        shifts = [0, *(range(radix - 1, 0, -1) if at == 0 else range(1, radix))]
        back = [shift if radix & (radix - 1) == 0 else (radix - shift) % radix for shift in shifts]
        steps = [(partner(digit, radix, shift) - digit) * stride for shift in back]
        owners = [owner + step for step in steps for owner in owners]
    return owners


def exchanged(held, size, stride, radix, backwards=False):
    mine = held[0] if len(held) == 1 else jnp.concatenate(held, axis=0)
    shifts = range(radix - 1, 0, -1) if backwards else range(1, radix)
    return [mine] + [swapped(mine, size, stride, radix, shift) for shift in shifts]


def on_device(acts, grads, proj_act, proj_grad, queries):
    size = lax.axis_size("dp")
    tok_total = acts.shape[0] * size
    far, near, core = gather_stages(size)
    first, second = sum_rounds(size)

    pieces = exchanged([queries], size, *far, backwards=True)
    act_t, grad_t, own = project(acts, grads, proj_act, proj_grad)
    *pieces, own = lax.optimization_barrier((*pieces, own))
    pieces = exchanged(pieces, size, *near)
    own = functools.reduce(jnp.add, exchanged([own], size, *first))
    terms = exchanged([own], size, *second)
    *both, = lax.optimization_barrier((*pieces, *terms))
    pieces, terms = both[: len(pieces)], both[len(pieces) :]
    pieces = exchanged(pieces, size, *core)
    moved = precondition(tok_total, terms, act_t, grad_t)
    return score(size, moved, pieces)


def solution(mesh):
    in_specs = (P(("parts", "dp"), None), P(("parts", "dp"), None), P(), P(), P("dp", None))
    out_specs = P(("parts", "dp"), None)
    return jax.shard_map(
        on_device, mesh=mesh, in_specs=in_specs, out_specs=out_specs, check_vma=False
    )
```

```python
import functools

import jax
import jax.numpy as jnp
from jax import lax
from jax.experimental import pallas as pl
from jax.experimental.pallas import tpu as pltpu
from jax.sharding import PartitionSpec as P

DAMP = 0.1
HIGHEST = lax.Precision.HIGHEST
COPY_ROWS = 128
IN_FLIGHT = 6
TOKENS_AT_ONCE = 256


def places(factor):
    return [lax.broadcasted_iota(jnp.int32, (factor, factor), axis) for axis in (0, 1)]


def packed(act, grad):
    factor = act.shape[0]
    row_at, lane = places(factor)
    mixed = jnp.where(row_at <= lane, act, grad)
    diagonal = jnp.sum(jnp.where(row_at == lane, grad, 0.0), axis=0, keepdims=True)
    last = jnp.broadcast_to(jnp.concatenate([diagonal, diagonal], axis=1), (8, 2 * factor))
    half = factor // 2
    return jnp.concatenate([jnp.concatenate([mixed[:half], mixed[half:]], axis=1), last], axis=0)


def unpacked(value):
    factor = value.shape[1] // 2
    half = factor // 2
    row_at, lane = places(factor)
    mixed = jnp.concatenate([value[:half, :factor], value[:half, factor:]], axis=0)
    flipped = mixed.T
    diagonal = jnp.broadcast_to(value[half : half + 1, :factor], (factor, factor))
    act = jnp.where(row_at <= lane, mixed, flipped)
    grad = jnp.where(row_at > lane, mixed, jnp.where(row_at < lane, flipped, diagonal))
    return jnp.concatenate([act, grad], axis=1)


def project_kernel(
    acts, grads, weight_act, weight_grad, act_t, grad_t, cov, tok_buf, weight_buf, weight_t, tok_sems, weight_sems
):
    width = weight_act.shape[1]
    n_parts = acts.shape[0] // COPY_ROWS
    weight_copies = [
        pltpu.make_async_copy(src, weight_buf.at[at], weight_sems.at[at])
        for at, src in enumerate((weight_act, weight_grad))
    ]
    tok_copies = [
        [
            pltpu.make_async_copy(
                src.at[pl.ds(part * COPY_ROWS, COPY_ROWS), :],
                tok_buf.at[at, pl.ds(part * COPY_ROWS, COPY_ROWS), :],
                tok_sems.at[at, part],
            )
            for part in range(n_parts)
        ]
        for at, src in enumerate((acts, grads))
    ]
    queue = [weight_copies[0], *tok_copies[0], *tok_copies[1]]
    queue.insert(3, weight_copies[1])

    def start_next(many):
        for copy in queue[:many]:
            copy.start()
        del queue[:many]

    def turned(at):
        for first in range(0, width, 512):
            block = weight_buf[at, :, first : first + 512].astype(jnp.float32)
            weight_t[at, first : first + 512, :] = block.T.astype(weight_t.dtype)

    steps = [(at, part, min(2, n_parts - part)) for at in range(2) for part in range(0, n_parts, 2)]
    last_act = len(steps) // 2 - 1
    at, part, many = steps.pop()
    steps += [(at, part + one, 1) for one in range(many)]
    blocks = [[], []]
    grams = [[], []]

    def add_gram(at):
        flipped, plain = [jnp.concatenate(parts, axis=axis) for parts, axis in zip(zip(*blocks[at]), (1, 0))]
        grams[at].append(jnp.dot(flipped, plain, precision=HIGHEST, preferred_element_type=jnp.float32))
        blocks[at].clear()

    start_next(1 + IN_FLIGHT)
    weight_copies[0].wait()
    turned(0)
    for step, (at, part, many) in enumerate(steps):
        for copy in tok_copies[at][part : part + many]:
            copy.wait()
            start_next(1)
        if step == last_act:
            weight_copies[1].wait()
            start_next(1)
        rows = slice(part * COPY_ROWS, (part + many) * COPY_ROWS)
        block = jnp.dot(tok_buf[at, rows, :], weight_t[at], preferred_element_type=jnp.float32)
        if step == last_act:
            turned(1)
        if step == last_act + 1:
            add_gram(0)
        if step == len(steps) - 1:
            add_gram(1)
        flipped = block.T
        (act_t, grad_t)[at][:, rows] = flipped
        blocks[at].append((flipped, block))
    add_gram(1)
    cov[...] = packed(*[functools.reduce(jnp.add, terms) for terms in grams])


def project(acts, grads, proj_act, proj_grad):
    tok_rows, width = acts.shape
    factor = proj_act.shape[1]
    operands = [
        pltpu.with_memory_space_constraint(value, pltpu.HBM) for value in (acts, grads, proj_act.T, proj_grad.T)
    ]
    return pl.pallas_call(
        project_kernel,
        out_shape=(
            jax.ShapeDtypeStruct((factor, tok_rows), jnp.float32),
            jax.ShapeDtypeStruct((factor, tok_rows), jnp.float32),
            jax.ShapeDtypeStruct((factor // 2 + 8, 2 * factor), jnp.float32),
        ),
        in_specs=[pl.BlockSpec(memory_space=pltpu.HBM)] * 4,
        out_specs=[pl.BlockSpec(memory_space=pltpu.VMEM)] * 3,
        scratch_shapes=[
            pltpu.VMEM((2, tok_rows, width), acts.dtype),
            pltpu.VMEM((2, factor, width), proj_act.dtype),
            pltpu.VMEM((2, width, factor), proj_act.dtype),
            pltpu.SemaphoreType.DMA((2, tok_rows // COPY_ROWS)),
            pltpu.SemaphoreType.DMA((2,)),
        ],
        compiler_params=pltpu.CompilerParams(vmem_limit_bytes=24 * 2**20),
        cost_estimate=pl.CostEstimate(
            flops=4 * tok_rows * width * factor, bytes_accessed=4 * tok_rows * width, transcendentals=0
        ),
        name="project",
    )(*operands)


def inverse_pair(both):
    factor = both.shape[0]
    tile = (8, both.shape[1])
    lane = lax.broadcasted_iota(jnp.int32, tile, 1)
    row_at = lax.broadcasted_iota(jnp.int32, tile, 0)
    left_half = lane < factor
    inner = jnp.where(left_half, lane, lane - factor)
    parts = [both[at : at + 8, :] for at in range(0, factor, 8)]

    def column(part, at):
        index = jnp.where(left_half, at, factor + at)
        return jnp.take_along_axis(part, index, axis=1, mode="promise_in_bounds")

    def row(part, at):
        return jnp.broadcast_to(part[at : at + 1, :], tile)

    for k in range(0, factor, 4):
        home, off = divmod(k, 8)
        columns = [[column(part, k + a) for part in parts] for a in range(4)]
        pivot = [[row(columns[b][home], off + a) if a <= b else None for b in range(4)] for a in range(4)]
        p00, p01, p02, p03 = pivot[0]
        _, p11, p12, p13 = pivot[1]
        _, _, p22, p23 = pivot[2]
        p33 = pivot[3][3]
        on_block = (inner >= k) & (inner < k + 4)
        r0, r1, r2, r3 = [
            jnp.where(on_block, jnp.where(inner == k + a, 1.0, 0.0), row(parts[home], off + a)) for a in range(4)
        ]
        scale = 1.0 / (p00 * p11 - p01 * p01)
        e02 = scale * (p11 * p02 - p01 * p12)
        e03 = scale * (p11 * p03 - p01 * p13)
        e12 = scale * (p00 * p12 - p01 * p02)
        e13 = scale * (p00 * p13 - p01 * p03)
        s22 = p22 - (p02 * e02 + p12 * e12)
        s23 = p23 - (p02 * e03 + p12 * e13)
        s33 = p33 - (p03 * e03 + p13 * e13)
        scale_s = 1.0 / (s22 * s33 - s23 * s23)
        y0 = scale * (p11 * r0 - p01 * r1)
        y1 = scale * (p00 * r1 - p01 * r0)
        t2 = r2 - (p02 * y0 + p12 * y1)
        t3 = r3 - (p03 * y0 + p13 * y1)
        w2 = scale_s * (s33 * t2 - s23 * t3)
        w3 = scale_s * (s22 * t3 - s23 * t2)
        w0 = y0 - (e02 * w2 + e03 * w3)
        w1 = y1 - (e12 * w2 + e13 * w3)
        solved = (w0, w1, w2, w3)
        for m, part in enumerate(parts):
            change = (columns[0][m] * w0 + columns[1][m] * w1) + (columns[2][m] * w2 + columns[3][m] * w3)
            part = jnp.where(on_block, 0.0, part) - change
            if m == home:
                for a in range(4):
                    part = jnp.where(row_at == off + a, solved[a], part)
            parts[m] = part
    return jnp.concatenate(parts, axis=0)


def precondition_kernel(tok_total, n_terms, *refs):
    terms, (act_t, grad_t, moved) = refs[:n_terms], refs[n_terms:]
    both = terms[0][...]
    for term in terms[1:]:
        both = both + term[...]
    both = unpacked(both)
    factor = both.shape[0]
    lane = lax.broadcasted_iota(jnp.int32, both.shape, 1)
    row_at = lax.broadcasted_iota(jnp.int32, both.shape, 0)
    left_half = lane < factor
    inner = jnp.where(left_half, lane, lane - factor)
    both = both / tok_total + jnp.where(inner == row_at, DAMP, 0.0)
    both = inverse_pair(both)
    blocks = jnp.concatenate(
        [jnp.where(left_half, both, 0.0), jnp.where(left_half, 0.0, both)], axis=0
    )
    proj_t = jnp.concatenate([act_t[...], grad_t[...]], axis=0)
    moved[...] = jnp.dot(blocks, proj_t, precision=HIGHEST, preferred_element_type=jnp.float32)


def precondition(tok_total, terms, act_t, grad_t):
    factor, tok_rows = act_t.shape
    n_terms = len(terms)
    return pl.pallas_call(
        functools.partial(precondition_kernel, tok_total, n_terms),
        out_shape=jax.ShapeDtypeStruct((2 * factor, tok_rows), jnp.float32),
        in_specs=[pl.BlockSpec(memory_space=pltpu.VMEM)] * (n_terms + 2),
        out_specs=pl.BlockSpec(memory_space=pltpu.VMEM),
        compiler_params=pltpu.CompilerParams(vmem_limit_bytes=24 * 2**20),
        cost_estimate=pl.CostEstimate(
            flops=1600 * factor * factor * tok_rows, bytes_accessed=16 * factor * tok_rows, transcendentals=0
        ),
        name="precondition",
    )(*terms, act_t, grad_t)


def score_kernel(size, n_pieces, moved, *refs):
    queries, (scores, ordered, result, sems) = refs[:n_pieces], refs[n_pieces:]
    factor = moved.shape[0] // 2
    owners = owners_of(lax.axis_index("dp"), size)
    group = 2
    copies = []
    for part, begin in enumerate(range(0, moved.shape[1], TOKENS_AT_ONCE)):
        tokens = slice(begin, begin + TOKENS_AT_ONCE)
        act_side = moved[:factor, tokens]

        def split(first):
            outer = jnp.concatenate(
                [act_side * moved[factor + i : factor + i + 1, tokens] for i in range(first, first + group)], axis=0
            )
            high = outer.astype(jnp.bfloat16)
            low = (outer - high.astype(jnp.float32)).astype(jnp.bfloat16)
            return jnp.concatenate([high, low], axis=0)

        total = None
        later = split(0)
        for first in range(0, factor, group):
            both = later
            if first + group < factor:
                later = split(first + group)
            columns = slice(first * factor, (first + group) * factor)
            values = jnp.concatenate([piece[:, columns] for piece in queries], axis=0)
            term = jnp.dot(jnp.concatenate([values, values], axis=1), both, preferred_element_type=jnp.float32)
            total = term if total is None else total + term
        rows = total.shape[0] // size
        for at, owner in enumerate(owners):
            place = pl.ds(pl.multiple_of(owner * rows, rows), rows)
            ordered[part, place, :] = total[at * rows : (at + 1) * rows, :]
        result[tokens, :] = ordered[part].T
        copies.append(
            pltpu.make_async_copy(
                result.at[pl.ds(begin, TOKENS_AT_ONCE), :], scores.at[pl.ds(begin, TOKENS_AT_ONCE), :], sems.at[part]
            )
        )
        copies[-1].start()
    for copy in copies:
        copy.wait()


def score(size, moved, queries):
    tok_rows = moved.shape[1]
    n_queries = sum(piece.shape[0] for piece in queries)
    n_pieces = len(queries)
    n_parts = tok_rows // TOKENS_AT_ONCE
    return pl.pallas_call(
        functools.partial(score_kernel, size, n_pieces),
        out_shape=jax.ShapeDtypeStruct((tok_rows, n_queries), jnp.float32),
        in_specs=[pl.BlockSpec(memory_space=pltpu.VMEM)] * (1 + n_pieces),
        out_specs=pl.BlockSpec(memory_space=pl.ANY),
        scratch_shapes=[
            pltpu.VMEM((n_parts, n_queries, TOKENS_AT_ONCE), jnp.float32),
            pltpu.VMEM((tok_rows, n_queries), jnp.float32),
            pltpu.SemaphoreType.DMA((n_parts,)),
        ],
        compiler_params=pltpu.CompilerParams(vmem_limit_bytes=32 * 2**20),
        name="score",
    )(moved, *queries)


def gather_stages(size):
    core = 2 if size % 2 == 0 else 1
    rest = size // core
    near = max(d for d in range(1, rest + 1) if rest % d == 0 and d * d <= rest)
    return [(core * near, rest // near), (core, near), (1, core)]


def sum_rounds(size):
    (stride, radix), *_ = gather_stages(size)
    return [(1, stride), (stride, radix)]


def after(value, other):
    return lax.optimization_barrier((value, other))[0]


def partner(digit, radix, shift):
    return digit ^ shift if radix & (radix - 1) == 0 else (digit + shift) % radix


def swapped(value, size, stride, radix, shift):
    perm = []
    for at in range(size):
        digit = at // stride % radix
        perm.append((at, at + (partner(digit, radix, shift) - digit) * stride))
    return lax.ppermute(value, "dp", perm)


def owners_of(me, size):
    owners = [me]
    for at, (stride, radix) in enumerate(gather_stages(size)):
        digit = lax.rem(lax.div(me, stride), radix)
        shifts = [0, *(range(radix - 1, 0, -1) if at == 0 else range(1, radix))]
        back = [shift if radix & (radix - 1) == 0 else (radix - shift) % radix for shift in shifts]
        steps = [(partner(digit, radix, shift) - digit) * stride for shift in back]
        owners = [owner + step for step in steps for owner in owners]
    return owners


def exchanged(held, size, stride, radix, backwards=False):
    mine = held[0] if len(held) == 1 else jnp.concatenate(held, axis=0)
    shifts = range(radix - 1, 0, -1) if backwards else range(1, radix)
    return [mine] + [swapped(mine, size, stride, radix, shift) for shift in shifts]


def on_device(acts, grads, proj_act, proj_grad, queries):
    size = lax.axis_size("dp")
    tok_total = acts.shape[0] * size
    far, near, core = gather_stages(size)
    first, second = sum_rounds(size)

    pieces = exchanged([queries], size, *far, backwards=True)
    act_t, grad_t, own = project(acts, grads, proj_act, proj_grad)
    *pieces, own = lax.optimization_barrier((*pieces, own))
    pieces = exchanged(pieces, size, *near)
    own = functools.reduce(jnp.add, exchanged([own], size, *first))
    terms = exchanged([own], size, *second)
    *both, = lax.optimization_barrier((*pieces, *terms))
    pieces, terms = both[: len(pieces)], both[len(pieces) :]
    pieces = exchanged(pieces, size, *core)
    moved = precondition(tok_total, terms, act_t, grad_t)
    return score(size, moved, pieces)


def solution(mesh):
    in_specs = (P(("parts", "dp"), None), P(("parts", "dp"), None), P(), P(), P("dp", None))
    out_specs = P(("parts", "dp"), None)
    return jax.shard_map(
        on_device, mesh=mesh, in_specs=in_specs, out_specs=out_specs, check_vma=False
    )
```

```python
import functools

import jax
import jax.numpy as jnp
from jax import lax
from jax.experimental import pallas as pl
from jax.experimental.pallas import tpu as pltpu
from jax.sharding import PartitionSpec as P

DAMP = 0.1
HIGHEST = lax.Precision.HIGHEST
COPY_ROWS = 128
IN_FLIGHT = 5
TOKENS_AT_ONCE = 256


def places(factor):
    return [lax.broadcasted_iota(jnp.int32, (factor, factor), axis) for axis in (0, 1)]


def packed(act, grad):
    factor = act.shape[0]
    row_at, lane = places(factor)
    mixed = jnp.where(row_at <= lane, act, grad)
    diagonal = jnp.sum(jnp.where(row_at == lane, grad, 0.0), axis=0, keepdims=True)
    last = jnp.broadcast_to(jnp.concatenate([diagonal, diagonal], axis=1), (8, 2 * factor))
    half = factor // 2
    return jnp.concatenate([jnp.concatenate([mixed[:half], mixed[half:]], axis=1), last], axis=0)


def unpacked(value):
    factor = value.shape[1] // 2
    half = factor // 2
    row_at, lane = places(factor)
    mixed = jnp.concatenate([value[:half, :factor], value[:half, factor:]], axis=0)
    flipped = mixed.T
    diagonal = jnp.broadcast_to(value[half : half + 1, :factor], (factor, factor))
    act = jnp.where(row_at <= lane, mixed, flipped)
    grad = jnp.where(row_at > lane, mixed, jnp.where(row_at < lane, flipped, diagonal))
    return jnp.concatenate([act, grad], axis=1)


def project_kernel(
    acts, grads, weight_act, weight_grad, act_t, grad_t, cov, tok_buf, weight_buf, weight_t, tok_sems, weight_sems
):
    width = weight_act.shape[1]
    n_parts = acts.shape[0] // COPY_ROWS
    weight_copies = [
        pltpu.make_async_copy(src, weight_buf.at[at], weight_sems.at[at])
        for at, src in enumerate((weight_act, weight_grad))
    ]
    tok_copies = [
        [
            pltpu.make_async_copy(
                src.at[pl.ds(part * COPY_ROWS, COPY_ROWS), :],
                tok_buf.at[at, pl.ds(part * COPY_ROWS, COPY_ROWS), :],
                tok_sems.at[at, part],
            )
            for part in range(n_parts)
        ]
        for at, src in enumerate((acts, grads))
    ]
    queue = [weight_copies[0], *tok_copies[0], *tok_copies[1]]
    queue.insert(3, weight_copies[1])

    def start_next(many):
        for copy in queue[:many]:
            copy.start()
        del queue[:many]

    def turned(at):
        for first in range(0, width, 512):
            block = weight_buf[at, :, first : first + 512].astype(jnp.float32)
            weight_t[at, first : first + 512, :] = block.T.astype(weight_t.dtype)

    steps = [(at, part, min(2, n_parts - part)) for at in range(2) for part in range(0, n_parts, 2)]
    last_act = len(steps) // 2 - 1
    blocks = [[], []]
    grams = [[], []]

    def add_gram(at):
        flipped, plain = [jnp.concatenate(parts, axis=axis) for parts, axis in zip(zip(*blocks[at]), (1, 0))]
        grams[at].append(jnp.dot(flipped, plain, precision=HIGHEST, preferred_element_type=jnp.float32))
        blocks[at].clear()

    start_next(1 + IN_FLIGHT)
    weight_copies[0].wait()
    turned(0)
    for step, (at, part, many) in enumerate(steps):
        for copy in tok_copies[at][part : part + many]:
            copy.wait()
            start_next(1)
        if step == last_act:
            weight_copies[1].wait()
            start_next(1)
        rows = slice(part * COPY_ROWS, (part + many) * COPY_ROWS)
        block = jnp.dot(tok_buf[at, rows, :], weight_t[at], preferred_element_type=jnp.float32)
        if step == last_act:
            turned(1)
        if step == last_act + 1:
            add_gram(0)
        if step == len(steps) - 1:
            add_gram(1)
        flipped = block.T
        (act_t, grad_t)[at][:, rows] = flipped
        blocks[at].append((flipped, block))
    add_gram(1)
    cov[...] = packed(*[functools.reduce(jnp.add, terms) for terms in grams])


def project(acts, grads, proj_act, proj_grad):
    tok_rows, width = acts.shape
    factor = proj_act.shape[1]
    operands = [
        pltpu.with_memory_space_constraint(value, pltpu.HBM) for value in (acts, grads, proj_act.T, proj_grad.T)
    ]
    return pl.pallas_call(
        project_kernel,
        out_shape=(
            jax.ShapeDtypeStruct((factor, tok_rows), jnp.float32),
            jax.ShapeDtypeStruct((factor, tok_rows), jnp.float32),
            jax.ShapeDtypeStruct((factor // 2 + 8, 2 * factor), jnp.float32),
        ),
        in_specs=[pl.BlockSpec(memory_space=pltpu.HBM)] * 4,
        out_specs=[pl.BlockSpec(memory_space=pltpu.VMEM)] * 3,
        scratch_shapes=[
            pltpu.VMEM((2, tok_rows, width), acts.dtype),
            pltpu.VMEM((2, factor, width), proj_act.dtype),
            pltpu.VMEM((2, width, factor), proj_act.dtype),
            pltpu.SemaphoreType.DMA((2, tok_rows // COPY_ROWS)),
            pltpu.SemaphoreType.DMA((2,)),
        ],
        compiler_params=pltpu.CompilerParams(vmem_limit_bytes=24 * 2**20),
        cost_estimate=pl.CostEstimate(
            flops=4 * tok_rows * width * factor, bytes_accessed=4 * tok_rows * width, transcendentals=0
        ),
        name="project",
    )(*operands)


def inverse_pair(both):
    factor = both.shape[0]
    tile = (8, both.shape[1])
    lane = lax.broadcasted_iota(jnp.int32, tile, 1)
    row_at = lax.broadcasted_iota(jnp.int32, tile, 0)
    left_half = lane < factor
    inner = jnp.where(left_half, lane, lane - factor)
    parts = [both[at : at + 8, :] for at in range(0, factor, 8)]

    def column(part, at):
        index = jnp.where(left_half, at, factor + at)
        return jnp.take_along_axis(part, index, axis=1, mode="promise_in_bounds")

    def row(part, at):
        return jnp.broadcast_to(part[at : at + 1, :], tile)

    for k in range(0, factor, 4):
        home, off = divmod(k, 8)
        columns = [[column(part, k + a) for part in parts] for a in range(4)]
        pivot = [[row(columns[b][home], off + a) if a <= b else None for b in range(4)] for a in range(4)]
        p00, p01, p02, p03 = pivot[0]
        _, p11, p12, p13 = pivot[1]
        _, _, p22, p23 = pivot[2]
        p33 = pivot[3][3]
        on_block = (inner >= k) & (inner < k + 4)
        r0, r1, r2, r3 = [
            jnp.where(on_block, jnp.where(inner == k + a, 1.0, 0.0), row(parts[home], off + a)) for a in range(4)
        ]
        scale = 1.0 / (p00 * p11 - p01 * p01)
        m02 = p11 * p02 - p01 * p12
        m03 = p11 * p03 - p01 * p13
        m12 = p00 * p12 - p01 * p02
        m13 = p00 * p13 - p01 * p03
        z0 = p11 * r0 - p01 * r1
        z1 = p00 * r1 - p01 * r0
        s22 = p22 - scale * (p02 * m02 + p12 * m12)
        s23 = p23 - scale * (p02 * m03 + p12 * m13)
        s33 = p33 - scale * (p03 * m03 + p13 * m13)
        t2 = r2 - scale * (p02 * z0 + p12 * z1)
        t3 = r3 - scale * (p03 * z0 + p13 * z1)
        scale_s = 1.0 / (s22 * s33 - s23 * s23)
        w2 = scale_s * (s33 * t2 - s23 * t3)
        w3 = scale_s * (s22 * t3 - s23 * t2)
        w0 = scale * (z0 - (m02 * w2 + m03 * w3))
        w1 = scale * (z1 - (m12 * w2 + m13 * w3))
        solved = (w0, w1, w2, w3)
        for m, part in enumerate(parts):
            change = (columns[0][m] * w0 + columns[1][m] * w1) + (columns[2][m] * w2 + columns[3][m] * w3)
            part = jnp.where(on_block, 0.0, part) - change
            if m == home:
                for a in range(4):
                    part = jnp.where(row_at == off + a, solved[a], part)
            parts[m] = part
    return jnp.concatenate(parts, axis=0)


def precondition_kernel(tok_total, n_terms, *refs):
    terms, (act_t, grad_t, moved) = refs[:n_terms], refs[n_terms:]
    both = terms[0][...]
    for term in terms[1:]:
        both = both + term[...]
    both = unpacked(both)
    factor = both.shape[0]
    lane = lax.broadcasted_iota(jnp.int32, both.shape, 1)
    row_at = lax.broadcasted_iota(jnp.int32, both.shape, 0)
    left_half = lane < factor
    inner = jnp.where(left_half, lane, lane - factor)
    both = both / tok_total + jnp.where(inner == row_at, DAMP, 0.0)
    both = inverse_pair(both)
    blocks = jnp.concatenate(
        [jnp.where(left_half, both, 0.0), jnp.where(left_half, 0.0, both)], axis=0
    )
    proj_t = jnp.concatenate([act_t[...], grad_t[...]], axis=0)
    moved[...] = jnp.dot(blocks, proj_t, precision=HIGHEST, preferred_element_type=jnp.float32)


def precondition(tok_total, terms, act_t, grad_t):
    factor, tok_rows = act_t.shape
    n_terms = len(terms)
    return pl.pallas_call(
        functools.partial(precondition_kernel, tok_total, n_terms),
        out_shape=jax.ShapeDtypeStruct((2 * factor, tok_rows), jnp.float32),
        in_specs=[pl.BlockSpec(memory_space=pltpu.VMEM)] * (n_terms + 2),
        out_specs=pl.BlockSpec(memory_space=pltpu.VMEM),
        compiler_params=pltpu.CompilerParams(vmem_limit_bytes=24 * 2**20),
        cost_estimate=pl.CostEstimate(
            flops=1600 * factor * factor * tok_rows, bytes_accessed=16 * factor * tok_rows, transcendentals=0
        ),
        name="precondition",
    )(*terms, act_t, grad_t)


def score_kernel(size, n_pieces, moved, *refs):
    queries, (scores, ordered, result, sems) = refs[:n_pieces], refs[n_pieces:]
    factor = moved.shape[0] // 2
    owners = owners_of(lax.axis_index("dp"), size)
    group = 2
    copies = []
    for part, begin in enumerate(range(0, moved.shape[1], TOKENS_AT_ONCE)):
        tokens = slice(begin, begin + TOKENS_AT_ONCE)
        act_side = moved[:factor, tokens]

        def split(first):
            outer = jnp.concatenate(
                [act_side * moved[factor + i : factor + i + 1, tokens] for i in range(first, first + group)], axis=0
            )
            high = outer.astype(jnp.bfloat16)
            low = (outer - high.astype(jnp.float32)).astype(jnp.bfloat16)
            return jnp.concatenate([high, low], axis=0)

        total = None
        later = split(0)
        for first in range(0, factor, group):
            both = later
            if first + group < factor:
                later = split(first + group)
            columns = slice(first * factor, (first + group) * factor)
            values = jnp.concatenate([piece[:, columns] for piece in queries], axis=0)
            term = jnp.dot(jnp.concatenate([values, values], axis=1), both, preferred_element_type=jnp.float32)
            total = term if total is None else total + term
        rows = total.shape[0] // size
        for at, owner in enumerate(owners):
            place = pl.ds(pl.multiple_of(owner * rows, rows), rows)
            ordered[part, place, :] = total[at * rows : (at + 1) * rows, :]
        result[tokens, :] = ordered[part].T
        copies.append(
            pltpu.make_async_copy(
                result.at[pl.ds(begin, TOKENS_AT_ONCE), :], scores.at[pl.ds(begin, TOKENS_AT_ONCE), :], sems.at[part]
            )
        )
        copies[-1].start()
    for copy in copies:
        copy.wait()


def score(size, moved, queries):
    tok_rows = moved.shape[1]
    n_queries = sum(piece.shape[0] for piece in queries)
    n_pieces = len(queries)
    n_parts = tok_rows // TOKENS_AT_ONCE
    return pl.pallas_call(
        functools.partial(score_kernel, size, n_pieces),
        out_shape=jax.ShapeDtypeStruct((tok_rows, n_queries), jnp.float32),
        in_specs=[pl.BlockSpec(memory_space=pltpu.VMEM)] * (1 + n_pieces),
        out_specs=pl.BlockSpec(memory_space=pl.ANY),
        scratch_shapes=[
            pltpu.VMEM((n_parts, n_queries, TOKENS_AT_ONCE), jnp.float32),
            pltpu.VMEM((tok_rows, n_queries), jnp.float32),
            pltpu.SemaphoreType.DMA((n_parts,)),
        ],
        compiler_params=pltpu.CompilerParams(vmem_limit_bytes=32 * 2**20),
        name="score",
    )(moved, *queries)


def gather_stages(size):
    core = 2 if size % 2 == 0 else 1
    rest = size // core
    near = max(d for d in range(1, rest + 1) if rest % d == 0 and d * d <= rest)
    return [(core * near, rest // near), (core, near), (1, core)]


def sum_rounds(size):
    (stride, radix), *_ = gather_stages(size)
    return [(1, stride), (stride, radix)]


def after(value, other):
    return lax.optimization_barrier((value, other))[0]


def partner(digit, radix, shift):
    return digit ^ shift if radix & (radix - 1) == 0 else (digit + shift) % radix


def swapped(value, size, stride, radix, shift):
    perm = []
    for at in range(size):
        digit = at // stride % radix
        perm.append((at, at + (partner(digit, radix, shift) - digit) * stride))
    return lax.ppermute(value, "dp", perm)


def owners_of(me, size):
    owners = [me]
    for at, (stride, radix) in enumerate(gather_stages(size)):
        digit = lax.rem(lax.div(me, stride), radix)
        shifts = [0, *(range(radix - 1, 0, -1) if at == 0 else range(1, radix))]
        back = [shift if radix & (radix - 1) == 0 else (radix - shift) % radix for shift in shifts]
        steps = [(partner(digit, radix, shift) - digit) * stride for shift in back]
        owners = [owner + step for step in steps for owner in owners]
    return owners


def exchanged(held, size, stride, radix, backwards=False):
    mine = held[0] if len(held) == 1 else jnp.concatenate(held, axis=0)
    shifts = range(radix - 1, 0, -1) if backwards else range(1, radix)
    return [mine] + [swapped(mine, size, stride, radix, shift) for shift in shifts]


def on_device(acts, grads, proj_act, proj_grad, queries):
    size = lax.axis_size("dp")
    tok_total = acts.shape[0] * size
    far, near, core = gather_stages(size)
    first, second = sum_rounds(size)

    pieces = exchanged([queries], size, *far, backwards=True)
    act_t, grad_t, own = project(acts, grads, proj_act, proj_grad)
    *pieces, own = lax.optimization_barrier((*pieces, own))
    pieces = exchanged(pieces, size, *near)
    own = functools.reduce(jnp.add, exchanged([own], size, *first))
    terms = exchanged([own], size, *second)
    *both, = lax.optimization_barrier((*pieces, *terms))
    pieces, terms = both[: len(pieces)], both[len(pieces) :]
    pieces = exchanged(pieces, size, *core)
    moved = precondition(tok_total, terms, act_t, grad_t)
    return score(size, moved, pieces)


def solution(mesh):
    in_specs = (P(("parts", "dp"), None), P(("parts", "dp"), None), P(), P(), P("dp", None))
    out_specs = P(("parts", "dp"), None)
    return jax.shard_map(
        on_device, mesh=mesh, in_specs=in_specs, out_specs=out_specs, check_vma=False
    )
```

```python
import functools

import jax
import jax.numpy as jnp
from jax import lax
from jax.experimental import pallas as pl
from jax.experimental.pallas import tpu as pltpu
from jax.sharding import PartitionSpec as P

DAMP = 0.1
HIGHEST = lax.Precision.HIGHEST
COPY_ROWS = 128
IN_FLIGHT = 5
TOKENS_AT_ONCE = 256


def places(factor):
    return [lax.broadcasted_iota(jnp.int32, (factor, factor), axis) for axis in (0, 1)]


def packed(act, grad):
    factor = act.shape[0]
    row_at, lane = places(factor)
    mixed = jnp.where(row_at <= lane, act, grad)
    diagonal = jnp.sum(jnp.where(row_at == lane, grad, 0.0), axis=0, keepdims=True)
    last = jnp.broadcast_to(jnp.concatenate([diagonal, diagonal], axis=1), (8, 2 * factor))
    half = factor // 2
    return jnp.concatenate([jnp.concatenate([mixed[:half], mixed[half:]], axis=1), last], axis=0)


def unpacked(value):
    factor = value.shape[1] // 2
    half = factor // 2
    row_at, lane = places(factor)
    mixed = jnp.concatenate([value[:half, :factor], value[:half, factor:]], axis=0)
    flipped = mixed.T
    diagonal = jnp.broadcast_to(value[half : half + 1, :factor], (factor, factor))
    act = jnp.where(row_at <= lane, mixed, flipped)
    grad = jnp.where(row_at > lane, mixed, jnp.where(row_at < lane, flipped, diagonal))
    return jnp.concatenate([act, grad], axis=1)


def project_kernel(
    acts, grads, weight_act, weight_grad, act_t, grad_t, cov, tok_buf, weight_buf, weight_t, tok_sems, weight_sems
):
    width = weight_act.shape[1]
    n_parts = acts.shape[0] // COPY_ROWS
    weight_copies = [
        pltpu.make_async_copy(src, weight_buf.at[at], weight_sems.at[at])
        for at, src in enumerate((weight_act, weight_grad))
    ]
    tok_copies = [
        [
            pltpu.make_async_copy(
                src.at[pl.ds(part * COPY_ROWS, COPY_ROWS), :],
                tok_buf.at[at, pl.ds(part * COPY_ROWS, COPY_ROWS), :],
                tok_sems.at[at, part],
            )
            for part in range(n_parts)
        ]
        for at, src in enumerate((acts, grads))
    ]
    queue = [weight_copies[0], *tok_copies[0], *tok_copies[1]]
    queue.insert(3, weight_copies[1])

    def start_next(many):
        for copy in queue[:many]:
            copy.start()
        del queue[:many]

    def turned(at):
        for first in range(0, width, 512):
            weight_t[at, first : first + 512, :] = weight_buf[at, :, first : first + 512].T

    steps = [(at, part, min(2, n_parts - part)) for at in range(2) for part in range(0, n_parts, 2)]
    last_act = len(steps) // 2 - 1
    blocks = [[], []]
    grams = [[], []]

    def add_gram(at):
        flipped, plain = [jnp.concatenate(parts, axis=axis) for parts, axis in zip(zip(*blocks[at]), (1, 0))]
        grams[at].append(jnp.dot(flipped, plain, precision=HIGHEST, preferred_element_type=jnp.float32))
        blocks[at].clear()

    start_next(1 + IN_FLIGHT)
    weight_copies[0].wait()
    turned(0)
    for step, (at, part, many) in enumerate(steps):
        for copy in tok_copies[at][part : part + many]:
            copy.wait()
            start_next(1)
        if step == last_act:
            weight_copies[1].wait()
            start_next(1)
        rows = slice(part * COPY_ROWS, (part + many) * COPY_ROWS)
        block = jnp.dot(tok_buf[at, rows, :], weight_t[at], preferred_element_type=jnp.float32)
        if step == last_act:
            turned(1)
        if step == last_act + 1:
            add_gram(0)
        if step == len(steps) - 1:
            add_gram(1)
        flipped = block.T
        (act_t, grad_t)[at][:, rows] = flipped
        blocks[at].append((flipped, block))
    add_gram(1)
    cov[...] = packed(*[functools.reduce(jnp.add, terms) for terms in grams])


def project(acts, grads, proj_act, proj_grad):
    tok_rows, width = acts.shape
    factor = proj_act.shape[1]
    operands = [
        pltpu.with_memory_space_constraint(value, pltpu.HBM) for value in (acts, grads, proj_act.T, proj_grad.T)
    ]
    return pl.pallas_call(
        project_kernel,
        out_shape=(
            jax.ShapeDtypeStruct((factor, tok_rows), jnp.float32),
            jax.ShapeDtypeStruct((factor, tok_rows), jnp.float32),
            jax.ShapeDtypeStruct((factor // 2 + 8, 2 * factor), jnp.float32),
        ),
        in_specs=[pl.BlockSpec(memory_space=pltpu.HBM)] * 4,
        out_specs=[pl.BlockSpec(memory_space=pltpu.VMEM)] * 3,
        scratch_shapes=[
            pltpu.VMEM((2, tok_rows, width), acts.dtype),
            pltpu.VMEM((2, factor, width), proj_act.dtype),
            pltpu.VMEM((2, width, factor), proj_act.dtype),
            pltpu.SemaphoreType.DMA((2, tok_rows // COPY_ROWS)),
            pltpu.SemaphoreType.DMA((2,)),
        ],
        compiler_params=pltpu.CompilerParams(vmem_limit_bytes=24 * 2**20),
        cost_estimate=pl.CostEstimate(
            flops=4 * tok_rows * width * factor, bytes_accessed=4 * tok_rows * width, transcendentals=0
        ),
        name="project",
    )(*operands)


def inverse_pair(both):
    factor = both.shape[0]
    tile = (8, both.shape[1])
    lane = lax.broadcasted_iota(jnp.int32, tile, 1)
    row_at = lax.broadcasted_iota(jnp.int32, tile, 0)
    left_half = lane < factor
    inner = jnp.where(left_half, lane, lane - factor)
    parts = [both[at : at + 8, :] for at in range(0, factor, 8)]

    def column(part, at):
        index = jnp.where(left_half, at, factor + at)
        return jnp.take_along_axis(part, index, axis=1, mode="promise_in_bounds")

    def row(part, at):
        return jnp.broadcast_to(part[at : at + 1, :], tile)

    for k in range(0, factor, 4):
        home, off = divmod(k, 8)
        columns = [[column(part, k + a) for part in parts] for a in range(4)]
        pivot = [[row(columns[b][home], off + a) if a <= b else None for b in range(4)] for a in range(4)]
        p00, p01, p02, p03 = pivot[0]
        _, p11, p12, p13 = pivot[1]
        _, _, p22, p23 = pivot[2]
        p33 = pivot[3][3]
        on_block = (inner >= k) & (inner < k + 4)
        r0, r1, r2, r3 = [
            jnp.where(on_block, jnp.where(inner == k + a, 1.0, 0.0), row(parts[home], off + a)) for a in range(4)
        ]
        scale = 1.0 / (p00 * p11 - p01 * p01)
        m02 = p11 * p02 - p01 * p12
        m03 = p11 * p03 - p01 * p13
        m12 = p00 * p12 - p01 * p02
        m13 = p00 * p13 - p01 * p03
        z0 = p11 * r0 - p01 * r1
        z1 = p00 * r1 - p01 * r0
        s22 = p22 - scale * (p02 * m02 + p12 * m12)
        s23 = p23 - scale * (p02 * m03 + p12 * m13)
        s33 = p33 - scale * (p03 * m03 + p13 * m13)
        t2 = r2 - scale * (p02 * z0 + p12 * z1)
        t3 = r3 - scale * (p03 * z0 + p13 * z1)
        scale_s = 1.0 / (s22 * s33 - s23 * s23)
        w2 = scale_s * (s33 * t2 - s23 * t3)
        w3 = scale_s * (s22 * t3 - s23 * t2)
        w0 = scale * (z0 - (m02 * w2 + m03 * w3))
        w1 = scale * (z1 - (m12 * w2 + m13 * w3))
        solved = (w0, w1, w2, w3)
        for m, part in enumerate(parts):
            change = (columns[0][m] * w0 + columns[1][m] * w1) + (columns[2][m] * w2 + columns[3][m] * w3)
            part = jnp.where(on_block, 0.0, part) - change
            if m == home:
                for a in range(4):
                    part = jnp.where(row_at == off + a, solved[a], part)
            parts[m] = part
    return jnp.concatenate(parts, axis=0)


def precondition_kernel(tok_total, n_terms, *refs):
    terms, (act_t, grad_t, moved) = refs[:n_terms], refs[n_terms:]
    both = terms[0][...]
    for term in terms[1:]:
        both = both + term[...]
    both = unpacked(both)
    factor = both.shape[0]
    lane = lax.broadcasted_iota(jnp.int32, both.shape, 1)
    row_at = lax.broadcasted_iota(jnp.int32, both.shape, 0)
    left_half = lane < factor
    inner = jnp.where(left_half, lane, lane - factor)
    both = both / tok_total + jnp.where(inner == row_at, DAMP, 0.0)
    both = inverse_pair(both)
    blocks = jnp.concatenate(
        [jnp.where(left_half, both, 0.0), jnp.where(left_half, 0.0, both)], axis=0
    )
    proj_t = jnp.concatenate([act_t[...], grad_t[...]], axis=0)
    moved[...] = jnp.dot(blocks, proj_t, precision=HIGHEST, preferred_element_type=jnp.float32)


def precondition(tok_total, terms, act_t, grad_t):
    factor, tok_rows = act_t.shape
    n_terms = len(terms)
    return pl.pallas_call(
        functools.partial(precondition_kernel, tok_total, n_terms),
        out_shape=jax.ShapeDtypeStruct((2 * factor, tok_rows), jnp.float32),
        in_specs=[pl.BlockSpec(memory_space=pltpu.VMEM)] * (n_terms + 2),
        out_specs=pl.BlockSpec(memory_space=pltpu.VMEM),
        compiler_params=pltpu.CompilerParams(vmem_limit_bytes=24 * 2**20),
        cost_estimate=pl.CostEstimate(
            flops=1600 * factor * factor * tok_rows, bytes_accessed=16 * factor * tok_rows, transcendentals=0
        ),
        name="precondition",
    )(*terms, act_t, grad_t)


def score_kernel(size, n_pieces, moved, *refs):
    queries, (scores, ordered, result, sems) = refs[:n_pieces], refs[n_pieces:]
    factor = moved.shape[0] // 2
    owners = owners_of(lax.axis_index("dp"), size)
    group = 2
    copies = []
    for part, begin in enumerate(range(0, moved.shape[1], TOKENS_AT_ONCE)):
        tokens = slice(begin, begin + TOKENS_AT_ONCE)
        act_side = moved[:factor, tokens]

        def split(first):
            outer = jnp.concatenate(
                [act_side * moved[factor + i : factor + i + 1, tokens] for i in range(first, first + group)], axis=0
            )
            high = outer.astype(jnp.bfloat16)
            low = (outer - high.astype(jnp.float32)).astype(jnp.bfloat16)
            return jnp.concatenate([high, low], axis=0)

        total = None
        later = split(0)
        for first in range(0, factor, group):
            both = later
            if first + group < factor:
                later = split(first + group)
            columns = slice(first * factor, (first + group) * factor)
            values = jnp.concatenate([piece[:, columns] for piece in queries], axis=0)
            term = jnp.dot(jnp.concatenate([values, values], axis=1), both, preferred_element_type=jnp.float32)
            total = term if total is None else total + term
        rows = total.shape[0] // size
        for at, owner in enumerate(owners):
            place = pl.ds(pl.multiple_of(owner * rows, rows), rows)
            ordered[part, place, :] = total[at * rows : (at + 1) * rows, :]
        result[tokens, :] = ordered[part].T
        copies.append(
            pltpu.make_async_copy(
                result.at[pl.ds(begin, TOKENS_AT_ONCE), :], scores.at[pl.ds(begin, TOKENS_AT_ONCE), :], sems.at[part]
            )
        )
        copies[-1].start()
    for copy in copies:
        copy.wait()


def score(size, moved, queries):
    tok_rows = moved.shape[1]
    n_queries = sum(piece.shape[0] for piece in queries)
    n_pieces = len(queries)
    n_parts = tok_rows // TOKENS_AT_ONCE
    return pl.pallas_call(
        functools.partial(score_kernel, size, n_pieces),
        out_shape=jax.ShapeDtypeStruct((tok_rows, n_queries), jnp.float32),
        in_specs=[pl.BlockSpec(memory_space=pltpu.VMEM)] * (1 + n_pieces),
        out_specs=pl.BlockSpec(memory_space=pl.ANY),
        scratch_shapes=[
            pltpu.VMEM((n_parts, n_queries, TOKENS_AT_ONCE), jnp.float32),
            pltpu.VMEM((tok_rows, n_queries), jnp.float32),
            pltpu.SemaphoreType.DMA((n_parts,)),
        ],
        compiler_params=pltpu.CompilerParams(vmem_limit_bytes=32 * 2**20),
        name="score",
    )(moved, *queries)


def gather_stages(size):
    core = 2 if size % 2 == 0 else 1
    rest = size // core
    near = max(d for d in range(1, rest + 1) if rest % d == 0 and d * d <= rest)
    return [(core * near, rest // near), (core, near), (1, core)]


def sum_rounds(size):
    (stride, radix), *_ = gather_stages(size)
    return [(1, stride), (stride, radix)]


def after(value, other):
    return lax.optimization_barrier((value, other))[0]


def partner(digit, radix, shift):
    return digit ^ shift if radix & (radix - 1) == 0 else (digit + shift) % radix


def swapped(value, size, stride, radix, shift):
    perm = []
    for at in range(size):
        digit = at // stride % radix
        perm.append((at, at + (partner(digit, radix, shift) - digit) * stride))
    return lax.ppermute(value, "dp", perm)


def owners_of(me, size):
    owners = [me]
    for at, (stride, radix) in enumerate(gather_stages(size)):
        digit = lax.rem(lax.div(me, stride), radix)
        shifts = [0, *(range(radix - 1, 0, -1) if at == 0 else range(1, radix))]
        back = [shift if radix & (radix - 1) == 0 else (radix - shift) % radix for shift in shifts]
        steps = [(partner(digit, radix, shift) - digit) * stride for shift in back]
        owners = [owner + step for step in steps for owner in owners]
    return owners


def exchanged(held, size, stride, radix, backwards=False):
    mine = held[0] if len(held) == 1 else jnp.concatenate(held, axis=0)
    shifts = range(radix - 1, 0, -1) if backwards else range(1, radix)
    return [mine] + [swapped(mine, size, stride, radix, shift) for shift in shifts]


def on_device(acts, grads, proj_act, proj_grad, queries):
    size = lax.axis_size("dp")
    tok_total = acts.shape[0] * size
    far, near, core = gather_stages(size)
    first, second = sum_rounds(size)

    pieces = exchanged([queries], size, *far, backwards=True)
    act_t, grad_t, own = project(acts, grads, proj_act, proj_grad)
    *pieces, own = lax.optimization_barrier((*pieces, own))
    pieces = exchanged(pieces, size, *near)
    own = functools.reduce(jnp.add, exchanged([own], size, *first))
    terms = exchanged([own], size, *second)
    *both, = lax.optimization_barrier((*pieces, *terms))
    pieces, terms = both[: len(pieces)], both[len(pieces) :]
    pieces = exchanged(pieces, size, *core)
    moved = precondition(tok_total, terms, act_t, grad_t)
    return score(size, moved, pieces)


def solution(mesh):
    in_specs = (P(("parts", "dp"), None), P(("parts", "dp"), None), P(), P(), P("dp", None))
    out_specs = P(("parts", "dp"), None)
    return jax.shard_map(
        on_device, mesh=mesh, in_specs=in_specs, out_specs=out_specs, check_vma=False
    )
```

```python
import functools

import jax
import jax.numpy as jnp
from jax import lax
from jax.experimental import pallas as pl
from jax.experimental.pallas import tpu as pltpu
from jax.sharding import PartitionSpec as P

DAMP = 0.1
HIGHEST = lax.Precision.HIGHEST
COPY_ROWS = 128
TOKENS_AT_ONCE = 256


def places(factor):
    return [lax.broadcasted_iota(jnp.int32, (factor, factor), axis) for axis in (0, 1)]


def packed(act, grad):
    factor = act.shape[0]
    row_at, lane = places(factor)
    mixed = jnp.where(row_at <= lane, act, grad)
    diagonal = jnp.sum(jnp.where(row_at == lane, grad, 0.0), axis=0, keepdims=True)
    last = jnp.broadcast_to(jnp.concatenate([diagonal, diagonal], axis=1), (8, 2 * factor))
    half = factor // 2
    return jnp.concatenate([jnp.concatenate([mixed[:half], mixed[half:]], axis=1), last], axis=0)


def unpacked(value):
    factor = value.shape[1] // 2
    half = factor // 2
    row_at, lane = places(factor)
    mixed = jnp.concatenate([value[:half, :factor], value[:half, factor:]], axis=0)
    flipped = mixed.T
    diagonal = jnp.broadcast_to(value[half : half + 1, :factor], (factor, factor))
    act = jnp.where(row_at <= lane, mixed, flipped)
    grad = jnp.where(row_at > lane, mixed, jnp.where(row_at < lane, flipped, diagonal))
    return jnp.concatenate([act, grad], axis=1)


def project_kernel(
    acts, grads, weight_act, weight_grad, act_t, grad_t, cov, tok_buf, weight_buf, weight_t, tok_sems, weight_sems
):
    width = weight_act.shape[1]
    n_parts = acts.shape[0] // COPY_ROWS
    weight_copies = [
        pltpu.make_async_copy(src, weight_buf.at[at], weight_sems.at[at])
        for at, src in enumerate((weight_act, weight_grad))
    ]
    tok_copies = [
        [
            pltpu.make_async_copy(
                src.at[pl.ds(part * COPY_ROWS, COPY_ROWS), :],
                tok_buf.at[at, pl.ds(part * COPY_ROWS, COPY_ROWS), :],
                tok_sems.at[at, part],
            )
            for part in range(n_parts)
        ]
        for at, src in enumerate((acts, grads))
    ]
    queue = [weight_copies[0], *tok_copies[0], *tok_copies[1]]
    queue.insert(5, weight_copies[1])

    def start_next(many):
        for copy in queue[:many]:
            copy.start()
        del queue[:many]

    def turned(at):
        for first in range(0, width, 512):
            weight_t[at, first : first + 512, :] = weight_buf[at, :, first : first + 512].T

    steps = [(at, part, min(2, n_parts - part)) for at in range(2) for part in range(0, n_parts, 2)]
    last_act = len(steps) // 2 - 1
    blocks = [[], []]
    grams = [[], []]

    def add_gram(at):
        flipped, plain = [jnp.concatenate(parts, axis=axis) for parts, axis in zip(zip(*blocks[at]), (1, 0))]
        grams[at].append(jnp.dot(flipped, plain, precision=HIGHEST, preferred_element_type=jnp.float32))
        blocks[at].clear()

    start_next(3)
    weight_copies[0].wait()
    start_next(3)
    turned(0)
    for step, (at, part, many) in enumerate(steps):
        for copy in tok_copies[at][part : part + many]:
            copy.wait()
            start_next(1)
        if step == last_act:
            weight_copies[1].wait()
        rows = slice(part * COPY_ROWS, (part + many) * COPY_ROWS)
        block = jnp.dot(tok_buf[at, rows, :], weight_t[at], preferred_element_type=jnp.float32)
        if step == last_act:
            turned(1)
        if step == last_act + 1:
            add_gram(0)
        if step == len(steps) - 1:
            add_gram(1)
        flipped = block.T
        (act_t, grad_t)[at][:, rows] = flipped
        blocks[at].append((flipped, block))
    add_gram(1)
    cov[...] = packed(*[functools.reduce(jnp.add, terms) for terms in grams])


def project(acts, grads, proj_act, proj_grad):
    tok_rows, width = acts.shape
    factor = proj_act.shape[1]
    operands = [
        pltpu.with_memory_space_constraint(value, pltpu.HBM) for value in (acts, grads, proj_act.T, proj_grad.T)
    ]
    return pl.pallas_call(
        project_kernel,
        out_shape=(
            jax.ShapeDtypeStruct((factor, tok_rows), jnp.float32),
            jax.ShapeDtypeStruct((factor, tok_rows), jnp.float32),
            jax.ShapeDtypeStruct((factor // 2 + 8, 2 * factor), jnp.float32),
        ),
        in_specs=[pl.BlockSpec(memory_space=pltpu.HBM)] * 4,
        out_specs=[pl.BlockSpec(memory_space=pltpu.VMEM)] * 3,
        scratch_shapes=[
            pltpu.VMEM((2, tok_rows, width), acts.dtype),
            pltpu.VMEM((2, factor, width), proj_act.dtype),
            pltpu.VMEM((2, width, factor), proj_act.dtype),
            pltpu.SemaphoreType.DMA((2, tok_rows // COPY_ROWS)),
            pltpu.SemaphoreType.DMA((2,)),
        ],
        compiler_params=pltpu.CompilerParams(vmem_limit_bytes=24 * 2**20),
        cost_estimate=pl.CostEstimate(
            flops=4 * tok_rows * width * factor, bytes_accessed=4 * tok_rows * width, transcendentals=0
        ),
        name="project",
    )(*operands)


def inverse_pair(both):
    factor = both.shape[0]
    tile = (8, both.shape[1])
    lane = lax.broadcasted_iota(jnp.int32, tile, 1)
    row_at = lax.broadcasted_iota(jnp.int32, tile, 0)
    left_half = lane < factor
    inner = jnp.where(left_half, lane, lane - factor)
    parts = [both[at : at + 8, :] for at in range(0, factor, 8)]

    def column(part, at):
        index = jnp.where(left_half, at, factor + at)
        return jnp.take_along_axis(part, index, axis=1, mode="promise_in_bounds")

    def row(part, at):
        return jnp.broadcast_to(part[at : at + 1, :], tile)

    for k in range(0, factor, 4):
        home, off = divmod(k, 8)
        columns = [[column(part, k + a) for part in parts] for a in range(4)]
        pivot = [[row(columns[b][home], off + a) if a <= b else None for b in range(4)] for a in range(4)]
        p00, p01, p02, p03 = pivot[0]
        _, p11, p12, p13 = pivot[1]
        _, _, p22, p23 = pivot[2]
        p33 = pivot[3][3]
        on_block = (inner >= k) & (inner < k + 4)
        r0, r1, r2, r3 = [
            jnp.where(on_block, jnp.where(inner == k + a, 1.0, 0.0), row(parts[home], off + a)) for a in range(4)
        ]
        scale = 1.0 / (p00 * p11 - p01 * p01)
        m02 = p11 * p02 - p01 * p12
        m03 = p11 * p03 - p01 * p13
        m12 = p00 * p12 - p01 * p02
        m13 = p00 * p13 - p01 * p03
        z0 = p11 * r0 - p01 * r1
        z1 = p00 * r1 - p01 * r0
        s22 = p22 - scale * (p02 * m02 + p12 * m12)
        s23 = p23 - scale * (p02 * m03 + p12 * m13)
        s33 = p33 - scale * (p03 * m03 + p13 * m13)
        t2 = r2 - scale * (p02 * z0 + p12 * z1)
        t3 = r3 - scale * (p03 * z0 + p13 * z1)
        scale_s = 1.0 / (s22 * s33 - s23 * s23)
        w2 = scale_s * (s33 * t2 - s23 * t3)
        w3 = scale_s * (s22 * t3 - s23 * t2)
        w0 = scale * (z0 - (m02 * w2 + m03 * w3))
        w1 = scale * (z1 - (m12 * w2 + m13 * w3))
        solved = (w0, w1, w2, w3)
        for m, part in enumerate(parts):
            change = (columns[0][m] * w0 + columns[1][m] * w1) + (columns[2][m] * w2 + columns[3][m] * w3)
            part = jnp.where(on_block, 0.0, part) - change
            if m == home:
                for a in range(4):
                    part = jnp.where(row_at == off + a, solved[a], part)
            parts[m] = part
    return jnp.concatenate(parts, axis=0)


def precondition_kernel(tok_total, n_terms, *refs):
    terms, (act_t, grad_t, moved) = refs[:n_terms], refs[n_terms:]
    both = terms[0][...]
    for term in terms[1:]:
        both = both + term[...]
    both = unpacked(both)
    factor = both.shape[0]
    lane = lax.broadcasted_iota(jnp.int32, both.shape, 1)
    row_at = lax.broadcasted_iota(jnp.int32, both.shape, 0)
    left_half = lane < factor
    inner = jnp.where(left_half, lane, lane - factor)
    both = both / tok_total + jnp.where(inner == row_at, DAMP, 0.0)
    both = inverse_pair(both)
    blocks = jnp.concatenate(
        [jnp.where(left_half, both, 0.0), jnp.where(left_half, 0.0, both)], axis=0
    )
    proj_t = jnp.concatenate([act_t[...], grad_t[...]], axis=0)
    moved[...] = jnp.dot(blocks, proj_t, precision=HIGHEST, preferred_element_type=jnp.float32)


def precondition(tok_total, terms, act_t, grad_t):
    factor, tok_rows = act_t.shape
    n_terms = len(terms)
    return pl.pallas_call(
        functools.partial(precondition_kernel, tok_total, n_terms),
        out_shape=jax.ShapeDtypeStruct((2 * factor, tok_rows), jnp.float32),
        in_specs=[pl.BlockSpec(memory_space=pltpu.VMEM)] * (n_terms + 2),
        out_specs=pl.BlockSpec(memory_space=pltpu.VMEM),
        compiler_params=pltpu.CompilerParams(vmem_limit_bytes=24 * 2**20),
        cost_estimate=pl.CostEstimate(
            flops=1600 * factor * factor * tok_rows, bytes_accessed=16 * factor * tok_rows, transcendentals=0
        ),
        name="precondition",
    )(*terms, act_t, grad_t)


def score_kernel(size, n_pieces, moved, *refs):
    queries, (scores, ordered, result, sems) = refs[:n_pieces], refs[n_pieces:]
    factor = moved.shape[0] // 2
    owners = owners_of(lax.axis_index("dp"), size)
    group = 2
    copies = []
    for part, begin in enumerate(range(0, moved.shape[1], TOKENS_AT_ONCE)):
        tokens = slice(begin, begin + TOKENS_AT_ONCE)
        act_side = moved[:factor, tokens]

        def split(first):
            outer = jnp.concatenate(
                [act_side * moved[factor + i : factor + i + 1, tokens] for i in range(first, first + group)], axis=0
            )
            high = outer.astype(jnp.bfloat16)
            low = (outer - high.astype(jnp.float32)).astype(jnp.bfloat16)
            return jnp.concatenate([high, low], axis=0)

        total = None
        later = split(0)
        for first in range(0, factor, group):
            both = later
            if first + group < factor:
                later = split(first + group)
            columns = slice(first * factor, (first + group) * factor)
            values = jnp.concatenate([piece[:, columns] for piece in queries], axis=0)
            term = jnp.dot(jnp.concatenate([values, values], axis=1), both, preferred_element_type=jnp.float32)
            total = term if total is None else total + term
        rows = total.shape[0] // size
        for at, owner in enumerate(owners):
            place = pl.ds(pl.multiple_of(owner * rows, rows), rows)
            ordered[part, place, :] = total[at * rows : (at + 1) * rows, :]
        result[tokens, :] = ordered[part].T
        copies.append(
            pltpu.make_async_copy(
                result.at[pl.ds(begin, TOKENS_AT_ONCE), :], scores.at[pl.ds(begin, TOKENS_AT_ONCE), :], sems.at[part]
            )
        )
        copies[-1].start()
    for copy in copies:
        copy.wait()


def score(size, moved, queries):
    tok_rows = moved.shape[1]
    n_queries = sum(piece.shape[0] for piece in queries)
    n_pieces = len(queries)
    n_parts = tok_rows // TOKENS_AT_ONCE
    return pl.pallas_call(
        functools.partial(score_kernel, size, n_pieces),
        out_shape=jax.ShapeDtypeStruct((tok_rows, n_queries), jnp.float32),
        in_specs=[pl.BlockSpec(memory_space=pltpu.VMEM)] * (1 + n_pieces),
        out_specs=pl.BlockSpec(memory_space=pl.ANY),
        scratch_shapes=[
            pltpu.VMEM((n_parts, n_queries, TOKENS_AT_ONCE), jnp.float32),
            pltpu.VMEM((tok_rows, n_queries), jnp.float32),
            pltpu.SemaphoreType.DMA((n_parts,)),
        ],
        compiler_params=pltpu.CompilerParams(vmem_limit_bytes=32 * 2**20),
        name="score",
    )(moved, *queries)


def gather_stages(size):
    core = 2 if size % 2 == 0 else 1
    rest = size // core
    near = max(d for d in range(1, rest + 1) if rest % d == 0 and d * d <= rest)
    return [(core * near, rest // near), (core, near), (1, core)]


def sum_rounds(size):
    (stride, radix), *_ = gather_stages(size)
    return [(1, stride), (stride, radix)]


def after(value, other):
    return lax.optimization_barrier((value, other))[0]


def partner(digit, radix, shift):
    return digit ^ shift if radix & (radix - 1) == 0 else (digit + shift) % radix


def swapped(value, size, stride, radix, shift):
    perm = []
    for at in range(size):
        digit = at // stride % radix
        perm.append((at, at + (partner(digit, radix, shift) - digit) * stride))
    return lax.ppermute(value, "dp", perm)


def owners_of(me, size):
    owners = [me]
    for at, (stride, radix) in enumerate(gather_stages(size)):
        digit = lax.rem(lax.div(me, stride), radix)
        shifts = [0, *(range(radix - 1, 0, -1) if at == 0 else range(1, radix))]
        back = [shift if radix & (radix - 1) == 0 else (radix - shift) % radix for shift in shifts]
        steps = [(partner(digit, radix, shift) - digit) * stride for shift in back]
        owners = [owner + step for step in steps for owner in owners]
    return owners


def exchanged(held, size, stride, radix, backwards=False):
    mine = held[0] if len(held) == 1 else jnp.concatenate(held, axis=0)
    shifts = range(radix - 1, 0, -1) if backwards else range(1, radix)
    return [mine] + [swapped(mine, size, stride, radix, shift) for shift in shifts]


def on_device(acts, grads, proj_act, proj_grad, queries):
    size = lax.axis_size("dp")
    tok_total = acts.shape[0] * size
    far, near, core = gather_stages(size)
    first, second = sum_rounds(size)

    pieces = exchanged([queries], size, *far, backwards=True)
    act_t, grad_t, own = project(acts, grads, proj_act, proj_grad)
    *pieces, own = lax.optimization_barrier((*pieces, own))
    pieces = exchanged(pieces, size, *near)
    own = functools.reduce(jnp.add, exchanged([own], size, *first))
    terms = exchanged([own], size, *second)
    *both, = lax.optimization_barrier((*pieces, *terms))
    pieces, terms = both[: len(pieces)], both[len(pieces) :]
    pieces = exchanged(pieces, size, *core)
    moved = precondition(tok_total, terms, act_t, grad_t)
    return score(size, moved, pieces)


def solution(mesh):
    in_specs = (P(("parts", "dp"), None), P(("parts", "dp"), None), P(), P(), P("dp", None))
    out_specs = P(("parts", "dp"), None)
    return jax.shard_map(
        on_device, mesh=mesh, in_specs=in_specs, out_specs=out_specs, check_vma=False
    )
```

```python
import functools

import jax
import jax.numpy as jnp
from jax import lax
from jax.experimental import pallas as pl
from jax.experimental.pallas import tpu as pltpu
from jax.sharding import PartitionSpec as P

DAMP = 0.1
HIGHEST = lax.Precision.HIGHEST
COPY_ROWS = 128
IN_FLIGHT = 5
TOKENS_AT_ONCE = 256


def places(factor):
    return [lax.broadcasted_iota(jnp.int32, (factor, factor), axis) for axis in (0, 1)]


def packed(act, grad):
    factor = act.shape[0]
    row_at, lane = places(factor)
    mixed = jnp.where(row_at <= lane, act, grad)
    diagonal = jnp.sum(jnp.where(row_at == lane, grad, 0.0), axis=0, keepdims=True)
    last = jnp.broadcast_to(jnp.concatenate([diagonal, diagonal], axis=1), (8, 2 * factor))
    half = factor // 2
    return jnp.concatenate([jnp.concatenate([mixed[:half], mixed[half:]], axis=1), last], axis=0)


def unpacked(value):
    factor = value.shape[1] // 2
    half = factor // 2
    row_at = lax.broadcasted_iota(jnp.int32, (factor, 2 * factor), 0)
    lane = lax.broadcasted_iota(jnp.int32, (factor, 2 * factor), 1)
    left_half = lane < factor
    inner = jnp.where(left_half, lane, lane - factor)
    rolled = pltpu.roll(value[:half], factor, axis=1)
    mixed = jnp.concatenate(
        [
            jnp.where(left_half[:half], value[:half], rolled),
            jnp.where(left_half[:half], rolled, value[:half]),
        ],
        axis=0,
    )
    flipped = jnp.concatenate([mixed, mixed], axis=0).T[:factor]
    diagonal = jnp.broadcast_to(value[half : half + 1], mixed.shape)
    below = jnp.where(row_at > inner, mixed, jnp.where(row_at < inner, flipped, diagonal))
    return jnp.where(left_half, jnp.where(row_at <= inner, mixed, flipped), below)


def project_kernel(
    acts, grads, weight_act, weight_grad, act_t, grad_t, cov, tok_buf, weight_buf, weight_t, tok_sems, weight_sems
):
    width = weight_act.shape[1]
    n_parts = acts.shape[0] // COPY_ROWS
    weight_copies = [
        pltpu.make_async_copy(src, weight_buf.at[at], weight_sems.at[at])
        for at, src in enumerate((weight_act, weight_grad))
    ]
    tok_copies = [
        [
            pltpu.make_async_copy(
                src.at[pl.ds(part * COPY_ROWS, COPY_ROWS), :],
                tok_buf.at[at, pl.ds(part * COPY_ROWS, COPY_ROWS), :],
                tok_sems.at[at, part],
            )
            for part in range(n_parts)
        ]
        for at, src in enumerate((acts, grads))
    ]
    queue = [weight_copies[0], *tok_copies[0], *tok_copies[1]]
    queue.insert(3, weight_copies[1])
    queue = [(copy, at % 2) for at, copy in enumerate(queue)]

    def start_next(many):
        for copy, lane in queue[:many]:
            copy.start(priority=lane)
        del queue[:many]

    def turned(at):
        for first in range(0, width, 512):
            weight_t[at, first : first + 512, :] = weight_buf[at, :, first : first + 512].T

    steps = [(at, part, min(2, n_parts - part)) for at in range(2) for part in range(0, n_parts, 2)]
    last_act = len(steps) // 2 - 1
    blocks = [[], []]
    grams = [[], []]

    def add_gram(at):
        flipped, plain = [jnp.concatenate(parts, axis=axis) for parts, axis in zip(zip(*blocks[at]), (1, 0))]
        grams[at].append(jnp.dot(flipped, plain, precision=HIGHEST, preferred_element_type=jnp.float32))
        blocks[at].clear()

    start_next(1 + IN_FLIGHT)
    weight_copies[0].wait()
    turned(0)
    for step, (at, part, many) in enumerate(steps):
        for copy in tok_copies[at][part : part + many]:
            copy.wait()
            start_next(1)
        if step == last_act:
            weight_copies[1].wait()
            start_next(1)
        rows = slice(part * COPY_ROWS, (part + many) * COPY_ROWS)
        block = jnp.dot(tok_buf[at, rows, :], weight_t[at], preferred_element_type=jnp.float32)
        if step == last_act:
            turned(1)
        if step == last_act + 1:
            add_gram(0)
        if step == len(steps) - 1:
            add_gram(1)
        flipped = block.T
        (act_t, grad_t)[at][:, rows] = flipped
        blocks[at].append((flipped, block))
    add_gram(1)
    cov[...] = packed(*[functools.reduce(jnp.add, terms) for terms in grams])


def project(acts, grads, proj_act, proj_grad):
    tok_rows, width = acts.shape
    factor = proj_act.shape[1]
    operands = [
        pltpu.with_memory_space_constraint(value, pltpu.HBM) for value in (acts, grads, proj_act.T, proj_grad.T)
    ]
    return pl.pallas_call(
        project_kernel,
        out_shape=(
            jax.ShapeDtypeStruct((factor, tok_rows), jnp.float32),
            jax.ShapeDtypeStruct((factor, tok_rows), jnp.float32),
            jax.ShapeDtypeStruct((factor // 2 + 8, 2 * factor), jnp.float32),
        ),
        in_specs=[pl.BlockSpec(memory_space=pltpu.HBM)] * 4,
        out_specs=[pl.BlockSpec(memory_space=pltpu.VMEM)] * 3,
        scratch_shapes=[
            pltpu.VMEM((2, tok_rows, width), acts.dtype),
            pltpu.VMEM((2, factor, width), proj_act.dtype),
            pltpu.VMEM((2, width, factor), proj_act.dtype),
            pltpu.SemaphoreType.DMA((2, tok_rows // COPY_ROWS)),
            pltpu.SemaphoreType.DMA((2,)),
        ],
        compiler_params=pltpu.CompilerParams(vmem_limit_bytes=24 * 2**20),
        cost_estimate=pl.CostEstimate(
            flops=4 * tok_rows * width * factor, bytes_accessed=4 * tok_rows * width, transcendentals=0
        ),
        name="project",
    )(*operands)


def inverse_pair(both):
    factor = both.shape[0]
    tile = (8, both.shape[1])
    lane = lax.broadcasted_iota(jnp.int32, tile, 1)
    row_at = lax.broadcasted_iota(jnp.int32, tile, 0)
    left_half = lane < factor
    inner = jnp.where(left_half, lane, lane - factor)
    parts = [both[at : at + 8, :] for at in range(0, factor, 8)]

    def column(part, at):
        index = jnp.where(left_half, at, factor + at)
        return jnp.take_along_axis(part, index, axis=1, mode="promise_in_bounds")

    def row(part, at):
        return jnp.broadcast_to(part[at : at + 1, :], tile)

    for k in range(0, factor, 4):
        home, off = divmod(k, 8)
        columns = [[column(part, k + a) for part in parts] for a in range(4)]
        pivot = [[row(columns[b][home], off + a) if a <= b else None for b in range(4)] for a in range(4)]
        p00, p01, p02, p03 = pivot[0]
        _, p11, p12, p13 = pivot[1]
        _, _, p22, p23 = pivot[2]
        p33 = pivot[3][3]
        on_block = (inner >= k) & (inner < k + 4)
        r0, r1, r2, r3 = [
            jnp.where(on_block, jnp.where(inner == k + a, 1.0, 0.0), row(parts[home], off + a)) for a in range(4)
        ]
        scale = 1.0 / (p00 * p11 - p01 * p01)
        m02 = p11 * p02 - p01 * p12
        m03 = p11 * p03 - p01 * p13
        m12 = p00 * p12 - p01 * p02
        m13 = p00 * p13 - p01 * p03
        z0 = p11 * r0 - p01 * r1
        z1 = p00 * r1 - p01 * r0
        s22 = p22 - scale * (p02 * m02 + p12 * m12)
        s23 = p23 - scale * (p02 * m03 + p12 * m13)
        s33 = p33 - scale * (p03 * m03 + p13 * m13)
        t2 = r2 - scale * (p02 * z0 + p12 * z1)
        t3 = r3 - scale * (p03 * z0 + p13 * z1)
        scale_s = 1.0 / (s22 * s33 - s23 * s23)
        w2 = scale_s * (s33 * t2 - s23 * t3)
        w3 = scale_s * (s22 * t3 - s23 * t2)
        w0 = scale * (z0 - (m02 * w2 + m03 * w3))
        w1 = scale * (z1 - (m12 * w2 + m13 * w3))
        solved = (w0, w1, w2, w3)
        for m, part in enumerate(parts):
            change = (columns[0][m] * w0 + columns[1][m] * w1) + (columns[2][m] * w2 + columns[3][m] * w3)
            part = jnp.where(on_block, 0.0, part) - change
            if m == home:
                for a in range(4):
                    part = jnp.where(row_at == off + a, solved[a], part)
            parts[m] = part
    return jnp.concatenate(parts, axis=0)


def precondition_kernel(tok_total, n_terms, *refs):
    terms, (act_t, grad_t, moved) = refs[:n_terms], refs[n_terms:]
    both = terms[0][...]
    for term in terms[1:]:
        both = both + term[...]
    both = unpacked(both)
    factor = both.shape[0]
    lane = lax.broadcasted_iota(jnp.int32, both.shape, 1)
    row_at = lax.broadcasted_iota(jnp.int32, both.shape, 0)
    left_half = lane < factor
    inner = jnp.where(left_half, lane, lane - factor)
    both = both * (1.0 / tok_total) + jnp.where(inner == row_at, DAMP, 0.0)
    both = inverse_pair(both)
    blocks = jnp.concatenate(
        [jnp.where(left_half, both, 0.0), jnp.where(left_half, 0.0, both)], axis=0
    )
    proj_t = jnp.concatenate([act_t[...], grad_t[...]], axis=0)
    moved[...] = jnp.dot(blocks, proj_t, precision=HIGHEST, preferred_element_type=jnp.float32)


def precondition(tok_total, terms, act_t, grad_t):
    factor, tok_rows = act_t.shape
    n_terms = len(terms)
    return pl.pallas_call(
        functools.partial(precondition_kernel, tok_total, n_terms),
        out_shape=jax.ShapeDtypeStruct((2 * factor, tok_rows), jnp.float32),
        in_specs=[pl.BlockSpec(memory_space=pltpu.VMEM)] * (n_terms + 2),
        out_specs=pl.BlockSpec(memory_space=pltpu.VMEM),
        compiler_params=pltpu.CompilerParams(vmem_limit_bytes=24 * 2**20),
        cost_estimate=pl.CostEstimate(
            flops=1600 * factor * factor * tok_rows, bytes_accessed=16 * factor * tok_rows, transcendentals=0
        ),
        name="precondition",
    )(*terms, act_t, grad_t)


def score_kernel(size, n_pieces, moved, *refs):
    queries, (scores, ordered, result, sems) = refs[:n_pieces], refs[n_pieces:]
    factor = moved.shape[0] // 2
    owners = owners_of(lax.axis_index("dp"), size)
    group = 2
    copies = []
    for part, begin in enumerate(range(0, moved.shape[1], TOKENS_AT_ONCE)):
        tokens = slice(begin, begin + TOKENS_AT_ONCE)
        act_side = moved[:factor, tokens]

        def split(first):
            outer = jnp.concatenate(
                [act_side * moved[factor + i : factor + i + 1, tokens] for i in range(first, first + group)], axis=0
            )
            high = outer.astype(jnp.bfloat16)
            low = (outer - high.astype(jnp.float32)).astype(jnp.bfloat16)
            return jnp.concatenate([high, low], axis=0)

        total = None
        later = split(0)
        for first in range(0, factor, group):
            both = later
            if first + group < factor:
                later = split(first + group)
            columns = slice(first * factor, (first + group) * factor)
            values = jnp.concatenate([piece[:, columns] for piece in queries], axis=0)
            term = jnp.dot(jnp.concatenate([values, values], axis=1), both, preferred_element_type=jnp.float32)
            total = term if total is None else total + term
        rows = total.shape[0] // size
        for at, owner in enumerate(owners):
            place = pl.ds(pl.multiple_of(owner * rows, rows), rows)
            ordered[part, place, :] = total[at * rows : (at + 1) * rows, :]
        result[tokens, :] = ordered[part].T
        copies.append(
            pltpu.make_async_copy(
                result.at[pl.ds(begin, TOKENS_AT_ONCE), :], scores.at[pl.ds(begin, TOKENS_AT_ONCE), :], sems.at[part]
            )
        )
        copies[-1].start()
    for copy in copies:
        copy.wait()


def score(size, moved, queries):
    tok_rows = moved.shape[1]
    n_queries = sum(piece.shape[0] for piece in queries)
    n_pieces = len(queries)
    n_parts = tok_rows // TOKENS_AT_ONCE
    return pl.pallas_call(
        functools.partial(score_kernel, size, n_pieces),
        out_shape=jax.ShapeDtypeStruct((tok_rows, n_queries), jnp.float32),
        in_specs=[pl.BlockSpec(memory_space=pltpu.VMEM)] * (1 + n_pieces),
        out_specs=pl.BlockSpec(memory_space=pl.ANY),
        scratch_shapes=[
            pltpu.VMEM((n_parts, n_queries, TOKENS_AT_ONCE), jnp.float32),
            pltpu.VMEM((tok_rows, n_queries), jnp.float32),
            pltpu.SemaphoreType.DMA((n_parts,)),
        ],
        compiler_params=pltpu.CompilerParams(vmem_limit_bytes=32 * 2**20),
        name="score",
    )(moved, *queries)


def gather_stages(size):
    core = 2 if size % 2 == 0 else 1
    rest = size // core
    near = max(d for d in range(1, rest + 1) if rest % d == 0 and d * d <= rest)
    return [(core * near, rest // near), (core, near), (1, core)]


def sum_rounds(size):
    (stride, radix), *_ = gather_stages(size)
    return [(1, stride), (stride, radix)]


def after(value, other):
    return lax.optimization_barrier((value, other))[0]


def partner(digit, radix, shift):
    return digit ^ shift if radix & (radix - 1) == 0 else (digit + shift) % radix


def swapped(value, size, stride, radix, shift):
    perm = []
    for at in range(size):
        digit = at // stride % radix
        perm.append((at, at + (partner(digit, radix, shift) - digit) * stride))
    return lax.ppermute(value, "dp", perm)


def owners_of(me, size):
    owners = [me]
    for at, (stride, radix) in enumerate(gather_stages(size)):
        digit = lax.rem(lax.div(me, stride), radix)
        shifts = [0, *(range(radix - 1, 0, -1) if at == 0 else range(1, radix))]
        back = [shift if radix & (radix - 1) == 0 else (radix - shift) % radix for shift in shifts]
        steps = [(partner(digit, radix, shift) - digit) * stride for shift in back]
        owners = [owner + step for step in steps for owner in owners]
    return owners


def exchanged(held, size, stride, radix, backwards=False):
    mine = held[0] if len(held) == 1 else jnp.concatenate(held, axis=0)
    shifts = range(radix - 1, 0, -1) if backwards else range(1, radix)
    return [mine] + [swapped(mine, size, stride, radix, shift) for shift in shifts]


def on_device(acts, grads, proj_act, proj_grad, queries):
    size = lax.axis_size("dp")
    tok_total = acts.shape[0] * size
    far, near, core = gather_stages(size)
    first, second = sum_rounds(size)

    pieces = exchanged([queries], size, *far, backwards=True)
    act_t, grad_t, own = project(acts, grads, proj_act, proj_grad)
    *pieces, own = lax.optimization_barrier((*pieces, own))
    pieces = exchanged(pieces, size, *near)
    own = functools.reduce(jnp.add, exchanged([own], size, *first))
    terms = exchanged([own], size, *second)
    *both, = lax.optimization_barrier((*pieces, *terms))
    pieces, terms = both[: len(pieces)], both[len(pieces) :]
    pieces = exchanged(pieces, size, *core)
    moved = precondition(tok_total, terms, act_t, grad_t)
    return score(size, moved, pieces)


def solution(mesh):
    in_specs = (P(("parts", "dp"), None), P(("parts", "dp"), None), P(), P(), P("dp", None))
    out_specs = P(("parts", "dp"), None)
    return jax.shard_map(
        on_device, mesh=mesh, in_specs=in_specs, out_specs=out_specs, check_vma=False
    )
```

```python
import functools

import jax
import jax.numpy as jnp
from jax import lax
from jax.experimental import pallas as pl
from jax.experimental.pallas import tpu as pltpu
from jax.sharding import PartitionSpec as P

DAMP = 0.1
HIGHEST = lax.Precision.HIGHEST
COPY_ROWS = 128
IN_FLIGHT = 5
TOKENS_AT_ONCE = 256


def places(factor):
    return [lax.broadcasted_iota(jnp.int32, (factor, factor), axis) for axis in (0, 1)]


def packed(act, grad):
    factor = act.shape[0]
    row_at, lane = places(factor)
    mixed = jnp.where(row_at <= lane, act, grad)
    diagonal = jnp.sum(jnp.where(row_at == lane, grad, 0.0), axis=0, keepdims=True)
    last = jnp.broadcast_to(jnp.concatenate([diagonal, diagonal], axis=1), (8, 2 * factor))
    half = factor // 2
    return jnp.concatenate([jnp.concatenate([mixed[:half], mixed[half:]], axis=1), last], axis=0)


def unpacked(value):
    factor = value.shape[1] // 2
    half = factor // 2
    row_at = lax.broadcasted_iota(jnp.int32, (factor, 2 * factor), 0)
    lane = lax.broadcasted_iota(jnp.int32, (factor, 2 * factor), 1)
    left_half = lane < factor
    inner = jnp.where(left_half, lane, lane - factor)
    rolled = pltpu.roll(value[:half], factor, axis=1)
    mixed = jnp.concatenate(
        [
            jnp.where(left_half[:half], value[:half], rolled),
            jnp.where(left_half[:half], rolled, value[:half]),
        ],
        axis=0,
    )
    flipped = jnp.concatenate([mixed, mixed], axis=0).T[:factor]
    diagonal = jnp.broadcast_to(value[half : half + 1], mixed.shape)
    below = jnp.where(row_at > inner, mixed, jnp.where(row_at < inner, flipped, diagonal))
    return jnp.where(left_half, jnp.where(row_at <= inner, mixed, flipped), below)


def project_kernel(
    acts, grads, weight_act, weight_grad, act_t, grad_t, cov, tok_buf, weight_buf, weight_t, tok_sems, weight_sems
):
    width = weight_act.shape[1]
    n_parts = acts.shape[0] // COPY_ROWS
    weight_copies = [
        pltpu.make_async_copy(src, weight_buf.at[at], weight_sems.at[at])
        for at, src in enumerate((weight_act, weight_grad))
    ]
    tok_copies = [
        [
            pltpu.make_async_copy(
                src.at[pl.ds(part * COPY_ROWS, COPY_ROWS), :],
                tok_buf.at[at, pl.ds(part * COPY_ROWS, COPY_ROWS), :],
                tok_sems.at[at, part],
            )
            for part in range(n_parts)
        ]
        for at, src in enumerate((acts, grads))
    ]
    queue = [weight_copies[0], *tok_copies[0], *tok_copies[1]]
    queue.insert(3, weight_copies[1])

    def start_next(many):
        for copy in queue[:many]:
            copy.start()
        del queue[:many]

    def turned(at):
        for first in range(0, width, 512):
            weight_t[at, first : first + 512, :] = weight_buf[at, :, first : first + 512].T

    steps = [(at, part, min(2, n_parts - part)) for at in range(2) for part in range(0, n_parts, 2)]
    last_act = len(steps) // 2 - 1
    blocks = [[], []]
    grams = [[], []]

    def add_gram(at):
        flipped, plain = [jnp.concatenate(parts, axis=axis) for parts, axis in zip(zip(*blocks[at]), (1, 0))]
        grams[at].append(jnp.dot(flipped, plain, precision=HIGHEST, preferred_element_type=jnp.float32))
        blocks[at].clear()

    start_next(1 + IN_FLIGHT)
    weight_copies[0].wait()
    turned(0)
    for step, (at, part, many) in enumerate(steps):
        if step == last_act:
            weight_copies[1].wait()
            start_next(1)
            turned(1)
        if step == last_act + 1:
            add_gram(0)
        if step == len(steps) - 1:
            add_gram(1)
        for copy in tok_copies[at][part : part + many]:
            copy.wait()
            start_next(1)
        rows = slice(part * COPY_ROWS, (part + many) * COPY_ROWS)
        block = jnp.dot(tok_buf[at, rows, :], weight_t[at], preferred_element_type=jnp.float32)
        flipped = block.T
        (act_t, grad_t)[at][:, rows] = flipped
        blocks[at].append((flipped, block))
    add_gram(1)
    cov[...] = packed(*[functools.reduce(jnp.add, terms) for terms in grams])


def project(acts, grads, proj_act, proj_grad):
    tok_rows, width = acts.shape
    factor = proj_act.shape[1]
    operands = [
        pltpu.with_memory_space_constraint(value, pltpu.HBM) for value in (acts, grads, proj_act.T, proj_grad.T)
    ]
    return pl.pallas_call(
        project_kernel,
        out_shape=(
            jax.ShapeDtypeStruct((factor, tok_rows), jnp.float32),
            jax.ShapeDtypeStruct((factor, tok_rows), jnp.float32),
            jax.ShapeDtypeStruct((factor // 2 + 8, 2 * factor), jnp.float32),
        ),
        in_specs=[pl.BlockSpec(memory_space=pltpu.HBM)] * 4,
        out_specs=[pl.BlockSpec(memory_space=pltpu.VMEM)] * 3,
        scratch_shapes=[
            pltpu.VMEM((2, tok_rows, width), acts.dtype),
            pltpu.VMEM((2, factor, width), proj_act.dtype),
            pltpu.VMEM((2, width, factor), proj_act.dtype),
            pltpu.SemaphoreType.DMA((2, tok_rows // COPY_ROWS)),
            pltpu.SemaphoreType.DMA((2,)),
        ],
        compiler_params=pltpu.CompilerParams(vmem_limit_bytes=24 * 2**20),
        cost_estimate=pl.CostEstimate(
            flops=4 * tok_rows * width * factor, bytes_accessed=4 * tok_rows * width, transcendentals=0
        ),
        name="project",
    )(*operands)


def inverse_pair(both):
    factor = both.shape[0]
    tile = (8, both.shape[1])
    lane = lax.broadcasted_iota(jnp.int32, tile, 1)
    row_at = lax.broadcasted_iota(jnp.int32, tile, 0)
    left_half = lane < factor
    inner = jnp.where(left_half, lane, lane - factor)
    parts = [both[at : at + 8, :] for at in range(0, factor, 8)]

    def column(part, at):
        index = jnp.where(left_half, at, factor + at)
        return jnp.take_along_axis(part, index, axis=1, mode="promise_in_bounds")

    def row(part, at):
        return jnp.broadcast_to(part[at : at + 1, :], tile)

    for k in range(0, factor, 4):
        home, off = divmod(k, 8)
        columns = [[column(part, k + a) for part in parts] for a in range(4)]
        pivot = [[row(columns[b][home], off + a) if a <= b else None for b in range(4)] for a in range(4)]
        p00, p01, p02, p03 = pivot[0]
        _, p11, p12, p13 = pivot[1]
        _, _, p22, p23 = pivot[2]
        p33 = pivot[3][3]
        on_block = (inner >= k) & (inner < k + 4)
        r0, r1, r2, r3 = [
            jnp.where(on_block, jnp.where(inner == k + a, 1.0, 0.0), row(parts[home], off + a)) for a in range(4)
        ]
        scale = 1.0 / (p00 * p11 - p01 * p01)
        m02 = p11 * p02 - p01 * p12
        m03 = p11 * p03 - p01 * p13
        m12 = p00 * p12 - p01 * p02
        m13 = p00 * p13 - p01 * p03
        z0 = p11 * r0 - p01 * r1
        z1 = p00 * r1 - p01 * r0
        s22 = p22 - scale * (p02 * m02 + p12 * m12)
        s23 = p23 - scale * (p02 * m03 + p12 * m13)
        s33 = p33 - scale * (p03 * m03 + p13 * m13)
        t2 = r2 - scale * (p02 * z0 + p12 * z1)
        t3 = r3 - scale * (p03 * z0 + p13 * z1)
        scale_s = 1.0 / (s22 * s33 - s23 * s23)
        w2 = scale_s * (s33 * t2 - s23 * t3)
        w3 = scale_s * (s22 * t3 - s23 * t2)
        w0 = scale * (z0 - (m02 * w2 + m03 * w3))
        w1 = scale * (z1 - (m12 * w2 + m13 * w3))
        solved = (w0, w1, w2, w3)
        for m, part in enumerate(parts):
            change = (columns[0][m] * w0 + columns[1][m] * w1) + (columns[2][m] * w2 + columns[3][m] * w3)
            part = jnp.where(on_block, 0.0, part) - change
            if m == home:
                for a in range(4):
                    part = jnp.where(row_at == off + a, solved[a], part)
            parts[m] = part
    return jnp.concatenate(parts, axis=0)


def precondition_kernel(tok_total, n_terms, *refs):
    terms, (act_t, grad_t, moved) = refs[:n_terms], refs[n_terms:]
    both = terms[0][...]
    for term in terms[1:]:
        both = both + term[...]
    both = unpacked(both)
    factor = both.shape[0]
    lane = lax.broadcasted_iota(jnp.int32, both.shape, 1)
    row_at = lax.broadcasted_iota(jnp.int32, both.shape, 0)
    left_half = lane < factor
    inner = jnp.where(left_half, lane, lane - factor)
    both = both * (1.0 / tok_total) + jnp.where(inner == row_at, DAMP, 0.0)
    both = inverse_pair(both)
    blocks = jnp.concatenate(
        [jnp.where(left_half, both, 0.0), jnp.where(left_half, 0.0, both)], axis=0
    )
    proj_t = jnp.concatenate([act_t[...], grad_t[...]], axis=0)
    moved[...] = jnp.dot(blocks, proj_t, precision=HIGHEST, preferred_element_type=jnp.float32)


def precondition(tok_total, terms, act_t, grad_t):
    factor, tok_rows = act_t.shape
    n_terms = len(terms)
    return pl.pallas_call(
        functools.partial(precondition_kernel, tok_total, n_terms),
        out_shape=jax.ShapeDtypeStruct((2 * factor, tok_rows), jnp.float32),
        in_specs=[pl.BlockSpec(memory_space=pltpu.VMEM)] * (n_terms + 2),
        out_specs=pl.BlockSpec(memory_space=pltpu.VMEM),
        compiler_params=pltpu.CompilerParams(vmem_limit_bytes=24 * 2**20),
        cost_estimate=pl.CostEstimate(
            flops=1600 * factor * factor * tok_rows, bytes_accessed=16 * factor * tok_rows, transcendentals=0
        ),
        name="precondition",
    )(*terms, act_t, grad_t)


def score_kernel(size, n_pieces, moved, *refs):
    queries, (scores, ordered, result, sems) = refs[:n_pieces], refs[n_pieces:]
    factor = moved.shape[0] // 2
    owners = owners_of(lax.axis_index("dp"), size)
    group = 2
    copies = []
    for part, begin in enumerate(range(0, moved.shape[1], TOKENS_AT_ONCE)):
        tokens = slice(begin, begin + TOKENS_AT_ONCE)
        act_side = moved[:factor, tokens]

        def split(first):
            outer = jnp.concatenate(
                [act_side * moved[factor + i : factor + i + 1, tokens] for i in range(first, first + group)], axis=0
            )
            high = outer.astype(jnp.bfloat16)
            low = (outer - high.astype(jnp.float32)).astype(jnp.bfloat16)
            return jnp.concatenate([high, low], axis=0)

        total = None
        later = split(0)
        for first in range(0, factor, group):
            both = later
            if first + group < factor:
                later = split(first + group)
            columns = slice(first * factor, (first + group) * factor)
            values = jnp.concatenate([piece[:, columns] for piece in queries], axis=0)
            term = jnp.dot(jnp.concatenate([values, values], axis=1), both, preferred_element_type=jnp.float32)
            total = term if total is None else total + term
        rows = total.shape[0] // size
        for at, owner in enumerate(owners):
            place = pl.ds(pl.multiple_of(owner * rows, rows), rows)
            ordered[part, place, :] = total[at * rows : (at + 1) * rows, :]
        result[tokens, :] = ordered[part].T
        copies.append(
            pltpu.make_async_copy(
                result.at[pl.ds(begin, TOKENS_AT_ONCE), :], scores.at[pl.ds(begin, TOKENS_AT_ONCE), :], sems.at[part]
            )
        )
        copies[-1].start()
    for copy in copies:
        copy.wait()


def score(size, moved, queries):
    tok_rows = moved.shape[1]
    n_queries = sum(piece.shape[0] for piece in queries)
    n_pieces = len(queries)
    n_parts = tok_rows // TOKENS_AT_ONCE
    return pl.pallas_call(
        functools.partial(score_kernel, size, n_pieces),
        out_shape=jax.ShapeDtypeStruct((tok_rows, n_queries), jnp.float32),
        in_specs=[pl.BlockSpec(memory_space=pltpu.VMEM)] * (1 + n_pieces),
        out_specs=pl.BlockSpec(memory_space=pl.ANY),
        scratch_shapes=[
            pltpu.VMEM((n_parts, n_queries, TOKENS_AT_ONCE), jnp.float32),
            pltpu.VMEM((tok_rows, n_queries), jnp.float32),
            pltpu.SemaphoreType.DMA((n_parts,)),
        ],
        compiler_params=pltpu.CompilerParams(vmem_limit_bytes=32 * 2**20),
        name="score",
    )(moved, *queries)


def gather_stages(size):
    core = 2 if size % 2 == 0 else 1
    rest = size // core
    near = max(d for d in range(1, rest + 1) if rest % d == 0 and d * d <= rest)
    return [(core * near, rest // near), (core, near), (1, core)]


def sum_rounds(size):
    (stride, radix), *_ = gather_stages(size)
    return [(1, stride), (stride, radix)]


def after(value, other):
    return lax.optimization_barrier((value, other))[0]


def partner(digit, radix, shift):
    return digit ^ shift if radix & (radix - 1) == 0 else (digit + shift) % radix


def swapped(value, size, stride, radix, shift):
    perm = []
    for at in range(size):
        digit = at // stride % radix
        perm.append((at, at + (partner(digit, radix, shift) - digit) * stride))
    return lax.ppermute(value, "dp", perm)


def owners_of(me, size):
    owners = [me]
    for at, (stride, radix) in enumerate(gather_stages(size)):
        digit = lax.rem(lax.div(me, stride), radix)
        shifts = [0, *(range(radix - 1, 0, -1) if at == 0 else range(1, radix))]
        back = [shift if radix & (radix - 1) == 0 else (radix - shift) % radix for shift in shifts]
        steps = [(partner(digit, radix, shift) - digit) * stride for shift in back]
        owners = [owner + step for step in steps for owner in owners]
    return owners


def exchanged(held, size, stride, radix, backwards=False):
    mine = held[0] if len(held) == 1 else jnp.concatenate(held, axis=0)
    shifts = range(radix - 1, 0, -1) if backwards else range(1, radix)
    return [mine] + [swapped(mine, size, stride, radix, shift) for shift in shifts]


def on_device(acts, grads, proj_act, proj_grad, queries):
    size = lax.axis_size("dp")
    tok_total = acts.shape[0] * size
    far, near, core = gather_stages(size)
    first, second = sum_rounds(size)

    pieces = exchanged([queries], size, *far, backwards=True)
    act_t, grad_t, own = project(acts, grads, proj_act, proj_grad)
    *pieces, own = lax.optimization_barrier((*pieces, own))
    pieces = exchanged(pieces, size, *near)
    own = functools.reduce(jnp.add, exchanged([own], size, *first))
    terms = exchanged([own], size, *second)
    *both, = lax.optimization_barrier((*pieces, *terms))
    pieces, terms = both[: len(pieces)], both[len(pieces) :]
    pieces = exchanged(pieces, size, *core)
    moved = precondition(tok_total, terms, act_t, grad_t)
    return score(size, moved, pieces)


def solution(mesh):
    in_specs = (P(("parts", "dp"), None), P(("parts", "dp"), None), P(), P(), P("dp", None))
    out_specs = P(("parts", "dp"), None)
    return jax.shard_map(
        on_device, mesh=mesh, in_specs=in_specs, out_specs=out_specs, check_vma=False
    )
```

```python
import functools

import jax
import jax.numpy as jnp
from jax import lax
from jax.experimental import pallas as pl
from jax.experimental.pallas import tpu as pltpu
from jax.sharding import PartitionSpec as P

DAMP = 0.1
HIGHEST = lax.Precision.HIGHEST
COPY_ROWS = 128
IN_FLIGHT = 5
TOKENS_AT_ONCE = 256


def places(factor):
    return [lax.broadcasted_iota(jnp.int32, (factor, factor), axis) for axis in (0, 1)]


def packed(act, grad):
    factor = act.shape[0]
    row_at, lane = places(factor)
    mixed = jnp.where(row_at <= lane, act, grad)
    diagonal = jnp.sum(jnp.where(row_at == lane, grad, 0.0), axis=0, keepdims=True)
    last = jnp.broadcast_to(jnp.concatenate([diagonal, diagonal], axis=1), (8, 2 * factor))
    half = factor // 2
    return jnp.concatenate([jnp.concatenate([mixed[:half], mixed[half:]], axis=1), last], axis=0)


def unpacked(value):
    factor = value.shape[1] // 2
    half = factor // 2
    row_at = lax.broadcasted_iota(jnp.int32, (factor, 2 * factor), 0)
    lane = lax.broadcasted_iota(jnp.int32, (factor, 2 * factor), 1)
    left_half = lane < factor
    inner = jnp.where(left_half, lane, lane - factor)
    rolled = pltpu.roll(value[:half], factor, axis=1)
    mixed = jnp.concatenate(
        [
            jnp.where(left_half[:half], value[:half], rolled),
            jnp.where(left_half[:half], rolled, value[:half]),
        ],
        axis=0,
    )
    flipped = jnp.concatenate([mixed, mixed], axis=0).T[:factor]
    diagonal = jnp.broadcast_to(value[half : half + 1], mixed.shape)
    below = jnp.where(row_at > inner, mixed, jnp.where(row_at < inner, flipped, diagonal))
    return jnp.where(left_half, jnp.where(row_at <= inner, mixed, flipped), below)


def project_kernel(
    acts, grads, weight_act, weight_grad, act_t, grad_t, cov, tok_buf, weight_buf, weight_t, tok_sems, weight_sems
):
    width = weight_act.shape[1]
    n_parts = acts.shape[0] // COPY_ROWS
    weight_copies = [
        pltpu.make_async_copy(src, weight_buf.at[at], weight_sems.at[at])
        for at, src in enumerate((weight_act, weight_grad))
    ]
    tok_copies = [
        [
            pltpu.make_async_copy(
                src.at[pl.ds(part * COPY_ROWS, COPY_ROWS), :],
                tok_buf.at[at, pl.ds(part * COPY_ROWS, COPY_ROWS), :],
                tok_sems.at[at, part],
            )
            for part in range(n_parts)
        ]
        for at, src in enumerate((acts, grads))
    ]
    queue = [weight_copies[0], *tok_copies[0], *tok_copies[1]]
    queue.insert(3, weight_copies[1])

    def start_next(many):
        for copy in queue[:many]:
            copy.start()
        del queue[:many]

    def turned(at):
        for first in range(0, width, 512):
            weight_t[at, first : first + 512, :] = weight_buf[at, :, first : first + 512].T

    steps = [(at, part, min(2, n_parts - part)) for at in range(2) for part in range(0, n_parts, 2)]
    last_act = len(steps) // 2 - 1
    blocks = [[], []]
    grams = [[], []]

    def add_gram(at):
        flipped, plain = [jnp.concatenate(parts, axis=axis) for parts, axis in zip(zip(*blocks[at]), (1, 0))]
        grams[at].append(jnp.dot(flipped, plain, precision=HIGHEST, preferred_element_type=jnp.float32))
        blocks[at].clear()

    start_next(1 + IN_FLIGHT)
    weight_copies[0].wait()
    turned(0)
    for step, (at, part, many) in enumerate(steps):
        for copy in tok_copies[at][part : part + many]:
            copy.wait()
            start_next(1)
        if step == last_act:
            weight_copies[1].wait()
            start_next(1)
        rows = slice(part * COPY_ROWS, (part + many) * COPY_ROWS)
        block = jnp.dot(tok_buf[at, rows, :], weight_t[at], preferred_element_type=jnp.float32)
        if step == last_act:
            turned(1)
        if step == last_act + 1:
            add_gram(0)
        if step == len(steps) - 1:
            add_gram(1)
        flipped = block.T
        (act_t, grad_t)[at][:, rows] = flipped
        blocks[at].append((flipped, block))
    add_gram(1)
    cov[...] = packed(*[functools.reduce(jnp.add, terms) for terms in grams])


def project(acts, grads, proj_act, proj_grad):
    tok_rows, width = acts.shape
    factor = proj_act.shape[1]
    operands = [
        pltpu.with_memory_space_constraint(value, pltpu.HBM) for value in (acts, grads, proj_act.T, proj_grad.T)
    ]
    return pl.pallas_call(
        project_kernel,
        out_shape=(
            jax.ShapeDtypeStruct((factor, tok_rows), jnp.float32),
            jax.ShapeDtypeStruct((factor, tok_rows), jnp.float32),
            jax.ShapeDtypeStruct((factor // 2 + 8, 2 * factor), jnp.float32),
        ),
        in_specs=[pl.BlockSpec(memory_space=pltpu.HBM)] * 4,
        out_specs=[pl.BlockSpec(memory_space=pltpu.VMEM)] * 3,
        scratch_shapes=[
            pltpu.VMEM((2, tok_rows, width), acts.dtype),
            pltpu.VMEM((2, factor, width), proj_act.dtype),
            pltpu.VMEM((2, width, factor), proj_act.dtype),
            pltpu.SemaphoreType.DMA((2, tok_rows // COPY_ROWS)),
            pltpu.SemaphoreType.DMA((2,)),
        ],
        compiler_params=pltpu.CompilerParams(vmem_limit_bytes=24 * 2**20),
        cost_estimate=pl.CostEstimate(
            flops=4 * tok_rows * width * factor, bytes_accessed=4 * tok_rows * width, transcendentals=0
        ),
        name="project",
    )(*operands)


def inverse_pair(both):
    factor = both.shape[0]
    tile = (8, both.shape[1])
    lane = lax.broadcasted_iota(jnp.int32, tile, 1)
    row_at = lax.broadcasted_iota(jnp.int32, tile, 0)
    left_half = lane < factor
    inner = jnp.where(left_half, lane, lane - factor)
    parts = [both[at : at + 8, :] for at in range(0, factor, 8)]

    def column(part, at):
        index = jnp.where(left_half, at, factor + at)
        return jnp.take_along_axis(part, index, axis=1, mode="promise_in_bounds")

    def row(part, at):
        return jnp.broadcast_to(part[at : at + 1, :], tile)

    for k in range(0, factor, 4):
        home, off = divmod(k, 8)
        columns = [[column(part, k + a) for part in parts] for a in range(4)]
        pivot = [[row(columns[b][home], off + a) if a <= b else None for b in range(4)] for a in range(4)]
        p00, p01, p02, p03 = pivot[0]
        _, p11, p12, p13 = pivot[1]
        _, _, p22, p23 = pivot[2]
        p33 = pivot[3][3]
        on_block = (inner >= k) & (inner < k + 4)
        r0, r1, r2, r3 = [
            jnp.where(on_block, jnp.where(inner == k + a, 1.0, 0.0), row(parts[home], off + a)) for a in range(4)
        ]
        scale = 1.0 / (p00 * p11 - p01 * p01)
        m02 = p11 * p02 - p01 * p12
        m03 = p11 * p03 - p01 * p13
        m12 = p00 * p12 - p01 * p02
        m13 = p00 * p13 - p01 * p03
        z0 = p11 * r0 - p01 * r1
        z1 = p00 * r1 - p01 * r0
        s22 = p22 - scale * (p02 * m02 + p12 * m12)
        s23 = p23 - scale * (p02 * m03 + p12 * m13)
        s33 = p33 - scale * (p03 * m03 + p13 * m13)
        t2 = r2 - scale * (p02 * z0 + p12 * z1)
        t3 = r3 - scale * (p03 * z0 + p13 * z1)
        scale_s = 1.0 / (s22 * s33 - s23 * s23)
        w2 = scale_s * (s33 * t2 - s23 * t3)
        w3 = scale_s * (s22 * t3 - s23 * t2)
        w0 = scale * (z0 - (m02 * w2 + m03 * w3))
        w1 = scale * (z1 - (m12 * w2 + m13 * w3))
        solved = (w0, w1, w2, w3)
        for m, part in enumerate(parts):
            change = (columns[0][m] * w0 + columns[1][m] * w1) + (columns[2][m] * w2 + columns[3][m] * w3)
            part = jnp.where(on_block, 0.0, part) - change
            if m == home:
                for a in range(4):
                    part = jnp.where(row_at == off + a, solved[a], part)
            parts[m] = part
    return jnp.concatenate(parts, axis=0)


def precondition_kernel(tok_total, n_terms, *refs):
    terms, (act_t, grad_t, moved) = refs[:n_terms], refs[n_terms:]
    both = terms[0][...]
    for term in terms[1:]:
        both = both + term[...]
    both = unpacked(both)
    factor = both.shape[0]
    lane = lax.broadcasted_iota(jnp.int32, both.shape, 1)
    row_at = lax.broadcasted_iota(jnp.int32, both.shape, 0)
    left_half = lane < factor
    inner = jnp.where(left_half, lane, lane - factor)
    both = both * (1.0 / tok_total) + jnp.where(inner == row_at, DAMP, 0.0)
    both = inverse_pair(both)
    blocks = jnp.concatenate(
        [jnp.where(left_half, both, 0.0), jnp.where(left_half, 0.0, both)], axis=0
    )
    proj_t = jnp.concatenate([act_t[...], grad_t[...]], axis=0)
    moved[...] = jnp.dot(blocks, proj_t, precision=HIGHEST, preferred_element_type=jnp.float32)


def precondition(tok_total, terms, act_t, grad_t):
    factor, tok_rows = act_t.shape
    n_terms = len(terms)
    return pl.pallas_call(
        functools.partial(precondition_kernel, tok_total, n_terms),
        out_shape=jax.ShapeDtypeStruct((2 * factor, tok_rows), jnp.float32),
        in_specs=[pl.BlockSpec(memory_space=pltpu.VMEM)] * (n_terms + 2),
        out_specs=pl.BlockSpec(memory_space=pltpu.VMEM),
        compiler_params=pltpu.CompilerParams(vmem_limit_bytes=24 * 2**20),
        cost_estimate=pl.CostEstimate(
            flops=1600 * factor * factor * tok_rows, bytes_accessed=16 * factor * tok_rows, transcendentals=0
        ),
        name="precondition",
    )(*terms, act_t, grad_t)


def score_kernel(size, n_pieces, moved, *refs):
    queries, (scores, ordered, result, sems) = refs[:n_pieces], refs[n_pieces:]
    factor = moved.shape[0] // 2
    owners = owners_of(lax.axis_index("dp"), size)
    group = 2
    copies = []
    for part, begin in enumerate(range(0, moved.shape[1], TOKENS_AT_ONCE)):
        tokens = slice(begin, begin + TOKENS_AT_ONCE)
        act_side = moved[:factor, tokens]

        def split(first):
            outer = jnp.concatenate(
                [act_side * moved[factor + i : factor + i + 1, tokens] for i in range(first, first + group)], axis=0
            )
            high = outer.astype(jnp.bfloat16)
            low = (outer - high.astype(jnp.float32)).astype(jnp.bfloat16)
            return jnp.concatenate([high, low], axis=0)

        total = None
        later = split(0)
        for first in range(0, factor, group):
            both = later
            if first + group < factor:
                later = split(first + group)
            columns = slice(first * factor, (first + group) * factor)
            values = jnp.concatenate([piece[:, columns] for piece in queries], axis=0)
            term = jnp.dot(jnp.concatenate([values, values], axis=1), both, preferred_element_type=jnp.float32)
            total = term if total is None else total + term
        rows = total.shape[0] // size
        for at, owner in enumerate(owners):
            place = pl.ds(pl.multiple_of(owner * rows, rows), rows)
            ordered[part, place, :] = total[at * rows : (at + 1) * rows, :]
        result[tokens, :] = ordered[part].T
        copies.append(
            pltpu.make_async_copy(
                result.at[pl.ds(begin, TOKENS_AT_ONCE), :], scores.at[pl.ds(begin, TOKENS_AT_ONCE), :], sems.at[part]
            )
        )
        copies[-1].start()
    for copy in copies:
        copy.wait()


def score(size, moved, queries):
    tok_rows = moved.shape[1]
    n_queries = sum(piece.shape[0] for piece in queries)
    n_pieces = len(queries)
    n_parts = tok_rows // TOKENS_AT_ONCE
    return pl.pallas_call(
        functools.partial(score_kernel, size, n_pieces),
        out_shape=jax.ShapeDtypeStruct((tok_rows, n_queries), jnp.float32),
        in_specs=[pl.BlockSpec(memory_space=pltpu.VMEM)] * (1 + n_pieces),
        out_specs=pl.BlockSpec(memory_space=pl.ANY),
        scratch_shapes=[
            pltpu.VMEM((n_parts, n_queries, TOKENS_AT_ONCE), jnp.float32),
            pltpu.VMEM((tok_rows, n_queries), jnp.float32),
            pltpu.SemaphoreType.DMA((n_parts,)),
        ],
        compiler_params=pltpu.CompilerParams(vmem_limit_bytes=32 * 2**20),
        name="score",
    )(moved, *queries)


def gather_stages(size):
    core = 2 if size % 2 == 0 else 1
    rest = size // core
    near = max(d for d in range(1, rest + 1) if rest % d == 0 and d * d <= rest)
    return [(core * near, rest // near), (core, near), (1, core)]


def sum_rounds(size):
    (stride, radix), *_ = gather_stages(size)
    return [(1, stride), (stride, radix)]


def after(value, other):
    return lax.optimization_barrier((value, other))[0]


def partner(digit, radix, shift):
    return digit ^ shift if radix & (radix - 1) == 0 else (digit + shift) % radix


def swapped(value, size, stride, radix, shift):
    perm = []
    for at in range(size):
        digit = at // stride % radix
        perm.append((at, at + (partner(digit, radix, shift) - digit) * stride))
    return lax.ppermute(value, "dp", perm)


def owners_of(me, size):
    owners = [me]
    for at, (stride, radix) in enumerate(gather_stages(size)):
        digit = lax.rem(lax.div(me, stride), radix)
        shifts = [0, *range(2, radix), 1] if at == 0 else range(radix)
        back = [shift if radix & (radix - 1) == 0 else (radix - shift) % radix for shift in shifts]
        steps = [(partner(digit, radix, shift) - digit) * stride for shift in back]
        owners = [owner + step for step in steps for owner in owners]
    return owners


def exchanged(held, size, stride, radix, near_last=False):
    mine = held[0] if len(held) == 1 else jnp.concatenate(held, axis=0)
    shifts = [*range(2, radix), 1] if near_last else range(1, radix)
    return [mine] + [swapped(mine, size, stride, radix, shift) for shift in shifts]


def on_device(acts, grads, proj_act, proj_grad, queries):
    size = lax.axis_size("dp")
    tok_total = acts.shape[0] * size
    far, near, core = gather_stages(size)
    first, second = sum_rounds(size)

    pieces = exchanged([queries], size, *far, near_last=True)
    act_t, grad_t, own = project(acts, grads, proj_act, proj_grad)
    *pieces, own = lax.optimization_barrier((*pieces, own))
    pieces = exchanged(pieces, size, *near)
    own = functools.reduce(jnp.add, exchanged([own], size, *first))
    terms = exchanged([own], size, *second)
    *both, = lax.optimization_barrier((*pieces, *terms))
    pieces, terms = both[: len(pieces)], both[len(pieces) :]
    pieces = exchanged(pieces, size, *core)
    moved = precondition(tok_total, terms, act_t, grad_t)
    return score(size, moved, pieces)


def solution(mesh):
    in_specs = (P(("parts", "dp"), None), P(("parts", "dp"), None), P(), P(), P("dp", None))
    out_specs = P(("parts", "dp"), None)
    return jax.shard_map(
        on_device, mesh=mesh, in_specs=in_specs, out_specs=out_specs, check_vma=False
    )
```

```python
import functools

import jax
import jax.numpy as jnp
from jax import lax
from jax.experimental import pallas as pl
from jax.experimental.pallas import tpu as pltpu
from jax.sharding import PartitionSpec as P

DAMP = 0.1
HIGHEST = lax.Precision.HIGHEST
COPY_ROWS = 128
IN_FLIGHT = 5
TOKENS_AT_ONCE = 256


def places(factor):
    return [lax.broadcasted_iota(jnp.int32, (factor, factor), axis) for axis in (0, 1)]


def packed(act, grad):
    factor = act.shape[0]
    row_at, lane = places(factor)
    mixed = jnp.where(row_at <= lane, act, grad)
    diagonal = jnp.sum(jnp.where(row_at == lane, grad, 0.0), axis=0, keepdims=True)
    last = jnp.broadcast_to(jnp.concatenate([diagonal, diagonal], axis=1), (8, 2 * factor))
    half = factor // 2
    return jnp.concatenate([jnp.concatenate([mixed[:half], mixed[half:]], axis=1), last], axis=0)


def unpacked(value):
    factor = value.shape[1] // 2
    half = factor // 2
    row_at = lax.broadcasted_iota(jnp.int32, (factor, 2 * factor), 0)
    lane = lax.broadcasted_iota(jnp.int32, (factor, 2 * factor), 1)
    left_half = lane < factor
    inner = jnp.where(left_half, lane, lane - factor)
    rolled = pltpu.roll(value[:half], factor, axis=1)
    mixed = jnp.concatenate(
        [
            jnp.where(left_half[:half], value[:half], rolled),
            jnp.where(left_half[:half], rolled, value[:half]),
        ],
        axis=0,
    )
    flipped = jnp.concatenate([mixed, mixed], axis=0).T[:factor]
    diagonal = jnp.broadcast_to(value[half : half + 1], mixed.shape)
    below = jnp.where(row_at > inner, mixed, jnp.where(row_at < inner, flipped, diagonal))
    return jnp.where(left_half, jnp.where(row_at <= inner, mixed, flipped), below)


def project_kernel(
    acts, grads, weight_act, weight_grad, act_t, grad_t, cov, tok_buf, weight_buf, weight_t, tok_sems, weight_sems
):
    width = weight_act.shape[1]
    n_parts = acts.shape[0] // COPY_ROWS
    weight_copies = [
        pltpu.make_async_copy(src, weight_buf.at[at], weight_sems.at[at])
        for at, src in enumerate((weight_act, weight_grad))
    ]
    tok_copies = [
        [
            pltpu.make_async_copy(
                src.at[pl.ds(part * COPY_ROWS, COPY_ROWS), :],
                tok_buf.at[at, pl.ds(part * COPY_ROWS, COPY_ROWS), :],
                tok_sems.at[at, part],
            )
            for part in range(n_parts)
        ]
        for at, src in enumerate((acts, grads))
    ]
    queue = [weight_copies[0], *tok_copies[0], *tok_copies[1]]
    queue.insert(3, weight_copies[1])

    def start_next(many):
        for copy in queue[:many]:
            copy.start()
        del queue[:many]

    def turned(at):
        for first in range(0, width, 512):
            weight_t[at, first : first + 512, :] = weight_buf[at, :, first : first + 512].T

    steps = [(at, part, min(2, n_parts - part)) for at in range(2) for part in range(0, n_parts, 2)]
    last_act = len(steps) // 2 - 1
    blocks = [[], []]
    grams = [[], []]

    def add_gram(at):
        flipped, plain = [jnp.concatenate(parts, axis=axis) for parts, axis in zip(zip(*blocks[at]), (1, 0))]
        grams[at].append(jnp.dot(flipped, plain, precision=HIGHEST, preferred_element_type=jnp.float32))
        blocks[at].clear()

    start_next(1 + IN_FLIGHT)
    weight_copies[0].wait()
    turned(0)
    for step, (at, part, many) in enumerate(steps):
        for copy in tok_copies[at][part : part + many]:
            copy.wait()
            start_next(1)
        if step == last_act:
            weight_copies[1].wait()
            start_next(1)
        rows = slice(part * COPY_ROWS, (part + many) * COPY_ROWS)
        block = jnp.dot(tok_buf[at, rows, :], weight_t[at], preferred_element_type=jnp.float32)
        if step == last_act:
            turned(1)
        if step == last_act + 1:
            add_gram(0)
        if step == len(steps) - 1:
            add_gram(1)
        flipped = block.T
        (act_t, grad_t)[at][:, rows] = flipped
        blocks[at].append((flipped, block))
    add_gram(1)
    cov[...] = packed(*[functools.reduce(jnp.add, terms) for terms in grams])


def project(acts, grads, proj_act, proj_grad):
    tok_rows, width = acts.shape
    factor = proj_act.shape[1]
    operands = [
        pltpu.with_memory_space_constraint(value, pltpu.HBM) for value in (acts, grads, proj_act.T, proj_grad.T)
    ]
    return pl.pallas_call(
        project_kernel,
        out_shape=(
            jax.ShapeDtypeStruct((factor, tok_rows), jnp.float32),
            jax.ShapeDtypeStruct((factor, tok_rows), jnp.float32),
            jax.ShapeDtypeStruct((factor // 2 + 8, 2 * factor), jnp.float32),
        ),
        in_specs=[pl.BlockSpec(memory_space=pltpu.HBM)] * 4,
        out_specs=[pl.BlockSpec(memory_space=pltpu.VMEM)] * 3,
        scratch_shapes=[
            pltpu.VMEM((2, tok_rows, width), acts.dtype),
            pltpu.VMEM((2, factor, width), proj_act.dtype),
            pltpu.VMEM((2, width, factor), proj_act.dtype),
            pltpu.SemaphoreType.DMA((2, tok_rows // COPY_ROWS)),
            pltpu.SemaphoreType.DMA((2,)),
        ],
        compiler_params=pltpu.CompilerParams(vmem_limit_bytes=24 * 2**20),
        cost_estimate=pl.CostEstimate(
            flops=4 * tok_rows * width * factor, bytes_accessed=4 * tok_rows * width, transcendentals=0
        ),
        name="project",
    )(*operands)


def inverse_pair(both):
    factor = both.shape[0]
    tile = (8, both.shape[1])
    lane = lax.broadcasted_iota(jnp.int32, tile, 1)
    row_at = lax.broadcasted_iota(jnp.int32, tile, 0)
    left_half = lane < factor
    inner = jnp.where(left_half, lane, lane - factor)
    parts = [both[at : at + 8, :] for at in range(0, factor, 8)]

    def column(part, at):
        index = jnp.where(left_half, at, factor + at)
        return jnp.take_along_axis(part, index, axis=1, mode="promise_in_bounds")

    def row(part, at):
        return jnp.broadcast_to(part[at : at + 1, :], tile)

    for k in range(0, factor, 4):
        home, off = divmod(k, 8)
        columns = [[column(part, k + a) for part in parts] for a in range(4)]
        pivot = [[row(columns[b][home], off + a) if a <= b else None for b in range(4)] for a in range(4)]
        p00, p01, p02, p03 = pivot[0]
        _, p11, p12, p13 = pivot[1]
        _, _, p22, p23 = pivot[2]
        p33 = pivot[3][3]
        on_block = (inner >= k) & (inner < k + 4)
        r0, r1, r2, r3 = [
            jnp.where(on_block, jnp.where(inner == k + a, 1.0, 0.0), row(parts[home], off + a)) for a in range(4)
        ]
        scale = 1.0 / (p00 * p11 - p01 * p01)
        m02 = p11 * p02 - p01 * p12
        m03 = p11 * p03 - p01 * p13
        m12 = p00 * p12 - p01 * p02
        m13 = p00 * p13 - p01 * p03
        z0 = p11 * r0 - p01 * r1
        z1 = p00 * r1 - p01 * r0
        s22 = p22 - scale * (p02 * m02 + p12 * m12)
        s23 = p23 - scale * (p02 * m03 + p12 * m13)
        s33 = p33 - scale * (p03 * m03 + p13 * m13)
        t2 = r2 - scale * (p02 * z0 + p12 * z1)
        t3 = r3 - scale * (p03 * z0 + p13 * z1)
        scale_s = 1.0 / (s22 * s33 - s23 * s23)
        w2 = scale_s * (s33 * t2 - s23 * t3)
        w3 = scale_s * (s22 * t3 - s23 * t2)
        w0 = scale * (z0 - (m02 * w2 + m03 * w3))
        w1 = scale * (z1 - (m12 * w2 + m13 * w3))
        solved = (w0, w1, w2, w3)
        for m, part in enumerate(parts):
            change = (columns[0][m] * w0 + columns[1][m] * w1) + (columns[2][m] * w2 + columns[3][m] * w3)
            part = jnp.where(on_block, 0.0, part) - change
            if m == home:
                for a in range(4):
                    part = jnp.where(row_at == off + a, solved[a], part)
            parts[m] = part
    return jnp.concatenate(parts, axis=0)


def precondition_kernel(tok_total, n_terms, *refs):
    terms, (act_t, grad_t, moved) = refs[:n_terms], refs[n_terms:]
    both = terms[0][...]
    for term in terms[1:]:
        both = both + term[...]
    both = unpacked(both)
    factor = both.shape[0]
    lane = lax.broadcasted_iota(jnp.int32, both.shape, 1)
    row_at = lax.broadcasted_iota(jnp.int32, both.shape, 0)
    left_half = lane < factor
    inner = jnp.where(left_half, lane, lane - factor)
    both = both * (1.0 / tok_total) + jnp.where(inner == row_at, DAMP, 0.0)
    both = inverse_pair(both)
    blocks = jnp.concatenate(
        [jnp.where(left_half, both, 0.0), jnp.where(left_half, 0.0, both)], axis=0
    )
    proj_t = jnp.concatenate([act_t[...], grad_t[...]], axis=0)
    moved[...] = jnp.dot(blocks, proj_t, precision=HIGHEST, preferred_element_type=jnp.float32)


def precondition(tok_total, terms, act_t, grad_t):
    factor, tok_rows = act_t.shape
    n_terms = len(terms)
    return pl.pallas_call(
        functools.partial(precondition_kernel, tok_total, n_terms),
        out_shape=jax.ShapeDtypeStruct((2 * factor, tok_rows), jnp.float32),
        in_specs=[pl.BlockSpec(memory_space=pltpu.VMEM)] * (n_terms + 2),
        out_specs=pl.BlockSpec(memory_space=pltpu.VMEM),
        compiler_params=pltpu.CompilerParams(vmem_limit_bytes=24 * 2**20),
        cost_estimate=pl.CostEstimate(
            flops=1600 * factor * factor * tok_rows, bytes_accessed=16 * factor * tok_rows, transcendentals=0
        ),
        name="precondition",
    )(*terms, act_t, grad_t)


def score_kernel(size, n_pieces, moved, *refs):
    queries, (scores, ordered, result, sems) = refs[:n_pieces], refs[n_pieces:]
    factor = moved.shape[0] // 2
    owners = owners_of(lax.axis_index("dp"), size)
    group = 2
    copies = []
    for part, begin in enumerate(range(0, moved.shape[1], TOKENS_AT_ONCE)):
        tokens = slice(begin, begin + TOKENS_AT_ONCE)
        act_side = moved[:factor, tokens]

        def split(first):
            outer = jnp.concatenate(
                [act_side * moved[factor + i : factor + i + 1, tokens] for i in range(first, first + group)], axis=0
            )
            high = outer.astype(jnp.bfloat16)
            low = (outer - high.astype(jnp.float32)).astype(jnp.bfloat16)
            return jnp.concatenate([high, low], axis=0)

        total = None
        later = split(0)
        for first in range(0, factor, group):
            both = later
            if first + group < factor:
                later = split(first + group)
            columns = slice(first * factor, (first + group) * factor)
            values = jnp.concatenate([piece[:, columns] for piece in queries], axis=0)
            term = jnp.dot(jnp.concatenate([values, values], axis=1), both, preferred_element_type=jnp.float32)
            total = term if total is None else total + term
        rows = total.shape[0] // size
        for at, owner in enumerate(owners):
            place = pl.ds(pl.multiple_of(owner * rows, rows), rows)
            ordered[part, place, :] = total[at * rows : (at + 1) * rows, :]
        result[tokens, :] = ordered[part].T
        copies.append(
            pltpu.make_async_copy(
                result.at[pl.ds(begin, TOKENS_AT_ONCE), :], scores.at[pl.ds(begin, TOKENS_AT_ONCE), :], sems.at[part]
            )
        )
        copies[-1].start()
    for copy in copies:
        copy.wait()


def score(size, moved, queries):
    tok_rows = moved.shape[1]
    n_queries = sum(piece.shape[0] for piece in queries)
    n_pieces = len(queries)
    n_parts = tok_rows // TOKENS_AT_ONCE
    return pl.pallas_call(
        functools.partial(score_kernel, size, n_pieces),
        out_shape=jax.ShapeDtypeStruct((tok_rows, n_queries), jnp.float32),
        in_specs=[pl.BlockSpec(memory_space=pltpu.VMEM)] * (1 + n_pieces),
        out_specs=pl.BlockSpec(memory_space=pl.ANY),
        scratch_shapes=[
            pltpu.VMEM((n_parts, n_queries, TOKENS_AT_ONCE), jnp.float32),
            pltpu.VMEM((tok_rows, n_queries), jnp.float32),
            pltpu.SemaphoreType.DMA((n_parts,)),
        ],
        compiler_params=pltpu.CompilerParams(vmem_limit_bytes=32 * 2**20),
        name="score",
    )(moved, *queries)


def gather_stages(size):
    core = 2 if size % 2 == 0 else 1
    rest = size // core
    near = max(d for d in range(1, rest + 1) if rest % d == 0 and d * d <= rest)
    return [(core * near, rest // near), (core, near), (1, core)]


def sum_rounds(size):
    (stride, radix), *_ = gather_stages(size)
    return [(1, stride), (stride, radix)]


def after(value, other):
    return lax.optimization_barrier((value, other))[0]


def partner(digit, radix, shift):
    return digit ^ shift if radix & (radix - 1) == 0 else (digit + shift) % radix


def swapped(value, size, stride, radix, shift):
    perm = []
    for at in range(size):
        digit = at // stride % radix
        perm.append((at, at + (partner(digit, radix, shift) - digit) * stride))
    return lax.ppermute(value, "dp", perm)


def owners_of(me, size):
    owners = [me]
    for at, (stride, radix) in enumerate(gather_stages(size)):
        digit = lax.rem(lax.div(me, stride), radix)
        shifts = [0, *(range(radix - 1, 0, -1) if at == 0 else range(1, radix))]
        back = [shift if radix & (radix - 1) == 0 else (radix - shift) % radix for shift in shifts]
        steps = [(partner(digit, radix, shift) - digit) * stride for shift in back]
        owners = [owner + step for step in steps for owner in owners]
    return owners


def exchanged(held, size, stride, radix, order=None):
    mine = held[0] if len(held) == 1 else jnp.concatenate(held, axis=0)
    return [mine] + [swapped(mine, size, stride, radix, shift) for shift in order or range(1, radix)]


def on_device(acts, grads, proj_act, proj_grad, queries):
    size = lax.axis_size("dp")
    tok_total = acts.shape[0] * size
    far, near, core = gather_stages(size)
    first, second = sum_rounds(size)

    pieces = exchanged([queries], size, *far, order=range(far[1] - 1, 0, -1))
    act_t, grad_t, own = project(acts, grads, proj_act, proj_grad)
    *pieces, own = lax.optimization_barrier((*pieces, own))
    pieces = exchanged(pieces, size, *near)
    own = functools.reduce(jnp.add, exchanged([own], size, *first))
    terms = exchanged([own], size, *second, order=[*range(1, min(2, second[1])), *range(second[1] - 1, 1, -1)])
    *both, = lax.optimization_barrier((*pieces, *terms))
    pieces, terms = both[: len(pieces)], both[len(pieces) :]
    pieces = exchanged(pieces, size, *core)
    moved = precondition(tok_total, terms, act_t, grad_t)
    return score(size, moved, pieces)


def solution(mesh):
    in_specs = (P(("parts", "dp"), None), P(("parts", "dp"), None), P(), P(), P("dp", None))
    out_specs = P(("parts", "dp"), None)
    return jax.shard_map(
        on_device, mesh=mesh, in_specs=in_specs, out_specs=out_specs, check_vma=False
    )
```

```python
import functools

import jax
import jax.numpy as jnp
from jax import lax
from jax.experimental import pallas as pl
from jax.experimental.pallas import tpu as pltpu
from jax.sharding import PartitionSpec as P

DAMP = 0.1
HIGHEST = lax.Precision.HIGHEST
COPY_ROWS = 128
IN_FLIGHT = 5
TOKENS_AT_ONCE = 256


def places(factor):
    return [lax.broadcasted_iota(jnp.int32, (factor, factor), axis) for axis in (0, 1)]


def packed(act, grad):
    factor = act.shape[0]
    row_at, lane = places(factor)
    mixed = jnp.where(row_at <= lane, act, grad)
    diagonal = jnp.sum(jnp.where(row_at == lane, grad, 0.0), axis=0, keepdims=True)
    last = jnp.broadcast_to(jnp.concatenate([diagonal, diagonal], axis=1), (8, 2 * factor))
    half = factor // 2
    return jnp.concatenate([jnp.concatenate([mixed[:half], mixed[half:]], axis=1), last], axis=0)


def unpacked(value):
    factor = value.shape[1] // 2
    half = factor // 2
    row_at = lax.broadcasted_iota(jnp.int32, (factor, 2 * factor), 0)
    lane = lax.broadcasted_iota(jnp.int32, (factor, 2 * factor), 1)
    left_half = lane < factor
    inner = jnp.where(left_half, lane, lane - factor)
    rolled = pltpu.roll(value[:half], factor, axis=1)
    mixed = jnp.concatenate(
        [
            jnp.where(left_half[:half], value[:half], rolled),
            jnp.where(left_half[:half], rolled, value[:half]),
        ],
        axis=0,
    )
    flipped = jnp.concatenate([mixed, mixed], axis=0).T[:factor]
    diagonal = jnp.broadcast_to(value[half : half + 1], mixed.shape)
    below = jnp.where(row_at > inner, mixed, jnp.where(row_at < inner, flipped, diagonal))
    return jnp.where(left_half, jnp.where(row_at <= inner, mixed, flipped), below)


def project_kernel(
    acts, grads, weight_act, weight_grad, act_t, grad_t, cov, tok_buf, weight_buf, weight_t, tok_sems, weight_sems
):
    width = weight_act.shape[1]
    n_parts = acts.shape[0] // COPY_ROWS
    weight_copies = [
        pltpu.make_async_copy(src, weight_buf.at[at], weight_sems.at[at])
        for at, src in enumerate((weight_act, weight_grad))
    ]
    tok_copies = [
        [
            pltpu.make_async_copy(
                src.at[pl.ds(part * COPY_ROWS, COPY_ROWS), :],
                tok_buf.at[at, pl.ds(part * COPY_ROWS, COPY_ROWS), :],
                tok_sems.at[at, part],
            )
            for part in range(n_parts)
        ]
        for at, src in enumerate((acts, grads))
    ]
    queue = [weight_copies[0], *tok_copies[0], *tok_copies[1]]
    queue.insert(3, weight_copies[1])

    def start_next(many):
        for copy in queue[:many]:
            copy.start()
        del queue[:many]

    def turned(at):
        for first in range(0, width, 512):
            weight_t[at, first : first + 512, :] = weight_buf[at, :, first : first + 512].T

    steps = [(at, part, min(2, n_parts - part)) for at in range(2) for part in range(0, n_parts, 2)]
    last_act = len(steps) // 2 - 1
    blocks = [[], []]
    grams = [[], []]

    def add_gram(at):
        flipped, plain = [jnp.concatenate(parts, axis=axis) for parts, axis in zip(zip(*blocks[at]), (1, 0))]
        grams[at].append(jnp.dot(flipped, plain, precision=HIGHEST, preferred_element_type=jnp.float32))
        blocks[at].clear()

    start_next(1 + IN_FLIGHT)
    weight_copies[0].wait()
    turned(0)
    for step, (at, part, many) in enumerate(steps):
        for copy in tok_copies[at][part : part + many]:
            copy.wait()
            start_next(1)
        if step == last_act:
            weight_copies[1].wait()
            start_next(1)
        rows = slice(part * COPY_ROWS, (part + many) * COPY_ROWS)
        block = jnp.dot(tok_buf[at, rows, :], weight_t[at], preferred_element_type=jnp.float32)
        if step == last_act:
            turned(1)
        if step == last_act + 1:
            add_gram(0)
        if step == len(steps) - 1:
            add_gram(1)
        flipped = block.T
        (act_t, grad_t)[at][:, rows] = flipped
        blocks[at].append((flipped, block))
    add_gram(1)
    cov[...] = packed(*[functools.reduce(jnp.add, terms) for terms in grams])


def project(acts, grads, proj_act, proj_grad):
    tok_rows, width = acts.shape
    factor = proj_act.shape[1]
    operands = [
        pltpu.with_memory_space_constraint(value, pltpu.HBM) for value in (acts, grads, proj_act.T, proj_grad.T)
    ]
    return pl.pallas_call(
        project_kernel,
        out_shape=(
            jax.ShapeDtypeStruct((factor, tok_rows), jnp.float32),
            jax.ShapeDtypeStruct((factor, tok_rows), jnp.float32),
            jax.ShapeDtypeStruct((factor // 2 + 8, 2 * factor), jnp.float32),
        ),
        in_specs=[pl.BlockSpec(memory_space=pltpu.HBM)] * 4,
        out_specs=[pl.BlockSpec(memory_space=pltpu.VMEM)] * 3,
        scratch_shapes=[
            pltpu.VMEM((2, tok_rows, width), acts.dtype),
            pltpu.VMEM((2, factor, width), proj_act.dtype),
            pltpu.VMEM((2, width, factor), proj_act.dtype),
            pltpu.SemaphoreType.DMA((2, tok_rows // COPY_ROWS)),
            pltpu.SemaphoreType.DMA((2,)),
        ],
        compiler_params=pltpu.CompilerParams(vmem_limit_bytes=24 * 2**20),
        cost_estimate=pl.CostEstimate(
            flops=4 * tok_rows * width * factor, bytes_accessed=4 * tok_rows * width, transcendentals=0
        ),
        name="project",
    )(*operands)


def inverse_pair(both):
    factor = both.shape[0]
    tile = (8, both.shape[1])
    lane = lax.broadcasted_iota(jnp.int32, tile, 1)
    row_at = lax.broadcasted_iota(jnp.int32, tile, 0)
    left_half = lane < factor
    inner = jnp.where(left_half, lane, lane - factor)
    parts = [both[at : at + 8, :] for at in range(0, factor, 8)]

    def column(part, at):
        index = jnp.where(left_half, at, factor + at)
        return jnp.take_along_axis(part, index, axis=1, mode="promise_in_bounds")

    def row(part, at):
        return jnp.broadcast_to(part[at : at + 1, :], tile)

    for k in range(0, factor, 4):
        home, off = divmod(k, 8)
        columns = [[column(part, k + a) for part in parts] for a in range(4)]
        pivot = [[row(columns[b][home], off + a) if a <= b else None for b in range(4)] for a in range(4)]
        p00, p01, p02, p03 = pivot[0]
        _, p11, p12, p13 = pivot[1]
        _, _, p22, p23 = pivot[2]
        p33 = pivot[3][3]
        on_block = (inner >= k) & (inner < k + 4)
        r0, r1, r2, r3 = [
            jnp.where(on_block, jnp.where(inner == k + a, 1.0, 0.0), row(parts[home], off + a)) for a in range(4)
        ]
        scale = 1.0 / (p00 * p11 - p01 * p01)
        m02 = p11 * p02 - p01 * p12
        m03 = p11 * p03 - p01 * p13
        m12 = p00 * p12 - p01 * p02
        m13 = p00 * p13 - p01 * p03
        z0 = p11 * r0 - p01 * r1
        z1 = p00 * r1 - p01 * r0
        s22 = p22 - scale * (p02 * m02 + p12 * m12)
        s23 = p23 - scale * (p02 * m03 + p12 * m13)
        s33 = p33 - scale * (p03 * m03 + p13 * m13)
        t2 = r2 - scale * (p02 * z0 + p12 * z1)
        t3 = r3 - scale * (p03 * z0 + p13 * z1)
        scale_s = 1.0 / (s22 * s33 - s23 * s23)
        w2 = scale_s * (s33 * t2 - s23 * t3)
        w3 = scale_s * (s22 * t3 - s23 * t2)
        w0 = scale * (z0 - (m02 * w2 + m03 * w3))
        w1 = scale * (z1 - (m12 * w2 + m13 * w3))
        solved = (w0, w1, w2, w3)
        for m, part in enumerate(parts):
            change = (columns[0][m] * w0 + columns[1][m] * w1) + (columns[2][m] * w2 + columns[3][m] * w3)
            part = jnp.where(on_block, 0.0, part) - change
            if m == home:
                for a in range(4):
                    part = jnp.where(row_at == off + a, solved[a], part)
            parts[m] = part
    return jnp.concatenate(parts, axis=0)


def precondition_kernel(tok_total, n_terms, *refs):
    terms, (act_t, grad_t, moved) = refs[:n_terms], refs[n_terms:]
    both = terms[0][...]
    for term in terms[1:]:
        both = both + term[...]
    both = unpacked(both)
    factor = both.shape[0]
    lane = lax.broadcasted_iota(jnp.int32, both.shape, 1)
    row_at = lax.broadcasted_iota(jnp.int32, both.shape, 0)
    left_half = lane < factor
    inner = jnp.where(left_half, lane, lane - factor)
    both = both * (1.0 / tok_total) + jnp.where(inner == row_at, DAMP, 0.0)
    both = inverse_pair(both)
    blocks = jnp.concatenate(
        [jnp.where(left_half, both, 0.0), jnp.where(left_half, 0.0, both)], axis=0
    )
    proj_t = jnp.concatenate([act_t[...], grad_t[...]], axis=0)
    moved[...] = jnp.dot(blocks, proj_t, precision=HIGHEST, preferred_element_type=jnp.float32)


def precondition(tok_total, terms, act_t, grad_t):
    factor, tok_rows = act_t.shape
    n_terms = len(terms)
    return pl.pallas_call(
        functools.partial(precondition_kernel, tok_total, n_terms),
        out_shape=jax.ShapeDtypeStruct((2 * factor, tok_rows), jnp.float32),
        in_specs=[pl.BlockSpec(memory_space=pltpu.VMEM)] * (n_terms + 2),
        out_specs=pl.BlockSpec(memory_space=pltpu.VMEM),
        compiler_params=pltpu.CompilerParams(vmem_limit_bytes=24 * 2**20),
        cost_estimate=pl.CostEstimate(
            flops=1600 * factor * factor * tok_rows, bytes_accessed=16 * factor * tok_rows, transcendentals=0
        ),
        name="precondition",
    )(*terms, act_t, grad_t)


def score_kernel(size, n_pieces, moved, *refs):
    queries, (scores, ordered, result, sems) = refs[:n_pieces], refs[n_pieces:]
    factor = moved.shape[0] // 2
    owners = owners_of(lax.axis_index("dp"), size)
    group = 2
    copies = []
    for part, begin in enumerate(range(0, moved.shape[1], TOKENS_AT_ONCE)):
        tokens = slice(begin, begin + TOKENS_AT_ONCE)
        act_side = moved[:factor, tokens]

        def split(first):
            outer = jnp.concatenate(
                [act_side * moved[factor + i : factor + i + 1, tokens] for i in range(first, first + group)], axis=0
            )
            high = outer.astype(jnp.bfloat16)
            low = (outer - high.astype(jnp.float32)).astype(jnp.bfloat16)
            return jnp.concatenate([high, low], axis=0)

        total = None
        later = split(0)
        for first in range(0, factor, group):
            both = later
            if first + group < factor:
                later = split(first + group)
            columns = slice(first * factor, (first + group) * factor)
            values = jnp.concatenate([piece[:, columns] for piece in queries], axis=0)
            term = jnp.dot(jnp.concatenate([values, values], axis=1), both, preferred_element_type=jnp.float32)
            total = term if total is None else total + term
        rows = total.shape[0] // size
        for at, owner in enumerate(owners):
            place = pl.ds(pl.multiple_of(owner * rows, rows), rows)
            ordered[part, place, :] = total[at * rows : (at + 1) * rows, :]
        result[tokens, :] = ordered[part].T
        copies.append(
            pltpu.make_async_copy(
                result.at[pl.ds(begin, TOKENS_AT_ONCE), :], scores.at[pl.ds(begin, TOKENS_AT_ONCE), :], sems.at[part]
            )
        )
        copies[-1].start()
    for copy in copies:
        copy.wait()


def score(size, moved, queries):
    tok_rows = moved.shape[1]
    n_queries = sum(piece.shape[0] for piece in queries)
    n_pieces = len(queries)
    n_parts = tok_rows // TOKENS_AT_ONCE
    return pl.pallas_call(
        functools.partial(score_kernel, size, n_pieces),
        out_shape=jax.ShapeDtypeStruct((tok_rows, n_queries), jnp.float32),
        in_specs=[pl.BlockSpec(memory_space=pltpu.VMEM)] * (1 + n_pieces),
        out_specs=pl.BlockSpec(memory_space=pl.ANY),
        scratch_shapes=[
            pltpu.VMEM((n_parts, n_queries, TOKENS_AT_ONCE), jnp.float32),
            pltpu.VMEM((tok_rows, n_queries), jnp.float32),
            pltpu.SemaphoreType.DMA((n_parts,)),
        ],
        compiler_params=pltpu.CompilerParams(vmem_limit_bytes=32 * 2**20),
        name="score",
    )(moved, *queries)


def gather_stages(size):
    core = 2 if size % 2 == 0 else 1
    rest = size // core
    near = max(d for d in range(1, rest + 1) if rest % d == 0 and d * d <= rest)
    return [(core * near, rest // near), (core, near), (1, core)]


def sum_rounds(size):
    (stride, radix), *_ = gather_stages(size)
    return [(1, stride), (stride, radix)]


def after(value, other):
    return lax.optimization_barrier((value, other))[0]


def partner(digit, radix, shift):
    return digit ^ shift if radix & (radix - 1) == 0 else (digit + shift) % radix


def swapped(value, size, stride, radix, shift):
    perm = []
    for at in range(size):
        digit = at // stride % radix
        perm.append((at, at + (partner(digit, radix, shift) - digit) * stride))
    return lax.ppermute(value, "dp", perm)


def owners_of(me, size):
    owners = [me]
    for at, (stride, radix) in enumerate(gather_stages(size)):
        digit = lax.rem(lax.div(me, stride), radix)
        shifts = [0, *(range(radix - 1, 0, -1) if at == 0 else range(1, radix))]
        back = [shift if radix & (radix - 1) == 0 else (radix - shift) % radix for shift in shifts]
        steps = [(partner(digit, radix, shift) - digit) * stride for shift in back]
        owners = [owner + step for step in steps for owner in owners]
    return owners


def exchanged(held, size, stride, radix, order=None):
    mine = held[0] if len(held) == 1 else jnp.concatenate(held, axis=0)
    return [mine] + [swapped(mine, size, stride, radix, shift) for shift in order or range(1, radix)]


def on_device(acts, grads, proj_act, proj_grad, queries):
    size = lax.axis_size("dp")
    tok_total = acts.shape[0] * size
    far, near, core = gather_stages(size)
    first, second = sum_rounds(size)

    pieces = exchanged([queries], size, *far, order=range(far[1] - 1, 0, -1))
    act_t, grad_t, own = project(acts, grads, proj_act, proj_grad)
    *pieces, own = lax.optimization_barrier((*pieces, own))
    pieces = exchanged(pieces, size, *near)
    own = functools.reduce(jnp.add, exchanged([own], size, *first))
    terms = exchanged([own], size, *second)
    *both, = lax.optimization_barrier((*pieces, *terms))
    pieces, terms = both[: len(pieces)], both[len(pieces) :]
    pieces = exchanged(pieces, size, *core)
    moved = precondition(tok_total, terms, act_t, grad_t)
    return score(size, moved, pieces)


def solution(mesh):
    in_specs = (P(("parts", "dp"), None), P(("parts", "dp"), None), P(), P(), P("dp", None))
    out_specs = P(("parts", "dp"), None)
    return jax.shard_map(
        on_device, mesh=mesh, in_specs=in_specs, out_specs=out_specs, check_vma=False
    )
```

```python
import functools

import jax
import jax.numpy as jnp
from jax import lax
from jax.experimental import pallas as pl
from jax.experimental.pallas import tpu as pltpu
from jax.sharding import PartitionSpec as P

DAMP = 0.1
HIGHEST = lax.Precision.HIGHEST
COPY_ROWS = 128
IN_FLIGHT = 5
TOKENS_AT_ONCE = 256


def places(factor):
    return [lax.broadcasted_iota(jnp.int32, (factor, factor), axis) for axis in (0, 1)]


def packed(act, grad):
    factor = act.shape[0]
    row_at, lane = places(factor)
    mixed = jnp.where(row_at <= lane, act, grad)
    diagonal = jnp.sum(jnp.where(row_at == lane, grad, 0.0), axis=0, keepdims=True)
    last = jnp.broadcast_to(jnp.concatenate([diagonal, diagonal], axis=1), (8, 2 * factor))
    half = factor // 2
    return jnp.concatenate([jnp.concatenate([mixed[:half], mixed[half:]], axis=1), last], axis=0)


def unpacked(value):
    factor = value.shape[1] // 2
    half = factor // 2
    row_at = lax.broadcasted_iota(jnp.int32, (factor, 2 * factor), 0)
    lane = lax.broadcasted_iota(jnp.int32, (factor, 2 * factor), 1)
    left_half = lane < factor
    inner = jnp.where(left_half, lane, lane - factor)
    rolled = pltpu.roll(value[:half], factor, axis=1)
    mixed = jnp.concatenate(
        [
            jnp.where(left_half[:half], value[:half], rolled),
            jnp.where(left_half[:half], rolled, value[:half]),
        ],
        axis=0,
    )
    flipped = jnp.concatenate([mixed, mixed], axis=0).T[:factor]
    diagonal = jnp.broadcast_to(value[half : half + 1], mixed.shape)
    below = jnp.where(row_at > inner, mixed, jnp.where(row_at < inner, flipped, diagonal))
    return jnp.where(left_half, jnp.where(row_at <= inner, mixed, flipped), below)


def project_kernel(
    acts, grads, weight_act, weight_grad, act_t, grad_t, cov, tok_buf, weight_buf, weight_t, tok_sems, weight_sems
):
    width = weight_act.shape[1]
    n_parts = acts.shape[0] // COPY_ROWS
    weight_copies = [
        pltpu.make_async_copy(src, weight_buf.at[at], weight_sems.at[at])
        for at, src in enumerate((weight_act, weight_grad))
    ]
    tok_copies = [
        [
            pltpu.make_async_copy(
                src.at[pl.ds(part * COPY_ROWS, COPY_ROWS), :],
                tok_buf.at[at, pl.ds(part * COPY_ROWS, COPY_ROWS), :],
                tok_sems.at[at, part],
            )
            for part in range(n_parts)
        ]
        for at, src in enumerate((acts, grads))
    ]
    queue = [weight_copies[0], *tok_copies[0], *tok_copies[1]]
    queue.insert(3, weight_copies[1])

    def start_next(many):
        for copy in queue[:many]:
            copy.start()
        del queue[:many]

    def turned(at):
        for first in range(0, width, 512):
            weight_t[at, first : first + 512, :] = weight_buf[at, :, first : first + 512].T

    steps = [(at, part, min(2, n_parts - part)) for at in range(2) for part in range(0, n_parts, 2)]
    last_act = len(steps) // 2 - 1
    blocks = [[], []]
    grams = [[], []]

    def add_gram(at):
        flipped, plain = [jnp.concatenate(parts, axis=axis) for parts, axis in zip(zip(*blocks[at]), (1, 0))]
        grams[at].append(jnp.dot(flipped, plain, precision=HIGHEST, preferred_element_type=jnp.float32))
        blocks[at].clear()

    start_next(1 + IN_FLIGHT)
    weight_copies[0].wait()
    turned(0)
    for step, (at, part, many) in enumerate(steps):
        for copy in tok_copies[at][part : part + many]:
            copy.wait()
            start_next(1)
        if step == last_act:
            weight_copies[1].wait()
            start_next(1)
        rows = slice(part * COPY_ROWS, (part + many) * COPY_ROWS)
        block = jnp.dot(tok_buf[at, rows, :], weight_t[at], preferred_element_type=jnp.float32)
        if step == last_act:
            turned(1)
        if step == last_act + 1:
            add_gram(0)
        if step == len(steps) - 1:
            add_gram(1)
        flipped = block.T
        (act_t, grad_t)[at][:, rows] = flipped
        blocks[at].append((flipped, block))
    add_gram(1)
    cov[...] = packed(*[functools.reduce(jnp.add, terms) for terms in grams])


def project(acts, grads, proj_act, proj_grad):
    tok_rows, width = acts.shape
    factor = proj_act.shape[1]
    operands = [
        pltpu.with_memory_space_constraint(value, pltpu.HBM) for value in (acts, grads, proj_act.T, proj_grad.T)
    ]
    return pl.pallas_call(
        project_kernel,
        out_shape=(
            jax.ShapeDtypeStruct((factor, tok_rows), jnp.float32),
            jax.ShapeDtypeStruct((factor, tok_rows), jnp.float32),
            jax.ShapeDtypeStruct((factor // 2 + 8, 2 * factor), jnp.float32),
        ),
        in_specs=[pl.BlockSpec(memory_space=pltpu.HBM)] * 4,
        out_specs=[pl.BlockSpec(memory_space=pltpu.VMEM)] * 3,
        scratch_shapes=[
            pltpu.VMEM((2, tok_rows, width), acts.dtype),
            pltpu.VMEM((2, factor, width), proj_act.dtype),
            pltpu.VMEM((2, width, factor), proj_act.dtype),
            pltpu.SemaphoreType.DMA((2, tok_rows // COPY_ROWS)),
            pltpu.SemaphoreType.DMA((2,)),
        ],
        compiler_params=pltpu.CompilerParams(vmem_limit_bytes=24 * 2**20),
        cost_estimate=pl.CostEstimate(
            flops=4 * tok_rows * width * factor, bytes_accessed=4 * tok_rows * width, transcendentals=0
        ),
        name="project",
    )(*operands)


def inverse_pair(both):
    factor = both.shape[0]
    tile = (8, both.shape[1])
    lane = lax.broadcasted_iota(jnp.int32, tile, 1)
    row_at = lax.broadcasted_iota(jnp.int32, tile, 0)
    left_half = lane < factor
    inner = jnp.where(left_half, lane, lane - factor)
    parts = [both[at : at + 8, :] for at in range(0, factor, 8)]

    def column(part, at):
        index = jnp.where(left_half, at, factor + at)
        return jnp.take_along_axis(part, index, axis=1, mode="promise_in_bounds")

    def row(part, at):
        return jnp.broadcast_to(part[at : at + 1, :], tile)

    for k in range(0, factor, 4):
        home, off = divmod(k, 8)
        columns = [[column(part, k + a) for part in parts] for a in range(4)]
        pivot = [[row(columns[b][home], off + a) if a <= b else None for b in range(4)] for a in range(4)]
        p00, p01, p02, p03 = pivot[0]
        _, p11, p12, p13 = pivot[1]
        _, _, p22, p23 = pivot[2]
        p33 = pivot[3][3]
        on_block = (inner >= k) & (inner < k + 4)
        r0, r1, r2, r3 = [
            jnp.where(on_block, jnp.where(inner == k + a, 1.0, 0.0), row(parts[home], off + a)) for a in range(4)
        ]
        scale = 1.0 / (p00 * p11 - p01 * p01)
        m02 = p11 * p02 - p01 * p12
        m03 = p11 * p03 - p01 * p13
        m12 = p00 * p12 - p01 * p02
        m13 = p00 * p13 - p01 * p03
        z0 = p11 * r0 - p01 * r1
        z1 = p00 * r1 - p01 * r0
        s22 = p22 - scale * (p02 * m02 + p12 * m12)
        s23 = p23 - scale * (p02 * m03 + p12 * m13)
        s33 = p33 - scale * (p03 * m03 + p13 * m13)
        t2 = r2 - scale * (p02 * z0 + p12 * z1)
        t3 = r3 - scale * (p03 * z0 + p13 * z1)
        scale_s = 1.0 / (s22 * s33 - s23 * s23)
        w2 = scale_s * (s33 * t2 - s23 * t3)
        w3 = scale_s * (s22 * t3 - s23 * t2)
        w0 = scale * (z0 - (m02 * w2 + m03 * w3))
        w1 = scale * (z1 - (m12 * w2 + m13 * w3))
        solved = (w0, w1, w2, w3)
        for m, part in enumerate(parts):
            change = (columns[0][m] * w0 + columns[1][m] * w1) + (columns[2][m] * w2 + columns[3][m] * w3)
            part = jnp.where(on_block, 0.0, part) - change
            if m == home:
                for a in range(4):
                    part = jnp.where(row_at == off + a, solved[a], part)
            parts[m] = part
    return jnp.concatenate(parts, axis=0)


def precondition_kernel(tok_total, n_terms, *refs):
    terms, (act_t, grad_t, moved) = refs[:n_terms], refs[n_terms:]
    both = terms[0][...]
    for term in terms[1:]:
        both = both + term[...]
    both = unpacked(both)
    factor = both.shape[0]
    lane = lax.broadcasted_iota(jnp.int32, both.shape, 1)
    row_at = lax.broadcasted_iota(jnp.int32, both.shape, 0)
    left_half = lane < factor
    inner = jnp.where(left_half, lane, lane - factor)
    both = both * (1.0 / tok_total) + jnp.where(inner == row_at, DAMP, 0.0)
    both = inverse_pair(both)
    blocks = jnp.concatenate(
        [jnp.where(left_half, both, 0.0), jnp.where(left_half, 0.0, both)], axis=0
    )
    proj_t = jnp.concatenate([act_t[...], grad_t[...]], axis=0)
    moved[...] = jnp.dot(blocks, proj_t, precision=HIGHEST, preferred_element_type=jnp.float32)


def precondition(tok_total, terms, act_t, grad_t):
    factor, tok_rows = act_t.shape
    n_terms = len(terms)
    return pl.pallas_call(
        functools.partial(precondition_kernel, tok_total, n_terms),
        out_shape=jax.ShapeDtypeStruct((2 * factor, tok_rows), jnp.float32),
        in_specs=[pl.BlockSpec(memory_space=pltpu.VMEM)] * (n_terms + 2),
        out_specs=pl.BlockSpec(memory_space=pltpu.VMEM),
        compiler_params=pltpu.CompilerParams(vmem_limit_bytes=24 * 2**20),
        cost_estimate=pl.CostEstimate(
            flops=1600 * factor * factor * tok_rows, bytes_accessed=16 * factor * tok_rows, transcendentals=0
        ),
        name="precondition",
    )(*terms, act_t, grad_t)


def score_kernel(size, n_pieces, moved, *refs):
    queries, (scores, ordered, result, sems) = refs[:n_pieces], refs[n_pieces:]
    factor = moved.shape[0] // 2
    owners = owners_of(lax.axis_index("dp"), size)
    group = 4
    copies = []
    for part, begin in enumerate(range(0, moved.shape[1], TOKENS_AT_ONCE)):
        tokens = slice(begin, begin + TOKENS_AT_ONCE)
        act_side = moved[:factor, tokens]

        def split(first):
            outer = jnp.concatenate(
                [act_side * moved[factor + i : factor + i + 1, tokens] for i in range(first, first + group)], axis=0
            )
            high = outer.astype(jnp.bfloat16)
            low = (outer - high.astype(jnp.float32)).astype(jnp.bfloat16)
            return jnp.concatenate([high, low], axis=0)

        total = None
        later = split(0)
        for first in range(0, factor, group):
            both = later
            if first + group < factor:
                later = split(first + group)
            columns = slice(first * factor, (first + group) * factor)
            values = jnp.concatenate([piece[:, columns] for piece in queries], axis=0)
            term = jnp.dot(jnp.concatenate([values, values], axis=1), both, preferred_element_type=jnp.float32)
            total = term if total is None else total + term
        rows = total.shape[0] // size
        for at, owner in enumerate(owners):
            place = pl.ds(pl.multiple_of(owner * rows, rows), rows)
            ordered[part, place, :] = total[at * rows : (at + 1) * rows, :]
        result[tokens, :] = ordered[part].T
        copies.append(
            pltpu.make_async_copy(
                result.at[pl.ds(begin, TOKENS_AT_ONCE), :], scores.at[pl.ds(begin, TOKENS_AT_ONCE), :], sems.at[part]
            )
        )
        copies[-1].start()
    for copy in copies:
        copy.wait()


def score(size, moved, queries):
    tok_rows = moved.shape[1]
    n_queries = sum(piece.shape[0] for piece in queries)
    n_pieces = len(queries)
    n_parts = tok_rows // TOKENS_AT_ONCE
    return pl.pallas_call(
        functools.partial(score_kernel, size, n_pieces),
        out_shape=jax.ShapeDtypeStruct((tok_rows, n_queries), jnp.float32),
        in_specs=[pl.BlockSpec(memory_space=pltpu.VMEM)] * (1 + n_pieces),
        out_specs=pl.BlockSpec(memory_space=pl.ANY),
        scratch_shapes=[
            pltpu.VMEM((n_parts, n_queries, TOKENS_AT_ONCE), jnp.float32),
            pltpu.VMEM((tok_rows, n_queries), jnp.float32),
            pltpu.SemaphoreType.DMA((n_parts,)),
        ],
        compiler_params=pltpu.CompilerParams(vmem_limit_bytes=32 * 2**20),
        name="score",
    )(moved, *queries)


def gather_stages(size):
    core = 2 if size % 2 == 0 else 1
    rest = size // core
    near = max(d for d in range(1, rest + 1) if rest % d == 0 and d * d <= rest)
    return [(core * near, rest // near), (core, near), (1, core)]


def sum_rounds(size):
    (stride, radix), *_ = gather_stages(size)
    return [(1, stride), (stride, radix)]


def after(value, other):
    return lax.optimization_barrier((value, other))[0]


def partner(digit, radix, shift):
    return digit ^ shift if radix & (radix - 1) == 0 else (digit + shift) % radix


def swapped(value, size, stride, radix, shift):
    perm = []
    for at in range(size):
        digit = at // stride % radix
        perm.append((at, at + (partner(digit, radix, shift) - digit) * stride))
    return lax.ppermute(value, "dp", perm)


def owners_of(me, size):
    owners = [me]
    for at, (stride, radix) in enumerate(gather_stages(size)):
        digit = lax.rem(lax.div(me, stride), radix)
        shifts = [0, *(range(radix - 1, 0, -1) if at == 0 else range(1, radix))]
        back = [shift if radix & (radix - 1) == 0 else (radix - shift) % radix for shift in shifts]
        steps = [(partner(digit, radix, shift) - digit) * stride for shift in back]
        owners = [owner + step for step in steps for owner in owners]
    return owners


def exchanged(held, size, stride, radix, order=None):
    mine = held[0] if len(held) == 1 else jnp.concatenate(held, axis=0)
    return [mine] + [swapped(mine, size, stride, radix, shift) for shift in order or range(1, radix)]


def on_device(acts, grads, proj_act, proj_grad, queries):
    size = lax.axis_size("dp")
    tok_total = acts.shape[0] * size
    far, near, core = gather_stages(size)
    first, second = sum_rounds(size)

    pieces = exchanged([queries], size, *far, order=range(far[1] - 1, 0, -1))
    act_t, grad_t, own = project(acts, grads, proj_act, proj_grad)
    *pieces, own = lax.optimization_barrier((*pieces, own))
    pieces = exchanged(pieces, size, *near)
    own = functools.reduce(jnp.add, exchanged([own], size, *first))
    terms = exchanged([own], size, *second)
    *both, = lax.optimization_barrier((*pieces, *terms))
    pieces, terms = both[: len(pieces)], both[len(pieces) :]
    pieces = exchanged(pieces, size, *core)
    moved = precondition(tok_total, terms, act_t, grad_t)
    return score(size, moved, pieces)


def solution(mesh):
    in_specs = (P(("parts", "dp"), None), P(("parts", "dp"), None), P(), P(), P("dp", None))
    out_specs = P(("parts", "dp"), None)
    return jax.shard_map(
        on_device, mesh=mesh, in_specs=in_specs, out_specs=out_specs, check_vma=False
    )
```

```python
import functools

import jax
import jax.numpy as jnp
from jax import lax
from jax.experimental import pallas as pl
from jax.experimental.pallas import tpu as pltpu
from jax.sharding import PartitionSpec as P

DAMP = 0.1
HIGHEST = lax.Precision.HIGHEST
COPY_ROWS = 256
IN_FLIGHT = 3
TOKENS_AT_ONCE = 256


def places(factor):
    return [lax.broadcasted_iota(jnp.int32, (factor, factor), axis) for axis in (0, 1)]


def packed(act, grad):
    factor = act.shape[0]
    row_at, lane = places(factor)
    mixed = jnp.where(row_at <= lane, act, grad)
    diagonal = jnp.sum(jnp.where(row_at == lane, grad, 0.0), axis=0, keepdims=True)
    last = jnp.broadcast_to(jnp.concatenate([diagonal, diagonal], axis=1), (8, 2 * factor))
    half = factor // 2
    return jnp.concatenate([jnp.concatenate([mixed[:half], mixed[half:]], axis=1), last], axis=0)


def unpacked(value):
    factor = value.shape[1] // 2
    half = factor // 2
    row_at = lax.broadcasted_iota(jnp.int32, (factor, 2 * factor), 0)
    lane = lax.broadcasted_iota(jnp.int32, (factor, 2 * factor), 1)
    left_half = lane < factor
    inner = jnp.where(left_half, lane, lane - factor)
    rolled = pltpu.roll(value[:half], factor, axis=1)
    mixed = jnp.concatenate(
        [
            jnp.where(left_half[:half], value[:half], rolled),
            jnp.where(left_half[:half], rolled, value[:half]),
        ],
        axis=0,
    )
    flipped = jnp.concatenate([mixed, mixed], axis=0).T[:factor]
    diagonal = jnp.broadcast_to(value[half : half + 1], mixed.shape)
    below = jnp.where(row_at > inner, mixed, jnp.where(row_at < inner, flipped, diagonal))
    return jnp.where(left_half, jnp.where(row_at <= inner, mixed, flipped), below)


def project_kernel(
    acts, grads, weight_act, weight_grad, act_t, grad_t, cov, tok_buf, weight_buf, weight_t, tok_sems, weight_sems
):
    width = weight_act.shape[1]
    n_parts = acts.shape[0] // COPY_ROWS
    weight_copies = [
        pltpu.make_async_copy(src, weight_buf.at[at], weight_sems.at[at])
        for at, src in enumerate((weight_act, weight_grad))
    ]
    tok_copies = [
        [
            pltpu.make_async_copy(
                src.at[pl.ds(part * COPY_ROWS, COPY_ROWS), :],
                tok_buf.at[at, pl.ds(part * COPY_ROWS, COPY_ROWS), :],
                tok_sems.at[at, part],
            )
            for part in range(n_parts)
        ]
        for at, src in enumerate((acts, grads))
    ]
    queue = [weight_copies[0], *tok_copies[0], *tok_copies[1]]
    queue.insert(2, weight_copies[1])

    def start_next(many):
        for copy in queue[:many]:
            copy.start()
        del queue[:many]

    def turned(at):
        for first in range(0, width, 512):
            weight_t[at, first : first + 512, :] = weight_buf[at, :, first : first + 512].T

    steps = [(at, part, 1) for at in range(2) for part in range(n_parts)]
    last_act = len(steps) // 2 - 1
    blocks = [[], []]
    grams = [[], []]

    def add_gram(at):
        flipped, plain = [jnp.concatenate(parts, axis=axis) for parts, axis in zip(zip(*blocks[at]), (1, 0))]
        grams[at].append(jnp.dot(flipped, plain, precision=HIGHEST, preferred_element_type=jnp.float32))
        blocks[at].clear()

    start_next(1 + IN_FLIGHT)
    weight_copies[0].wait()
    turned(0)
    for step, (at, part, many) in enumerate(steps):
        for copy in tok_copies[at][part : part + many]:
            copy.wait()
            start_next(1)
        if step == last_act:
            weight_copies[1].wait()
            start_next(1)
        rows = slice(part * COPY_ROWS, (part + many) * COPY_ROWS)
        block = jnp.dot(tok_buf[at, rows, :], weight_t[at], preferred_element_type=jnp.float32)
        if step == last_act:
            turned(1)
        if step == last_act + 1:
            add_gram(0)
        if step == len(steps) - 1:
            add_gram(1)
        flipped = block.T
        (act_t, grad_t)[at][:, rows] = flipped
        blocks[at].append((flipped, block))
    add_gram(1)
    cov[...] = packed(*[functools.reduce(jnp.add, terms) for terms in grams])


def project(acts, grads, proj_act, proj_grad):
    tok_rows, width = acts.shape
    factor = proj_act.shape[1]
    operands = [
        pltpu.with_memory_space_constraint(value, pltpu.HBM) for value in (acts, grads, proj_act.T, proj_grad.T)
    ]
    return pl.pallas_call(
        project_kernel,
        out_shape=(
            jax.ShapeDtypeStruct((factor, tok_rows), jnp.float32),
            jax.ShapeDtypeStruct((factor, tok_rows), jnp.float32),
            jax.ShapeDtypeStruct((factor // 2 + 8, 2 * factor), jnp.float32),
        ),
        in_specs=[pl.BlockSpec(memory_space=pltpu.HBM)] * 4,
        out_specs=[pl.BlockSpec(memory_space=pltpu.VMEM)] * 3,
        scratch_shapes=[
            pltpu.VMEM((2, tok_rows, width), acts.dtype),
            pltpu.VMEM((2, factor, width), proj_act.dtype),
            pltpu.VMEM((2, width, factor), proj_act.dtype),
            pltpu.SemaphoreType.DMA((2, tok_rows // COPY_ROWS)),
            pltpu.SemaphoreType.DMA((2,)),
        ],
        compiler_params=pltpu.CompilerParams(vmem_limit_bytes=24 * 2**20),
        cost_estimate=pl.CostEstimate(
            flops=4 * tok_rows * width * factor, bytes_accessed=4 * tok_rows * width, transcendentals=0
        ),
        name="project",
    )(*operands)


def inverse_pair(both):
    factor = both.shape[0]
    tile = (8, both.shape[1])
    lane = lax.broadcasted_iota(jnp.int32, tile, 1)
    row_at = lax.broadcasted_iota(jnp.int32, tile, 0)
    left_half = lane < factor
    inner = jnp.where(left_half, lane, lane - factor)
    parts = [both[at : at + 8, :] for at in range(0, factor, 8)]

    def column(part, at):
        index = jnp.where(left_half, at, factor + at)
        return jnp.take_along_axis(part, index, axis=1, mode="promise_in_bounds")

    def row(part, at):
        return jnp.broadcast_to(part[at : at + 1, :], tile)

    for k in range(0, factor, 4):
        home, off = divmod(k, 8)
        columns = [[column(part, k + a) for part in parts] for a in range(4)]
        pivot = [[row(columns[b][home], off + a) if a <= b else None for b in range(4)] for a in range(4)]
        p00, p01, p02, p03 = pivot[0]
        _, p11, p12, p13 = pivot[1]
        _, _, p22, p23 = pivot[2]
        p33 = pivot[3][3]
        on_block = (inner >= k) & (inner < k + 4)
        r0, r1, r2, r3 = [
            jnp.where(on_block, jnp.where(inner == k + a, 1.0, 0.0), row(parts[home], off + a)) for a in range(4)
        ]
        scale = 1.0 / (p00 * p11 - p01 * p01)
        m02 = p11 * p02 - p01 * p12
        m03 = p11 * p03 - p01 * p13
        m12 = p00 * p12 - p01 * p02
        m13 = p00 * p13 - p01 * p03
        z0 = p11 * r0 - p01 * r1
        z1 = p00 * r1 - p01 * r0
        s22 = p22 - scale * (p02 * m02 + p12 * m12)
        s23 = p23 - scale * (p02 * m03 + p12 * m13)
        s33 = p33 - scale * (p03 * m03 + p13 * m13)
        t2 = r2 - scale * (p02 * z0 + p12 * z1)
        t3 = r3 - scale * (p03 * z0 + p13 * z1)
        scale_s = 1.0 / (s22 * s33 - s23 * s23)
        w2 = scale_s * (s33 * t2 - s23 * t3)
        w3 = scale_s * (s22 * t3 - s23 * t2)
        w0 = scale * (z0 - (m02 * w2 + m03 * w3))
        w1 = scale * (z1 - (m12 * w2 + m13 * w3))
        solved = (w0, w1, w2, w3)
        for m, part in enumerate(parts):
            change = (columns[0][m] * w0 + columns[1][m] * w1) + (columns[2][m] * w2 + columns[3][m] * w3)
            part = jnp.where(on_block, 0.0, part) - change
            if m == home:
                for a in range(4):
                    part = jnp.where(row_at == off + a, solved[a], part)
            parts[m] = part
    return jnp.concatenate(parts, axis=0)


def precondition_kernel(tok_total, n_terms, *refs):
    terms, (act_t, grad_t, moved) = refs[:n_terms], refs[n_terms:]
    both = terms[0][...]
    for term in terms[1:]:
        both = both + term[...]
    both = unpacked(both)
    factor = both.shape[0]
    lane = lax.broadcasted_iota(jnp.int32, both.shape, 1)
    row_at = lax.broadcasted_iota(jnp.int32, both.shape, 0)
    left_half = lane < factor
    inner = jnp.where(left_half, lane, lane - factor)
    both = both * (1.0 / tok_total) + jnp.where(inner == row_at, DAMP, 0.0)
    both = inverse_pair(both)
    blocks = jnp.concatenate(
        [jnp.where(left_half, both, 0.0), jnp.where(left_half, 0.0, both)], axis=0
    )
    proj_t = jnp.concatenate([act_t[...], grad_t[...]], axis=0)
    moved[...] = jnp.dot(blocks, proj_t, precision=HIGHEST, preferred_element_type=jnp.float32)


def precondition(tok_total, terms, act_t, grad_t):
    factor, tok_rows = act_t.shape
    n_terms = len(terms)
    return pl.pallas_call(
        functools.partial(precondition_kernel, tok_total, n_terms),
        out_shape=jax.ShapeDtypeStruct((2 * factor, tok_rows), jnp.float32),
        in_specs=[pl.BlockSpec(memory_space=pltpu.VMEM)] * (n_terms + 2),
        out_specs=pl.BlockSpec(memory_space=pltpu.VMEM),
        compiler_params=pltpu.CompilerParams(vmem_limit_bytes=24 * 2**20),
        cost_estimate=pl.CostEstimate(
            flops=1600 * factor * factor * tok_rows, bytes_accessed=16 * factor * tok_rows, transcendentals=0
        ),
        name="precondition",
    )(*terms, act_t, grad_t)


def score_kernel(size, n_pieces, moved, *refs):
    queries, (scores, ordered, result, sems) = refs[:n_pieces], refs[n_pieces:]
    factor = moved.shape[0] // 2
    owners = owners_of(lax.axis_index("dp"), size)
    group = 2
    copies = []
    for part, begin in enumerate(range(0, moved.shape[1], TOKENS_AT_ONCE)):
        tokens = slice(begin, begin + TOKENS_AT_ONCE)
        act_side = moved[:factor, tokens]

        def split(first):
            outer = jnp.concatenate(
                [act_side * moved[factor + i : factor + i + 1, tokens] for i in range(first, first + group)], axis=0
            )
            high = outer.astype(jnp.bfloat16)
            low = (outer - high.astype(jnp.float32)).astype(jnp.bfloat16)
            return jnp.concatenate([high, low], axis=0)

        total = None
        later = split(0)
        for first in range(0, factor, group):
            both = later
            if first + group < factor:
                later = split(first + group)
            columns = slice(first * factor, (first + group) * factor)
            values = jnp.concatenate([piece[:, columns] for piece in queries], axis=0)
            term = jnp.dot(jnp.concatenate([values, values], axis=1), both, preferred_element_type=jnp.float32)
            total = term if total is None else total + term
        rows = total.shape[0] // size
        for at, owner in enumerate(owners):
            place = pl.ds(pl.multiple_of(owner * rows, rows), rows)
            ordered[part, place, :] = total[at * rows : (at + 1) * rows, :]
        result[tokens, :] = ordered[part].T
        copies.append(
            pltpu.make_async_copy(
                result.at[pl.ds(begin, TOKENS_AT_ONCE), :], scores.at[pl.ds(begin, TOKENS_AT_ONCE), :], sems.at[part]
            )
        )
        copies[-1].start()
    for copy in copies:
        copy.wait()


def score(size, moved, queries):
    tok_rows = moved.shape[1]
    n_queries = sum(piece.shape[0] for piece in queries)
    n_pieces = len(queries)
    n_parts = tok_rows // TOKENS_AT_ONCE
    return pl.pallas_call(
        functools.partial(score_kernel, size, n_pieces),
        out_shape=jax.ShapeDtypeStruct((tok_rows, n_queries), jnp.float32),
        in_specs=[pl.BlockSpec(memory_space=pltpu.VMEM)] * (1 + n_pieces),
        out_specs=pl.BlockSpec(memory_space=pl.ANY),
        scratch_shapes=[
            pltpu.VMEM((n_parts, n_queries, TOKENS_AT_ONCE), jnp.float32),
            pltpu.VMEM((tok_rows, n_queries), jnp.float32),
            pltpu.SemaphoreType.DMA((n_parts,)),
        ],
        compiler_params=pltpu.CompilerParams(vmem_limit_bytes=32 * 2**20),
        name="score",
    )(moved, *queries)


def gather_stages(size):
    core = 2 if size % 2 == 0 else 1
    rest = size // core
    near = max(d for d in range(1, rest + 1) if rest % d == 0 and d * d <= rest)
    return [(core * near, rest // near), (core, near), (1, core)]


def sum_rounds(size):
    (stride, radix), *_ = gather_stages(size)
    return [(1, stride), (stride, radix)]


def after(value, other):
    return lax.optimization_barrier((value, other))[0]


def partner(digit, radix, shift):
    return digit ^ shift if radix & (radix - 1) == 0 else (digit + shift) % radix


def swapped(value, size, stride, radix, shift):
    perm = []
    for at in range(size):
        digit = at // stride % radix
        perm.append((at, at + (partner(digit, radix, shift) - digit) * stride))
    return lax.ppermute(value, "dp", perm)


def owners_of(me, size):
    owners = [me]
    for at, (stride, radix) in enumerate(gather_stages(size)):
        digit = lax.rem(lax.div(me, stride), radix)
        shifts = [0, *(range(radix - 1, 0, -1) if at == 0 else range(1, radix))]
        back = [shift if radix & (radix - 1) == 0 else (radix - shift) % radix for shift in shifts]
        steps = [(partner(digit, radix, shift) - digit) * stride for shift in back]
        owners = [owner + step for step in steps for owner in owners]
    return owners


def exchanged(held, size, stride, radix, order=None):
    mine = held[0] if len(held) == 1 else jnp.concatenate(held, axis=0)
    return [mine] + [swapped(mine, size, stride, radix, shift) for shift in order or range(1, radix)]


def on_device(acts, grads, proj_act, proj_grad, queries):
    size = lax.axis_size("dp")
    tok_total = acts.shape[0] * size
    far, near, core = gather_stages(size)
    first, second = sum_rounds(size)

    pieces = exchanged([queries], size, *far, order=range(far[1] - 1, 0, -1))
    act_t, grad_t, own = project(acts, grads, proj_act, proj_grad)
    *pieces, own = lax.optimization_barrier((*pieces, own))
    pieces = exchanged(pieces, size, *near)
    own = functools.reduce(jnp.add, exchanged([own], size, *first))
    terms = exchanged([own], size, *second)
    *both, = lax.optimization_barrier((*pieces, *terms))
    pieces, terms = both[: len(pieces)], both[len(pieces) :]
    pieces = exchanged(pieces, size, *core)
    moved = precondition(tok_total, terms, act_t, grad_t)
    return score(size, moved, pieces)


def solution(mesh):
    in_specs = (P(("parts", "dp"), None), P(("parts", "dp"), None), P(), P(), P("dp", None))
    out_specs = P(("parts", "dp"), None)
    return jax.shard_map(
        on_device, mesh=mesh, in_specs=in_specs, out_specs=out_specs, check_vma=False
    )
```

```python
import functools

import jax
import jax.numpy as jnp
from jax import lax
from jax.experimental import pallas as pl
from jax.experimental.pallas import tpu as pltpu
from jax.sharding import PartitionSpec as P

DAMP = 0.1
HIGHEST = lax.Precision.HIGHEST
COPY_ROWS = 256
IN_FLIGHT = 4
TOKENS_AT_ONCE = 256


def places(factor):
    return [lax.broadcasted_iota(jnp.int32, (factor, factor), axis) for axis in (0, 1)]


def packed(act, grad):
    factor = act.shape[0]
    row_at, lane = places(factor)
    mixed = jnp.where(row_at <= lane, act, grad)
    diagonal = jnp.sum(jnp.where(row_at == lane, grad, 0.0), axis=0, keepdims=True)
    last = jnp.broadcast_to(jnp.concatenate([diagonal, diagonal], axis=1), (8, 2 * factor))
    half = factor // 2
    return jnp.concatenate([jnp.concatenate([mixed[:half], mixed[half:]], axis=1), last], axis=0)


def unpacked(value):
    factor = value.shape[1] // 2
    half = factor // 2
    row_at = lax.broadcasted_iota(jnp.int32, (factor, 2 * factor), 0)
    lane = lax.broadcasted_iota(jnp.int32, (factor, 2 * factor), 1)
    left_half = lane < factor
    inner = jnp.where(left_half, lane, lane - factor)
    rolled = pltpu.roll(value[:half], factor, axis=1)
    mixed = jnp.concatenate(
        [
            jnp.where(left_half[:half], value[:half], rolled),
            jnp.where(left_half[:half], rolled, value[:half]),
        ],
        axis=0,
    )
    flipped = jnp.concatenate([mixed, mixed], axis=0).T[:factor]
    diagonal = jnp.broadcast_to(value[half : half + 1], mixed.shape)
    below = jnp.where(row_at > inner, mixed, jnp.where(row_at < inner, flipped, diagonal))
    return jnp.where(left_half, jnp.where(row_at <= inner, mixed, flipped), below)


def project_kernel(
    acts, grads, weight_act, weight_grad, act_t, grad_t, cov, tok_buf, weight_buf, weight_t, tok_sems, weight_sems
):
    width = weight_act.shape[1]
    n_parts = acts.shape[0] // COPY_ROWS
    weight_copies = [
        pltpu.make_async_copy(src, weight_buf.at[at], weight_sems.at[at])
        for at, src in enumerate((weight_act, weight_grad))
    ]
    tok_copies = [
        [
            pltpu.make_async_copy(
                src.at[pl.ds(part * COPY_ROWS, COPY_ROWS), :],
                tok_buf.at[at, pl.ds(part * COPY_ROWS, COPY_ROWS), :],
                tok_sems.at[at, part],
            )
            for part in range(n_parts)
        ]
        for at, src in enumerate((acts, grads))
    ]
    queue = [weight_copies[0], *tok_copies[0], *tok_copies[1]]
    queue.insert(2, weight_copies[1])

    def start_next(many):
        for copy in queue[:many]:
            copy.start()
        del queue[:many]

    def turned(at):
        for first in range(0, width, 512):
            weight_t[at, first : first + 512, :] = weight_buf[at, :, first : first + 512].T

    steps = [(at, part, 1) for at in range(2) for part in range(n_parts)]
    last_act = len(steps) // 2 - 1
    blocks = [[], []]
    grams = [[], []]

    def add_gram(at):
        flipped, plain = [jnp.concatenate(parts, axis=axis) for parts, axis in zip(zip(*blocks[at]), (1, 0))]
        grams[at].append(jnp.dot(flipped, plain, precision=HIGHEST, preferred_element_type=jnp.float32))
        blocks[at].clear()

    start_next(1 + IN_FLIGHT)
    weight_copies[0].wait()
    turned(0)
    for step, (at, part, many) in enumerate(steps):
        for copy in tok_copies[at][part : part + many]:
            copy.wait()
            start_next(1)
        if step == last_act:
            weight_copies[1].wait()
            start_next(1)
        rows = slice(part * COPY_ROWS, (part + many) * COPY_ROWS)
        block = jnp.dot(tok_buf[at, rows, :], weight_t[at], preferred_element_type=jnp.float32)
        if step == last_act:
            turned(1)
        if step == last_act + 1:
            add_gram(0)
        if step == len(steps) - 1:
            add_gram(1)
        flipped = block.T
        (act_t, grad_t)[at][:, rows] = flipped
        blocks[at].append((flipped, block))
    add_gram(1)
    cov[...] = packed(*[functools.reduce(jnp.add, terms) for terms in grams])


def project(acts, grads, proj_act, proj_grad):
    tok_rows, width = acts.shape
    factor = proj_act.shape[1]
    operands = [
        pltpu.with_memory_space_constraint(value, pltpu.HBM) for value in (acts, grads, proj_act.T, proj_grad.T)
    ]
    return pl.pallas_call(
        project_kernel,
        out_shape=(
            jax.ShapeDtypeStruct((factor, tok_rows), jnp.float32),
            jax.ShapeDtypeStruct((factor, tok_rows), jnp.float32),
            jax.ShapeDtypeStruct((factor // 2 + 8, 2 * factor), jnp.float32),
        ),
        in_specs=[pl.BlockSpec(memory_space=pltpu.HBM)] * 4,
        out_specs=[pl.BlockSpec(memory_space=pltpu.VMEM)] * 3,
        scratch_shapes=[
            pltpu.VMEM((2, tok_rows, width), acts.dtype),
            pltpu.VMEM((2, factor, width), proj_act.dtype),
            pltpu.VMEM((2, width, factor), proj_act.dtype),
            pltpu.SemaphoreType.DMA((2, tok_rows // COPY_ROWS)),
            pltpu.SemaphoreType.DMA((2,)),
        ],
        compiler_params=pltpu.CompilerParams(vmem_limit_bytes=24 * 2**20),
        cost_estimate=pl.CostEstimate(
            flops=4 * tok_rows * width * factor, bytes_accessed=4 * tok_rows * width, transcendentals=0
        ),
        name="project",
    )(*operands)


def inverse_pair(both):
    factor = both.shape[0]
    tile = (8, both.shape[1])
    lane = lax.broadcasted_iota(jnp.int32, tile, 1)
    row_at = lax.broadcasted_iota(jnp.int32, tile, 0)
    left_half = lane < factor
    inner = jnp.where(left_half, lane, lane - factor)
    parts = [both[at : at + 8, :] for at in range(0, factor, 8)]

    def column(part, at):
        index = jnp.where(left_half, at, factor + at)
        return jnp.take_along_axis(part, index, axis=1, mode="promise_in_bounds")

    def row(part, at):
        return jnp.broadcast_to(part[at : at + 1, :], tile)

    for k in range(0, factor, 4):
        home, off = divmod(k, 8)
        columns = [[column(part, k + a) for part in parts] for a in range(4)]
        pivot = [[row(columns[b][home], off + a) if a <= b else None for b in range(4)] for a in range(4)]
        p00, p01, p02, p03 = pivot[0]
        _, p11, p12, p13 = pivot[1]
        _, _, p22, p23 = pivot[2]
        p33 = pivot[3][3]
        on_block = (inner >= k) & (inner < k + 4)
        r0, r1, r2, r3 = [
            jnp.where(on_block, jnp.where(inner == k + a, 1.0, 0.0), row(parts[home], off + a)) for a in range(4)
        ]
        scale = 1.0 / (p00 * p11 - p01 * p01)
        m02 = p11 * p02 - p01 * p12
        m03 = p11 * p03 - p01 * p13
        m12 = p00 * p12 - p01 * p02
        m13 = p00 * p13 - p01 * p03
        z0 = p11 * r0 - p01 * r1
        z1 = p00 * r1 - p01 * r0
        s22 = p22 - scale * (p02 * m02 + p12 * m12)
        s23 = p23 - scale * (p02 * m03 + p12 * m13)
        s33 = p33 - scale * (p03 * m03 + p13 * m13)
        t2 = r2 - scale * (p02 * z0 + p12 * z1)
        t3 = r3 - scale * (p03 * z0 + p13 * z1)
        scale_s = 1.0 / (s22 * s33 - s23 * s23)
        w2 = scale_s * (s33 * t2 - s23 * t3)
        w3 = scale_s * (s22 * t3 - s23 * t2)
        w0 = scale * (z0 - (m02 * w2 + m03 * w3))
        w1 = scale * (z1 - (m12 * w2 + m13 * w3))
        solved = (w0, w1, w2, w3)
        for m, part in enumerate(parts):
            change = (columns[0][m] * w0 + columns[1][m] * w1) + (columns[2][m] * w2 + columns[3][m] * w3)
            part = jnp.where(on_block, 0.0, part) - change
            if m == home:
                for a in range(4):
                    part = jnp.where(row_at == off + a, solved[a], part)
            parts[m] = part
    return jnp.concatenate(parts, axis=0)


def precondition_kernel(tok_total, n_terms, *refs):
    terms, (act_t, grad_t, moved) = refs[:n_terms], refs[n_terms:]
    both = terms[0][...]
    for term in terms[1:]:
        both = both + term[...]
    both = unpacked(both)
    factor = both.shape[0]
    lane = lax.broadcasted_iota(jnp.int32, both.shape, 1)
    row_at = lax.broadcasted_iota(jnp.int32, both.shape, 0)
    left_half = lane < factor
    inner = jnp.where(left_half, lane, lane - factor)
    both = both * (1.0 / tok_total) + jnp.where(inner == row_at, DAMP, 0.0)
    both = inverse_pair(both)
    blocks = jnp.concatenate(
        [jnp.where(left_half, both, 0.0), jnp.where(left_half, 0.0, both)], axis=0
    )
    proj_t = jnp.concatenate([act_t[...], grad_t[...]], axis=0)
    moved[...] = jnp.dot(blocks, proj_t, precision=HIGHEST, preferred_element_type=jnp.float32)


def precondition(tok_total, terms, act_t, grad_t):
    factor, tok_rows = act_t.shape
    n_terms = len(terms)
    return pl.pallas_call(
        functools.partial(precondition_kernel, tok_total, n_terms),
        out_shape=jax.ShapeDtypeStruct((2 * factor, tok_rows), jnp.float32),
        in_specs=[pl.BlockSpec(memory_space=pltpu.VMEM)] * (n_terms + 2),
        out_specs=pl.BlockSpec(memory_space=pltpu.VMEM),
        compiler_params=pltpu.CompilerParams(vmem_limit_bytes=24 * 2**20),
        cost_estimate=pl.CostEstimate(
            flops=1600 * factor * factor * tok_rows, bytes_accessed=16 * factor * tok_rows, transcendentals=0
        ),
        name="precondition",
    )(*terms, act_t, grad_t)


def score_kernel(size, n_pieces, moved, *refs):
    queries, (scores, ordered, result, sems) = refs[:n_pieces], refs[n_pieces:]
    factor = moved.shape[0] // 2
    owners = owners_of(lax.axis_index("dp"), size)
    group = 2
    copies = []
    for part, begin in enumerate(range(0, moved.shape[1], TOKENS_AT_ONCE)):
        tokens = slice(begin, begin + TOKENS_AT_ONCE)
        act_side = moved[:factor, tokens]

        def split(first):
            outer = jnp.concatenate(
                [act_side * moved[factor + i : factor + i + 1, tokens] for i in range(first, first + group)], axis=0
            )
            high = outer.astype(jnp.bfloat16)
            low = (outer - high.astype(jnp.float32)).astype(jnp.bfloat16)
            return jnp.concatenate([high, low], axis=0)

        total = None
        later = split(0)
        for first in range(0, factor, group):
            both = later
            if first + group < factor:
                later = split(first + group)
            columns = slice(first * factor, (first + group) * factor)
            values = jnp.concatenate([piece[:, columns] for piece in queries], axis=0)
            term = jnp.dot(jnp.concatenate([values, values], axis=1), both, preferred_element_type=jnp.float32)
            total = term if total is None else total + term
        rows = total.shape[0] // size
        for at, owner in enumerate(owners):
            place = pl.ds(pl.multiple_of(owner * rows, rows), rows)
            ordered[part, place, :] = total[at * rows : (at + 1) * rows, :]
        result[tokens, :] = ordered[part].T
        copies.append(
            pltpu.make_async_copy(
                result.at[pl.ds(begin, TOKENS_AT_ONCE), :], scores.at[pl.ds(begin, TOKENS_AT_ONCE), :], sems.at[part]
            )
        )
        copies[-1].start()
    for copy in copies:
        copy.wait()


def score(size, moved, queries):
    tok_rows = moved.shape[1]
    n_queries = sum(piece.shape[0] for piece in queries)
    n_pieces = len(queries)
    n_parts = tok_rows // TOKENS_AT_ONCE
    return pl.pallas_call(
        functools.partial(score_kernel, size, n_pieces),
        out_shape=jax.ShapeDtypeStruct((tok_rows, n_queries), jnp.float32),
        in_specs=[pl.BlockSpec(memory_space=pltpu.VMEM)] * (1 + n_pieces),
        out_specs=pl.BlockSpec(memory_space=pl.ANY),
        scratch_shapes=[
            pltpu.VMEM((n_parts, n_queries, TOKENS_AT_ONCE), jnp.float32),
            pltpu.VMEM((tok_rows, n_queries), jnp.float32),
            pltpu.SemaphoreType.DMA((n_parts,)),
        ],
        compiler_params=pltpu.CompilerParams(vmem_limit_bytes=32 * 2**20),
        name="score",
    )(moved, *queries)


def gather_stages(size):
    core = 2 if size % 2 == 0 else 1
    rest = size // core
    near = max(d for d in range(1, rest + 1) if rest % d == 0 and d * d <= rest)
    return [(core * near, rest // near), (core, near), (1, core)]


def sum_rounds(size):
    (stride, radix), *_ = gather_stages(size)
    return [(1, stride), (stride, radix)]


def after(value, other):
    return lax.optimization_barrier((value, other))[0]


def partner(digit, radix, shift):
    return digit ^ shift if radix & (radix - 1) == 0 else (digit + shift) % radix


def swapped(value, size, stride, radix, shift):
    perm = []
    for at in range(size):
        digit = at // stride % radix
        perm.append((at, at + (partner(digit, radix, shift) - digit) * stride))
    return lax.ppermute(value, "dp", perm)


def owners_of(me, size):
    owners = [me]
    for at, (stride, radix) in enumerate(gather_stages(size)):
        digit = lax.rem(lax.div(me, stride), radix)
        shifts = [0, *(range(radix - 1, 0, -1) if at == 0 else range(1, radix))]
        back = [shift if radix & (radix - 1) == 0 else (radix - shift) % radix for shift in shifts]
        steps = [(partner(digit, radix, shift) - digit) * stride for shift in back]
        owners = [owner + step for step in steps for owner in owners]
    return owners


def exchanged(held, size, stride, radix, order=None):
    mine = held[0] if len(held) == 1 else jnp.concatenate(held, axis=0)
    return [mine] + [swapped(mine, size, stride, radix, shift) for shift in order or range(1, radix)]


def on_device(acts, grads, proj_act, proj_grad, queries):
    size = lax.axis_size("dp")
    tok_total = acts.shape[0] * size
    far, near, core = gather_stages(size)
    first, second = sum_rounds(size)

    pieces = exchanged([queries], size, *far, order=range(far[1] - 1, 0, -1))
    act_t, grad_t, own = project(acts, grads, proj_act, proj_grad)
    *pieces, own = lax.optimization_barrier((*pieces, own))
    pieces = exchanged(pieces, size, *near)
    own = functools.reduce(jnp.add, exchanged([own], size, *first))
    terms = exchanged([own], size, *second)
    *both, = lax.optimization_barrier((*pieces, *terms))
    pieces, terms = both[: len(pieces)], both[len(pieces) :]
    pieces = exchanged(pieces, size, *core)
    moved = precondition(tok_total, terms, act_t, grad_t)
    return score(size, moved, pieces)


def solution(mesh):
    in_specs = (P(("parts", "dp"), None), P(("parts", "dp"), None), P(), P(), P("dp", None))
    out_specs = P(("parts", "dp"), None)
    return jax.shard_map(
        on_device, mesh=mesh, in_specs=in_specs, out_specs=out_specs, check_vma=False
    )
```

```python
import functools

import jax
import jax.numpy as jnp
from jax import lax
from jax.experimental import pallas as pl
from jax.experimental.pallas import tpu as pltpu
from jax.sharding import PartitionSpec as P

DAMP = 0.1
HIGHEST = lax.Precision.HIGHEST
COPY_ROWS = 256
IN_FLIGHT = 5
TOKENS_AT_ONCE = 256


def places(factor):
    return [lax.broadcasted_iota(jnp.int32, (factor, factor), axis) for axis in (0, 1)]


def packed(act, grad):
    factor = act.shape[0]
    row_at, lane = places(factor)
    mixed = jnp.where(row_at <= lane, act, grad)
    diagonal = jnp.sum(jnp.where(row_at == lane, grad, 0.0), axis=0, keepdims=True)
    last = jnp.broadcast_to(jnp.concatenate([diagonal, diagonal], axis=1), (8, 2 * factor))
    half = factor // 2
    return jnp.concatenate([jnp.concatenate([mixed[:half], mixed[half:]], axis=1), last], axis=0)


def unpacked(value):
    factor = value.shape[1] // 2
    half = factor // 2
    row_at = lax.broadcasted_iota(jnp.int32, (factor, 2 * factor), 0)
    lane = lax.broadcasted_iota(jnp.int32, (factor, 2 * factor), 1)
    left_half = lane < factor
    inner = jnp.where(left_half, lane, lane - factor)
    rolled = pltpu.roll(value[:half], factor, axis=1)
    mixed = jnp.concatenate(
        [
            jnp.where(left_half[:half], value[:half], rolled),
            jnp.where(left_half[:half], rolled, value[:half]),
        ],
        axis=0,
    )
    flipped = jnp.concatenate([mixed, mixed], axis=0).T[:factor]
    diagonal = jnp.broadcast_to(value[half : half + 1], mixed.shape)
    below = jnp.where(row_at > inner, mixed, jnp.where(row_at < inner, flipped, diagonal))
    return jnp.where(left_half, jnp.where(row_at <= inner, mixed, flipped), below)


def project_kernel(
    acts, grads, weight_act, weight_grad, act_t, grad_t, cov, tok_buf, weight_buf, weight_t, tok_sems, weight_sems
):
    width = weight_act.shape[1]
    n_parts = acts.shape[0] // COPY_ROWS
    weight_copies = [
        pltpu.make_async_copy(src, weight_buf.at[at], weight_sems.at[at])
        for at, src in enumerate((weight_act, weight_grad))
    ]
    tok_copies = [
        [
            pltpu.make_async_copy(
                src.at[pl.ds(part * COPY_ROWS, COPY_ROWS), :],
                tok_buf.at[at, pl.ds(part * COPY_ROWS, COPY_ROWS), :],
                tok_sems.at[at, part],
            )
            for part in range(n_parts)
        ]
        for at, src in enumerate((acts, grads))
    ]
    queue = [weight_copies[0], *tok_copies[0], *tok_copies[1]]
    queue.insert(2, weight_copies[1])

    def start_next(many):
        for copy in queue[:many]:
            copy.start()
        del queue[:many]

    def turned(at):
        for first in range(0, width, 512):
            weight_t[at, first : first + 512, :] = weight_buf[at, :, first : first + 512].T

    steps = [(at, part, 1) for at in range(2) for part in range(n_parts)]
    last_act = len(steps) // 2 - 1
    blocks = [[], []]
    grams = [[], []]

    def add_gram(at):
        flipped, plain = [jnp.concatenate(parts, axis=axis) for parts, axis in zip(zip(*blocks[at]), (1, 0))]
        grams[at].append(jnp.dot(flipped, plain, precision=HIGHEST, preferred_element_type=jnp.float32))
        blocks[at].clear()

    start_next(1 + IN_FLIGHT)
    weight_copies[0].wait()
    turned(0)
    for step, (at, part, many) in enumerate(steps):
        for copy in tok_copies[at][part : part + many]:
            copy.wait()
            start_next(1)
        if step == last_act:
            weight_copies[1].wait()
            start_next(1)
        rows = slice(part * COPY_ROWS, (part + many) * COPY_ROWS)
        block = jnp.dot(tok_buf[at, rows, :], weight_t[at], preferred_element_type=jnp.float32)
        if step == last_act:
            turned(1)
        if step == last_act + 1:
            add_gram(0)
        if step == len(steps) - 1:
            add_gram(1)
        flipped = block.T
        (act_t, grad_t)[at][:, rows] = flipped
        blocks[at].append((flipped, block))
    add_gram(1)
    cov[...] = packed(*[functools.reduce(jnp.add, terms) for terms in grams])


def project(acts, grads, proj_act, proj_grad):
    tok_rows, width = acts.shape
    factor = proj_act.shape[1]
    operands = [
        pltpu.with_memory_space_constraint(value, pltpu.HBM) for value in (acts, grads, proj_act.T, proj_grad.T)
    ]
    return pl.pallas_call(
        project_kernel,
        out_shape=(
            jax.ShapeDtypeStruct((factor, tok_rows), jnp.float32),
            jax.ShapeDtypeStruct((factor, tok_rows), jnp.float32),
            jax.ShapeDtypeStruct((factor // 2 + 8, 2 * factor), jnp.float32),
        ),
        in_specs=[pl.BlockSpec(memory_space=pltpu.HBM)] * 4,
        out_specs=[pl.BlockSpec(memory_space=pltpu.VMEM)] * 3,
        scratch_shapes=[
            pltpu.VMEM((2, tok_rows, width), acts.dtype),
            pltpu.VMEM((2, factor, width), proj_act.dtype),
            pltpu.VMEM((2, width, factor), proj_act.dtype),
            pltpu.SemaphoreType.DMA((2, tok_rows // COPY_ROWS)),
            pltpu.SemaphoreType.DMA((2,)),
        ],
        compiler_params=pltpu.CompilerParams(vmem_limit_bytes=24 * 2**20),
        cost_estimate=pl.CostEstimate(
            flops=4 * tok_rows * width * factor, bytes_accessed=4 * tok_rows * width, transcendentals=0
        ),
        name="project",
    )(*operands)


def inverse_pair(both):
    factor = both.shape[0]
    tile = (8, both.shape[1])
    lane = lax.broadcasted_iota(jnp.int32, tile, 1)
    row_at = lax.broadcasted_iota(jnp.int32, tile, 0)
    left_half = lane < factor
    inner = jnp.where(left_half, lane, lane - factor)
    parts = [both[at : at + 8, :] for at in range(0, factor, 8)]

    def column(part, at):
        index = jnp.where(left_half, at, factor + at)
        return jnp.take_along_axis(part, index, axis=1, mode="promise_in_bounds")

    def row(part, at):
        return jnp.broadcast_to(part[at : at + 1, :], tile)

    for k in range(0, factor, 4):
        home, off = divmod(k, 8)
        columns = [[column(part, k + a) for part in parts] for a in range(4)]
        pivot = [[row(columns[b][home], off + a) if a <= b else None for b in range(4)] for a in range(4)]
        p00, p01, p02, p03 = pivot[0]
        _, p11, p12, p13 = pivot[1]
        _, _, p22, p23 = pivot[2]
        p33 = pivot[3][3]
        on_block = (inner >= k) & (inner < k + 4)
        r0, r1, r2, r3 = [
            jnp.where(on_block, jnp.where(inner == k + a, 1.0, 0.0), row(parts[home], off + a)) for a in range(4)
        ]
        scale = 1.0 / (p00 * p11 - p01 * p01)
        m02 = p11 * p02 - p01 * p12
        m03 = p11 * p03 - p01 * p13
        m12 = p00 * p12 - p01 * p02
        m13 = p00 * p13 - p01 * p03
        z0 = p11 * r0 - p01 * r1
        z1 = p00 * r1 - p01 * r0
        s22 = p22 - scale * (p02 * m02 + p12 * m12)
        s23 = p23 - scale * (p02 * m03 + p12 * m13)
        s33 = p33 - scale * (p03 * m03 + p13 * m13)
        t2 = r2 - scale * (p02 * z0 + p12 * z1)
        t3 = r3 - scale * (p03 * z0 + p13 * z1)
        scale_s = 1.0 / (s22 * s33 - s23 * s23)
        w2 = scale_s * (s33 * t2 - s23 * t3)
        w3 = scale_s * (s22 * t3 - s23 * t2)
        w0 = scale * (z0 - (m02 * w2 + m03 * w3))
        w1 = scale * (z1 - (m12 * w2 + m13 * w3))
        solved = (w0, w1, w2, w3)
        for m, part in enumerate(parts):
            change = (columns[0][m] * w0 + columns[1][m] * w1) + (columns[2][m] * w2 + columns[3][m] * w3)
            part = jnp.where(on_block, 0.0, part) - change
            if m == home:
                for a in range(4):
                    part = jnp.where(row_at == off + a, solved[a], part)
            parts[m] = part
    return jnp.concatenate(parts, axis=0)


def precondition_kernel(tok_total, n_terms, *refs):
    terms, (act_t, grad_t, moved) = refs[:n_terms], refs[n_terms:]
    both = terms[0][...]
    for term in terms[1:]:
        both = both + term[...]
    both = unpacked(both)
    factor = both.shape[0]
    lane = lax.broadcasted_iota(jnp.int32, both.shape, 1)
    row_at = lax.broadcasted_iota(jnp.int32, both.shape, 0)
    left_half = lane < factor
    inner = jnp.where(left_half, lane, lane - factor)
    both = both * (1.0 / tok_total) + jnp.where(inner == row_at, DAMP, 0.0)
    both = inverse_pair(both)
    blocks = jnp.concatenate(
        [jnp.where(left_half, both, 0.0), jnp.where(left_half, 0.0, both)], axis=0
    )
    proj_t = jnp.concatenate([act_t[...], grad_t[...]], axis=0)
    moved[...] = jnp.dot(blocks, proj_t, precision=HIGHEST, preferred_element_type=jnp.float32)


def precondition(tok_total, terms, act_t, grad_t):
    factor, tok_rows = act_t.shape
    n_terms = len(terms)
    return pl.pallas_call(
        functools.partial(precondition_kernel, tok_total, n_terms),
        out_shape=jax.ShapeDtypeStruct((2 * factor, tok_rows), jnp.float32),
        in_specs=[pl.BlockSpec(memory_space=pltpu.VMEM)] * (n_terms + 2),
        out_specs=pl.BlockSpec(memory_space=pltpu.VMEM),
        compiler_params=pltpu.CompilerParams(vmem_limit_bytes=24 * 2**20),
        cost_estimate=pl.CostEstimate(
            flops=1600 * factor * factor * tok_rows, bytes_accessed=16 * factor * tok_rows, transcendentals=0
        ),
        name="precondition",
    )(*terms, act_t, grad_t)


def score_kernel(size, n_pieces, moved, *refs):
    queries, (scores, ordered, result, sems) = refs[:n_pieces], refs[n_pieces:]
    factor = moved.shape[0] // 2
    owners = owners_of(lax.axis_index("dp"), size)
    group = 2
    copies = []
    for part, begin in enumerate(range(0, moved.shape[1], TOKENS_AT_ONCE)):
        tokens = slice(begin, begin + TOKENS_AT_ONCE)
        act_side = moved[:factor, tokens]

        def split(first):
            outer = jnp.concatenate(
                [act_side * moved[factor + i : factor + i + 1, tokens] for i in range(first, first + group)], axis=0
            )
            high = outer.astype(jnp.bfloat16)
            low = (outer - high.astype(jnp.float32)).astype(jnp.bfloat16)
            return jnp.concatenate([high, low], axis=0)

        total = None
        later = split(0)
        for first in range(0, factor, group):
            both = later
            if first + group < factor:
                later = split(first + group)
            columns = slice(first * factor, (first + group) * factor)
            values = jnp.concatenate([piece[:, columns] for piece in queries], axis=0)
            term = jnp.dot(jnp.concatenate([values, values], axis=1), both, preferred_element_type=jnp.float32)
            total = term if total is None else total + term
        rows = total.shape[0] // size
        for at, owner in enumerate(owners):
            place = pl.ds(pl.multiple_of(owner * rows, rows), rows)
            ordered[part, place, :] = total[at * rows : (at + 1) * rows, :]
        result[tokens, :] = ordered[part].T
        copies.append(
            pltpu.make_async_copy(
                result.at[pl.ds(begin, TOKENS_AT_ONCE), :], scores.at[pl.ds(begin, TOKENS_AT_ONCE), :], sems.at[part]
            )
        )
        copies[-1].start()
    for copy in copies:
        copy.wait()


def score(size, moved, queries):
    tok_rows = moved.shape[1]
    n_queries = sum(piece.shape[0] for piece in queries)
    n_pieces = len(queries)
    n_parts = tok_rows // TOKENS_AT_ONCE
    return pl.pallas_call(
        functools.partial(score_kernel, size, n_pieces),
        out_shape=jax.ShapeDtypeStruct((tok_rows, n_queries), jnp.float32),
        in_specs=[pl.BlockSpec(memory_space=pltpu.VMEM)] * (1 + n_pieces),
        out_specs=pl.BlockSpec(memory_space=pl.ANY),
        scratch_shapes=[
            pltpu.VMEM((n_parts, n_queries, TOKENS_AT_ONCE), jnp.float32),
            pltpu.VMEM((tok_rows, n_queries), jnp.float32),
            pltpu.SemaphoreType.DMA((n_parts,)),
        ],
        compiler_params=pltpu.CompilerParams(vmem_limit_bytes=32 * 2**20),
        name="score",
    )(moved, *queries)


def gather_stages(size):
    core = 2 if size % 2 == 0 else 1
    rest = size // core
    near = max(d for d in range(1, rest + 1) if rest % d == 0 and d * d <= rest)
    return [(core * near, rest // near), (core, near), (1, core)]


def sum_rounds(size):
    (stride, radix), *_ = gather_stages(size)
    return [(1, stride), (stride, radix)]


def after(value, other):
    return lax.optimization_barrier((value, other))[0]


def partner(digit, radix, shift):
    return digit ^ shift if radix & (radix - 1) == 0 else (digit + shift) % radix


def swapped(value, size, stride, radix, shift):
    perm = []
    for at in range(size):
        digit = at // stride % radix
        perm.append((at, at + (partner(digit, radix, shift) - digit) * stride))
    return lax.ppermute(value, "dp", perm)


def owners_of(me, size):
    owners = [me]
    for at, (stride, radix) in enumerate(gather_stages(size)):
        digit = lax.rem(lax.div(me, stride), radix)
        shifts = [0, *(range(radix - 1, 0, -1) if at == 0 else range(1, radix))]
        back = [shift if radix & (radix - 1) == 0 else (radix - shift) % radix for shift in shifts]
        steps = [(partner(digit, radix, shift) - digit) * stride for shift in back]
        owners = [owner + step for step in steps for owner in owners]
    return owners


def exchanged(held, size, stride, radix, order=None):
    mine = held[0] if len(held) == 1 else jnp.concatenate(held, axis=0)
    return [mine] + [swapped(mine, size, stride, radix, shift) for shift in order or range(1, radix)]


def on_device(acts, grads, proj_act, proj_grad, queries):
    size = lax.axis_size("dp")
    tok_total = acts.shape[0] * size
    far, near, core = gather_stages(size)
    first, second = sum_rounds(size)

    pieces = exchanged([queries], size, *far, order=range(far[1] - 1, 0, -1))
    act_t, grad_t, own = project(acts, grads, proj_act, proj_grad)
    *pieces, own = lax.optimization_barrier((*pieces, own))
    pieces = exchanged(pieces, size, *near)
    own = functools.reduce(jnp.add, exchanged([own], size, *first))
    terms = exchanged([own], size, *second)
    *both, = lax.optimization_barrier((*pieces, *terms))
    pieces, terms = both[: len(pieces)], both[len(pieces) :]
    pieces = exchanged(pieces, size, *core)
    moved = precondition(tok_total, terms, act_t, grad_t)
    return score(size, moved, pieces)


def solution(mesh):
    in_specs = (P(("parts", "dp"), None), P(("parts", "dp"), None), P(), P(), P("dp", None))
    out_specs = P(("parts", "dp"), None)
    return jax.shard_map(
        on_device, mesh=mesh, in_specs=in_specs, out_specs=out_specs, check_vma=False
    )
```
